32 devices in a mesh: rows: 2 (over x), frames: 16 (over z, y, core).
Axes of the slice: x: 2, y: 2, z: 4, core: 2. Of those that a mesh axis runs over, the one named last changes fastest.
Arguments:
- features: bfloat16 [4, 4096, 512], P('rows', 'frames'), may hold values from -16 to 16
- lengths: int32 [4, 17], replicated, may hold values from 0 to 4096, as said below
- windows: int32 [4], P('rows'), may hold values from 64 to 128, as said below
- feed_in: bfloat16 [2, 512, 2048], replicated, may hold values from -0.25 to 0.25
- feed_in_bias: float32 [2, 2048], replicated, may hold values from -1.75 to 1.75
- feed_out: bfloat16 [2, 2048, 512], replicated, may hold values from -0.125 to 0.125
- attend_in: bfloat16 [512, 1536], replicated, may hold values from -0.25 to 0.25
- attend_out: bfloat16 [512, 512], replicated, may hold values from -1 to 1
- position_proj: bfloat16 [512, 512], replicated, may hold values from -0.375 to 0.375
- convolve_in: bfloat16 [512, 1024], replicated, may hold values from -0.25 to 0.25
- convolve_out: bfloat16 [512, 512], replicated, may hold values from -0.25 to 0.25
- depthwise: float32 [9, 512], replicated, may hold values from -2 to 2
- norm_gain: float32 [6, 512], replicated, may hold values from 0.25 to 1.75
- norm_shift: float32 [6, 512], replicated, may hold values from -1.25 to 1.25
- biases: float32 [10, 512], replicated, may hold values from -1.75 to 1.75
- cotangent: bfloat16 [4, 4096, 512], P('rows', 'frames'), may hold values from -6 to 6
Outputs:
- out: bfloat16 [4, 4096, 512], P('rows', 'frames')
- grad_features: float32 [4, 4096, 512], P('rows', 'frames')
- grad_feed_in: float32 [2, 512, 2048], P(None, None, 'frames')
- grad_feed_in_bias: float32 [2, 2048], P(None, 'frames')
- grad_feed_out: float32 [2, 2048, 512], P(None, 'frames')
- grad_attend_in: float32 [512, 1536], P('frames')
- grad_attend_out: float32 [512, 512], P('frames')
- grad_position_proj: float32 [512, 512], P('frames')
- grad_convolve_in: float32 [512, 1024], P('frames')
- grad_convolve_out: float32 [512, 512], P('frames')
- grad_depthwise: float32 [9, 512], P(None, 'frames')
- grad_norm_gain: float32 [6, 512], P(None, 'frames')
- grad_norm_shift: float32 [6, 512], P(None, 'frames')
- grad_biases: float32 [10, 512], P(None, 'frames')
The draws below stay inside these ranges and needn't reach their ends.
Inputs may be any that keep to these rules, and one draw needn't show every extreme that they name: Row r holds utterances of lengths[r, 0], lengths[r, 1], ... frames one after the other from frame 0, then zeros; the frames after their sum are padding. In each aligned block of 2 rows one row holds a single utterance of 4096 frames; in the other rows every utterance but the last has 256 to 1024 frames, and fewer than 256 frames are padding. `windows`: some row's reach is 128.
All inputs are finite; a program needn't handle non-finite values.
Results may differ from the reference program's by a relative error of at most 0.035.
Values may be sent and summed in bfloat16 or wider, within the bound.
No kernel may reach another device: no remote copies, remote signals or barrier semaphores. Data moves between devices by JAX's collectives and lax.ppermute only.
A program may use at most 192 MiB of HBM per device.

```python
import math
import jax
import jax.numpy as jnp
from jax import lax

D = 512
H = 8
DH = 64
FF = 2048
KERNEL = 9
WIN = 128
FR_DEV = 256
ROWS_DEV = 2
MINLEN = 256
MAXLEN = 1024
ROWS = 4
ROW_LEN = 4096
SEGS = 17


def draw_features(key, part):
    key = jax.random.fold_in(key, 11)
    noise_key, common_key = jax.random.split(key, 2)
    where = jnp.arange(ROW_LEN, dtype=jnp.int32).astype(jnp.float32) / ROW_LEN
    common = jax.random.truncated_normal(common_key, -4.0, 4.0, (ROWS, 1, D))
    noise = jax.random.truncated_normal(noise_key, -4.0, 4.0, (ROWS, ROW_LEN, D))
    ramp = 1.5 * where
    return (noise + ramp[None, :, None] * common).astype(jnp.bfloat16)


def draw_lengths(key, part):
    key = jax.random.fold_in(key, 23)
    pick_key, piece_key, pad_key = jax.random.split(key, 3)
    pieces = jax.random.randint(piece_key, (ROWS, SEGS), MINLEN, MAXLEN + 1, dtype=jnp.int32)
    padding = jax.random.randint(pad_key, (ROWS, 1), 0, FR_DEV, dtype=jnp.int32)
    chosen = jax.random.randint(pick_key, (ROWS // ROWS_DEV, 1), 0, ROWS_DEV, dtype=jnp.int32)
    longest = (jnp.arange(ROWS_DEV, dtype=jnp.int32)[None, :] == chosen).reshape(ROWS, 1)
    used = ROW_LEN - padding
    starts = jnp.cumsum(pieces, axis=1, dtype=jnp.int32) - pieces
    short = jnp.minimum(jnp.maximum(used - starts, 0), pieces)
    single = jnp.where(jnp.arange(SEGS, dtype=jnp.int32)[None, :] == 0, ROW_LEN, 0)
    return jnp.where(longest, single, short).astype(jnp.int32)


def draw_windows(key, part):
    key = jax.random.fold_in(key, 37)
    pick_key, value_key = jax.random.split(key, 2)
    values = jax.random.randint(value_key, (ROWS,), WIN // 2, WIN + 1, dtype=jnp.int32)
    widest = jax.random.randint(pick_key, (), 0, ROWS, dtype=jnp.int32)
    return jnp.where(jnp.arange(ROWS, dtype=jnp.int32) == widest, WIN, values).astype(jnp.int32)


def level_of(own_key, shape, cuts, smallest, top_value):
    loudness = 1.0
    for dim, blocks in cuts:
        steps = jax.random.uniform(jax.random.fold_in(jax.random.fold_in(own_key, 6), dim), (blocks,), jnp.float32, smallest / len(cuts), top_value / len(cuts))
        loudness = loudness * jnp.repeat(jnp.exp(steps), shape[dim] // blocks).reshape((-1,) + (1,) * (len(shape) - 1 - dim))
    return loudness


def normal_values(key, dims, scale, most, shards=(), kind=jnp.bfloat16):
    loudness = level_of(key, dims, shards, -0.22, 0.18) if shards else 1.0
    array = jax.random.normal(key, dims, jnp.float32) * scale * loudness
    return jnp.minimum(jnp.maximum(array, -most), most).astype(kind)


def setup_inputs(seed: int = 0) -> dict:
    arg_keys = jax.random.split(jax.random.key(seed), 17)
    features = draw_features(jax.random.fold_in(arg_keys[16], 71), 0)
    lengths = draw_lengths(jax.random.fold_in(arg_keys[16], 71), 0)
    windows = draw_windows(jax.random.fold_in(arg_keys[16], 71), 0)
    feed_in = normal_values(arg_keys[3], (2, D, FF), D ** -0.5, 0.25)
    feed_in_bias = normal_values(arg_keys[4], (2, FF), 0.3, 1.75, (), jnp.float32)
    feed_out = normal_values(arg_keys[5], (2, FF, D), FF ** -0.5, 0.125)
    attend_in = normal_values(arg_keys[6], (D, 3 * D), D ** -0.5, 0.25)
    attend_out = normal_values(arg_keys[7], (D, D), (D // 16) ** -0.5, 1.0)
    position_proj = normal_values(arg_keys[8], (D, D), (D // 2) ** -0.5, 0.375)
    convolve_in = normal_values(arg_keys[9], (D, 2 * D), D ** -0.5, 0.25)
    convolve_out = normal_values(arg_keys[10], (D, D), D ** -0.5, 0.25)
    depthwise = normal_values(arg_keys[11], (KERNEL, D), KERNEL ** -0.5, 2.0, (), jnp.float32)
    norm_gain = jnp.clip(1.0 + 0.15 * jax.random.normal(arg_keys[12], (6, D), jnp.float32), 0.25, 1.75)
    norm_shift = normal_values(arg_keys[13], (6, D), 0.2, 1.25, (), jnp.float32)
    biases = normal_values(arg_keys[14], (10, D), 0.3, 1.75, (), jnp.float32)
    cotangent = normal_values(arg_keys[15], (ROWS, ROW_LEN, D), 1.0, 6.0, ((0, 2), (1, 16)))
    return {"features": features, "lengths": lengths, "windows": windows, "feed_in": feed_in, "feed_in_bias": feed_in_bias, "feed_out": feed_out, "attend_in": attend_in, "attend_out": attend_out, "position_proj": position_proj, "convolve_in": convolve_in, "convolve_out": convolve_out, "depthwise": depthwise, "norm_gain": norm_gain, "norm_shift": norm_shift, "biases": biases, "cotangent": cotangent}


@jax.custom_vjp
def low(v):
    return lax.optimization_barrier(v.astype(jnp.bfloat16)).astype(jnp.float32)

@jax.custom_vjp
def low_back(v):
    return v

def low_keep(v):
    return (low(v), None)

def low_pass(kept, grad):
    return (grad,)

def back_keep(v):
    return (v, None)

def back_low(kept, grad):
    return (low(grad),)
low.defvjp(low_keep, low_pass)
low_back.defvjp(back_keep, back_low)
eps_norm = 1e-05
negative = -1e+30
highest = lax.Precision.HIGHEST

def product(left, right):
    return jnp.matmul(left, right, precision=highest)

def layer_norm(values, gain, shift):
    centered = values - lax.optimization_barrier(jnp.mean(values, axis=-1, keepdims=True))
    spread = lax.optimization_barrier(jnp.mean(centered * centered, axis=-1, keepdims=True))
    return centered * lax.rsqrt(spread + eps_norm) * gain + shift

def position_table(width, model):
    offsets = (jnp.arange(2 * width + 1, dtype=jnp.int32) - width).astype(jnp.float32)
    rates = jnp.exp(jnp.arange(model // 2, dtype=jnp.int32).astype(jnp.float32) * (-2.0 * math.log(10000.0) / model))
    angles = offsets[:, None] * rates[None, :]
    return jnp.stack([jnp.sin(angles), jnp.cos(angles)], axis=2).reshape(2 * width + 1, model)

def into_band(table):
    heads, queries, band = table.shape
    width = queries + band - 1
    padded = jnp.pad(table, ((0, 0), (0, 0), (0, width + 1 - band)))
    flat = padded.reshape(heads, queries * (width + 1))[:, :queries * width]
    return flat.reshape(heads, queries, width)

def documents(positions, ends):
    return lax.optimization_barrier(jnp.sum((ends[None, :] <= positions[:, None]).astype(jnp.int32), axis=1, dtype=jnp.int32))

def pair_mask(query_pos, key_pos, ends, limit, row_len):
    same = documents(query_pos, ends)[:, None] == documents(key_pos, ends)[None, :]
    near = jnp.abs(key_pos[None, :] - query_pos[:, None]) <= limit
    inside = (key_pos >= 0) & (key_pos < row_len)
    return same & near & inside[None, :]

def feed_forward(hidden, gain, shift, weight_in, bias_in, weight_out, bias_out):
    normed = low(layer_norm(hidden, gain, shift))
    inner = low_back(product(normed, weight_in) + bias_in)
    active = low(inner * jax.nn.sigmoid(inner))
    return low_back(product(active, weight_out) + bias_out)

def attention(normed, attend_in, attend_out, position_proj, biases, ends_all, windows):
    joined = product(normed, attend_in)
    query = low_back(joined[..., :D] + biases[0])
    keys = low(low_back(joined[..., D:2 * D]))
    values = low(low_back(joined[..., 2 * D:] + biases[1]))
    query_u = low(query + biases[8]).reshape(ROWS, ROW_LEN, H, DH)
    query_v = low(query + biases[9]).reshape(ROWS, ROW_LEN, H, DH)
    table = low(product(low(position_table(WIN, D)), position_proj)).reshape(2 * WIN + 1, H, DH)
    padding = ((0, 0), (WIN, WIN), (0, 0), (0, 0))
    keys = jnp.pad(keys.reshape(ROWS, ROW_LEN, H, DH), padding)
    values = jnp.pad(values.reshape(ROWS, ROW_LEN, H, DH), padding)
    blocks = ROW_LEN // FR_DEV
    factor = 1.0 / math.sqrt(DH)

    def one_block(index):
        zero = jnp.zeros((), jnp.int32)
        row = (index // blocks).astype(jnp.int32)
        start = (index % blocks * FR_DEV).astype(jnp.int32)
        content_query = lax.dynamic_slice(query_u, (row, start, zero, zero), (1, FR_DEV, H, DH))[0]
        spread_query = lax.dynamic_slice(query_v, (row, start, zero, zero), (1, FR_DEV, H, DH))[0]
        key_block = lax.dynamic_slice(keys, (row, start, zero, zero), (1, FR_DEV + 2 * WIN, H, DH))[0]
        value_block = lax.dynamic_slice(values, (row, start, zero, zero), (1, FR_DEV + 2 * WIN, H, DH))[0]
        query_pos = start + jnp.arange(FR_DEV, dtype=jnp.int32)
        key_pos = start - WIN + jnp.arange(FR_DEV + 2 * WIN, dtype=jnp.int32)
        ends = lax.dynamic_index_in_dim(ends_all, row, 0, keepdims=False)
        limit = lax.dynamic_index_in_dim(windows, row, 0, keepdims=False)
        allowed = pair_mask(query_pos, key_pos, ends, limit, ROW_LEN)
        content = jnp.einsum('qhd,khd->hqk', content_query, key_block, precision=highest)
        spread = jnp.einsum('qhd,bhd->hqb', spread_query, table, precision=highest)
        raw = low_back(content + into_band(spread))
        scores = jnp.where(allowed[None], raw * factor, negative)
        top = lax.optimization_barrier(jnp.max(scores, axis=2, keepdims=True))
        powers = jnp.exp(scores - top)
        weights = powers / lax.optimization_barrier(jnp.sum(powers, axis=2, keepdims=True))
        mixed = jnp.einsum('hqk,khd->qhd', low(weights), value_block, precision=highest)
        return low(low_back(mixed)).reshape(FR_DEV, D)
    mixed = lax.map(jax.checkpoint(one_block), jnp.arange(ROWS * blocks, dtype=jnp.int32))
    return low_back(product(mixed.reshape(ROWS, ROW_LEN, D), attend_out) + biases[2])

def convolution(normed, convolve_in, convolve_out, depthwise, norm_gain, norm_shift, biases, ends_all, valid):
    half = KERNEL // 2
    paired = low_back(product(normed, convolve_in) + jnp.concatenate([biases[3], biases[4]]))
    gated = low(paired[..., :D] * jax.nn.sigmoid(paired[..., D:]))
    padded = jnp.pad(gated, ((0, 0), (half, half), (0, 0)))
    positions = jnp.arange(ROW_LEN + 2 * half, dtype=jnp.int32) - half
    docs_all = jax.vmap(lambda ends: documents(positions, ends))(ends_all)
    inside = (positions >= 0) & (positions < ROW_LEN)
    centre = docs_all[:, half:half + ROW_LEN]
    depth = jnp.zeros_like(gated)
    for tap in range(KERNEL):
        keep = ((docs_all[:, tap:tap + ROW_LEN] == centre) & inside[None, tap:tap + ROW_LEN]).astype(jnp.float32)
        depth = depth + depthwise[tap] * padded[:, tap:tap + ROW_LEN] * keep[..., None]
    depth = low_back(depth)
    weight = valid[..., None]
    count = jnp.sum(valid)
    mean = lax.optimization_barrier(jnp.sum(depth * weight, axis=(0, 1))) / count
    centered = depth - mean
    variance = lax.optimization_barrier(jnp.sum(centered * centered * weight, axis=(0, 1))) / count
    batch = centered * lax.rsqrt(variance + eps_norm) * norm_gain[5] + norm_shift[5]
    swished = low(batch * jax.nn.sigmoid(batch))
    return low_back(product(swished, convolve_out) + biases[5])

def reference(features, lengths, windows, feed_in, feed_in_bias, feed_out, attend_in, attend_out, position_proj, convolve_in, convolve_out, depthwise, norm_gain, norm_shift, biases, cotangent):
    ends_all = jnp.cumsum(lengths, axis=1, dtype=jnp.int32)
    frame_positions = jnp.arange(ROW_LEN, dtype=jnp.int32)
    valid = (frame_positions[None, :] < ends_all[:, -1:]).astype(jnp.float32)
    weights_all = (feed_in.astype(jnp.float32), feed_in_bias, feed_out.astype(jnp.float32), attend_in.astype(jnp.float32), attend_out.astype(jnp.float32), position_proj.astype(jnp.float32), convolve_in.astype(jnp.float32), convolve_out.astype(jnp.float32), depthwise, norm_gain, norm_shift, biases)

    def forward(inputs, weights_all):
        w_feed_in, w_feed_bias, w_feed_out, w_attend_in, w_attend_out, w_position, w_conv_in, w_conv_out, w_depth, gains, shifts, bias_rows = weights_all
        first = inputs + 0.5 * jax.checkpoint(feed_forward)(inputs, gains[0], shifts[0], w_feed_in[0], w_feed_bias[0], w_feed_out[0], bias_rows[6])
        normed_a = low(layer_norm(first, gains[1], shifts[1]))
        second = first + attention(normed_a, w_attend_in, w_attend_out, w_position, bias_rows, ends_all, windows)
        normed_c = low(layer_norm(second, gains[2], shifts[2]))
        third = second + jax.checkpoint(convolution)(normed_c, w_conv_in, w_conv_out, w_depth, gains, shifts, bias_rows, ends_all, valid)
        fourth = third + 0.5 * jax.checkpoint(feed_forward)(third, gains[3], shifts[3], w_feed_in[1], w_feed_bias[1], w_feed_out[1], bias_rows[7])
        return valid[..., None] * layer_norm(fourth, gains[4], shifts[4])
    result, pullback = jax.vjp(forward, features.astype(jnp.float32), weights_all)
    grad_inputs, grads = pullback(cotangent.astype(jnp.float32))
    return (result.astype(jnp.bfloat16), grad_inputs, grads[0], grads[1], grads[2], grads[3], grads[4], grads[5], grads[6], grads[7], grads[8], grads[9], grads[10], grads[11])
```

```python
import math

import jax
import jax.numpy as jnp
import ml_dtypes
import numpy as np
from jax import lax
from jax.sharding import PartitionSpec as P

H = 8
DH = 64
KERNEL = 9
WIN = 128


eps_norm = 1e-05
negative = -1e30
rows_first = (((0,), (0,)), ((), ()))
columns_last = (((1,), (1,)), ((), ()))


def padded_2(x, sides, width):
    for axis, dim in sides:
        devices, length = (lax.axis_size(axis), x.shape[dim])
        up = [(i, (i + 1) % devices) for i in range(devices - 1)]
        down = [(j, i) for i, j in up]
        last = lax.slice_in_dim(x, length - width, length, axis=dim)
        first = lax.slice_in_dim(x, 0, width, axis=dim)
        before = lax.ppermute(last, axis, up)
        after = lax.ppermute(first, axis, down)
        x = jnp.concatenate([before, x, after], axis=dim)
    return x


def product(left, right):
    return jnp.dot(left, right, preferred_element_type=jnp.float32)


def left_product(left, right):
    return lax.dot_general(left, right, rows_first, preferred_element_type=jnp.float32)


def right_product(left, right):
    return lax.dot_general(left, right, columns_last, preferred_element_type=jnp.float32)


def position_table(width, model):
    offsets = (np.arange(2 * width + 1) - width).astype(np.float32)
    rates = np.exp(
        np.arange(model // 2).astype(np.float32) * np.float32(-2.0 * math.log(10000.0) / model)
    )
    angles = (offsets[:, None] * rates[None, :]).astype(np.float32)
    both = np.stack([np.sin(angles), np.cos(angles)], axis=2)
    return both.reshape(2 * width + 1, model).astype(ml_dtypes.bfloat16)


def gather_all(block):
    axes = ("rows", "frames")
    devices = lax.axis_size("rows") * lax.axis_size("frames")
    copies = jnp.broadcast_to(block[None], (devices,) + block.shape)
    return lax.all_to_all(copies, axes, 0, 0, tiled=True)


def into_band(table):
    heads, queries, band = table.shape
    width = queries + band - 1
    padded = jnp.pad(table, ((0, 0), (0, 0), (0, width + 1 - band)))
    flat = padded.reshape(heads, queries * (width + 1))[:, : queries * width]
    return flat.reshape(heads, queries, width)


def from_band(grid, band):
    heads, queries, width = grid.shape
    flat = jnp.pad(grid.reshape(heads, queries * width), ((0, 0), (0, queries)))
    return flat.reshape(heads, queries, width + 1)[:, :, :band]


def documents(positions, ends):
    return jnp.sum((ends[None, :] <= positions[:, None]).astype(jnp.int32), axis=1, dtype=jnp.int32)


def pair_mask(query_pos, key_pos, ends, limit, row_len):
    same = documents(query_pos, ends)[:, None] == documents(key_pos, ends)[None, :]
    near = jnp.abs(key_pos[None, :] - query_pos[:, None]) <= limit
    inside = (key_pos >= 0) & (key_pos < row_len)
    return same & near & inside[None, :]


def layer_norm_keep(values, gain, shift):
    centered = values - jnp.mean(values, axis=-1, keepdims=True)
    inverse = lax.rsqrt(jnp.mean(centered * centered, axis=-1, keepdims=True) + eps_norm)
    normal = centered * inverse
    return (normal * gain + shift, normal, inverse)


def layer_norm_back(grad_out, normal, inverse, gain):
    scaled = grad_out * gain
    centred = scaled - jnp.mean(scaled, axis=-1, keepdims=True)
    grad_in = inverse * (centred - normal * jnp.mean(scaled * normal, axis=-1, keepdims=True))
    return (grad_in, jnp.sum(grad_out * normal, axis=0), jnp.sum(grad_out, axis=0))


def feed_forward(hidden, gain, shift, weight_in, bias_in, weight_out, bias_out):
    normed, normal, inverse = layer_norm_keep(hidden, gain, shift)
    normed = normed.astype(jnp.bfloat16)
    inner = product(normed, weight_in) + bias_in
    sigma = jax.nn.sigmoid(inner)
    active = (inner * sigma).astype(jnp.bfloat16)
    return (product(active, weight_out) + bias_out, (normal, inverse, normed, inner, sigma, active))


def feed_back(grad_branch, kept, gain, weight_in, weight_out):
    normal, inverse, normed, inner, sigma, active = kept
    grad_low = grad_branch.astype(jnp.bfloat16)
    grad_active = right_product(grad_low, weight_out)
    grad_inner = (grad_active * sigma * (1.0 + inner * (1.0 - sigma))).astype(jnp.bfloat16)
    grad_normed = right_product(grad_inner, weight_in)
    grad_hidden, grad_gain, grad_shift = layer_norm_back(grad_normed, normal, inverse, gain)
    grads = (
        left_product(normed, grad_inner),
        jnp.sum(grad_inner.astype(jnp.float32), axis=0),
        left_product(active, grad_low),
        jnp.sum(grad_low.astype(jnp.float32), axis=0),
        grad_gain,
        grad_shift,
    )
    return (grad_hidden, grads)


def per_device(
    features,
    lengths,
    windows,
    feed_in,
    feed_in_bias,
    feed_out,
    attend_in,
    attend_out,
    position_proj,
    convolve_in,
    convolve_out,
    depthwise,
    norm_gain,
    norm_shift,
    biases,
    cotangent,
):
    rows_here, frames_here, model = features.shape
    tokens = rows_here * frames_here
    half = KERNEL // 2
    band = 2 * WIN + 1
    factor = 1.0 / math.sqrt(DH)
    row_len = frames_here * lax.axis_size("frames")
    start = lax.axis_index("frames") * frames_here
    ends_every = jnp.cumsum(lengths, axis=1, dtype=jnp.int32)
    count = jnp.sum(ends_every[:, -1].astype(jnp.float32))
    ends_all = lax.dynamic_slice_in_dim(
        ends_every, lax.axis_index("rows") * rows_here, rows_here, 0
    )
    local_pos = start + jnp.arange(frames_here, dtype=jnp.int32)
    valid = (local_pos[None, :] < ends_all[:, -1:]).astype(jnp.float32).reshape(tokens, 1)
    stream_in = features.reshape(tokens, model).astype(jnp.float32)
    first_branch, first_kept = feed_forward(
        stream_in, norm_gain[0], norm_shift[0], feed_in[0], feed_in_bias[0], feed_out[0], biases[6]
    )
    after_first = stream_in + 0.5 * first_branch
    normed_a, normal_a, inverse_a = layer_norm_keep(after_first, norm_gain[1], norm_shift[1])
    normed_a = normed_a.astype(jnp.bfloat16)
    joined = product(normed_a, attend_in)
    query = joined[:, :model] + biases[0]
    query_u = (query + biases[8]).astype(jnp.bfloat16).reshape(rows_here, frames_here, H, DH)
    query_v = (query + biases[9]).astype(jnp.bfloat16).reshape(rows_here, frames_here, H, DH)
    pair = jnp.concatenate(
        [joined[:, model : 2 * model], joined[:, 2 * model :] + biases[1]], axis=1
    )
    pair = pair.astype(jnp.bfloat16).reshape(rows_here, frames_here, 2 * model)
    window = padded_2(pair, (("frames", 1),), WIN)
    key_rows = window[..., :model].reshape(rows_here, frames_here + 2 * WIN, H, DH)
    value_rows = window[..., model:].reshape(rows_here, frames_here + 2 * WIN, H, DH)
    sinusoid = jnp.asarray(position_table(WIN, model))
    table = product(sinusoid, position_proj).astype(jnp.bfloat16).reshape(band, H, DH)
    key_pos = start - WIN + jnp.arange(frames_here + 2 * WIN, dtype=jnp.int32)

    def scores_of(row_index):
        allowed = pair_mask(local_pos, key_pos, ends_all[row_index], windows[row_index], row_len)
        content = jnp.einsum(
            "qhd,khd->hqk",
            query_u[row_index],
            key_rows[row_index],
            preferred_element_type=jnp.float32,
        )
        spread = jnp.einsum(
            "qhd,bhd->hqb", query_v[row_index], table, preferred_element_type=jnp.float32
        )
        return jnp.where(allowed[None], (content + into_band(spread)) * factor, negative)

    mixed_rows = []
    logsum_rows = []
    for row_index in range(rows_here):
        scores = scores_of(row_index)
        top = jnp.max(scores, axis=2, keepdims=True)
        powers = jnp.exp(scores - top)
        total = jnp.sum(powers, axis=2, keepdims=True)
        weights = (powers / total).astype(jnp.bfloat16)
        mixed = jnp.einsum(
            "hqk,khd->qhd", weights, value_rows[row_index], preferred_element_type=jnp.float32
        )
        mixed_rows.append(mixed.astype(jnp.bfloat16).reshape(frames_here, model))
        logsum_rows.append(top + jnp.log(total))
    mixed_low = jnp.concatenate(mixed_rows, axis=0)
    after_attend = after_first + product(mixed_low, attend_out) + biases[2]
    normed_c, normal_c, inverse_c = layer_norm_keep(after_attend, norm_gain[2], norm_shift[2])
    normed_c = normed_c.astype(jnp.bfloat16)
    paired = product(normed_c, convolve_in) + jnp.concatenate([biases[3], biases[4]])
    gate_sigma = jax.nn.sigmoid(paired[:, model:])
    gated = (
        (paired[:, :model] * gate_sigma).astype(jnp.bfloat16).reshape(rows_here, frames_here, model)
    )
    rim = padded_2(gated, (("frames", 1),), half)
    rim_positions = start - half + jnp.arange(frames_here + 2 * half, dtype=jnp.int32)
    rim_documents = jax.vmap(lambda ends: documents(rim_positions, ends))(ends_all)
    rim_inside = (rim_positions >= 0) & (rim_positions < row_len)
    centre = rim_documents[:, half : half + frames_here]
    keeps = []
    for tap in range(KERNEL):
        keep = (rim_documents[:, tap : tap + frames_here] == centre) & rim_inside[
            None, tap : tap + frames_here
        ]
        keeps.append(keep.astype(jnp.float32)[..., None])
    depth = jnp.zeros((rows_here, frames_here, model), jnp.float32)
    for tap in range(KERNEL):
        depth = depth + depthwise[tap] * rim[:, tap : tap + frames_here] * keeps[tap]
    depth = depth.reshape(tokens, model)
    frames_axis = lax.axis_size("frames")
    devices = lax.axis_size("rows") * frames_axis
    here_count = jnp.maximum(jnp.sum(valid), 1.0)
    here_sum = jnp.sum(depth * valid, axis=0)
    here_mean = here_sum / here_count
    off = depth - here_mean
    here_spread = jnp.sum(off * off * valid, axis=0)
    counts = jnp.full((model,), jnp.sum(valid))
    stats = gather_all(jnp.stack([here_sum, here_spread, counts]))
    mean = jnp.sum(stats[:, 0], axis=0) / count
    off_means = stats[:, 0] / jnp.maximum(stats[:, 2], 1.0) - mean
    variance = jnp.sum(stats[:, 1] + stats[:, 2] * off_means * off_means, axis=0) / count
    centered = depth - mean
    batch_inverse = lax.rsqrt(variance + eps_norm)
    batch_normal = centered * batch_inverse
    batch = batch_normal * norm_gain[5] + norm_shift[5]
    batch_sigma = jax.nn.sigmoid(batch)
    swished = (batch * batch_sigma).astype(jnp.bfloat16)
    after_conv = after_attend + product(swished, convolve_out) + biases[5]
    second_branch, second_kept = feed_forward(
        after_conv, norm_gain[3], norm_shift[3], feed_in[1], feed_in_bias[1], feed_out[1], biases[7]
    )
    after_second = after_conv + 0.5 * second_branch
    final, normal_o, inverse_o = layer_norm_keep(after_second, norm_gain[4], norm_shift[4])
    out = (valid * final).astype(jnp.bfloat16).reshape(rows_here, frames_here, model)
    grad_final = valid * cotangent.reshape(tokens, model).astype(jnp.float32)
    grad_second, gain_out, shift_out = layer_norm_back(
        grad_final, normal_o, inverse_o, norm_gain[4]
    )
    grad_from_second, second_grads = feed_back(
        0.5 * grad_second, second_kept, norm_gain[3], feed_in[1], feed_out[1]
    )
    grad_conv_stream = grad_second + grad_from_second
    grad_conv_low = grad_conv_stream.astype(jnp.bfloat16)
    grad_convolve_out = left_product(swished, grad_conv_low)
    conv_out_bias = jnp.sum(grad_conv_low.astype(jnp.float32), axis=0)
    grad_swished = right_product(grad_conv_low, convolve_out)
    grad_batch = grad_swished * batch_sigma * (1.0 + batch * (1.0 - batch_sigma))
    totals = jnp.sum(
        gather_all(
            jnp.stack([jnp.sum(grad_batch, axis=0), jnp.sum(grad_batch * batch_normal, axis=0)])
        ),
        axis=0,
    )
    total_a, total_b = totals[0], totals[1]
    batch_gain = norm_gain[5]
    grad_depth = batch_inverse * (
        grad_batch * batch_gain - valid * batch_gain * (total_a + batch_normal * total_b) / count
    )
    grad_depth = grad_depth.astype(jnp.bfloat16).reshape(rows_here, frames_here, model)
    grad_rim = padded_2(grad_depth, (("frames", 1),), half)
    grad_depth_wide = grad_depth.astype(jnp.float32)
    depth_grads = []
    grad_gated = jnp.zeros((rows_here, frames_here, model), jnp.float32)
    for tap in range(KERNEL):
        depth_grads.append(
            jnp.sum(grad_depth_wide * rim[:, tap : tap + frames_here] * keeps[tap], axis=(0, 1))
        )
        mirror = 2 * half - tap
        grad_gated = (
            grad_gated + depthwise[tap] * grad_rim[:, mirror : mirror + frames_here] * keeps[mirror]
        )
    grad_gated = grad_gated.reshape(tokens, model)
    value_half = paired[:, :model]
    grad_paired = jnp.concatenate(
        [grad_gated * gate_sigma, grad_gated * value_half * gate_sigma * (1.0 - gate_sigma)], axis=1
    ).astype(jnp.bfloat16)
    grad_convolve_in = left_product(normed_c, grad_paired)
    conv_in_bias = jnp.sum(grad_paired.astype(jnp.float32), axis=0)
    grad_normed_c = right_product(grad_paired, convolve_in)
    grad_from_conv, gain_c, shift_c = layer_norm_back(
        grad_normed_c, normal_c, inverse_c, norm_gain[2]
    )
    grad_attend_stream = grad_conv_stream + grad_from_conv
    grad_attend_low = grad_attend_stream.astype(jnp.bfloat16)
    grad_attend_out = left_product(mixed_low, grad_attend_low)
    attend_out_bias = jnp.sum(grad_attend_low.astype(jnp.float32), axis=0)
    grad_mixed = (
        right_product(grad_attend_low, attend_out)
        .astype(jnp.bfloat16)
        .reshape(rows_here, frames_here, H, DH)
    )
    grad_table = jnp.zeros((band, H, DH), jnp.float32)
    key_grads = []
    value_grads = []
    content_grads = []
    spread_grads = []
    for row_index in range(rows_here):
        scores = scores_of(row_index)
        probability = jnp.exp(scores - logsum_rows[row_index])
        grad_probability = jnp.einsum(
            "qhd,khd->hqk",
            grad_mixed[row_index],
            value_rows[row_index],
            preferred_element_type=jnp.float32,
        )
        delta = jnp.sum(probability * grad_probability, axis=2, keepdims=True)
        grad_raw = (probability * (grad_probability - delta) * factor).astype(jnp.bfloat16)
        value_grads.append(
            jnp.einsum(
                "hqk,qhd->khd",
                probability.astype(jnp.bfloat16),
                grad_mixed[row_index],
                preferred_element_type=jnp.float32,
            )
        )
        key_grads.append(
            jnp.einsum(
                "hqk,qhd->khd", grad_raw, query_u[row_index], preferred_element_type=jnp.float32
            )
        )
        content_grads.append(
            jnp.einsum(
                "hqk,khd->qhd", grad_raw, key_rows[row_index], preferred_element_type=jnp.float32
            )
        )
        band_grad = from_band(grad_raw, band)
        spread_grads.append(
            jnp.einsum("hqb,bhd->qhd", band_grad, table, preferred_element_type=jnp.float32)
        )
        grad_table = grad_table + jnp.einsum(
            "hqb,qhd->bhd", band_grad, query_v[row_index], preferred_element_type=jnp.float32
        )
    window_span = frames_here + 2 * WIN
    grad_window = jnp.concatenate(
        [
            jnp.stack(key_grads).reshape(rows_here, window_span, model),
            jnp.stack(value_grads).reshape(rows_here, window_span, model),
        ],
        axis=2,
    )
    edges = jnp.concatenate([grad_window[:, :WIN], grad_window[:, frames_here + WIN :]], axis=1)
    returned = padded_2(edges.astype(jnp.bfloat16), (("frames", 1),), WIN).astype(edges.dtype)
    from_left = jnp.pad(returned[:, :WIN], ((0, 0), (0, frames_here - WIN), (0, 0)))
    from_right = jnp.pad(returned[:, 3 * WIN :], ((0, 0), (frames_here - WIN, 0), (0, 0)))
    grad_pair = (grad_window[:, WIN : WIN + frames_here] + from_left + from_right).reshape(
        tokens, 2 * model
    )
    grad_pair_low = grad_pair.astype(jnp.bfloat16)
    grad_query_u = jnp.stack(content_grads).reshape(tokens, model)
    grad_query_v = jnp.stack(spread_grads).reshape(tokens, model)
    grad_query = (grad_query_u + grad_query_v).astype(jnp.bfloat16)
    grad_joined = jnp.concatenate([grad_query, grad_pair_low], axis=1)
    grad_attend_in = left_product(normed_a, grad_joined)
    grad_normed_a = right_product(grad_joined, attend_in)
    grad_from_attend, gain_a, shift_a = layer_norm_back(
        grad_normed_a, normal_a, inverse_a, norm_gain[1]
    )
    grad_first_stream = grad_attend_stream + grad_from_attend
    grad_position_proj = lax.dot_general(
        sinusoid.astype(jnp.float32),
        grad_table.reshape(band, model),
        rows_first,
        precision=lax.Precision.HIGHEST,
        preferred_element_type=jnp.float32,
    )
    grad_from_first, first_grads = feed_back(
        0.5 * grad_first_stream, first_kept, norm_gain[0], feed_in[0], feed_out[0]
    )
    grad_features = (grad_first_stream + grad_from_first).reshape(rows_here, frames_here, model)
    bias_rows = jnp.stack(
        [
            jnp.sum(grad_query.astype(jnp.float32), axis=0),
            jnp.sum(grad_pair_low[:, model:].astype(jnp.float32), axis=0),
            attend_out_bias,
            conv_in_bias[:model],
            conv_in_bias[model:],
            conv_out_bias,
            first_grads[3],
            second_grads[3],
            jnp.sum(grad_query_u, axis=0),
            jnp.sum(grad_query_v, axis=0),
        ]
    )
    depth_rows = jnp.stack(depth_grads)
    gain_rows = jnp.stack([first_grads[4], gain_a, gain_c, second_grads[4], gain_out])
    shift_rows = jnp.stack([first_grads[5], shift_a, shift_c, second_grads[5], shift_out])
    width = feed_in.shape[2] // frames_axis
    slim = model // frames_axis

    def chunks(grad):
        return grad.astype(jnp.bfloat16).reshape(frames_axis, -1, model)

    bulk = jnp.concatenate(
        [
            chunks(first_grads[0].T),
            chunks(second_grads[0].T),
            chunks(first_grads[2]),
            chunks(second_grads[2]),
            chunks(grad_attend_in),
            chunks(grad_attend_out),
            chunks(grad_position_proj),
            chunks(grad_convolve_in),
            chunks(grad_convolve_out),
        ],
        axis=1,
    )
    bulk = lax.psum_scatter(bulk, "frames", scatter_dimension=0, tiled=True)[0]
    both = [(0, 1), (1, 0)]
    bulk = bulk.astype(jnp.float32) + lax.ppermute(bulk, "rows", both).astype(jnp.float32)
    cuts = [width] * 4 + [3 * slim, slim, slim, 2 * slim, slim]
    parts = []
    at = 0
    for cut in cuts:
        parts.append(bulk[at : at + cut])
        at += cut
    vectors = jnp.concatenate([depth_rows, gain_rows, shift_rows, bias_rows], axis=0)
    vectors = vectors.reshape(-1, frames_axis, slim).transpose(1, 0, 2).reshape(frames_axis, -1)
    feed_vectors = jnp.stack([first_grads[1], second_grads[1]])
    feed_vectors = feed_vectors.reshape(2, frames_axis, width).transpose(1, 0, 2)
    small = jnp.concatenate([vectors, feed_vectors.reshape(frames_axis, -1)], axis=1)
    small = jnp.concatenate([small] * lax.axis_size("rows"), axis=0)
    small = jnp.sum(lax.all_to_all(small, ("rows", "frames"), 0, 0, tiled=True), axis=0)
    n_vectors = KERNEL + 5 + 5 + 10
    thin = small[: n_vectors * slim].reshape(n_vectors, slim)
    feed_bias_part = small[n_vectors * slim :].reshape(2, width)
    feed_parts = (
        jnp.stack([parts[0].T, parts[1].T]),
        feed_bias_part,
        jnp.stack([parts[2], parts[3]]),
    )
    rest = (
        parts[4].reshape(slim, 3 * model),
        parts[5],
        parts[6],
        parts[7].reshape(slim, 2 * model),
        parts[8],
        thin[:KERNEL],
        thin[KERNEL : KERNEL + 5],
        thin[KERNEL + 5 : KERNEL + 10],
        thin[KERNEL + 10 :],
    )
    slice_width = model // lax.axis_size("frames")
    slice_start = lax.axis_index("frames") * slice_width
    total_b_part = lax.dynamic_slice_in_dim(total_b, slice_start, slice_width, 0)
    total_a_part = lax.dynamic_slice_in_dim(total_a, slice_start, slice_width, 0)
    grad_norm_gain = jnp.concatenate([rest[6], total_b_part[None, :]], axis=0)
    grad_norm_shift = jnp.concatenate([rest[7], total_a_part[None, :]], axis=0)
    return (
        out,
        grad_features,
        feed_parts[0],
        feed_parts[1],
        feed_parts[2],
        rest[0],
        rest[1],
        rest[2],
        rest[3],
        rest[4],
        rest[5],
        grad_norm_gain,
        grad_norm_shift,
        rest[8],
    )


def solution(mesh):
    placed = (
        P("rows", "frames", None),
        P(),
        P("rows"),
        P(),
        P(),
        P(),
        P(),
        P(),
        P(),
        P(),
        P(),
        P(),
        P(),
        P(),
        P(),
        P("rows", "frames", None),
    )
    return jax.shard_map(
        per_device,
        mesh=mesh,
        in_specs=placed,
        out_specs=(
            P("rows", "frames", None),
            P("rows", "frames", None),
            P(None, None, "frames"),
            P(None, "frames"),
            P(None, "frames", None),
            P("frames", None),
            P("frames", None),
            P("frames", None),
            P("frames", None),
            P("frames", None),
            P(None, "frames"),
            P(None, "frames"),
            P(None, "frames"),
            P(None, "frames"),
        ),
        check_vma=False,
    )
```

```python
import functools
import math

import jax
import jax.numpy as jnp
import ml_dtypes
import numpy as np
from jax import lax
from jax.experimental import pallas as pl
from jax.experimental.pallas import tpu as pltpu
from jax.sharding import PartitionSpec as P

H = 8
DH = 64
KERNEL = 9
WIN = 128

HALF = KERNEL // 2
SPAN = 3 * WIN
PAIRS = H // 2
RIM = 16
RIM_GRAD = 8
eps_norm = 1e-05
negative = -1e30
f32 = jnp.float32
bf16 = jnp.bfloat16
DEVICES = ("rows", "frames")
VMEM_LIMIT = 60 * 1024 * 1024


def dot(left, right):
    return jnp.dot(left, right, preferred_element_type=f32)


def dot_last(left, right):
    return lax.dot_general(left, right, (((1,), (1,)), ((), ())), preferred_element_type=f32)


def dot_first(left, right):
    return lax.dot_general(left, right, (((0,), (0,)), ((), ())), preferred_element_type=f32)


def sigmoid(x):
    return 0.5 * jnp.tanh(0.5 * x) + 0.5


def total(x):
    return jnp.sum(x, axis=0, keepdims=True)


def normalize(values):
    centered = values - jnp.mean(values, axis=-1, keepdims=True)
    inverse = lax.rsqrt(jnp.mean(centered * centered, axis=-1, keepdims=True) + eps_norm)
    return centered * inverse, inverse


def norm_back(grad_out, normal, inverse, gain):
    scaled = grad_out * gain
    centred = scaled - jnp.mean(scaled, axis=-1, keepdims=True)
    grad_in = inverse * (centred - normal * jnp.mean(scaled * normal, axis=-1, keepdims=True))
    return grad_in, total(grad_out * normal), total(grad_out)


def position_table(width, model):
    offsets = (np.arange(2 * width + 1) - width).astype(np.float32)
    rates = np.exp(
        np.arange(model // 2).astype(np.float32) * np.float32(-2.0 * math.log(10000.0) / model)
    )
    angles = (offsets[:, None] * rates[None, :]).astype(np.float32)
    both = np.stack([np.sin(angles), np.cos(angles)], axis=2).reshape(2 * width + 1, model)
    padded = np.zeros((3 * width, model), np.float32)
    padded[: 2 * width + 1] = both
    return padded.astype(ml_dtypes.bfloat16)


def bounds(ends, at, row_len):
    low = jnp.max(jnp.where(ends <= at, ends, 0.0), axis=1, keepdims=True)
    high = jnp.min(jnp.where(ends > at, ends, row_len), axis=1, keepdims=True)
    return low, high


def column(count, offset):
    return lax.broadcasted_iota(jnp.int32, (count, 1), 0).astype(f32) + offset


def lane_low(rows):
    return lax.broadcasted_iota(jnp.int32, (rows, 2 * DH), 1) < DH


def two_heads(pair):
    low = lane_low(pair.shape[0])
    zero = jnp.zeros_like(pair)
    return jnp.concatenate([jnp.where(low, pair, zero), jnp.where(low, zero, pair)], axis=0)


def one_pair(stacked):
    rows = stacked.shape[0] // 2
    return jnp.where(lane_low(rows), stacked[:rows], stacked[rows:])


def flip(rows, blocks):
    i = lax.broadcasted_iota(jnp.int32, (rows * blocks, rows * blocks), 0)
    j = lax.broadcasted_iota(jnp.int32, (rows * blocks, rows * blocks), 1)
    base = (i // rows) * (2 * rows) + rows - 1
    return (i + j == base).astype(f32).astype(bf16)


def whole(shape):
    return pl.BlockSpec(shape, lambda i: (0,) * len(shape))


SMEM = pl.BlockSpec(memory_space=pltpu.SMEM)


def call(body, grid, in_specs, out_specs, out_shape, scratch=(), flops=0, moved=0, name=None):
    return pl.pallas_call(
        body,
        grid=grid,
        in_specs=in_specs,
        out_specs=out_specs,
        out_shape=out_shape,
        scratch_shapes=scratch,
        compiler_params=pltpu.CompilerParams(vmem_limit_bytes=VMEM_LIMIT),
        cost_estimate=pl.CostEstimate(flops=flops, bytes_accessed=moved, transcendentals=0),
        name=name,
    )


def sds(shape, dtype):
    return jax.ShapeDtypeStruct(shape, dtype)


def front_body(
    x_ref, w_in, b_in, w_out, attend_in, gain, shift, bias,
    after_ref, n0_ref, na_ref, qu_ref, qv_ref, lo_ref, hi_ref, act_ref, slope_ref,
    acc,
):
    step, steps = pl.program_id(0), pl.num_programs(0)
    rows = lo_ref.shape[0]
    model = x_ref.shape[1]

    @pl.when(step == 0)
    def _():
        normal, _ = normalize(x_ref[...].astype(f32))
        n0_ref[...] = (normal * gain[0:1] + shift[0:1]).astype(bf16)
        acc[...] = jnp.zeros_like(acc)

    inner = dot(n0_ref[...], w_in[0]) + b_in[0:1]
    sigma = sigmoid(inner)
    active = (inner * sigma).astype(bf16)
    act_ref[...] = active
    slope_ref[...] = (sigma * (1.0 + inner * (1.0 - sigma))).astype(bf16)
    acc[...] += dot(active, w_out[0])

    @pl.when(step == steps - 1)
    def _():
        after = x_ref[...].astype(f32) + 0.5 * (acc[...] + bias[6:7])
        after_ref[...] = after
        normal, _ = normalize(after)
        normed = (normal * gain[1:2] + shift[1:2]).astype(bf16)
        na_ref[...] = normed
        query = dot(normed, attend_in[:, :model]) + bias[0:1]
        factor = 1.0 / math.sqrt(DH)
        qu_ref[...] = ((query + bias[8:9]) * factor).astype(bf16)
        qv_ref[...] = ((query + bias[9:10]) * factor).astype(bf16)
        keys = dot(normed, attend_in[:, model : 2 * model]).astype(bf16)
        values = (dot(normed, attend_in[:, 2 * model :]) + bias[1:2]).astype(bf16)
        for row in range(rows):
            at = 2 * WIN * row
            lo_ref[row, :, :model] = keys[at : at + WIN]
            lo_ref[row, :, model:] = values[at : at + WIN]
            hi_ref[row, :, :model] = keys[at + WIN : at + 2 * WIN]
            hi_ref[row, :, model:] = values[at + WIN : at + 2 * WIN]


def front(features, feed_in, feed_in_bias, feed_out, attend_in, gain, shift, bias, rows):
    tokens, model = features.shape
    hidden = feed_in.shape[2]
    part = 512
    steps = hidden // part
    kv = (rows, WIN, 2 * model)
    return call(
        front_body,
        (steps,),
        [
            whole((tokens, model)),
            pl.BlockSpec((1, model, part), lambda i: (0, 0, i)),
            pl.BlockSpec((2, part), lambda i: (0, i)),
            pl.BlockSpec((1, part, model), lambda i: (0, i, 0)),
            whole(attend_in.shape),
            whole(gain.shape),
            whole(shift.shape),
            whole(bias.shape),
        ],
        [
            whole((tokens, model)),
            whole((tokens, model)),
            whole((tokens, model)),
            whole((tokens, model)),
            whole((tokens, model)),
            whole(kv),
            whole(kv),
            pl.BlockSpec((tokens, part), lambda i: (0, i)),
            pl.BlockSpec((tokens, part), lambda i: (0, i)),
        ],
        [
            sds((tokens, model), f32),
            sds((tokens, model), bf16),
            sds((tokens, model), bf16),
            sds((tokens, model), bf16),
            sds((tokens, model), bf16),
            sds(kv, bf16),
            sds(kv, bf16),
            sds((tokens, hidden), bf16),
            sds((tokens, hidden), bf16),
        ],
        [pltpu.VMEM((tokens, model), f32)],
        flops=2 * tokens * model * (2 * hidden + 3 * model),
        moved=20 << 20,
        name="front",
    )(features, feed_in, feed_in_bias, feed_out, attend_in, gain, shift, bias)


def attend_body(
    row_len, info, ends, qu, qv, before, lo, hi, after, sinusoid, proj, stream, attend_out,
    convolve_in, gain, shift, bias,
    prob_ref, mixed_ref, out_ref, nc_ref, paired_ref, gated_ref, first_ref, last_ref, table_ref,
):
    row = pl.program_id(0)
    model = stream.shape[1]
    frames = 2 * WIN

    @pl.when(row == 0)
    def _():
        table_ref[...] = dot(sinusoid[...], proj[...]).astype(bf16)

    start = info[0].astype(f32)
    reach = info[1 + row].astype(f32)
    row_ends = ends[pl.ds(row, 1), :]
    blocks = (before, lo, hi, after)
    turn = flip(WIN, 2)
    key_at = lax.broadcasted_iota(jnp.int32, (WIN, SPAN), 1).astype(f32)
    for block in range(2):
        at = column(WIN, start + WIN * block)
        low, high = bounds(row_ends, at, row_len)
        base = start + (WIN * (block - 1))
        low = jnp.maximum(low, at - reach) - base
        high = jnp.minimum(high - 1.0, at + reach) - base
        allowed = ((key_at >= low) & (key_at <= high))[None]
        here = slice(WIN * block, WIN * (block + 1))
        for pair in range(PAIRS):
            cut = slice(2 * DH * pair, 2 * DH * (pair + 1))
            cut_v = slice(model + 2 * DH * pair, model + 2 * DH * (pair + 1))
            keys = jnp.concatenate([b[0, :, cut] for b in blocks[block : block + 3]], axis=0)
            values = jnp.concatenate([b[0, :, cut_v] for b in blocks[block : block + 3]], axis=0)
            content = dot_last(two_heads(qu[here, cut]), keys)
            spread = dot_last(two_heads(qv[here, cut]), table_ref[:, cut])
            spread = pltpu.roll(spread.reshape(2, WIN, SPAN), 0, 2, stride=1, stride_axis=1)
            scores = jnp.where(allowed, content.reshape(2, WIN, SPAN) + spread, negative)
            powers = jnp.exp(scores - jnp.max(scores, axis=2, keepdims=True))
            weights = powers * (1.0 / jnp.sum(powers, axis=2, keepdims=True))
            weights = weights.astype(bf16).reshape(2 * WIN, SPAN)
            mixed_ref[here, cut] = one_pair(dot(weights, values)).astype(bf16)
            prob_ref[0, block, pair] = dot(turn, weights).astype(bf16)
    after_attend = stream[...] + dot(mixed_ref[...], attend_out[...]) + bias[2:3]
    out_ref[...] = after_attend
    normal, _ = normalize(after_attend)
    normed = (normal * gain[2:3] + shift[2:3]).astype(bf16)
    nc_ref[...] = normed
    paired = dot(normed, convolve_in[...])
    value = paired[:, :model] + bias[3:4]
    gate = paired[:, model:] + bias[4:5]
    paired_ref[:, :model] = value
    paired_ref[:, model:] = gate
    gated = (value * sigmoid(gate)).astype(bf16)
    gated_ref[...] = gated
    first_ref[0] = gated[:RIM]
    last_ref[0] = gated[frames - RIM :]


def attend(
    row_len, info, ends, qu, qv, before, lo, hi, after, sinusoid, proj, stream, attend_out,
    convolve_in, gain, shift, bias,
):
    tokens, model = stream.shape
    rows = lo.shape[0]
    frames = tokens // rows

    def tile(width):
        return pl.BlockSpec((frames, width), lambda i: (i, 0))

    kv = pl.BlockSpec((1, WIN, 2 * model), lambda i: (i, 0, 0))
    rim = pl.BlockSpec((1, RIM, model), lambda i: (i, 0, 0))
    prob = (rows, 2, PAIRS, 2 * WIN, SPAN)
    return call(
        functools.partial(attend_body, row_len),
        (rows,),
        [
            SMEM, whole(ends.shape), tile(model), tile(model), kv, kv, kv, kv,
            whole(sinusoid.shape), whole(proj.shape), tile(model), whole(attend_out.shape),
            whole(convolve_in.shape), whole(gain.shape), whole(shift.shape), whole(bias.shape),
        ],
        [
            pl.BlockSpec((1,) + prob[1:], lambda i: (i, 0, 0, 0, 0)),
            tile(model), tile(model), tile(model), tile(2 * model), tile(model), rim, rim,
            whole((SPAN, model)),
        ],
        [
            sds(prob, bf16),
            sds((tokens, model), bf16),
            sds((tokens, model), f32),
            sds((tokens, model), bf16),
            sds((tokens, 2 * model), f32),
            sds((tokens, model), bf16),
            sds((rows, RIM, model), bf16),
            sds((rows, RIM, model), bf16),
            sds((SPAN, model), bf16),
        ],
        flops=16 * 8 * 256 * 384 * 128,
        moved=16 << 20,
        name="attend",
    )(
        info, ends, qu, qv, before, lo, hi, after, sinusoid, proj, stream, attend_out,
        convolve_in, gain, shift, bias,
    )


def valid_column(info, row, rows, frames):
    at = column(frames, info[0].astype(f32))
    return (at < info[1 + rows + row].astype(f32)).astype(f32)


def pack(ref, vectors):
    at = 0
    for vector in vectors:
        for k in range(0, vector.shape[1], 128):
            ref[at : at + 1, :] = vector[:, k : k + 128]
            at += 1


def depth_body(row_len, info, ends, gated, before, after, taps, depth_ref, stats_ref, rim, tile):
    rows = before.shape[0]
    frames = gated.shape[0] // rows
    start = info[0].astype(f32)
    sums, spreads, counts = 0.0, [], 0.0
    valids = []
    for row in range(rows):
        here = slice(row * frames, (row + 1) * frames)
        rim[0:RIM] = before[row].astype(f32)
        rim[RIM : RIM + frames] = gated[here].astype(f32)
        rim[RIM + frames :] = after[row].astype(f32)
        at = column(frames, start)
        low, high = bounds(ends[row : row + 1, :], at, row_len)
        depth = jnp.zeros((frames, gated.shape[1]), f32)
        for tap in range(KERNEL):
            off = tap - HALF
            keep = ((at + off >= low) & (at + off < high)).astype(f32)
            depth += taps[tap : tap + 1] * (rim[RIM + off : RIM + off + frames] * keep)
        depth_ref[here] = depth
        valid = valid_column(info, row, rows, frames)
        valids.append(valid)
        sums += total(depth * valid)
        counts += total(valid)
    mean = sums / jnp.maximum(counts, 1.0)
    spread = 0.0
    for row in range(rows):
        here = slice(row * frames, (row + 1) * frames)
        centered = depth_ref[here] - mean
        spread += total(centered * centered * valids[row])
    pack(tile, [sums, spread])
    stats_ref[...] = jnp.broadcast_to(tile[...][None], stats_ref.shape)


def depth_conv(row_len, devices, info, ends, gated, before, after, taps):
    tokens, model = gated.shape
    rows = before.shape[0]
    return call(
        functools.partial(depth_body, row_len),
        (1,),
        [
            SMEM, whole(ends.shape), whole(gated.shape), whole(before.shape), whole(after.shape),
            whole(taps.shape),
        ],
        [whole((tokens, model)), whole((devices, 8, 128))],
        [sds((tokens, model), f32), sds((devices, 8, 128), f32)],
        [
            pltpu.VMEM((tokens // rows + 2 * RIM, model), f32),
            pltpu.VMEM((8, 128), f32),
        ],
        flops=tokens * model * 30,
        moved=2 << 20,
        name="depth_conv",
    )(info, ends, gated, before, after, taps)


def middle_body(
    info, stats, counts, depth, stream, w_in, b_in, w_out, convolve_out, gain, shift, bias,
    cotangent,
    out_ref, act_ref, gi_ref, nf_ref, gl_ref, sw_ref, gcl_ref, gcs_ref, gb_ref, bn_ref,
    inv_ref, totals_ref, first_ref, last_ref, vec_ref, fb_ref,
    conv_s, slope_s, acc, gs_s, tile,
):
    step, steps = pl.program_id(0), pl.num_programs(0)
    half = steps // 2
    rows = first_ref.shape[0]
    tokens, model = depth.shape
    frames = tokens // rows

    @pl.when(step == 0)
    def _():
        each = counts[...]
        count = total(each)
        means, inverses = [], []
        for k in range(model // 128):
            sums = stats[:, k, :]
            mean = total(sums) / count
            off = sums / jnp.maximum(each, 1.0) - mean
            spread = total(stats[:, model // 128 + k, :]) + total(each * off * off)
            means.append(mean)
            inverses.append(lax.rsqrt(spread / count + eps_norm))
        mean = jnp.concatenate(means, axis=1)
        inverse = jnp.concatenate(inverses, axis=1)
        inv_ref[0:1] = inverse
        inv_ref[1:2] = jnp.broadcast_to(1.0 / count, (1, model))
        normal = (depth[...] - mean) * inverse
        bn_ref[...] = normal
        batch = normal * gain[5:6] + shift[5:6]
        swished = (batch * sigmoid(batch)).astype(bf16)
        sw_ref[...] = swished
        after_conv = stream[...] + dot(swished, convolve_out[...]) + bias[5:6]
        conv_s[...] = after_conv
        normal, _ = normalize(after_conv)
        nf_ref[...] = (normal * gain[3:4] + shift[3:4]).astype(bf16)
        acc[...] = jnp.zeros_like(acc)

    @pl.when(step < half)
    def _():
        inner = dot(nf_ref[...], w_in[0]) + b_in[1:2]
        sigma = sigmoid(inner)
        active = (inner * sigma).astype(bf16)
        act_ref[...] = active
        slope_s[step] = sigma * (1.0 + inner * (1.0 - sigma))
        acc[...] += dot(active, w_out[0])

    @pl.when(step == half - 1)
    def _():
        after_second = conv_s[...] + 0.5 * (acc[...] + bias[7:8])
        normal, inverse = normalize(after_second)
        valid = jnp.concatenate(
            [valid_column(info, row, rows, frames) for row in range(rows)], axis=0
        )
        out_ref[...] = (valid * (normal * gain[4:5] + shift[4:5])).astype(bf16)
        grad = valid * cotangent[...].astype(f32)
        grad, gain_grad, shift_grad = norm_back(grad, normal, inverse, gain[4:5])
        gs_s[...] = grad
        low = (0.5 * grad).astype(bf16)
        gl_ref[...] = low
        vec_ref[2:3] = gain_grad
        vec_ref[3:4] = shift_grad
        vec_ref[5:6] = total(low.astype(f32))
        acc[...] = jnp.zeros_like(acc)

    @pl.when(step >= half)
    def _():
        grad = (dot_last(gl_ref[...], w_out[0]) * slope_s[steps - 1 - step]).astype(bf16)
        gi_ref[...] = grad
        fb_ref[...] = total(grad.astype(f32))
        acc[...] += dot_last(grad, w_in[0])

    @pl.when(step == steps - 1)
    def _():
        normal, inverse = normalize(conv_s[...])
        grad, gain_grad, shift_grad = norm_back(acc[...], normal, inverse, gain[3:4])
        vec_ref[0:1] = gain_grad
        vec_ref[1:2] = shift_grad
        grad = gs_s[...] + grad
        gcs_ref[...] = grad
        low = grad.astype(bf16)
        gcl_ref[...] = low
        vec_ref[4:5] = total(low.astype(f32))
        bn = bn_ref[...]
        batch = bn * gain[5:6] + shift[5:6]
        sigma = sigmoid(batch)
        grad = dot_last(low, convolve_out[...]) * sigma * (1.0 + batch * (1.0 - sigma))
        gb_ref[...] = grad
        pack(tile, [total(grad), total(grad * bn)])
        totals_ref[...] = jnp.broadcast_to(tile[...][None], totals_ref.shape)
        for row in range(rows):
            at, end = row * frames, (row + 1) * frames
            first_ref[row, :, :model] = gb_ref[at : at + RIM_GRAD]
            first_ref[row, :, model:] = bn_ref[at : at + RIM_GRAD]
            last_ref[row, :, :model] = gb_ref[end - RIM_GRAD : end]
            last_ref[row, :, model:] = bn_ref[end - RIM_GRAD : end]


def middle(
    devices, rows, info, stats, counts, depth, stream, feed_in, feed_in_bias, feed_out,
    convolve_out, gain, shift, bias, cotangent,
):
    tokens, model = depth.shape
    hidden = feed_in.shape[2]
    part = 512
    half = hidden // part
    steps = 2 * half
    token = whole((tokens, model))
    rim = (rows, RIM_GRAD, 2 * model)

    def turn(i):
        return jnp.minimum(i, steps - 1 - i)

    def late(i):
        return jnp.minimum(half - 1, steps - 1 - i)

    return call(
        middle_body,
        (steps,),
        [
            SMEM, whole(stats.shape), whole(counts.shape), token, token,
            pl.BlockSpec((1, model, part), lambda i: (1, 0, turn(i))),
            pl.BlockSpec((2, part), lambda i: (0, turn(i))),
            pl.BlockSpec((1, part, model), lambda i: (1, turn(i), 0)),
            whole(convolve_out.shape), whole(gain.shape), whole(shift.shape), whole(bias.shape),
            token,
        ],
        [
            token,
            pl.BlockSpec((tokens, part), lambda i: (0, jnp.minimum(i, half - 1))),
            pl.BlockSpec((tokens, part), lambda i: (0, late(i))),
            token, token, token, token, token, token, token,
            whole((8, model)), whole((devices, 8, 128)), whole(rim), whole(rim),
            whole((8, model)),
            pl.BlockSpec((1, part), lambda i: (0, late(i))),
        ],
        [
            sds((tokens, model), bf16),
            sds((tokens, hidden), bf16),
            sds((tokens, hidden), bf16),
            sds((tokens, model), bf16),
            sds((tokens, model), bf16),
            sds((tokens, model), bf16),
            sds((tokens, model), bf16),
            sds((tokens, model), f32),
            sds((tokens, model), f32),
            sds((tokens, model), f32),
            sds((8, model), f32),
            sds((devices, 8, 128), f32),
            sds(rim, f32),
            sds(rim, f32),
            sds((8, model), f32),
            sds((1, hidden), f32),
        ],
        [
            pltpu.VMEM((tokens, model), f32),
            pltpu.VMEM((half, tokens, part), f32),
            pltpu.VMEM((tokens, model), f32),
            pltpu.VMEM((tokens, model), f32),
            pltpu.VMEM((8, 128), f32),
        ],
        flops=2 * tokens * model * (4 * hidden + 2 * model),
        moved=24 << 20,
        name="middle",
    )(
        info, stats, counts, depth, stream, feed_in, feed_in_bias, feed_out, convolve_out, gain,
        shift, bias, cotangent,
    )


def conv_back_body(
    row_len, info, ends, totals, inv, gb, bn, edge_before, edge_after, gated, rim_before,
    rim_after, paired, taps, after_attend, gcs, convolve_in, attend_out, gain,
    gp_ref, gas_ref, gal_ref, gm_ref, vec_ref,
    grads, rim,
):
    rows = rim_before.shape[0]
    tokens, model = gb.shape
    frames = tokens // rows
    start = info[0].astype(f32)
    parts = model // 128
    sums = [total(totals[:, k, :]) for k in range(2 * parts)]
    total_a = jnp.concatenate(sums[:parts], axis=1)
    total_b = jnp.concatenate(sums[parts:], axis=1)
    inverse, per_count = inv[0:1], inv[1:2]
    scale = gain[5:6]

    def grad_of(grad, normal, valid):
        shared = valid * (scale * (total_a + normal * total_b) * per_count)
        return (inverse * (grad * scale - shared)).astype(bf16).astype(f32)

    tap_grads = [0.0] * KERNEL
    for row in range(rows):
        here = slice(row * frames, (row + 1) * frames)
        last = info[1 + rows + row].astype(f32)
        at = column(frames, start)
        edge_at = column(RIM_GRAD, start - RIM_GRAD)
        grads[0:RIM_GRAD] = grad_of(
            edge_before[row, :, :model],
            edge_before[row, :, model:],
            (edge_at < last).astype(f32),
        )
        grads[RIM_GRAD : RIM_GRAD + frames] = grad_of(
            gb[here], bn[here], (at < last).astype(f32)
        )
        edge_at = column(RIM_GRAD, start + frames)
        grads[RIM_GRAD + frames :] = grad_of(
            edge_after[row, :, :model],
            edge_after[row, :, model:],
            (edge_at < last).astype(f32),
        )
        rim[0:RIM] = rim_before[row].astype(f32)
        rim[RIM : RIM + frames] = gated[here].astype(f32)
        rim[RIM + frames :] = rim_after[row].astype(f32)
        low, high = bounds(ends[row : row + 1, :], at, row_len)
        own = grads[RIM_GRAD : RIM_GRAD + frames]
        grad_gated = jnp.zeros((frames, model), f32)
        for tap in range(KERNEL):
            off = tap - HALF
            keep = ((at + off >= low) & (at + off < high)).astype(f32)
            tap_grads[tap] += total(own * (rim[RIM + off : RIM + off + frames] * keep))
            mirror = KERNEL - 1 - tap
            grad_gated += taps[mirror : mirror + 1] * (
                grads[RIM_GRAD + off : RIM_GRAD + off + frames] * keep
            )
        value, gate = paired[here, :model], paired[here, model:]
        sigma = sigmoid(gate)
        first = grad_gated * sigma
        gp_ref[here, :model] = first.astype(bf16)
        gp_ref[here, model:] = (first * value * (1.0 - sigma)).astype(bf16)
    for tap in range(KERNEL):
        vec_ref[tap : tap + 1] = tap_grads[tap]
    grad_paired = gp_ref[...]
    vec_ref[11:12] = total(grad_paired[:, :model].astype(f32))
    vec_ref[12:13] = total(grad_paired[:, model:].astype(f32))
    grad = dot_last(grad_paired, convolve_in[...])
    normal, inverse = normalize(after_attend[...])
    grad, gain_grad, shift_grad = norm_back(grad, normal, inverse, gain[2:3])
    vec_ref[9:10] = gain_grad
    vec_ref[10:11] = shift_grad
    vec_ref[14:15] = total_a
    vec_ref[15:16] = total_b
    grad = gcs[...] + grad
    gas_ref[...] = grad
    low = grad.astype(bf16)
    gal_ref[...] = low
    vec_ref[13:14] = total(low.astype(f32))
    gm_ref[...] = dot_last(low, attend_out[...]).astype(bf16)


def conv_back(
    row_len, info, ends, totals, inv, gb, bn, edge_before, edge_after, gated, rim_before,
    rim_after, paired, taps, after_attend, gcs, convolve_in, attend_out, gain,
):
    tokens, model = gb.shape
    rows = rim_before.shape[0]
    frames = tokens // rows
    arrays = (
        ends, totals, inv, gb, bn, edge_before, edge_after, gated, rim_before, rim_after, paired,
        taps, after_attend, gcs, convolve_in, attend_out, gain,
    )
    token = whole((tokens, model))
    return call(
        functools.partial(conv_back_body, row_len),
        (1,),
        [SMEM] + [whole(a.shape) for a in arrays],
        [whole((tokens, 2 * model)), token, token, token, whole((16, model))],
        [
            sds((tokens, 2 * model), bf16),
            sds((tokens, model), f32),
            sds((tokens, model), bf16),
            sds((tokens, model), bf16),
            sds((16, model), f32),
        ],
        [
            pltpu.VMEM((frames + 2 * RIM_GRAD, model), f32),
            pltpu.VMEM((frames + 2 * RIM, model), f32),
        ],
        flops=2 * tokens * model * 3 * model,
        moved=12 << 20,
        name="conv_back",
    )(info, *arrays)


def attend_back_body(
    qu, qv, before, lo, hi, after, prob, table, gm,
    gq_ref, g_before, g_lo, g_hi, g_after, g_table, vec_ref,
    acc,
):
    row = pl.program_id(0)
    model = qu.shape[1]
    factor = 1.0 / math.sqrt(DH)

    @pl.when(row == 0)
    def _():
        g_table[...] = jnp.zeros_like(g_table)
        vec_ref[...] = jnp.zeros_like(vec_ref)

    acc[...] = jnp.zeros_like(acc)
    blocks = (before, lo, hi, after)
    turn = flip(WIN, 1)
    for block in range(2):
        here = slice(WIN * block, WIN * (block + 1))
        span = slice(WIN * block, WIN * block + SPAN)
        qu_here = dot(turn, qu[here]).astype(bf16)
        qv_here = dot(turn, qv[here]).astype(bf16)
        gm_here = dot(turn, gm[here]).astype(bf16)
        for pair in range(PAIRS):
            cut = slice(2 * DH * pair, 2 * DH * (pair + 1))
            cut_v = slice(model + 2 * DH * pair, model + 2 * DH * (pair + 1))
            keys = jnp.concatenate([b[0, :, cut] for b in blocks[block : block + 3]], axis=0)
            values = jnp.concatenate([b[0, :, cut_v] for b in blocks[block : block + 3]], axis=0)
            weights = prob[0, block, pair]
            grad_mixed = two_heads(gm_here[:, cut])
            grad = dot_last(grad_mixed, values)
            wide = weights.astype(f32)
            delta = jnp.sum(wide * grad, axis=1, keepdims=True)
            raw_wide = wide * (grad - delta)
            raw = raw_wide.astype(bf16)
            acc[span, cut_v] += dot_first(weights, grad_mixed)
            acc[span, cut] += dot_first(raw, two_heads(qu_here[:, cut]))
            grad_u = one_pair(dot(raw, keys)) * factor
            band = pltpu.roll(
                raw.astype(f32).reshape(2, WIN, SPAN),
                SPAN - (WIN - 1),
                2,
                stride=1,
                stride_axis=1,
            )
            band = band.astype(bf16).reshape(2 * WIN, SPAN)
            grad_v = one_pair(dot(band, table[:, cut])) * factor
            g_table[:, cut] += dot_first(band, two_heads(qv_here[:, cut]))
            vec_ref[0:1, cut] += total(grad_u)
            vec_ref[1:2, cut] += total(grad_v)
            gq_ref[here, cut] = dot(turn, (grad_u + grad_v).astype(bf16)).astype(bf16)
    g_before[0] = acc[0:WIN].astype(bf16)
    g_lo[0] = acc[WIN : 2 * WIN]
    g_hi[0] = acc[2 * WIN : 3 * WIN]
    g_after[0] = acc[3 * WIN :].astype(bf16)


def attend_back(qu, qv, before, lo, hi, after, prob, table, gm):
    tokens, model = qu.shape
    rows = lo.shape[0]
    frames = tokens // rows
    tile = pl.BlockSpec((frames, model), lambda i: (i, 0))
    kv = pl.BlockSpec((1, WIN, 2 * model), lambda i: (i, 0, 0))
    return call(
        attend_back_body,
        (rows,),
        [
            tile, tile, kv, kv, kv, kv,
            pl.BlockSpec((1,) + prob.shape[1:], lambda i: (i, 0, 0, 0, 0)),
            whole(table.shape),
            tile,
        ],
        [tile, kv, kv, kv, kv, whole((SPAN, model)), whole((8, model))],
        [
            sds((tokens, model), bf16),
            sds((rows, WIN, 2 * model), bf16),
            sds((rows, WIN, 2 * model), f32),
            sds((rows, WIN, 2 * model), f32),
            sds((rows, WIN, 2 * model), bf16),
            sds((SPAN, model), f32),
            sds((8, model), f32),
        ],
        [pltpu.VMEM((4 * WIN, 2 * model), f32)],
        flops=16 * 14 * 256 * 384 * 128,
        moved=16 << 20,
        name="attend_back",
    )(qu, qv, before, lo, hi, after, prob, table, gm)


def back_body(
    gq, g_lo, g_hi, from_left, from_right, attend_in, after_first, gas, gain,
    gj_ref, gfs_ref, gl_ref, vec_ref,
):
    rows = g_lo.shape[0]
    tokens, model = after_first.shape
    frames = tokens // rows
    gj_ref[:, :model] = gq[...]
    for row in range(rows):
        at = row * frames
        lower = g_lo[row] + from_left[row].astype(f32)
        upper = g_hi[row] + from_right[row].astype(f32)
        gj_ref[at : at + WIN, model:] = lower.astype(bf16)
        gj_ref[at + WIN : at + 2 * WIN, model:] = upper.astype(bf16)
    joined = gj_ref[...]
    vec_ref[0:1] = total(joined[:, :model].astype(f32))
    vec_ref[1:2] = total(joined[:, 2 * model :].astype(f32))
    grad = dot_last(joined, attend_in[...])
    normal, inverse = normalize(after_first[...])
    grad, gain_grad, shift_grad = norm_back(grad, normal, inverse, gain[1:2])
    vec_ref[2:3] = gain_grad
    vec_ref[3:4] = shift_grad
    grad = gas[...] + grad
    gfs_ref[...] = grad
    low = (0.5 * grad).astype(bf16)
    gl_ref[...] = low
    vec_ref[4:5] = total(low.astype(f32))


def back(gq, g_lo, g_hi, from_left, from_right, attend_in, after_first, gas, gain):
    tokens, model = after_first.shape
    arrays = (gq, g_lo, g_hi, from_left, from_right, attend_in, after_first, gas, gain)
    token = whole((tokens, model))
    return call(
        back_body,
        (1,),
        [whole(a.shape) for a in arrays],
        [whole((tokens, 3 * model)), token, token, whole((8, model))],
        [
            sds((tokens, 3 * model), bf16),
            sds((tokens, model), f32),
            sds((tokens, model), bf16),
            sds((8, model), f32),
        ],
        flops=2 * tokens * model * 3 * model,
        moved=10 << 20,
        name="back",
    )(*arrays)


def keep_half(block, core, mine_ref, other_ref):
    chunks, width, model = mine_ref.shape
    shaped = block.reshape(chunks, 2, width, model)
    even, odd = shaped[:, 0], shaped[:, 1]
    mine_ref[...] = jnp.where(core == 0, even, odd).astype(bf16)
    other_ref[...] = jnp.where(core == 0, odd, even).astype(bf16)


def out_weights_body(core, act, gl, mine_ref, other_ref):
    keep_half(dot_first(act[...], gl[...]), core[0], mine_ref, other_ref)


def out_weights(core, n, act, gl):
    tokens, model = gl.shape
    hidden = act.shape[1]
    part = 512
    width = hidden // n
    half = pl.BlockSpec((part // (2 * width), width, model), lambda i: (i, 0, 0))
    return call(
        out_weights_body,
        (hidden // part,),
        [SMEM, pl.BlockSpec((tokens, part), lambda i: (0, i)), whole((tokens, model))],
        [half, half],
        [sds((n // 2, width, model), bf16)] * 2,
        flops=2 * tokens * model * hidden,
        moved=5 << 20,
        name="out_weights",
    )(core, act, gl)


def first_back_body(core, gl, slope, w_in, w_out, n0, mine_ref, other_ref, fb_ref, gn_ref):
    step = pl.program_id(0)

    @pl.when(step == 0)
    def _():
        gn_ref[...] = jnp.zeros_like(gn_ref)

    grad = (dot_last(gl[...], w_out[0]) * slope[...].astype(f32)).astype(bf16)
    keep_half(dot_first(grad, n0[...]), core[0], mine_ref, other_ref)
    fb_ref[...] = total(grad.astype(f32))
    gn_ref[...] += dot_last(grad, w_in[0])


def first_back(core, n, gl, slope, feed_in, feed_out, n0):
    tokens, model = gl.shape
    hidden = feed_in.shape[2]
    part = 512
    width = hidden // n
    token = whole((tokens, model))
    half = pl.BlockSpec((part // (2 * width), width, model), lambda i: (i, 0, 0))
    return call(
        first_back_body,
        (hidden // part,),
        [
            SMEM, token,
            pl.BlockSpec((tokens, part), lambda i: (0, i)),
            pl.BlockSpec((1, model, part), lambda i: (0, 0, i)),
            pl.BlockSpec((1, part, model), lambda i: (0, i, 0)),
            token,
        ],
        [half, half, pl.BlockSpec((1, part), lambda i: (0, i)), token],
        [
            sds((n // 2, width, model), bf16),
            sds((n // 2, width, model), bf16),
            sds((1, hidden), f32),
            sds((tokens, model), f32),
        ],
        flops=2 * tokens * model * hidden * 3,
        moved=12 << 20,
        name="first_back",
    )(core, gl, slope, feed_in, feed_out, n0)


def last_body(features, gn, gfs, gain, out_ref, vec_ref):
    normal, inverse = normalize(features[...].astype(f32))
    grad, gain_grad, shift_grad = norm_back(gn[...], normal, inverse, gain[0:1])
    out_ref[...] = gfs[...] + grad
    vec_ref[0:1] = gain_grad
    vec_ref[1:2] = shift_grad


def last(features, gn, gfs, gain):
    tokens, model = gn.shape
    token = whole((tokens, model))
    return call(
        last_body,
        (1,),
        [token, token, token, whole(gain.shape)],
        [token, whole((8, model))],
        [sds((tokens, model), f32), sds((8, model), f32)],
        flops=tokens * model * 20,
        moved=4 << 20,
        name="last",
    )(features, gn, gfs, gain)


def outer_body(lefts, rights, places, *refs):
    ins, out = refs[:-1], refs[-1]
    for (left, right), at in zip(zip(lefts, rights), places):
        block = dot_first(ins[left][...], ins[right][...])
        out[:, at : at + block.shape[1]] = block.astype(bf16)


def feed_weights(gi, nf, act, gl):
    tokens, model = nf.shape
    hidden = gi.shape[1]
    part = 512
    tile = pl.BlockSpec((tokens, part), lambda i: (0, i))
    return call(
        functools.partial(outer_body, (0, 2), (1, 3), (0, model)),
        (hidden // part,),
        [tile, whole((tokens, model)), tile, whole((tokens, model))],
        pl.BlockSpec((part, 2 * model), lambda i: (i, 0)),
        sds((hidden, 2 * model), bf16),
        flops=4 * tokens * model * hidden,
        moved=10 << 20,
        name="feed_weights",
    )(gi, nf, act, gl)


def side_body(sw, gcl, nc, gp, mixed, gal, sinusoid, g_table, first, second):
    model = sw.shape[1]
    first[:, 0:model] = dot_first(sw[...], gcl[...]).astype(bf16)
    first[:, model:] = dot_first(nc[...], gp[...]).astype(bf16)
    second[:, 0:model] = dot_first(mixed[...], gal[...]).astype(bf16)
    high = g_table[...].astype(bf16)
    low = (g_table[...] - high.astype(f32)).astype(bf16)
    grad = dot_first(sinusoid[...], high) + dot_first(sinusoid[...], low)
    second[:, model:] = grad.astype(bf16)


def side_weights(sw, gcl, nc, gp, mixed, gal, sinusoid, g_table):
    tokens, model = sw.shape
    arrays = (sw, gcl, nc, gp, mixed, gal, sinusoid, g_table)
    return call(
        side_body,
        (1,),
        [whole(a.shape) for a in arrays],
        [whole((model, 3 * model)), whole((model, 2 * model))],
        [sds((model, 3 * model), bf16), sds((model, 2 * model), bf16)],
        flops=2 * tokens * model * model * 6,
        moved=8 << 20,
        name="side_weights",
    )(*arrays)


def joined_body(na, gj, out):
    out[...] = dot_first(na[...], gj[...]).astype(bf16)


def joined_weights(na, gj):
    tokens, model = na.shape
    return call(
        joined_body,
        (1,),
        [whole(na.shape), whole(gj.shape)],
        whole((model, 3 * model)),
        sds((model, 3 * model), bf16),
        flops=2 * tokens * model * 3 * model,
        moved=5 << 20,
        name="joined_weights",
    )(na, gj)


def neighbours(last_block, first_block):
    devices = lax.axis_size("frames")
    up = [(i, i + 1) for i in range(devices - 1)]
    down = [(i + 1, i) for i in range(devices - 1)]
    return lax.ppermute(last_block, "frames", up), lax.ppermute(first_block, "frames", down)


def gather(copies):
    return lax.all_to_all(copies, DEVICES, 0, 0, tiled=True)


def scatter_sum(grads):
    part = lax.psum_scatter(grads, "frames", scatter_dimension=0, tiled=True)
    other = lax.ppermute(part, "rows", [(0, 1), (1, 0)])
    return part.astype(f32) + other.astype(f32)


ROW_PAIR = [(0, 1), (1, 0)]


def swap(x, k):
    n = lax.axis_size("frames")
    return lax.ppermute(x, "frames", [(i, i ^ k) for i in range(n)])


def parted(x, k):
    shaped = x.reshape((x.shape[0] // 2, 2) + x.shape[1:])
    bit = (lax.axis_index("frames") // k) % 2
    mine = lax.dynamic_index_in_dim(shaped, bit, 1, keepdims=False)
    other = lax.dynamic_index_in_dim(shaped, 1 - bit, 1, keepdims=False)
    return mine, other


def chunked(x):
    n = lax.axis_size("frames")
    return parted(x.reshape((n, -1) + x.shape[1:]), 1)


def sum_rows_last(mine, other):
    x = mine + swap(other, 1)
    k = 2
    while k < lax.axis_size("frames"):
        mine, other = parted(x, k)
        x = mine + swap(other, k)
        k *= 2
    x = x[0]
    return x.astype(f32) + lax.ppermute(x, "rows", ROW_PAIR).astype(f32)


def sum_rows_first(mine, other):
    x = mine + swap(other, 1)
    my_row = lax.axis_index("rows")
    half = x.shape[2] // 2
    left, right = x[:, :, :half], x[:, :, half:]
    mine = jnp.where(my_row == 0, left, right)
    other = jnp.where(my_row == 0, right, left)
    x = mine + lax.ppermute(other, "rows", ROW_PAIR)
    k = 2
    while k < lax.axis_size("frames"):
        mine, other = parted(x, k)
        x = mine + swap(other, k)
        k *= 2
    x = x[0]
    other = lax.ppermute(x, "rows", ROW_PAIR)
    left = jnp.where(my_row == 0, x, other)
    right = jnp.where(my_row == 0, other, x)
    return jnp.concatenate([left, right], axis=1).astype(f32)


def per_device(
    features,
    lengths,
    windows,
    feed_in,
    feed_in_bias,
    feed_out,
    attend_in,
    attend_out,
    position_proj,
    convolve_in,
    convolve_out,
    depthwise,
    norm_gain,
    norm_shift,
    biases,
    cotangent,
):
    rows, frames, model = features.shape
    tokens = rows * frames
    n = lax.axis_size("frames")
    devices = lax.axis_size("rows") * n
    row_len = float(frames * n)
    me = lax.axis_index("frames")
    start = me * frames
    hidden = feed_in.shape[2]
    ends_every = jnp.cumsum(lengths, axis=1, dtype=jnp.int32)
    ends_here = lax.dynamic_slice_in_dim(ends_every, lax.axis_index("rows") * rows, rows, 0)
    ends = ends_here.astype(f32)
    info = jnp.concatenate([start[None].astype(jnp.int32), windows, ends_here[:, -1]])
    starts = jnp.arange(n, dtype=jnp.int32) * frames
    counts = jnp.clip(ends_every[:, -1][:, None] - starts[None, :], 0, frames)
    counts = jnp.sum(counts.reshape(-1, rows, n), axis=1).astype(f32).reshape(devices, 1)
    flat = features.reshape(tokens, model)
    sinusoid = jnp.asarray(position_table(WIN, model))

    after_first, n0, na, qu, qv, lo, hi, act0, slope0 = front(
        flat, feed_in, feed_in_bias, feed_out, attend_in, norm_gain, norm_shift, biases, rows
    )
    before, after = neighbours(hi, lo)
    prob, mixed, after_attend, nc, paired, gated, first, final, table = attend(
        row_len, info, ends, qu, qv, before, lo, hi, after, sinusoid, position_proj, after_first,
        attend_out, convolve_in, norm_gain, norm_shift, biases,
    )
    rim_before, rim_after = neighbours(final, first)
    depth, stats = depth_conv(
        row_len, devices, info, ends, gated, rim_before, rim_after, depthwise
    )
    stats = gather(stats)
    (
        out, act1, gi1, nf, gl1, sw, gcl, gcs, gb, bn, inv, totals, first, final, vec_middle, fb1,
    ) = middle(
        devices, rows, info, stats, counts, depth, after_attend, feed_in, feed_in_bias, feed_out,
        convolve_out, norm_gain, norm_shift, biases, cotangent.reshape(tokens, model),
    )
    edge_before, edge_after = neighbours(final, first)
    totals = gather(totals)
    feed1 = feed_weights(gi1, nf, act1, gl1)
    totals, feed1 = lax.optimization_barrier((totals, feed1))
    feed1 = scatter_sum(feed1)
    gp, gas, gal, gm, vec_conv = conv_back(
        row_len, info, ends, totals, inv, gb, bn, edge_before, edge_after, gated, rim_before,
        rim_after, paired, depthwise, after_attend, gcs, convolve_in, attend_out, norm_gain,
    )
    gq, g_before, g_lo, g_hi, g_after, g_table, vec_attend = attend_back(
        qu, qv, before, lo, hi, after, prob, table, gm
    )
    from_left, from_right = neighbours(g_after, g_before)
    side_a, side_b = side_weights(sw, gcl, nc, gp, mixed, gal, sinusoid, g_table)
    from_left, from_right, side_a, side_b = lax.optimization_barrier(
        (from_left, from_right, side_a, side_b)
    )
    side_a = sum_rows_first(*chunked(side_a))
    side_b = sum_rows_last(*chunked(side_b))
    core = (me % 2)[None].astype(jnp.int32)
    gj, gfs, gl0, vec_back = back(
        gq, g_lo, g_hi, from_left, from_right, attend_in, after_first, gas, norm_gain
    )
    out0 = out_weights(core, n, act0, gl0)
    out0 = sum_rows_first(*out0)
    in0_mine, in0_other, fb0, gn = first_back(core, n, gl0, slope0, feed_in, feed_out, n0)
    in0 = sum_rows_last(in0_mine, in0_other)
    joined = sum_rows_last(*chunked(joined_weights(na, gj)))
    grad_features, vec_last = last(flat, gn, gfs, norm_gain)

    slim = model // n
    width = hidden // n
    vectors = jnp.concatenate(
        [
            vec_conv[:KERNEL],
            vec_last[0:1], vec_back[2:3], vec_conv[9:10], vec_middle[0:1], vec_middle[2:3],
            vec_last[1:2], vec_back[3:4], vec_conv[10:11], vec_middle[1:2], vec_middle[3:4],
            vec_back[0:2], vec_conv[13:14], vec_conv[11:13], vec_middle[4:5], vec_back[4:5],
            vec_middle[5:6], vec_attend[0:2],
        ],
        axis=0,
    )
    n_vectors = vectors.shape[0]
    vectors = vectors.reshape(n_vectors, n, slim).transpose(1, 0, 2).reshape(n, -1)
    feed_bias = jnp.concatenate([fb0, fb1], axis=0).reshape(2, n, width).transpose(1, 0, 2)
    small = jnp.concatenate([vectors, feed_bias.reshape(n, -1)], axis=1)
    small = jnp.concatenate([small] * lax.axis_size("rows"), axis=0)
    small = jnp.sum(lax.all_to_all(small, DEVICES, 0, 0, tiled=True), axis=0)
    thin = small[: n_vectors * slim].reshape(n_vectors, slim)
    feed_bias = small[n_vectors * slim :].reshape(2, width)
    total_rows = lax.dynamic_slice_in_dim(vec_conv[14:16], me * slim, slim, 1)
    return (
        out.reshape(rows, frames, model),
        grad_features.reshape(rows, frames, model),
        jnp.stack([in0.T, feed1[:, :model].T]),
        feed_bias,
        jnp.stack([out0, feed1[:, model:]]),
        joined,
        side_b[:, :model],
        side_b[:, model:],
        side_a[:, model:],
        side_a[:, :model],
        thin[:KERNEL],
        jnp.concatenate([thin[KERNEL : KERNEL + 5], total_rows[1:2]], axis=0),
        jnp.concatenate([thin[KERNEL + 5 : KERNEL + 10], total_rows[0:1]], axis=0),
        thin[KERNEL + 10 :],
    )


def solution(mesh):
    placed = (
        P("rows", "frames", None),
        P(),
        P("rows"),
        P(),
        P(),
        P(),
        P(),
        P(),
        P(),
        P(),
        P(),
        P(),
        P(),
        P(),
        P(),
        P("rows", "frames", None),
    )
    return jax.shard_map(
        per_device,
        mesh=mesh,
        in_specs=placed,
        out_specs=(
            P("rows", "frames", None),
            P("rows", "frames", None),
            P(None, None, "frames"),
            P(None, "frames"),
            P(None, "frames", None),
            P("frames", None),
            P("frames", None),
            P("frames", None),
            P("frames", None),
            P("frames", None),
            P(None, "frames"),
            P(None, "frames"),
            P(None, "frames"),
            P(None, "frames"),
        ),
        check_vma=False,
    )
```

```python
import functools
import math

import jax
import jax.numpy as jnp
import ml_dtypes
import numpy as np
from jax import lax
from jax.experimental import pallas as pl
from jax.experimental.pallas import tpu as pltpu
from jax.sharding import PartitionSpec as P

H = 8
DH = 64
KERNEL = 9
WIN = 128

HALF = KERNEL // 2
SPAN = 3 * WIN
MANY = 4
GROUPS = H // MANY
WIDE = MANY * DH
RIM = 16
RIM_GRAD = 8
eps_norm = 1e-05
negative = -1e30
f32 = jnp.float32
bf16 = jnp.bfloat16
DEVICES = ("rows", "frames")
VMEM_LIMIT = 60 * 1024 * 1024
FOLD_LIMIT = 14 * 1024 * 1024


def dot(left, right):
    return jnp.dot(left, right, preferred_element_type=f32)


def dot_last(left, right):
    return lax.dot_general(left, right, (((1,), (1,)), ((), ())), preferred_element_type=f32)


def dot_first(left, right):
    return lax.dot_general(left, right, (((0,), (0,)), ((), ())), preferred_element_type=f32)


def sigmoid(x):
    return 0.5 * jnp.tanh(0.5 * x) + 0.5


def total(x):
    return jnp.sum(x, axis=0, keepdims=True)


def normalize(values):
    centered = values - jnp.mean(values, axis=-1, keepdims=True)
    inverse = lax.rsqrt(jnp.mean(centered * centered, axis=-1, keepdims=True) + eps_norm)
    return centered * inverse, inverse


def norm_back(grad_out, normal, inverse, gain):
    scaled = grad_out * gain
    centred = scaled - jnp.mean(scaled, axis=-1, keepdims=True)
    grad_in = inverse * (centred - normal * jnp.mean(scaled * normal, axis=-1, keepdims=True))
    return grad_in, total(grad_out * normal), total(grad_out)


def position_table(width, model):
    offsets = (np.arange(2 * width + 1) - width).astype(np.float32)
    rates = np.exp(
        np.arange(model // 2).astype(np.float32) * np.float32(-2.0 * math.log(10000.0) / model)
    )
    angles = (offsets[:, None] * rates[None, :]).astype(np.float32)
    both = np.stack([np.sin(angles), np.cos(angles)], axis=2).reshape(2 * width + 1, model)
    padded = np.zeros((3 * width, model), np.float32)
    padded[: 2 * width + 1] = both
    return padded.astype(ml_dtypes.bfloat16)


def bounds(ends, at, row_len):
    low = jnp.max(jnp.where(ends <= at, ends, 0.0), axis=1, keepdims=True)
    high = jnp.min(jnp.where(ends > at, ends, row_len), axis=1, keepdims=True)
    return low, high


def column(count, offset):
    return lax.broadcasted_iota(jnp.int32, (count, 1), 0).astype(f32) + offset


def head_lanes(rows):
    return lax.broadcasted_iota(jnp.int32, (rows, WIDE), 1) // DH


def heads_apart(group):
    at = head_lanes(group.shape[0])
    zero = jnp.zeros_like(group)
    return jnp.concatenate([jnp.where(at == k, group, zero) for k in range(MANY)], axis=0)


def heads_joined(stacked):
    rows = stacked.shape[0] // MANY
    at = head_lanes(rows)
    joined = stacked[:rows]
    for k in range(1, MANY):
        joined = jnp.where(at == k, stacked[k * rows : (k + 1) * rows], joined)
    return joined


def beside(stacked):
    rows = stacked.shape[0] // MANY
    return jnp.concatenate([stacked[k * rows : (k + 1) * rows] for k in range(MANY)], axis=1)


def below(joined):
    width = joined.shape[1] // MANY
    return jnp.concatenate([joined[:, k * width : (k + 1) * width] for k in range(MANY)], axis=0)


def flip(rows):
    i = lax.broadcasted_iota(jnp.int32, (rows, rows), 0)
    j = lax.broadcasted_iota(jnp.int32, (rows, rows), 1)
    return (i + j == rows - 1).astype(f32).astype(bf16)


class Stage:
    def __init__(self, loads, stores, sems):
        self.loads, self.stores, self.sems = loads, stores, sems
        self.copies, self.waited, self.sent, self.pending = {}, set(), set(), []
        self.used = 0
        for key, (source, buffer) in loads.items():
            self.copies[key] = pltpu.make_async_copy(source, buffer, self.sem())
            self.copies[key].start()

    def sem(self):
        self.used += 1
        return self.sems.at[self.used - 1]

    def __getitem__(self, key):
        if key in self.stores:
            return self.stores[key][1]
        if key not in self.waited:
            self.copies[key].wait()
            self.waited.add(key)
        return self.loads[key][1]

    def send(self, key, at=None):
        target, buffer = self.stores[key]
        if at is not None:
            target, buffer = target.at[at], buffer.at[at]
        copy = pltpu.make_async_copy(buffer, target, self.sem())
        copy.start()
        self.pending.append(copy)
        self.sent.add(key)

    def finish(self):
        for key in self.stores:
            if key not in self.sent:
                self.send(key)
        for key in self.loads:
            self[key]
        for copy in self.pending:
            copy.wait()


def staged(
    name, body, ins, outs, smem=(), scratch=(), flops=0, moved=0, sends=0, filled=None,
    limit=VMEM_LIMIT,
):
    operands, loads = [], []
    for key, item in ins.items():
        array, view, shape = item if isinstance(item, tuple) else (item, None, item.shape)
        at = next((i for i, other in enumerate(operands) if other is array), None)
        if at is None:
            at = len(operands)
            operands.append(array)
        loads.append((key, at, view, shape, array.dtype))
    outs = {
        key: item if isinstance(item, tuple) else (item, None, item.shape)
        for key, item in outs.items()
    }
    aliases = {}
    if filled is not None:
        aliases = {len(smem) + len(operands): 0}
        operands.append(filled)
    n_smem, n_ops, n_outs, n_loads = len(smem), len(operands), len(outs), len(loads)

    def run(*refs):
        cuts = [n_smem, n_ops, n_outs, n_loads, n_outs, 1]
        groups, at = [], 0
        for cut in cuts:
            groups.append(refs[at : at + cut])
            at += cut
        scalars, given, targets, buffers, results, sems = groups
        stage = Stage(
            {
                key: (given[at] if view is None else view(given[at]), buffer)
                for (key, at, view, _, _), buffer in zip(loads, buffers)
            },
            {
                key: (target if view is None else view(target), result)
                for (key, (_, view, _)), target, result in zip(outs.items(), targets, results)
            },
            sems[0],
        )
        body(stage, *scalars, *refs[at:])
        stage.finish()

    hbm = pl.BlockSpec(memory_space=pl.ANY)
    got = pl.pallas_call(
        run,
        in_specs=[pl.BlockSpec(memory_space=pltpu.SMEM)] * n_smem + [hbm] * n_ops,
        out_specs=[hbm] * n_outs,
        out_shape=[whole for whole, _, _ in outs.values()],
        scratch_shapes=[pltpu.VMEM(shape, dtype) for _, _, _, shape, dtype in loads]
        + [pltpu.VMEM(shape, whole.dtype) for whole, _, shape in outs.values()]
        + [pltpu.SemaphoreType.DMA((n_loads + n_outs + sends,))]
        + list(scratch),
        input_output_aliases=aliases,
        compiler_params=pltpu.CompilerParams(vmem_limit_bytes=limit),
        cost_estimate=pl.CostEstimate(flops=flops, bytes_accessed=moved, transcendentals=0),
        name=name,
    )(*smem, *operands)
    return dict(zip(outs, got))


def sds(shape, dtype):
    return jax.ShapeDtypeStruct(shape, dtype)


def slab(array, *at):
    shape = tuple(a[1] for a in at if isinstance(a, tuple))
    index = tuple(pl.ds(*a) if isinstance(a, tuple) else a for a in at)
    return (array, lambda ref: ref.at[index], shape)


PART = 1024


def activate(inner):
    half = 0.5 * inner
    turn = jnp.tanh(half)
    up = 1.0 + turn
    active = half * up
    return active, 0.5 * (up + active * (1.0 - turn))


def feed_slabs(feed_in, feed_out, module):
    _, model, hidden = feed_in.shape
    slabs = {}
    for k in range(hidden // PART):
        slabs[f"w_in{k}"] = slab(feed_in, module, (0, model), (k * PART, PART))
        slabs[f"w_out{k}"] = slab(feed_out, module, (k * PART, PART), (0, model))
    return slabs


def front(row, features, feed_in, feed_in_bias, feed_out, attend_in, gain, shift, bias):
    _, frames, model = features.shape
    hidden = feed_in.shape[2]
    parts = hidden // PART
    low = sds((frames, model), bf16)

    def body(k):
        gain, shift = k["gain"], k["shift"]
        x = k["x"][...].astype(f32)
        normal, _ = normalize(x)
        k["n0"][...] = (normal * gain[0:1] + shift[0:1]).astype(bf16)
        k.send("n0")
        for part in range(parts):
            cut = slice(part * PART, (part + 1) * PART)
            inner = dot(k["n0"][...], k[f"w_in{part}"][...]) + k["b_in"][0:1, cut]
            active, slope = activate(inner)
            k["act"][:, cut] = active.astype(bf16)
            k["slope"][:, cut] = slope.astype(bf16)
        k.send("slope")
        k.send("act")
        branch = k["bias"][6:7]
        for part in range(parts):
            cut = slice(part * PART, (part + 1) * PART)
            branch = branch + dot(k["act"][:, cut], k[f"w_out{part}"][...])
        after = x + 0.5 * branch
        k["after"][...] = after
        k.send("after")
        normal, _ = normalize(after)
        normed = (normal * gain[1:2] + shift[1:2]).astype(bf16)
        k["na"][...] = normed
        k.send("na")
        attend_in, bias = k["attend_in"], k["bias"]
        keys = dot(normed, attend_in[:, model : 2 * model]).astype(bf16)
        values = (dot(normed, attend_in[:, 2 * model :]) + bias[1:2]).astype(bf16)
        k["lo"][:, :model] = keys[:WIN]
        k["lo"][:, model:] = values[:WIN]
        k["hi"][:, :model] = keys[WIN:]
        k["hi"][:, model:] = values[WIN:]
        k.send("lo")
        k.send("hi")
        query = dot(normed, attend_in[:, :model]) + bias[0:1]
        factor = 1.0 / math.sqrt(DH)
        k["qu"][...] = ((query + bias[8:9]) * factor).astype(bf16)
        k["qv"][...] = ((query + bias[9:10]) * factor).astype(bf16)

    ins = {"x": slab(features, row, (0, frames), (0, model)), "gain": gain, "shift": shift}
    ins["b_in"] = feed_in_bias
    weights = feed_slabs(feed_in, feed_out, 0)
    ins |= {key: weights[key] for key in weights if "in" in key}
    ins["bias"] = bias
    ins |= {key: weights[key] for key in weights if "out" in key}
    ins["attend_in"] = attend_in
    return staged(
        "front",
        body,
        ins,
        {
            "after": sds((frames, model), f32), "n0": low, "na": low, "qu": low, "qv": low,
            "lo": sds((WIN, 2 * model), bf16), "hi": sds((WIN, 2 * model), bf16),
            "act": sds((frames, hidden), bf16), "slope": sds((frames, hidden), bf16),
        },
        flops=2 * frames * model * (2 * hidden + 3 * model),
        moved=10 << 20,
    )


def attend(
    row_len, row, rows, info, ends, got, before, after, sinusoid, proj, table, attend_out,
    convolve_in, gain, shift, bias, edges,
):
    frames, model = got["after"].shape
    low = sds((frames, model), bf16)
    final = row == rows - 1

    def body(k, info):
        if table is None:
            k["table"][...] = dot(k["sinusoid"][...], k["proj"][...]).astype(bf16)
            k.send("table")
        bands = k["table"]
        start = info[0].astype(f32)
        reach = info[1 + row].astype(f32)
        row_ends = k["ends"][row : row + 1, :]
        turn = flip(WIN)
        key_at = lax.broadcasted_iota(jnp.int32, (WIN, SPAN), 1).astype(f32)
        blocks = (k["before"], k["lo"], k["hi"], k["next"])
        qu, qv = k["qu"], k["qv"]
        for block in range(2):
            at = column(WIN, start + WIN * block)
            lower, upper = bounds(row_ends, at, row_len)
            base = start + (WIN * (block - 1))
            lower = jnp.maximum(lower, at - reach) - base
            upper = jnp.minimum(upper - 1.0, at + reach) - base
            allowed = ((key_at >= lower) & (key_at <= upper))[None]
            here = slice(WIN * block, WIN * (block + 1))
            some = blocks[block : block + 3]

            for group in range(GROUPS):
                cut = slice(WIDE * group, WIDE * (group + 1))
                cut_v = slice(model + WIDE * group, model + WIDE * (group + 1))
                keys = jnp.concatenate([b[:, cut] for b in some], axis=0)
                values = jnp.concatenate([b[:, cut_v] for b in some], axis=0)
                spread = dot_last(heads_apart(qv[here, cut]), bands[:, cut])
                content = dot_last(heads_apart(qu[here, cut]), keys)
                spread = pltpu.roll(
                    spread.reshape(MANY, WIN, SPAN), 0, 2, stride=1, stride_axis=1
                )
                scores = jnp.where(allowed, content.reshape(MANY, WIN, SPAN) + spread, negative)
                powers = jnp.exp(scores - jnp.max(scores, axis=2, keepdims=True))
                weights = powers * (1.0 / jnp.sum(powers, axis=2, keepdims=True))
                weights = weights.astype(bf16).reshape(MANY * WIN, SPAN)
                k["mixed"][here, cut] = heads_joined(dot(weights, values)).astype(bf16)
                k["prob"][block, group] = dot(turn, beside(weights)).astype(bf16)
            k.send("prob", block)
        k.send("mixed")
        after_attend = k["after"][...] + dot(k["mixed"][...], k["attend_out"][...])
        after_attend = after_attend + k["bias"][2:3]
        k["out"][...] = after_attend
        k.send("out")
        normal, _ = normalize(after_attend)
        normed = (normal * k["gain"][2:3] + k["shift"][2:3]).astype(bf16)
        k["nc"][...] = normed
        k.send("nc")
        value = dot(normed, k["convolve_in"][:, :model]) + k["bias"][3:4]
        k["paired"][:, :model] = value
        gate = dot(normed, k["convolve_in"][:, model:]) + k["bias"][4:5]
        k["paired"][:, model:] = gate
        k.send("paired")
        gated = (value * sigmoid(gate)).astype(bf16)
        k["gated"][...] = gated
        if final:
            for other in range(row):
                k["first"][other] = k[f"first{other}"][...]
                k["last"][other] = k[f"last{other}"][...]
            k["first"][row] = gated[:RIM]
            k["last"][row] = gated[frames - RIM :]
        else:
            k["first"][...] = gated[:RIM]
            k["last"][...] = gated[frames - RIM :]

    ins = {"ends": ends}
    if table is None:
        ins |= {"sinusoid": sinusoid, "proj": proj}
    else:
        ins["table"] = table
    ins |= {
        "qu": got["qu"], "qv": got["qv"], "before": before, "lo": got["lo"], "hi": got["hi"],
        "next": after, "after": got["after"], "attend_out": attend_out, "bias": bias,
        "gain": gain, "shift": shift, "convolve_in": convolve_in,
    }
    for other, (first, last) in enumerate(edges):
        ins |= {f"first{other}": first, f"last{other}": last}
    rim = sds((rows, RIM, model) if final else (RIM, model), bf16)
    outs = {
        "prob": sds((2, GROUPS, WIN, MANY * SPAN), bf16), "mixed": low,
        "out": sds((frames, model), f32), "nc": low, "paired": sds((frames, 2 * model), f32),
        "gated": low, "first": rim, "last": rim,
    }
    if table is None:
        outs["table"] = sds((SPAN, model), bf16)
    return staged(
        "attend",
        body,
        ins,
        outs,
        smem=[info],
        flops=8 * 8 * 256 * 384 * 128,
        moved=8 << 20,
        sends=1,
    )


def valid_column(info, row, rows, frames):
    at = column(frames, info[0].astype(f32))
    return (at < info[1 + rows + row].astype(f32)).astype(f32)


def pack(ref, vectors):
    at = 0
    for vector in vectors:
        for k in range(0, vector.shape[1], 128):
            ref[at : at + 1, :] = vector[:, k : k + 128]
            at += 1


def by_rows(count, size, step, init=None):
    def one(i, carry):
        return step(pl.ds(pl.multiple_of(i * size, size), size), carry)

    return lax.fori_loop(0, count // size, one, init)


def by_lanes(width, step):
    def one(i, carry):
        step(pl.ds(pl.multiple_of(i * 128, 128), 128))
        return carry

    lax.fori_loop(0, width // 128, one, 0)


def spread(column):
    return jnp.broadcast_to(column, (column.shape[0], 128))


def tap_masks(keep_s, at, low, high):
    for tap in range(KERNEL):
        off = tap - HALF
        keep_s[tap] = spread(((at + off >= low) & (at + off < high)).astype(f32))


def depth_conv(row_len, devices, info, ends, gated, before, after, taps):
    frames, model = gated[0].shape
    rows = len(gated)

    def body(k, info, rim, keep_s, valid_s, sums, tile):
        start = info[0].astype(f32)
        counts = 0.0
        taps = k["taps"]
        for row in range(rows):
            here = slice(row * frames, (row + 1) * frames)
            at = column(frames, start)
            low, high = bounds(k["ends"][row : row + 1, :], at, row_len)
            tap_masks(keep_s, at, low, high)
            valid = valid_column(info, row, rows, frames)
            valid_s[here] = spread(valid)
            counts += total(valid)
            rim[0:RIM] = k["before"][row].astype(f32)
            rim[RIM : RIM + frames] = k[f"gated{row}"][...].astype(f32)
            rim[RIM + frames :] = k["after"][row].astype(f32)

            def one(lanes):
                depth = jnp.zeros((frames, 128), f32)
                for tap in range(KERNEL):
                    off = tap - HALF
                    part = rim[RIM + off : RIM + off + frames, lanes] * keep_s[tap]
                    depth += taps[tap : tap + 1, lanes] * part
                k["depth"][here, lanes] = depth
                sums[row : row + 1, lanes] = total(depth * valid_s[here])

            by_lanes(model, one)
            k.send("depth", pl.ds(row * frames, frames))
        first = total(sums[0:rows, :])
        mean = first / jnp.maximum(counts, 1.0)
        sums[rows : rows + 1, :] = mean

        def two(lanes):
            centered = k["depth"][:, lanes] - sums[rows : rows + 1, lanes]
            sums[rows + 1 : rows + 2, lanes] = total(centered * centered * valid_s[...])

        by_lanes(model, two)
        pack(tile, [first, sums[rows + 1 : rows + 2, :]])
        k["stats"][...] = jnp.broadcast_to(tile[...][None], k["stats"].shape)

    ins = {"ends": ends, "before": before, "taps": taps}
    ins |= {f"gated{row}": gated[row] for row in range(rows)}
    ins["after"] = after
    return staged(
        "depth_conv",
        body,
        ins,
        {"depth": sds((rows * frames, model), f32), "stats": sds((devices, 8, 128), f32)},
        smem=[info],
        scratch=[
            pltpu.VMEM((frames + 2 * RIM, model), f32),
            pltpu.VMEM((KERNEL, frames, 128), f32),
            pltpu.VMEM((rows * frames, 128), f32),
            pltpu.VMEM((8, model), f32),
            pltpu.VMEM((8, 128), f32),
        ],
        flops=rows * frames * model * 30,
        moved=2 << 20,
        sends=rows - 1,
    )


def middle(
    devices, rows, info, stats, counts, depth, stream, feed_in, feed_in_bias, feed_out,
    convolve_out, gain, shift, bias, cotangent,
):
    tokens, model = depth.shape
    frames = tokens // rows
    hidden = feed_in.shape[2]
    parts = hidden // PART

    def body(k, info, conv_s, slope_s, tile):
        stats, each = k["stats"], k["counts"][:, 0:1]
        gain, shift, bias = k["gain"], k["shift"], k["bias"]
        count = total(each)
        means, inverses = [], []
        for at in range(model // 128):
            sums = stats[:, at, :]
            mean = total(sums) / count
            off = sums / jnp.maximum(each, 1.0) - mean
            spread = total(stats[:, model // 128 + at, :]) + total(each * off * off)
            means.append(mean)
            inverses.append(lax.rsqrt(spread / count + eps_norm))
        mean = jnp.concatenate(means, axis=1)
        inverse = jnp.concatenate(inverses, axis=1)
        k["inv"][0:1] = inverse
        k["inv"][1:2] = jnp.broadcast_to(1.0 / count, (1, model))
        normal = (k["depth"][...] - mean) * inverse
        k["bn"][...] = normal
        k.send("bn")
        batch = normal * gain[5:6] + shift[5:6]
        swished = (batch * sigmoid(batch)).astype(bf16)
        k["sw"][...] = swished
        k.send("sw")
        streams = jnp.concatenate([k[f"stream{row}"][...] for row in range(rows)], axis=0)
        after_conv = streams + dot(swished, k["convolve_out"][...]) + bias[5:6]
        conv_s[...] = after_conv
        normal, _ = normalize(after_conv)
        k["nf"][...] = (normal * gain[3:4] + shift[3:4]).astype(bf16)
        k.send("nf")
        for part in range(parts):
            cut = slice(part * PART, (part + 1) * PART)
            inner = dot(k["nf"][...], k[f"w_in{part}"][...]) + k["b_in"][1:2, cut]
            active, slope = activate(inner)
            k["act"][:, cut] = active.astype(bf16)
            slope_s[:, cut] = slope
        k.send("act")
        branch = bias[7:8]
        for part in range(parts):
            cut = slice(part * PART, (part + 1) * PART)
            branch = branch + dot(k["act"][:, cut], k[f"w_out{part}"][...])
        normal, inverse = normalize(conv_s[...] + 0.5 * branch)
        valid = jnp.concatenate(
            [valid_column(info, row, rows, frames) for row in range(rows)], axis=0
        )
        k["out"][...] = (valid * (normal * gain[4:5] + shift[4:5])).astype(bf16)
        k.send("out")
        grad = valid * k["cotangent"][...].astype(f32)
        grad, gain_grad, shift_grad = norm_back(grad, normal, inverse, gain[4:5])
        k["gcs"][...] = grad
        low = (0.5 * grad).astype(bf16)
        k["gl"][...] = low
        k.send("gl")
        vec = k["vec"]
        vec[2:3] = gain_grad
        vec[3:4] = shift_grad
        vec[5:6] = total(low.astype(f32))
        back = 0.0
        for part in range(parts):
            cut = slice(part * PART, (part + 1) * PART)
            grad = (dot_last(k["gl"][...], k[f"w_out{part}"][...]) * slope_s[:, cut]).astype(bf16)
            k["gi"][:, cut] = grad
            k["fb"][:, cut] = total(grad.astype(f32))
            back = back + dot_last(grad, k[f"w_in{part}"][...])
        k.send("gi")
        normal, inverse = normalize(conv_s[...])
        grad, gain_grad, shift_grad = norm_back(back, normal, inverse, gain[3:4])
        vec[0:1] = gain_grad
        vec[1:2] = shift_grad
        grad = k["gcs"][...] + grad
        k["gcs"][...] = grad
        k.send("gcs")
        low = grad.astype(bf16)
        k["gcl"][...] = low
        k.send("gcl")
        vec[4:5] = total(low.astype(f32))
        bn = k["bn"][...]
        batch = bn * gain[5:6] + shift[5:6]
        _, slope = activate(batch)
        grad = dot_last(low, k["convolve_out"][...]) * slope
        k["gb"][...] = grad
        k.send("gb")
        pack(tile, [total(grad), total(grad * bn)])
        k["totals"][...] = jnp.broadcast_to(tile[...][None], k["totals"].shape)
        k.send("totals")
        for row in range(rows):
            at, end = row * frames, (row + 1) * frames
            k["first"][row, :, :model] = k["gb"][at : at + RIM_GRAD]
            k["first"][row, :, model:] = k["bn"][at : at + RIM_GRAD]
            k["last"][row, :, :model] = k["gb"][end - RIM_GRAD : end]
            k["last"][row, :, model:] = k["bn"][end - RIM_GRAD : end]

    ins = {"stats": stats, "counts": counts, "gain": gain, "shift": shift, "depth": depth}
    ins |= {"bias": bias, "convolve_out": convolve_out}
    ins |= {f"stream{row}": stream[row] for row in range(rows)}
    weights = feed_slabs(feed_in, feed_out, 1)
    ins["b_in"] = feed_in_bias
    ins |= {key: weights[key] for key in weights if "in" in key}
    ins |= {key: weights[key] for key in weights if "out" in key}
    ins["cotangent"] = cotangent
    low = sds((tokens, model), bf16)
    wide = sds((tokens, model), f32)
    rim = sds((rows, RIM_GRAD, 2 * model), f32)
    return staged(
        "middle",
        body,
        ins,
        {
            "out": low, "act": sds((tokens, hidden), bf16), "gi": sds((tokens, hidden), bf16),
            "nf": low, "gl": low, "sw": low, "gcl": low, "gcs": wide, "gb": wide, "bn": wide,
            "inv": sds((8, model), f32), "totals": sds((devices, 8, 128), f32), "first": rim,
            "last": rim, "vec": sds((8, model), f32), "fb": sds((1, hidden), f32),
        },
        smem=[info],
        scratch=[
            pltpu.VMEM((tokens, model), f32),
            pltpu.VMEM((tokens, hidden), f32),
            pltpu.VMEM((8, 128), f32),
        ],
        flops=2 * tokens * model * (4 * hidden + 2 * model),
        moved=24 << 20,
    )


def conv_back(
    row_len, info, ends, taps, convolve_in, attend_out, gain, totals, mid, edge_before,
    edge_after, rim_before, rim_after, gated, paired, after_attend,
):
    tokens, model = mid["gb"].shape
    rows = len(gated)
    frames = tokens // rows

    def body(k, info, grads, rim, keep_s):
        start = info[0].astype(f32)
        parts = model // 128
        sums = [total(k["totals"][:, at, :]) for at in range(2 * parts)]
        total_a = jnp.concatenate(sums[:parts], axis=1)
        total_b = jnp.concatenate(sums[parts:], axis=1)
        inverse, per_count = k["inv"][0:1], k["inv"][1:2]
        gain, taps, vec = k["gain"], k["taps"], k["vec"]
        own_scale = inverse * gain[5:6]
        share_a = own_scale * total_a * per_count
        share_b = own_scale * total_b * per_count
        vec[14:15] = total_a
        vec[15:16] = total_b
        vec[0:9] = jnp.zeros((9, model), f32)
        vec[9:14] = jnp.zeros((5, model), f32)

        def grad_of(grad, normal, valid):
            grad = grad * own_scale - valid * (share_a + normal * share_b)
            return grad.astype(bf16).astype(f32)

        for row in range(rows):
            first = row * frames
            last = info[1 + rows + row].astype(f32)
            at = column(frames, start)
            low, high = bounds(k["ends"][row : row + 1, :], at, row_len)
            tap_masks(keep_s, at, low, high)
            before, after = k["edge_before"], k["edge_after"]
            edge_at = column(RIM_GRAD, start - RIM_GRAD)
            grads[0:RIM_GRAD] = grad_of(
                before[row, :, :model], before[row, :, model:], (edge_at < last).astype(f32)
            )
            for step in range(0, frames, 32):
                here = slice(step, step + 32)
                at = column(32, start + step)
                grads[RIM_GRAD + step : RIM_GRAD + step + 32] = grad_of(
                    k[f"gb{row}"][here], k[f"bn{row}"][here], (at < last).astype(f32)
                )
            edge_at = column(RIM_GRAD, start + frames)
            grads[RIM_GRAD + frames :] = grad_of(
                after[row, :, :model], after[row, :, model:], (edge_at < last).astype(f32)
            )
            rim[0:RIM] = k["rim_before"][row].astype(f32)
            rim[RIM : RIM + frames] = k[f"gated{row}"][...].astype(f32)
            rim[RIM + frames :] = k["rim_after"][row].astype(f32)
            paired = k[f"paired{row}"]
            half = frames // 2

            def one(i, carry):
                lane = pl.multiple_of(i * 128, 128)
                lanes, gates = pl.ds(lane, 128), pl.ds(model + lane, 128)
                for base in range(0, frames, half):
                    own = grads[RIM_GRAD + base : RIM_GRAD + base + half, lanes]
                    grad = jnp.zeros((half, 128), f32)
                    for tap in range(KERNEL):
                        off = base + tap - HALF
                        keep = keep_s[tap, base : base + half]
                        part = own * (rim[RIM + off : RIM + off + half, lanes] * keep)
                        vec[tap : tap + 1, lanes] += total(part)
                        mirror = KERNEL - 1 - tap
                        part = grads[RIM_GRAD + off : RIM_GRAD + off + half, lanes] * keep
                        grad += taps[mirror : mirror + 1, lanes] * part
                    sigma = sigmoid(paired[base : base + half, gates])
                    one = (grad * sigma).astype(bf16)
                    value = paired[base : base + half, lanes]
                    two = (grad * sigma * value * (1.0 - sigma)).astype(bf16)
                    here = slice(first + base, first + base + half)
                    k["gp"][here, lanes] = one
                    k["gp"][here, gates] = two
                    vec[11:12, lanes] += total(one.astype(f32))
                    vec[12:13, lanes] += total(two.astype(f32))
                return carry

            lax.fori_loop(0, model // 128, one, 0)
            k.send("gp", pl.ds(first, frames))
        grad = dot_last(k["gp"][...], k["convolve_in"][...])
        streams = jnp.concatenate([k[f"after{row}"][...] for row in range(rows)], axis=0)
        normal, inverse = normalize(streams)
        grad, gain_grad, shift_grad = norm_back(grad, normal, inverse, gain[2:3])
        vec[9:10] = gain_grad
        vec[10:11] = shift_grad
        grad = k["gcs"][...] + grad
        k["gas"][...] = grad
        k.send("gas")
        low = grad.astype(bf16)
        k["gal"][...] = low
        k.send("gal")
        vec[13:14] = total(low.astype(f32))
        k["gm"][...] = dot_last(k["gal"][...], k["attend_out"][...]).astype(bf16)

    ins = {"totals": totals, "inv": mid["inv"], "gain": gain, "ends": ends, "taps": taps}
    ins |= {"edge_before": edge_before, "edge_after": edge_after}
    ins |= {"rim_before": rim_before, "rim_after": rim_after}
    for row in range(rows):
        span = (row * frames, frames)
        ins |= {
            f"gb{row}": slab(mid["gb"], span, (0, model)),
            f"bn{row}": slab(mid["bn"], span, (0, model)),
            f"gated{row}": gated[row], f"paired{row}": paired[row],
        }
    ins["convolve_in"] = convolve_in
    ins |= {f"after{row}": after_attend[row] for row in range(rows)}
    ins |= {"gcs": mid["gcs"], "attend_out": attend_out}
    low = sds((tokens, model), bf16)
    return staged(
        "conv_back",
        body,
        ins,
        {
            "gp": sds((tokens, 2 * model), bf16), "gas": sds((tokens, model), f32), "gal": low,
            "gm": low, "vec": sds((16, model), f32),
        },
        smem=[info],
        scratch=[
            pltpu.VMEM((frames + 2 * RIM_GRAD, model), f32),
            pltpu.VMEM((frames + 2 * RIM, model), f32),
            pltpu.VMEM((KERNEL, frames, 128), f32),
        ],
        flops=2 * tokens * model * 3 * model,
        moved=12 << 20,
        sends=rows - 1,
    )


def attend_back(row, got, before, after, prob, table, gm, sofar):
    frames, model = got["qu"].shape
    factor = 1.0 / math.sqrt(DH)

    def body(k, acc, turned):
        g_table, vec = k["g_table"], k["vec"]
        if sofar:
            g_table[...] = k["g_table_in"][...]
            vec[...] = k["vec_in"][...]
        else:
            g_table[...] = jnp.zeros_like(g_table)
            vec[...] = jnp.zeros_like(vec)
        acc[...] = jnp.zeros_like(acc)
        turn = flip(WIN)
        table = k["table"]
        for block in range(2):
            here = slice(WIN * block, WIN * (block + 1))
            span = slice(WIN * block, WIN * block + SPAN)
            blocks = ("before", "lo", "hi", "next")[block : block + 3]
            blocks = [k[name] for name in blocks]
            turned[0] = dot(turn, k["gm"][here]).astype(bf16)
            turned[1] = dot(turn, k["qu"][here]).astype(bf16)
            turned[2] = dot(turn, k["qv"][here]).astype(bf16)
            prob = k[f"prob{block}"]

            for group in range(GROUPS):
                cut = slice(WIDE * group, WIDE * (group + 1))
                cut_v = slice(model + WIDE * group, model + WIDE * (group + 1))
                keys = jnp.concatenate([b[:, cut] for b in blocks], axis=0)
                values = jnp.concatenate([b[:, cut_v] for b in blocks], axis=0)
                weights = below(prob[group])
                grad_mixed = heads_apart(turned[0, :, cut])
                grad = dot_last(grad_mixed, values)
                wide = weights.astype(f32)
                delta = jnp.sum(wide * grad, axis=1, keepdims=True)
                raw = (wide * (grad - delta)).astype(bf16)
                acc[span, cut_v] += dot_first(weights, grad_mixed)
                acc[span, cut] += dot_first(raw, heads_apart(turned[1, :, cut]))
                grad_u = heads_joined(dot(raw, keys)) * factor
                band = pltpu.roll(
                    raw.astype(f32).reshape(MANY, WIN, SPAN),
                    SPAN - (WIN - 1),
                    2,
                    stride=1,
                    stride_axis=1,
                )
                band = band.astype(bf16).reshape(MANY * WIN, SPAN)
                grad_v = heads_joined(dot(band, table[:, cut])) * factor
                g_table[:, cut] += dot_first(band, heads_apart(turned[2, :, cut]))
                vec[0:1, cut] += total(grad_u)
                vec[1:2, cut] += total(grad_v)
                k["gq"][here, cut] = dot(turn, (grad_u + grad_v).astype(bf16)).astype(bf16)
            if block == 0:
                k["g_before"][...] = acc[0:WIN].astype(bf16)
                k.send("g_before")
        k["g_after"][...] = acc[3 * WIN :].astype(bf16)
        k.send("g_after")
        k["g_lo"][...] = acc[WIN : 2 * WIN]
        k["g_hi"][...] = acc[2 * WIN : 3 * WIN]

    ins = {"gm": slab(gm, (row * frames, frames), (0, model)), "qu": got["qu"], "qv": got["qv"]}
    ins |= {"before": before, "lo": got["lo"], "hi": got["hi"]}
    ins["prob0"] = slab(prob, 0, (0, GROUPS), (0, WIN), (0, MANY * SPAN))
    ins |= {"table": table, "next": after}
    ins["prob1"] = slab(prob, 1, (0, GROUPS), (0, WIN), (0, MANY * SPAN))
    if sofar:
        ins |= {"g_table_in": sofar[0], "vec_in": sofar[1]}
    kv = (WIN, 2 * model)
    return staged(
        "attend_back",
        body,
        ins,
        {
            "gq": sds((frames, model), bf16), "g_before": sds(kv, bf16), "g_lo": sds(kv, f32),
            "g_hi": sds(kv, f32), "g_after": sds(kv, bf16), "g_table": sds((SPAN, model), f32),
            "vec": sds((8, model), f32),
        },
        scratch=[
            pltpu.VMEM((4 * WIN, 2 * model), f32),
            pltpu.VMEM((3, WIN, model), bf16),
        ],
        flops=8 * 14 * 256 * 384 * 128,
        moved=8 << 20,
    )


def back(row, grads, halo, attend_in, after_first, gas, gain):
    frames, model = after_first.shape

    def body(k):
        joined, vec, gain = k["gj"], k["vec"], k["gain"]
        joined[:, :model] = k["gq"][...]
        joined[:WIN, model:] = (k["g_lo"][...] + k["left"][...].astype(f32)).astype(bf16)
        joined[WIN:, model:] = (k["g_hi"][...] + k["right"][...].astype(f32)).astype(bf16)
        k.send("gj")
        joined = joined[...]
        vec[0:1] = total(joined[:, :model].astype(f32))
        vec[1:2] = total(joined[:, 2 * model :].astype(f32))
        grad = dot_last(joined, k["attend_in"][...])
        normal, inverse = normalize(k["after"][...])
        grad, gain_grad, shift_grad = norm_back(grad, normal, inverse, gain[1:2])
        vec[2:3] = gain_grad
        vec[3:4] = shift_grad
        grad = k["gas"][...] + grad
        k["gfs"][...] = grad
        k.send("gfs")
        low = (0.5 * grad).astype(bf16)
        k["gl"][...] = low
        vec[4:5] = total(low.astype(f32))

    ins = {
        "gain": gain, "gq": grads["gq"], "g_lo": grads["g_lo"], "left": halo[0],
        "g_hi": grads["g_hi"], "right": halo[1], "attend_in": attend_in, "after": after_first,
        "gas": slab(gas, (row * frames, frames), (0, model)),
    }
    return staged(
        "back",
        body,
        ins,
        {
            "gj": sds((frames, 3 * model), bf16), "gfs": sds((frames, model), f32),
            "gl": sds((frames, model), bf16), "vec": sds((8, model), f32),
        },
        flops=2 * frames * model * 3 * model,
        moved=5 << 20,
    )


def keep_half(block, core, mine_ref, other_ref, rows, at=0):
    model = mine_ref.shape[2]
    pairs = rows[1] - rows[0]
    size = block.shape[0] // (2 * pairs)
    shaped = block.reshape(pairs, 2, size, model)
    even, odd = shaped[:, 0], shaped[:, 1]
    here = slice(*rows)
    mine_ref[here, at : at + size] = jnp.where(core == 0, even, odd).astype(bf16)
    other_ref[here, at : at + size] = jnp.where(core == 0, odd, even).astype(bf16)


def sum_first(lefts, rights):
    return sum(dot_first(left, right) for left, right in zip(lefts, rights))


def late_weights(info, place_of_core, n, act, gl, na, gj, sinusoid, g_table):
    rows = len(act)
    frames, hidden = act[0].shape
    model = gl[0].shape[1]
    parts = hidden // PART
    width, slim = hidden // n, model // n
    pairs = (0, n // 2)

    def body(k, info):
        core = info[place_of_core]
        for part in range(2):
            cut = slice(part * model, (part + 1) * model)
            block = sum_first(
                [k[f"na{row}"][...] for row in range(rows)],
                [k[f"gj{row}"][:, cut] for row in range(rows)],
            )
            keep_half(block, core, k["mine"], k["other"], pairs, width + part * slim)
        high = k["g_table"][...].astype(bf16)
        low = (k["g_table"][...] - high.astype(f32)).astype(bf16)
        place = dot_first(k["sinusoid"][...], high) + dot_first(k["sinusoid"][...], low)
        keep_half(place, core, k["mine"], k["other"], pairs, width + 2 * slim)
        step = n // 2 // parts
        for part in range(parts):
            block = sum_first(
                [k[f"act{row}_{part}"][...] for row in range(rows)],
                [k[f"gl{row}"][...] for row in range(rows)],
            )
            some = (part * step, (part + 1) * step)
            keep_half(block, core, k["mine"], k["other"], some)
            k.send("other", pl.ds(part * step, step))
            k.send("mine", pl.ds(part * step, step))

    half = sds((n // 2, width + 3 * slim, model), bf16)
    ins = {f"na{row}": na[row] for row in range(rows)}
    ins |= {f"gj{row}": slab(gj[row], (0, frames), (0, 2 * model)) for row in range(rows)}
    ins |= {"g_table": g_table, "sinusoid": sinusoid}
    ins |= {f"gl{row}": gl[row] for row in range(rows)}
    for part in range(parts):
        for row in range(rows):
            ins[f"act{row}_{part}"] = slab(act[row], (0, frames), (part * PART, PART))
    got = staged(
        "late_weights",
        body,
        ins,
        {"other": half, "mine": half},
        smem=[info],
        flops=2 * rows * frames * model * (hidden + 3 * model),
        moved=9 << 20,
        sends=2 * parts - 2,
    )
    return got["mine"], got["other"]


def first_back(info, place_of_core, n, gl, slope, feed_in, feed_out, n0, na, gj):
    rows = len(slope)
    frames, hidden = slope[0].shape
    model = gl[0].shape[1]
    tokens = rows * frames
    parts = hidden // PART

    def body(k, info):
        core = info[place_of_core]
        low = jnp.concatenate([k[f"gl{row}"][...] for row in range(rows)], axis=0)
        step = n // 2 // parts
        back = 0.0
        block = sum_first(
            [k[f"na{row}"][...] for row in range(rows)],
            [k[f"gj{row}"][...] for row in range(rows)],
        )
        keep_half(block, core, k["mine"], k["other"], (0, n // 2), hidden // n)
        for part in range(parts):
            cut = slice(part * PART, (part + 1) * PART)
            grad = dot_last(low, k[f"w_out{part}"][...])
            scale = jnp.concatenate([k[f"slope{row}_{part}"][...] for row in range(rows)], axis=0)
            grad = (grad * scale.astype(f32)).astype(bf16)
            k["fb"][:, cut] = total(grad.astype(f32))
            block = sum_first(
                [grad[row * frames : (row + 1) * frames] for row in range(rows)],
                [k[f"n0{row}"][...] for row in range(rows)],
            )
            pairs = (part * step, (part + 1) * step)
            keep_half(block, core, k["mine"], k["other"], pairs)
            k.send("other", pl.ds(part * step, step))
            k.send("mine", pl.ds(part * step, step))
            back = back + dot_last(grad, k[f"w_in{part}"][...])
        k["gn"][...] = back

    half = sds((n // 2, hidden // n + model // n, model), bf16)
    ins = {f"na{row}": na[row] for row in range(rows)}
    ins |= {f"gj{row}": slab(gj[row], (0, frames), (2 * model, model)) for row in range(rows)}
    ins |= {f"gl{row}": gl[row] for row in range(rows)}
    weights = feed_slabs(feed_in, feed_out, 0)
    for part in range(parts):
        ins[f"w_out{part}"] = weights[f"w_out{part}"]
        for row in range(rows):
            ins[f"slope{row}_{part}"] = slab(slope[row], (0, frames), (part * PART, PART))
        if part == 0:
            ins |= {f"n0{row}": n0[row] for row in range(rows)}
        ins[f"w_in{part}"] = weights[f"w_in{part}"]
    return staged(
        "first_back",
        body,
        ins,
        {
            "other": half, "mine": half, "fb": sds((1, hidden), f32),
            "gn": sds((tokens, model), f32),
        },
        smem=[info],
        flops=2 * tokens * model * hidden * 3,
        moved=12 << 20,
        sends=2 * parts - 2,
    )


def last(features, gn, gfs, gain):
    rows, frames, model = features.shape

    def body(k):
        gain_grads, shift_grads = 0.0, 0.0
        for row in range(rows):
            here = slice(row * frames, (row + 1) * frames)
            normal, inverse = normalize(k[f"x{row}"][...].astype(f32))
            grad = k[f"gn{row}"][...]
            grad, gain_grad, shift_grad = norm_back(grad, normal, inverse, k["gain"][0:1])
            k["out"][row] = k[f"gfs{row}"][...] + grad
            k.send("out", row)
            gain_grads += gain_grad
            shift_grads += shift_grad
        k["vec"][0:1] = gain_grads
        k["vec"][1:2] = shift_grads

    ins = {"gain": gain}
    for row in range(rows):
        span = (row * frames, frames)
        ins |= {
            f"x{row}": slab(features, row, (0, frames), (0, model)),
            f"gn{row}": slab(gn, span, (0, model)),
            f"gfs{row}": gfs[row],
        }
    return staged(
        "last",
        body,
        ins,
        {"out": sds(features.shape, f32), "vec": sds((8, model), f32)},
        flops=rows * frames * model * 20,
        moved=4 << 20,
        sends=rows - 1,
        limit=FOLD_LIMIT,
    )


def feed_weights(n, gi, nf, act, gl):
    tokens, model = nf.shape
    hidden = gi.shape[1]
    parts = hidden // PART
    size, slim = hidden // n, model // n
    step = n // parts
    room = 2 * slim if slim % 8 == 0 else 0

    def body(k):
        for part in range(parts):
            here = slice(part * step, (part + 1) * step)
            block = dot_first(k[f"gi{part}"][...], k["nf"][...]).astype(bf16)
            k["out"][here, :, :model] = block.reshape(step, size, model)
            block = dot_first(k[f"act{part}"][...], k["gl"][...]).astype(bf16)
            k["out"][here, :, model:] = block.reshape(step, size, model)
            k.send("out", pl.ds(part * step, step))

    ins = {"nf": nf}
    for part in range(parts):
        ins[f"gi{part}"] = slab(gi, (0, tokens), (part * PART, PART))
        if part == 0:
            ins["gl"] = gl
        ins[f"act{part}"] = slab(act, (0, tokens), (part * PART, PART))
    own = (n, size, 2 * model)
    shape = sds((n, size + room, 2 * model), bf16)
    return staged(
        "feed_weights",
        body,
        ins,
        {"out": (shape, lambda ref: ref.at[:, pl.ds(0, size)] if room else ref, own)},
        flops=4 * tokens * model * hidden,
        moved=10 << 20,
        sends=parts - 1,
    )["out"]


def side_weights(n, early, nc, gp, sw, gcl, mixed, gal):
    rows = len(nc)
    tokens, model = sw.shape
    frames = tokens // rows
    slim = model // n
    room = slim % 8 == 0
    own = (n, 2 * slim, 2 * model)

    def body(k):
        out = k["out"]
        spans = [slice(row * frames, (row + 1) * frames) for row in range(rows)]
        for part in range(2):
            cut = slice(part * model, (part + 1) * model)
            block = sum_first(
                [k[f"nc{row}"][...] for row in range(rows)], [k["gp"][at, cut] for at in spans]
            )
            out[:, :slim, cut] = block.astype(bf16).reshape(n, slim, model)
        block = dot_first(k["sw"][...], k["gcl"][...]).astype(bf16)
        out[:, slim:, :model] = block.reshape(n, slim, model)
        block = sum_first(
            [k[f"mixed{row}"][...] for row in range(rows)], [k["gal"][at] for at in spans]
        )
        out[:, slim:, model:] = block.astype(bf16).reshape(n, slim, model)

    ins = {f"nc{row}": nc[row] for row in range(rows)}
    ins |= {"gp": gp, "sw": sw, "gcl": gcl}
    ins |= {f"mixed{row}": mixed[row] for row in range(rows)}
    ins["gal"] = gal
    size = early.shape[1] - 2 * slim
    if room:
        out = (sds(early.shape, bf16), lambda ref: ref.at[:, pl.ds(size, 2 * slim)], own)
    else:
        out = sds(own, bf16)
    got = staged(
        "side_weights",
        body,
        ins,
        {"out": out},
        flops=2 * tokens * model * model * 4,
        moved=6 << 20,
        filled=early if room else None,
    )["out"]
    return got if room else jnp.concatenate([early, got], axis=1)


def neighbours(last_block, first_block):
    devices = lax.axis_size("frames")
    up = [(i, i + 1) for i in range(devices - 1)]
    down = [(i + 1, i) for i in range(devices - 1)]
    return lax.ppermute(last_block, "frames", up), lax.ppermute(first_block, "frames", down)


def gather(copies):
    return lax.all_to_all(copies, DEVICES, 0, 0, tiled=True)


def scatter_sum(grads):
    return lax.psum_scatter(grads, "frames", scatter_dimension=0, tiled=True)


ROW_PAIR = [(0, 1), (1, 0)]


def swap(x, k):
    n = lax.axis_size("frames")
    return lax.ppermute(x, "frames", [(i, i ^ k) for i in range(n)])


def swaps(sends, group):
    k, size = group
    return [swap(send, k * one) for one, send in zip(range(1, size), sends)]


def fold(name, info, row_at, states, small=None):
    ins, outs, plans = {}, {}, []
    for at, (mine, got, how) in enumerate(states):
        size, height, model = mine.shape
        if isinstance(how, tuple):
            _, place, range_ = how
            view = (size // (range_ * place), range_, place, height, model)
            half = (view[0], place, height, model)
        else:
            view = mine.shape
            half = (size, height, model // 2) if how == "columns" else mine.shape
        ins[f"mine{at}"] = mine.reshape(view)
        ins |= {f"got{at}_{k}": one.reshape(view) for k, one in enumerate(got)}
        outs[f"keep{at}"] = sds(half, f32 if how == "wide" else bf16)
        sends = how[2] - 1 if isinstance(how, tuple) else int(how == "columns")
        outs |= {f"send{at}_{k}": sds(half, bf16) for k in range(sends)}
        plans.append((len(got), how))
    if small is not None:
        ins |= {f"small{k}": one for k, one in enumerate(small)}
        outs["sum"] = sds(small[0].shape, f32)

    def body(k, info):
        for at, (count, how) in enumerate(plans):
            parts = [k[f"mine{at}"]] + [k[f"got{at}_{one}"] for one in range(count)]

            def added(*index):
                return sum(part[index].astype(f32) for part in parts)

            keep = k[f"keep{at}"]
            if how is None or how == "wide":
                keep[...] = added(...).astype(keep.dtype)
            elif how == "columns":
                half = keep.shape[2]
                both = [
                    added(slice(None), slice(None), slice(one * half, (one + 1) * half))
                    for one in range(2)
                ]
                first = info[row_at] == 0
                k[f"send{at}_0"][...] = jnp.where(first, both[1], both[0]).astype(bf16)
                k.send(f"send{at}_0")
                keep[...] = jnp.where(first, both[0], both[1]).astype(bf16)
            else:
                digit = info[how[0]]
                for one in range(1, how[2]):
                    other = digit
                    for bit in (1, 2):
                        if one & bit:
                            other = other + bit * (1 - 2 * ((digit // bit) % 2))
                    k[f"send{at}_{one - 1}"][...] = added(slice(None), other).astype(bf16)
                    k.send(f"send{at}_{one - 1}")
                keep[...] = added(slice(None), digit).astype(bf16)
        if small is not None:
            k["sum"][...] = sum(k[f"small{one}"][...] for one in range(len(small)))

    got = staged(name, body, ins, outs, smem=[info], flops=1 << 20, moved=2 << 20, limit=FOLD_LIMIT)
    results = []
    for at, (mine, _, how) in enumerate(states):
        size, height, model = mine.shape
        shape = (size // how[2], height, model) if isinstance(how, tuple) else None
        keys = [key for key in got if key.startswith((f"keep{at}", f"send{at}_"))]
        keep, *sends = [got[key].reshape(shape) if shape else got[key] for key in keys]
        results.append((keep, sends))
    if small is not None:
        results.append(got["sum"])
    return results


def per_device(
    features,
    lengths,
    windows,
    feed_in,
    feed_in_bias,
    feed_out,
    attend_in,
    attend_out,
    position_proj,
    convolve_in,
    convolve_out,
    depthwise,
    norm_gain,
    norm_shift,
    biases,
    cotangent,
):
    rows, frames, model = features.shape
    tokens = rows * frames
    n = lax.axis_size("frames")
    devices = lax.axis_size("rows") * n
    row_len = float(frames * n)
    me = lax.axis_index("frames")
    start = me * frames
    hidden = feed_in.shape[2]
    ends_every = jnp.cumsum(lengths, axis=1, dtype=jnp.int32)
    ends_here = lax.dynamic_slice_in_dim(ends_every, lax.axis_index("rows") * rows, rows, 0)
    slots = ends_here.shape[1]
    ends = jnp.pad(
        ends_here.astype(f32), ((0, 8 - rows), (0, -slots % 128)), constant_values=row_len
    )
    groups, k = [(2, 2)], 4
    while k < n:
        groups.append((k, min(4, n // k)))
        k *= groups[-1][1]
    places = [lax.axis_index("rows"), me % 2] + [(me // k) % size for k, size in groups]
    info = jnp.concatenate(
        [start[None].astype(jnp.int32), windows, ends_here[:, -1], jnp.stack(places)]
    )
    row_at = 1 + 2 * rows
    core_at = row_at + 1
    starts = jnp.arange(n, dtype=jnp.int32) * frames
    counts = jnp.clip(ends_every[:, -1][:, None] - starts[None, :], 0, frames)
    counts = jnp.sum(counts.reshape(-1, rows, n), axis=1).astype(f32).reshape(devices, 1)
    counts = jnp.broadcast_to(counts, (devices, 128))
    sinusoid = jnp.asarray(position_table(WIN, model))
    each = range(rows)

    fronts, befores, afters = [], [], []
    for row in each:
        got = front(
            row, features, feed_in, feed_in_bias, feed_out, attend_in, norm_gain, norm_shift,
            biases,
        )
        fronts.append(got)
        left, right = neighbours(got["hi"], got["lo"])
        befores.append(left)
        afters.append(right)
    attends, edges, table = [], [], None
    for row in each:
        got = attend(
            row_len, row, rows, info, ends, fronts[row], befores[row], afters[row], sinusoid,
            position_proj, table, attend_out, convolve_in, norm_gain, norm_shift, biases, edges,
        )
        if row == 0:
            table = got["table"]
        attends.append(got)
        edges.append((got["first"], got["last"]))
    first, final = edges[-1]
    rim_before, rim_after = neighbours(final, first)
    gated = [got["gated"] for got in attends]
    after_attend = [got["out"] for got in attends]
    got = depth_conv(row_len, devices, info, ends, gated, rim_before, rim_after, depthwise)
    mid = middle(
        devices, rows, info, gather(got["stats"]), counts, got["depth"], after_attend, feed_in,
        feed_in_bias, feed_out, convolve_out, norm_gain, norm_shift, biases,
        cotangent.reshape(tokens, model),
    )
    edge_before, edge_after = neighbours(mid["last"], mid["first"])
    totals = gather(mid["totals"])
    early = feed_weights(n, mid["gi"], mid["nf"], mid["act"], mid["gl"])
    totals, early = lax.optimization_barrier((totals, early))
    conv = conv_back(
        row_len, info, ends, depthwise, convolve_in, attend_out, norm_gain, totals, mid,
        edge_before, edge_after, rim_before, rim_after, gated,
        [got["paired"] for got in attends], after_attend,
    )
    early = side_weights(
        n, early, [got["nc"] for got in attends], conv["gp"], mid["sw"], mid["gcl"],
        [got["mixed"] for got in attends], conv["gal"],
    )
    early, gm = lax.optimization_barrier((early, conv["gm"]))
    early = scatter_sum(early)
    grads, halos, sofar = [], [], ()
    for row in each:
        got = attend_back(
            row, fronts[row], befores[row], afters[row], attends[row]["prob"], table, gm, sofar
        )
        sofar = (got["g_table"], got["vec"])
        grads.append(got)
        halos.append(neighbours(got["g_after"], got["g_before"]))
    end = [
        back(
            row, grads[row], halos[row], attend_in, fronts[row]["after"], conv["gas"], norm_gain
        )
        for row in each
    ]
    acts, normeds = [got["act"] for got in fronts], [got["na"] for got in fronts]
    lows, joined = [got["gl"] for got in end], [got["gj"] for got in end]
    b, b_send = late_weights(info, core_at, n, acts, lows, normeds, joined, sinusoid, sofar[0])
    b_got = [swap(b_send, 1)]
    got = first_back(
        info, core_at, n, lows, [got["slope"] for got in fronts], feed_in, feed_out,
        [got["n0"] for got in fronts], normeds, joined,
    )
    a, a_send = got["mine"], got["other"]
    a_got = [swap(a_send, 1)]
    ((b, b_send),) = fold("fold_b", info, row_at, [(b, b_got, "columns")])
    b_got = [lax.ppermute(b_send[0], "rows", ROW_PAIR)]
    ((a, a_send),) = fold("fold_a", info, row_at, [(a, a_got, (core_at + 1, 1, 2))])
    a_got = swaps(a_send, groups[0])
    gn, a = lax.optimization_barrier((got["gn"], a))
    ending = last(features, gn, [one["gfs"] for one in end], norm_gain)

    vec_conv, vec_mid, vec_back, vec_last = conv["vec"], mid["vec"], sum(one["vec"] for one in end), ending["vec"]
    small = jnp.concatenate(
        [
            vec_conv[:KERNEL],
            vec_last[0:1], vec_back[2:3], vec_conv[9:10], vec_mid[0:1], vec_mid[2:3],
            vec_last[1:2], vec_back[3:4], vec_conv[10:11], vec_mid[1:2], vec_mid[3:4],
            vec_back[0:2], vec_conv[13:14], vec_conv[11:13], vec_mid[4:5], vec_back[4:5],
            vec_mid[5:6], sofar[1][0:2],
            got["fb"].reshape(-1, model), mid["fb"].reshape(-1, model),
            jnp.zeros((3, model), f32),
        ],
        axis=0,
    )
    small = [small, swap(small, 1)]
    for at, group in enumerate(groups):
        deeper = at + 1 < len(groups)
        a_how = (core_at + 2 + at, 1, groups[at + 1][1]) if deeper else None
        states = [(a, a_got, a_how), (b, b_got, (core_at + 1 + at, 1, group[1]))]
        if at == 1:
            states.append((early, early_got, "wide"))
        folded = fold(f"fold_{at}", info, row_at, states, small)
        one = folded.pop()
        if at == 1:
            early = folded.pop()[0][0]
        (a, a_send), (b, b_send) = folded
        if at == 0:
            early, a = lax.optimization_barrier((early, a))
            early_got = [lax.ppermute(early, "rows", ROW_PAIR)]
        if deeper:
            a_got = swaps(a_send, groups[at + 1])
        else:
            a_got = [lax.ppermute(a, "rows", ROW_PAIR)]
        b_got = swaps(b_send, group)
        small = [one] + swaps([one] * (group[1] - 1), group)
    (b, _), one = fold("fold_last", info, row_at, [(b, b_got, None)], small)
    b_got = lax.ppermute(b, "rows", ROW_PAIR)
    small = one + lax.ppermute(one, "rows", ROW_PAIR)
    a = a[0].astype(f32) + a_got[0][0].astype(f32)
    first = lax.axis_index("rows") == 0
    b = jnp.concatenate(
        [jnp.where(first, b[0], b_got[0]), jnp.where(first, b_got[0], b[0])], axis=1
    ).astype(f32)
    slim = model // n
    width = hidden // n
    n_vectors = small.shape[0] - 3 - 2 * (hidden // model)
    vectors = jnp.concatenate([small[:n_vectors], vec_conv[14:16]], axis=0)
    thin = lax.dynamic_slice_in_dim(vectors, me * slim, slim, 1)
    feed_bias = small[n_vectors:-3].reshape(2, hidden)
    feed_bias = lax.dynamic_slice_in_dim(feed_bias, me * width, width, 1)
    return (
        mid["out"].reshape(rows, frames, model),
        ending["out"],
        jnp.stack([a[:width].T, early[:width, :model].T]),
        feed_bias,
        jnp.stack([b[:width], early[:width, model:]]),
        jnp.concatenate(
            [b[width : width + slim], b[width + slim : width + 2 * slim], a[width:]], axis=1
        ),
        early[width + slim :, model:],
        b[width + 2 * slim :],
        early[width : width + slim],
        early[width + slim :, :model],
        thin[:KERNEL],
        jnp.concatenate([thin[KERNEL : KERNEL + 5], thin[n_vectors + 1 :]], axis=0),
        jnp.concatenate([thin[KERNEL + 5 : KERNEL + 10], thin[n_vectors : n_vectors + 1]], axis=0),
        thin[KERNEL + 10 : n_vectors],
    )


def solution(mesh):
    placed = (
        P("rows", "frames", None),
        P(),
        P("rows"),
        P(),
        P(),
        P(),
        P(),
        P(),
        P(),
        P(),
        P(),
        P(),
        P(),
        P(),
        P(),
        P("rows", "frames", None),
    )
    return jax.shard_map(
        per_device,
        mesh=mesh,
        in_specs=placed,
        out_specs=(
            P("rows", "frames", None),
            P("rows", "frames", None),
            P(None, None, "frames"),
            P(None, "frames"),
            P(None, "frames", None),
            P("frames", None),
            P("frames", None),
            P("frames", None),
            P("frames", None),
            P("frames", None),
            P(None, "frames"),
            P(None, "frames"),
            P(None, "frames"),
            P(None, "frames"),
        ),
        check_vma=False,
    )
```

```python
import functools
import math
import types

import jax
import jax.numpy as jnp
import ml_dtypes
import numpy as np
from jax import lax
from jax.experimental import pallas as pl
from jax.experimental.pallas import tpu as pltpu
from jax.sharding import PartitionSpec as P

H = 8
DH = 64
KERNEL = 9
WIN = 128

HALF = KERNEL // 2
SPAN = 3 * WIN
MANY = 4
GROUPS = H // MANY
WIDE = MANY * DH
RIM = 16
RIM_GRAD = 8
eps_norm = 1e-05
negative = -1e30
f32 = jnp.float32
bf16 = jnp.bfloat16
DEVICES = ("rows", "frames")
VMEM_LIMIT = 60 * 1024 * 1024
FOLD_LIMIT = 14 * 1024 * 1024


def dot(left, right):
    return jnp.dot(left, right, preferred_element_type=f32)


def dot_last(left, right):
    return lax.dot_general(left, right, (((1,), (1,)), ((), ())), preferred_element_type=f32)


def dot_first(left, right):
    return lax.dot_general(left, right, (((0,), (0,)), ((), ())), preferred_element_type=f32)


def sigmoid(x):
    return 0.5 * jnp.tanh(0.5 * x) + 0.5


def total(x):
    return jnp.sum(x, axis=0, keepdims=True)


def normalize(values):
    centered = values - jnp.mean(values, axis=-1, keepdims=True)
    inverse = lax.rsqrt(jnp.mean(centered * centered, axis=-1, keepdims=True) + eps_norm)
    return centered * inverse, inverse


def norm_back(grad_out, normal, inverse, gain):
    scaled = grad_out * gain
    centred = scaled - jnp.mean(scaled, axis=-1, keepdims=True)
    grad_in = inverse * (centred - normal * jnp.mean(scaled * normal, axis=-1, keepdims=True))
    return grad_in, total(grad_out * normal), total(grad_out)


def position_table(width, model):
    offsets = (np.arange(2 * width + 1) - width).astype(np.float32)
    rates = np.exp(
        np.arange(model // 2).astype(np.float32) * np.float32(-2.0 * math.log(10000.0) / model)
    )
    angles = (offsets[:, None] * rates[None, :]).astype(np.float32)
    both = np.stack([np.sin(angles), np.cos(angles)], axis=2).reshape(2 * width + 1, model)
    padded = np.zeros((3 * width, model), np.float32)
    padded[: 2 * width + 1] = both
    return padded.astype(ml_dtypes.bfloat16)


def bounds(ends, at, row_len):
    low = jnp.max(jnp.where(ends <= at, ends, 0.0), axis=1, keepdims=True)
    high = jnp.min(jnp.where(ends > at, ends, row_len), axis=1, keepdims=True)
    return low, high


def column(count, offset):
    return lax.broadcasted_iota(jnp.int32, (count, 1), 0).astype(f32) + offset


def head_lanes(rows):
    return lax.broadcasted_iota(jnp.int32, (rows, WIDE), 1) // DH


def heads_apart(group):
    at = head_lanes(group.shape[0])
    zero = jnp.zeros_like(group)
    return jnp.concatenate([jnp.where(at == k, group, zero) for k in range(MANY)], axis=0)


def heads_joined(stacked):
    rows = stacked.shape[0] // MANY
    at = head_lanes(rows)
    joined = stacked[:rows]
    for k in range(1, MANY):
        joined = jnp.where(at == k, stacked[k * rows : (k + 1) * rows], joined)
    return joined


def beside(stacked):
    rows = stacked.shape[0] // MANY
    return jnp.concatenate([stacked[k * rows : (k + 1) * rows] for k in range(MANY)], axis=1)


def below(joined):
    width = joined.shape[1] // MANY
    return jnp.concatenate([joined[:, k * width : (k + 1) * width] for k in range(MANY)], axis=0)


def flip(rows):
    i = lax.broadcasted_iota(jnp.int32, (rows, rows), 0)
    j = lax.broadcasted_iota(jnp.int32, (rows, rows), 1)
    return (i + j == rows - 1).astype(f32).astype(bf16)


class Load:
    def __init__(self, source, buffer, sem):
        self.buffer, self.waited = buffer, False
        self.copy = pltpu.make_async_copy(source, buffer, sem)
        self.copy.start()

    def ready(self):
        if not self.waited:
            self.copy.wait()
            self.waited = True
        return self.buffer


class Loads:
    def __init__(self, items):
        self.items = items

    def __getitem__(self, at):
        return self.items[at].ready()


class Stage:
    def __init__(self, loads, stores, sems):
        self.sems, self.used, self.pending, self.targets = sems, 0, [], []
        self.named, self.all_loads = {}, []
        for name, pairs, single in loads:
            items = [Load(source, buffer, self.sem()) for source, buffer in pairs]
            self.all_loads += items
            self.named[name] = items[0] if single else Loads(items)
        for name, pairs, single in stores:
            self.targets += [[target, buffer, False] for target, buffer in pairs]
            buffers = [buffer for _, buffer in pairs]
            self.named[name] = buffers[0] if single else buffers

    def sem(self):
        self.used += 1
        return self.sems.at[self.used - 1]

    def __getattr__(self, name):
        found = self.named[name]
        return found.ready() if isinstance(found, Load) else found

    def send(self, buffer, at=None):
        entry = next(entry for entry in self.targets if entry[1] is buffer)
        target = entry[0]
        entry[2] = True
        if at is not None:
            target, buffer = target.at[at], buffer.at[at]
        copy = pltpu.make_async_copy(buffer, target, self.sem())
        copy.start()
        self.pending.append(copy)

    def finish(self):
        for _, buffer, sent in self.targets:
            if not sent:
                self.send(buffer)
        for load in self.all_loads:
            load.ready()
        for copy in self.pending:
            copy.wait()


def staged(
    name, body, ins, outs, smem=(), scratch=(), flops=0, moved=0, sends=0, filled=None,
    limit=VMEM_LIMIT,
):
    operands, loads, stores = [], [], []
    for key, items in ins.items():
        single = not isinstance(items, list)
        entries = []
        for item in [items] if single else items:
            array, view, shape = item if isinstance(item, tuple) else (item, None, item.shape)
            at = next((i for i, other in enumerate(operands) if other is array), None)
            if at is None:
                at = len(operands)
                operands.append(array)
            entries.append((at, view, shape, array.dtype))
        loads.append((key, entries, single))
    for key, items in outs.items():
        single = not isinstance(items, list)
        entries = [
            item if isinstance(item, tuple) else (item, None, item.shape)
            for item in ([items] if single else items)
        ]
        stores.append((key, entries, single))
    aliases = {}
    if filled is not None:
        aliases = {len(smem) + len(operands): 0}
        operands.append(filled)
    every_load = [entry for _, entries, _ in loads for entry in entries]
    every_store = [entry for _, entries, _ in stores for entry in entries]
    n_smem, n_ops, n_outs, n_loads = len(smem), len(operands), len(every_store), len(every_load)

    def run(*refs):
        cuts = [n_smem, n_ops, n_outs, n_loads, n_outs, 1]
        taken, at = [], 0
        for cut in cuts:
            taken.append(refs[at : at + cut])
            at += cut
        scalars, given, targets, buffers, results, sems = taken
        buffers, places = iter(buffers), iter(zip(targets, results))
        placed_loads = [
            (
                key,
                [(given[i] if view is None else view(given[i]), next(buffers)) for i, view, _, _ in entries],
                single,
            )
            for key, entries, single in loads
        ]
        placed_stores = []
        for key, entries, single in stores:
            pairs = []
            for _, view, _ in entries:
                target, result = next(places)
                pairs.append((target if view is None else view(target), result))
            placed_stores.append((key, pairs, single))
        stage = Stage(placed_loads, placed_stores, sems[0])
        body(stage, *scalars, *refs[at:])
        stage.finish()

    hbm = pl.BlockSpec(memory_space=pl.ANY)
    got = iter(
        pl.pallas_call(
            run,
            in_specs=[pl.BlockSpec(memory_space=pltpu.SMEM)] * n_smem + [hbm] * n_ops,
            out_specs=[hbm] * n_outs,
            out_shape=[shape for shape, _, _ in every_store],
            scratch_shapes=[pltpu.VMEM(shape, dtype) for _, _, shape, dtype in every_load]
            + [pltpu.VMEM(shape, whole.dtype) for whole, _, shape in every_store]
            + [pltpu.SemaphoreType.DMA((n_loads + n_outs + sends,))]
            + list(scratch),
            input_output_aliases=aliases,
            compiler_params=pltpu.CompilerParams(vmem_limit_bytes=limit),
            cost_estimate=pl.CostEstimate(flops=flops, bytes_accessed=moved, transcendentals=0),
            name=name,
        )(*smem, *operands)
    )
    result = types.SimpleNamespace()
    for key, entries, single in stores:
        values = [next(got) for _ in entries]
        setattr(result, key, values[0] if single else values)
    return result


def sds(shape, dtype):
    return jax.ShapeDtypeStruct(shape, dtype)


def slab(array, *at):
    shape = tuple(a[1] for a in at if isinstance(a, tuple))
    index = tuple(pl.ds(*a) if isinstance(a, tuple) else a for a in at)
    return (array, lambda ref: ref.at[index], shape)


def by_row(array, rows):
    tokens, width = array.shape
    return [slab(array, (row * (tokens // rows), tokens // rows), (0, width)) for row in range(rows)]


def each_of(array):
    rows, size, width = array.shape
    return [slab(array, row, (0, size), (0, width)) for row in range(rows)]


PART = 1024


def activate(inner):
    half = 0.5 * inner
    turn = jnp.tanh(half)
    up = 1.0 + turn
    active = half * up
    return active, 0.5 * (up + active * (1.0 - turn))


def feed_slabs(feed_in, feed_out, module):
    _, model, hidden = feed_in.shape
    spans = [(part, PART) for part in range(0, hidden, PART)]
    w_in = [slab(feed_in, module, (0, model), span) for span in spans]
    w_out = [slab(feed_out, module, span, (0, model)) for span in spans]
    return w_in, w_out


def front(features, feed_in, feed_in_bias, feed_out, attend_in, gain, shift, bias):
    rows, frames, model = features.shape
    tokens = rows * frames
    hidden = feed_in.shape[2]
    parts = hidden // PART
    low = sds((tokens, model), bf16)

    def body(k):
        gain, shift = k.gain, k.shift
        x = k.x[...].reshape(tokens, model).astype(f32)
        normal, _ = normalize(x)
        k.n0[...] = (normal * gain[0:1] + shift[0:1]).astype(bf16)
        k.send(k.n0)
        for part in range(parts):
            cut = slice(part * PART, (part + 1) * PART)
            inner = dot(k.n0[...], k.w_in[part][...]) + k.b_in[0:1, cut]
            active, slope = activate(inner)
            k.act[:, cut] = active.astype(bf16)
            k.slope[:, cut] = slope.astype(bf16)
        k.send(k.slope)
        k.send(k.act)
        branch = k.bias[6:7]
        for part in range(parts):
            cut = slice(part * PART, (part + 1) * PART)
            branch = branch + dot(k.act[:, cut], k.w_out[part][...])
        after = x + 0.5 * branch
        k.after[...] = after
        k.send(k.after)
        normal, _ = normalize(after)
        normed = (normal * gain[1:2] + shift[1:2]).astype(bf16)
        k.na[...] = normed
        k.send(k.na)
        both = dot(normed, k.attend_in[...])
        keys = both[:, :model].astype(bf16)
        values = (both[:, model:] + k.bias[1:2]).astype(bf16)
        for row in range(rows):
            at = row * frames
            k.lo[row, :, :model] = keys[at : at + WIN]
            k.lo[row, :, model:] = values[at : at + WIN]
            k.hi[row, :, :model] = keys[at + WIN : at + frames]
            k.hi[row, :, model:] = values[at + WIN : at + frames]

    w_in, w_out = feed_slabs(feed_in, feed_out, 0)
    kv = sds((rows, WIN, 2 * model), bf16)
    return staged(
        "front",
        body,
        dict(
            x=features, gain=gain, shift=shift, b_in=feed_in_bias, w_in=w_in, bias=bias,
            w_out=w_out, attend_in=slab(attend_in, (0, model), (model, 2 * model)),
        ),
        dict(
            after=sds((tokens, model), f32), n0=low, na=low, lo=kv, hi=kv,
            act=sds((tokens, hidden), bf16), slope=sds((tokens, hidden), bf16),
        ),
        flops=2 * tokens * model * (2 * hidden + 2 * model),
        moved=16 << 20,
    )


def queries(na, attend_in, bias, sinusoid, proj):
    tokens, model = na.shape

    def body(k):
        query = dot(k.na[...], k.attend_in[...]) + k.bias[0:1]
        factor = 1.0 / math.sqrt(DH)
        k.qu[...] = ((query + k.bias[8:9]) * factor).astype(bf16)
        k.qv[...] = ((query + k.bias[9:10]) * factor).astype(bf16)
        k.table[...] = dot(k.sinusoid[...], k.proj[...]).astype(bf16)

    low = sds((tokens, model), bf16)
    return staged(
        "queries",
        body,
        dict(
            na=na, attend_in=slab(attend_in, (0, model), (0, model)), bias=bias,
            sinusoid=sinusoid, proj=proj,
        ),
        dict(qu=low, qv=low, table=sds((SPAN, model), bf16)),
        flops=2 * tokens * model * 2 * model,
        moved=4 << 20,
    )


def attend(
    row_len, info, ends, start, query, before, after, attend_out, convolve_in, gain, shift, bias
):
    rows = before.shape[0]
    tokens, model = start.after.shape
    frames = tokens // rows
    low = sds((tokens, model), bf16)

    def body(k, info):
        first_frame = info[0].astype(f32)
        turn = flip(WIN)
        key_at = lax.broadcasted_iota(jnp.int32, (WIN, SPAN), 1).astype(f32)
        table = k.table
        for row in range(rows):
            reach = info[1 + row].astype(f32)
            row_ends = k.ends[row : row + 1, :]
            for block in range(2):
                at = column(WIN, first_frame + WIN * block)
                lower, upper = bounds(row_ends, at, row_len)
                base = first_frame + (WIN * (block - 1))
                lower = jnp.maximum(lower, at - reach) - base
                upper = jnp.minimum(upper - 1.0, at + reach) - base
                allowed = ((key_at >= lower) & (key_at <= upper))[None]
                here = slice(row * frames + WIN * block, row * frames + WIN * (block + 1))
                some = [k.lo[row], k.hi[row]]
                some = some + [k.next[row]] if block else [k.before[row]] + some
                for group in range(GROUPS):
                    cut = slice(WIDE * group, WIDE * (group + 1))
                    cut_v = slice(model + WIDE * group, model + WIDE * (group + 1))
                    keys = jnp.concatenate([b[:, cut] for b in some], axis=0)
                    values = jnp.concatenate([b[:, cut_v] for b in some], axis=0)
                    spread = dot_last(heads_apart(k.qv[here, cut]), table[:, cut])
                    content = dot_last(heads_apart(k.qu[here, cut]), keys)
                    spread = pltpu.roll(
                        spread.reshape(MANY, WIN, SPAN), 0, 2, stride=1, stride_axis=1
                    )
                    scores = content.reshape(MANY, WIN, SPAN) + spread
                    scores = jnp.where(allowed, scores, negative)
                    powers = jnp.exp(scores - jnp.max(scores, axis=2, keepdims=True))
                    weights = powers * (1.0 / jnp.sum(powers, axis=2, keepdims=True))
                    weights = weights.astype(bf16).reshape(MANY * WIN, SPAN)
                    k.mixed[here, cut] = heads_joined(dot(weights, values)).astype(bf16)
                    k.prob[row][block, group] = dot(turn, beside(weights)).astype(bf16)
            k.send(k.prob[row])
        k.send(k.mixed)
        after_attend = k.after[...] + dot(k.mixed[...], k.attend_out[...]) + k.bias[2:3]
        k.out[...] = after_attend
        k.send(k.out)
        normal, _ = normalize(after_attend)
        normed = (normal * k.gain[2:3] + k.shift[2:3]).astype(bf16)
        k.nc[...] = normed
        k.send(k.nc)
        paired = dot(normed, k.convolve_in[...])
        value = paired[:, :model] + k.bias[3:4]
        gate = paired[:, model:] + k.bias[4:5]
        k.paired[:, :model] = value
        k.paired[:, model:] = gate
        k.send(k.paired)
        gated = (value * sigmoid(gate)).astype(bf16)
        k.gated[...] = gated
        for row in range(rows):
            k.first[row] = gated[row * frames : row * frames + RIM]
            k.last[row] = gated[(row + 1) * frames - RIM : (row + 1) * frames]

    rim = sds((rows, RIM, model), bf16)
    return staged(
        "attend",
        body,
        dict(
            ends=ends, table=query.table, qv=query.qv, qu=query.qu, lo=each_of(start.lo),
            hi=each_of(start.hi), before=each_of(before), next=each_of(after), after=start.after,
            attend_out=attend_out, bias=bias, gain=gain, shift=shift, convolve_in=convolve_in,
        ),
        dict(
            prob=[sds((2, GROUPS, WIN, MANY * SPAN), bf16)] * rows, mixed=low,
            out=sds((tokens, model), f32), nc=low, paired=sds((tokens, 2 * model), f32),
            gated=low, first=rim, last=rim,
        ),
        smem=[info],
        flops=16 * 8 * 256 * 384 * 128,
        moved=16 << 20,
    )


def valid_column(info, row, rows, frames):
    at = column(frames, info[0].astype(f32))
    return (at < info[1 + rows + row].astype(f32)).astype(f32)


def pack(ref, vectors):
    at = 0
    for vector in vectors:
        for k in range(0, vector.shape[1], 128):
            ref[at : at + 1, :] = vector[:, k : k + 128]
            at += 1


def by_rows(count, size, step, init=None):
    def one(i, carry):
        return step(pl.ds(pl.multiple_of(i * size, size), size), carry)

    return lax.fori_loop(0, count // size, one, init)


def by_lanes(width, step):
    def one(i, carry):
        step(pl.ds(pl.multiple_of(i * 128, 128), 128))
        return carry

    lax.fori_loop(0, width // 128, one, 0)


def spread(column):
    return jnp.broadcast_to(column, (column.shape[0], 128))


def tap_masks(keep_s, at, low, high):
    for tap in range(KERNEL):
        off = tap - HALF
        keep_s[tap] = spread(((at + off >= low) & (at + off < high)).astype(f32))


def depth_conv(row_len, devices, info, ends, gated, before, after, taps):
    rows = before.shape[0]
    tokens, model = gated.shape
    frames = tokens // rows

    def body(k, info, rim, keep_s, valid_s, sums, tile):
        start = info[0].astype(f32)
        counts = 0.0
        taps = k.taps
        for row in range(rows):
            here = slice(row * frames, (row + 1) * frames)
            at = column(frames, start)
            low, high = bounds(k.ends[row : row + 1, :], at, row_len)
            tap_masks(keep_s, at, low, high)
            valid = valid_column(info, row, rows, frames)
            valid_s[here] = spread(valid)
            counts += total(valid)
            rim[0:RIM] = k.before[row].astype(f32)
            rim[RIM : RIM + frames] = k.gated[row][...].astype(f32)
            rim[RIM + frames :] = k.after[row].astype(f32)

            def one(lanes):
                depth = jnp.zeros((frames, 128), f32)
                for tap in range(KERNEL):
                    off = tap - HALF
                    part = rim[RIM + off : RIM + off + frames, lanes] * keep_s[tap]
                    depth += taps[tap : tap + 1, lanes] * part
                k.depth[here, lanes] = depth
                sums[row : row + 1, lanes] = total(depth * valid_s[here])

            by_lanes(model, one)
            k.send(k.depth, pl.ds(row * frames, frames))
        first = total(sums[0:rows, :])
        mean = first / jnp.maximum(counts, 1.0)
        sums[rows : rows + 1, :] = mean

        def two(lanes):
            centered = k.depth[:, lanes] - sums[rows : rows + 1, lanes]
            sums[rows + 1 : rows + 2, lanes] = total(centered * centered * valid_s[...])

        by_lanes(model, two)
        pack(tile, [first, sums[rows + 1 : rows + 2, :]])
        k.stats[...] = jnp.broadcast_to(tile[...][None], k.stats.shape)

    return staged(
        "depth_conv",
        body,
        dict(ends=ends, before=before, taps=taps, gated=by_row(gated, rows), after=after),
        dict(depth=sds((rows * frames, model), f32), stats=sds((devices, 8, 128), f32)),
        smem=[info],
        scratch=[
            pltpu.VMEM((frames + 2 * RIM, model), f32),
            pltpu.VMEM((KERNEL, frames, 128), f32),
            pltpu.VMEM((rows * frames, 128), f32),
            pltpu.VMEM((8, model), f32),
            pltpu.VMEM((8, 128), f32),
        ],
        flops=rows * frames * model * 30,
        moved=2 << 20,
        sends=rows - 1,
    )


def middle(
    devices, rows, info, stats, counts, depth, stream, feed_in, feed_in_bias, feed_out,
    convolve_out, gain, shift, bias, cotangent,
):
    tokens, model = depth.shape
    frames = tokens // rows
    hidden = feed_in.shape[2]
    parts = hidden // PART

    def body(k, info, conv_s, slope_s, tile):
        stats, each = k.stats, k.counts[:, 0:1]
        gain, shift, bias = k.gain, k.shift, k.bias
        count = total(each)
        means, inverses = [], []
        for at in range(model // 128):
            sums = stats[:, at, :]
            mean = total(sums) / count
            off = sums / jnp.maximum(each, 1.0) - mean
            spread = total(stats[:, model // 128 + at, :]) + total(each * off * off)
            means.append(mean)
            inverses.append(lax.rsqrt(spread / count + eps_norm))
        mean = jnp.concatenate(means, axis=1)
        inverse = jnp.concatenate(inverses, axis=1)
        k.inv[0:1] = inverse
        k.inv[1:2] = jnp.broadcast_to(1.0 / count, (1, model))
        normal = (k.depth[...] - mean) * inverse
        k.bn[...] = normal
        k.send(k.bn)
        batch = normal * gain[5:6] + shift[5:6]
        swished = (batch * sigmoid(batch)).astype(bf16)
        k.sw[...] = swished
        k.send(k.sw)
        after_conv = k.stream[...] + dot(swished, k.convolve_out[...]) + bias[5:6]
        conv_s[...] = after_conv
        normal, _ = normalize(after_conv)
        k.nf[...] = (normal * gain[3:4] + shift[3:4]).astype(bf16)
        k.send(k.nf)
        for part in range(parts):
            cut = slice(part * PART, (part + 1) * PART)
            inner = dot(k.nf[...], k.w_in[part][...]) + k.b_in[1:2, cut]
            active, slope = activate(inner)
            k.act[:, cut] = active.astype(bf16)
            slope_s[:, cut] = slope
        k.send(k.act)
        branch = bias[7:8]
        for part in range(parts):
            cut = slice(part * PART, (part + 1) * PART)
            branch = branch + dot(k.act[:, cut], k.w_out[part][...])
        normal, inverse = normalize(conv_s[...] + 0.5 * branch)
        valid = jnp.concatenate(
            [valid_column(info, row, rows, frames) for row in range(rows)], axis=0
        )
        k.out[...] = (valid * (normal * gain[4:5] + shift[4:5])).astype(bf16)
        k.send(k.out)
        grad = valid * k.cotangent[...].astype(f32)
        grad, gain_grad, shift_grad = norm_back(grad, normal, inverse, gain[4:5])
        k.gcs[...] = grad
        low = (0.5 * grad).astype(bf16)
        k.gl[...] = low
        k.send(k.gl)
        vec = k.vec
        vec[2:3] = gain_grad
        vec[3:4] = shift_grad
        vec[5:6] = total(low.astype(f32))
        back = 0.0
        for part in range(parts):
            cut = slice(part * PART, (part + 1) * PART)
            grad = (dot_last(k.gl[...], k.w_out[part][...]) * slope_s[:, cut]).astype(bf16)
            k.gi[:, cut] = grad
            k.fb[:, cut] = total(grad.astype(f32))
            back = back + dot_last(grad, k.w_in[part][...])
        k.send(k.gi)
        normal, inverse = normalize(conv_s[...])
        grad, gain_grad, shift_grad = norm_back(back, normal, inverse, gain[3:4])
        vec[0:1] = gain_grad
        vec[1:2] = shift_grad
        grad = k.gcs[...] + grad
        k.gcs[...] = grad
        k.send(k.gcs)
        low = grad.astype(bf16)
        k.gcl[...] = low
        k.send(k.gcl)
        vec[4:5] = total(low.astype(f32))
        bn = k.bn[...]
        batch = bn * gain[5:6] + shift[5:6]
        _, slope = activate(batch)
        grad = dot_last(low, k.convolve_out[...]) * slope
        k.gb[...] = grad
        k.send(k.gb)
        pack(tile, [total(grad), total(grad * bn)])
        k.totals[...] = jnp.broadcast_to(tile[...][None], k.totals.shape)
        k.send(k.totals)
        for row in range(rows):
            at, end = row * frames, (row + 1) * frames
            k.first[row, :, :model] = k.gb[at : at + RIM_GRAD]
            k.first[row, :, model:] = k.bn[at : at + RIM_GRAD]
            k.last[row, :, :model] = k.gb[end - RIM_GRAD : end]
            k.last[row, :, model:] = k.bn[end - RIM_GRAD : end]

    w_in, w_out = feed_slabs(feed_in, feed_out, 1)
    ins = dict(
        stats=stats, counts=counts, gain=gain, shift=shift, depth=depth, bias=bias,
        convolve_out=convolve_out, stream=stream, b_in=feed_in_bias, w_in=w_in, w_out=w_out,
        cotangent=cotangent,
    )
    low = sds((tokens, model), bf16)
    wide = sds((tokens, model), f32)
    rim = sds((rows, RIM_GRAD, 2 * model), f32)
    return staged(
        "middle",
        body,
        ins,
        dict(
            out=low, act=sds((tokens, hidden), bf16), gi=sds((tokens, hidden), bf16), nf=low,
            gl=low, sw=low, gcl=low, gcs=wide, gb=wide, bn=wide, inv=sds((8, model), f32),
            totals=sds((devices, 8, 128), f32), first=rim, last=rim, vec=sds((8, model), f32),
            fb=sds((1, hidden), f32),
        ),
        smem=[info],
        scratch=[
            pltpu.VMEM((tokens, model), f32),
            pltpu.VMEM((tokens, hidden), f32),
            pltpu.VMEM((8, 128), f32),
        ],
        flops=2 * tokens * model * (4 * hidden + 2 * model),
        moved=24 << 20,
    )


def conv_back(
    row_len, n, info, ends, taps, convolve_in, attend_out, gain, totals, mid, edge_before,
    edge_after, rim_before, rim_after, mix, early,
):
    tokens, model = mid.gb.shape
    rows = rim_before.shape[0]
    frames = tokens // rows
    slim = model // n
    room = slim % 8 == 0

    def body(k, info, grads, rim, keep_s, gp, gal):
        start = info[0].astype(f32)
        parts = model // 128
        sums = [total(k.totals[:, at, :]) for at in range(2 * parts)]
        total_a = jnp.concatenate(sums[:parts], axis=1)
        total_b = jnp.concatenate(sums[parts:], axis=1)
        inverse, per_count = k.inv[0:1], k.inv[1:2]
        gain, taps, vec = k.gain, k.taps, k.vec
        own_scale = inverse * gain[5:6]
        share_a = own_scale * total_a * per_count
        share_b = own_scale * total_b * per_count
        vec[14:15] = total_a
        vec[15:16] = total_b
        vec[0:9] = jnp.zeros((9, model), f32)
        vec[9:14] = jnp.zeros((5, model), f32)

        def grad_of(grad, normal, valid):
            grad = grad * own_scale - valid * (share_a + normal * share_b)
            return grad.astype(bf16).astype(f32)

        for row in range(rows):
            first = row * frames
            last = info[1 + rows + row].astype(f32)
            at = column(frames, start)
            low, high = bounds(k.ends[row : row + 1, :], at, row_len)
            tap_masks(keep_s, at, low, high)
            before, after = k.edge_before, k.edge_after
            edge_at = column(RIM_GRAD, start - RIM_GRAD)
            grads[0:RIM_GRAD] = grad_of(
                before[row, :, :model], before[row, :, model:], (edge_at < last).astype(f32)
            )
            for step in range(0, frames, 32):
                here = slice(step, step + 32)
                at = column(32, start + step)
                grads[RIM_GRAD + step : RIM_GRAD + step + 32] = grad_of(
                    k.gb[row][here], k.bn[row][here], (at < last).astype(f32)
                )
            edge_at = column(RIM_GRAD, start + frames)
            grads[RIM_GRAD + frames :] = grad_of(
                after[row, :, :model], after[row, :, model:], (edge_at < last).astype(f32)
            )
            rim[0:RIM] = k.rim_before[row].astype(f32)
            rim[RIM : RIM + frames] = k.gated[row][...].astype(f32)
            rim[RIM + frames :] = k.rim_after[row].astype(f32)
            paired = k.paired[row]
            half = frames // 2

            def one(i, carry):
                lane = pl.multiple_of(i * 128, 128)
                lanes, gates = pl.ds(lane, 128), pl.ds(model + lane, 128)
                for base in range(0, frames, half):
                    own = grads[RIM_GRAD + base : RIM_GRAD + base + half, lanes]
                    grad = jnp.zeros((half, 128), f32)
                    for tap in range(KERNEL):
                        off = base + tap - HALF
                        keep = keep_s[tap, base : base + half]
                        part = own * (rim[RIM + off : RIM + off + half, lanes] * keep)
                        vec[tap : tap + 1, lanes] += total(part)
                        mirror = KERNEL - 1 - tap
                        part = grads[RIM_GRAD + off : RIM_GRAD + off + half, lanes] * keep
                        grad += taps[mirror : mirror + 1, lanes] * part
                    sigma = sigmoid(paired[base : base + half, gates])
                    one = (grad * sigma).astype(bf16)
                    value = paired[base : base + half, lanes]
                    two = (grad * sigma * value * (1.0 - sigma)).astype(bf16)
                    here = slice(first + base, first + base + half)
                    gp[here, lanes] = one
                    gp[here, gates] = two
                    vec[11:12, lanes] += total(one.astype(f32))
                    vec[12:13, lanes] += total(two.astype(f32))
                return carry

            lax.fori_loop(0, model // 128, one, 0)
        grad = dot_last(gp[...], k.convolve_in[...])
        normal, inverse = normalize(k.after[...])
        grad, gain_grad, shift_grad = norm_back(grad, normal, inverse, gain[2:3])
        vec[9:10] = gain_grad
        vec[10:11] = shift_grad
        grad = k.gcs[...] + grad
        k.gas[...] = grad
        k.send(k.gas)
        low = grad.astype(bf16)
        gal[...] = low
        vec[13:14] = total(low.astype(f32))
        k.gm[...] = dot_last(gal[...], k.attend_out[...]).astype(bf16)
        k.send(k.gm)
        out = k.early
        out[:, :slim] = dot_first(k.nc[...], gp[...]).astype(bf16).reshape(n, slim, 2 * model)
        block = dot_first(k.sw[...], k.gcl[...]).astype(bf16)
        out[:, slim:, :model] = block.reshape(n, slim, model)
        block = dot_first(k.mixed[...], gal[...]).astype(bf16)
        out[:, slim:, model:] = block.reshape(n, slim, model)

    own = (n, 2 * slim, 2 * model)
    size = early.shape[1] - 2 * slim
    if room:
        out = (sds(early.shape, bf16), lambda ref: ref.at[:, pl.ds(size, 2 * slim)], own)
    else:
        out = sds(own, bf16)
    got = staged(
        "conv_back",
        body,
        dict(
            totals=totals, inv=mid.inv, gain=gain, ends=ends, taps=taps, edge_before=edge_before,
            edge_after=edge_after, rim_before=rim_before, rim_after=rim_after,
            gb=by_row(mid.gb, rows), bn=by_row(mid.bn, rows), gated=by_row(mix.gated, rows),
            paired=by_row(mix.paired, rows), convolve_in=convolve_in, after=mix.out, gcs=mid.gcs,
            attend_out=attend_out, nc=mix.nc, sw=mid.sw, gcl=mid.gcl, mixed=mix.mixed,
        ),
        dict(
            early=out, gas=sds((tokens, model), f32), gm=sds((tokens, model), bf16),
            vec=sds((16, model), f32),
        ),
        smem=[info],
        scratch=[
            pltpu.VMEM((frames + 2 * RIM_GRAD, model), f32),
            pltpu.VMEM((frames + 2 * RIM, model), f32),
            pltpu.VMEM((KERNEL, frames, 128), f32),
            pltpu.VMEM((tokens, 2 * model), bf16),
            pltpu.VMEM((tokens, model), bf16),
        ],
        flops=2 * tokens * model * 7 * model,
        moved=16 << 20,
        filled=early if room else None,
    )
    if not room:
        got.early = jnp.concatenate([early, got.early], axis=1)
    return got


def attend_back(start, query, before, after, probs, gm):
    rows = before.shape[0]
    tokens, model = query.qu.shape
    frames = tokens // rows
    factor = 1.0 / math.sqrt(DH)

    def body(k, acc, turned):
        g_table, vec, table = k.g_table, k.vec, k.table
        g_table[...] = jnp.zeros_like(g_table)
        vec[...] = jnp.zeros_like(vec)
        turn = flip(WIN)
        for row in range(rows):
            acc[...] = jnp.zeros_like(acc)
            for block in range(2):
                here = slice(WIN * block, WIN * (block + 1))
                span = slice(WIN * block, WIN * block + SPAN)
                turned[0] = dot(turn, k.gm[row][here]).astype(bf16)
                turned[1] = dot(turn, k.qu[row][here]).astype(bf16)
                turned[2] = dot(turn, k.qv[row][here]).astype(bf16)
                blocks = [k.lo[row], k.hi[row]]
                blocks = blocks + [k.next[row]] if block else [k.before[row]] + blocks
                prob = k.prob[2 * row + block]
                for group in range(GROUPS):
                    cut = slice(WIDE * group, WIDE * (group + 1))
                    cut_v = slice(model + WIDE * group, model + WIDE * (group + 1))
                    keys = jnp.concatenate([b[:, cut] for b in blocks], axis=0)
                    values = jnp.concatenate([b[:, cut_v] for b in blocks], axis=0)
                    weights = below(prob[group])
                    grad_mixed = heads_apart(turned[0, :, cut])
                    grad = dot_last(grad_mixed, values)
                    wide = weights.astype(f32)
                    delta = jnp.sum(wide * grad, axis=1, keepdims=True)
                    raw = (wide * (grad - delta)).astype(bf16)
                    acc[span, cut_v] += dot_first(weights, grad_mixed)
                    acc[span, cut] += dot_first(raw, heads_apart(turned[1, :, cut]))
                    grad_u = heads_joined(dot(raw, keys)) * factor
                    band = pltpu.roll(
                        raw.astype(f32).reshape(MANY, WIN, SPAN),
                        SPAN - (WIN - 1),
                        2,
                        stride=1,
                        stride_axis=1,
                    )
                    band = band.astype(bf16).reshape(MANY * WIN, SPAN)
                    grad_v = heads_joined(dot(band, table[:, cut])) * factor
                    g_table[:, cut] += dot_first(band, heads_apart(turned[2, :, cut]))
                    vec[0:1, cut] += total(grad_u)
                    vec[1:2, cut] += total(grad_v)
                    both = (grad_u + grad_v).astype(bf16)
                    k.gq[row][here, cut] = dot(turn, both).astype(bf16)
                if block == 0:
                    k.g_before[row] = acc[0:WIN].astype(bf16)
                    k.send(k.g_before, row)
            k.g_after[row] = acc[3 * WIN :].astype(bf16)
            k.send(k.g_after, row)
            k.g_lo[row][...] = acc[WIN : 2 * WIN]
            k.send(k.g_lo[row])
            k.g_hi[row][...] = acc[2 * WIN : 3 * WIN]
            k.send(k.g_hi[row])
            k.send(k.gq[row])

    ins = dict(
        gm=by_row(gm, rows), qu=by_row(query.qu, rows), qv=by_row(query.qv, rows),
        before=each_of(before), lo=each_of(start.lo), hi=each_of(start.hi),
        prob=[
            slab(prob, block, (0, GROUPS), (0, WIN), (0, MANY * SPAN))
            for prob in probs
            for block in range(2)
        ],
        table=query.table, next=each_of(after),
    )
    kv = (WIN, 2 * model)
    return staged(
        "attend_back",
        body,
        ins,
        dict(
            gq=[sds((frames, model), bf16)] * rows, g_before=sds((rows,) + kv, bf16),
            g_lo=[sds(kv, f32)] * rows, g_hi=[sds(kv, f32)] * rows,
            g_after=sds((rows,) + kv, bf16), g_table=sds((SPAN, model), f32),
            vec=sds((8, model), f32),
        ),
        scratch=[
            pltpu.VMEM((4 * WIN, 2 * model), f32),
            pltpu.VMEM((3, WIN, model), bf16),
        ],
        flops=16 * 14 * 256 * 384 * 128,
        moved=16 << 20,
        sends=2 * rows - 2,
    )


def back(info, core_at, n, grads, halo, attend_in, start, gas, gain, sinusoid):
    rows = len(grads.gq)
    tokens, model = start.after.shape
    frames = tokens // rows
    hidden = start.act.shape[1]
    parts = hidden // PART
    width, slim = hidden // n, model // n

    def body(k, info, joined):
        core = info[core_at]
        vec, gain = k.vec, k.gain
        sums = [0.0] * 5
        for row in range(rows):
            here = slice(row * frames, (row + 1) * frames)
            low_half = slice(row * frames, row * frames + WIN)
            high_half = slice(row * frames + WIN, (row + 1) * frames)
            joined[here, :model] = k.gq[row][...]
            pair = (k.g_lo[row][...] + k.left[row][...].astype(f32)).astype(bf16)
            joined[low_half, model:] = pair
            pair = (k.g_hi[row][...] + k.right[row][...].astype(f32)).astype(bf16)
            joined[high_half, model:] = pair
            both = joined[here]
            k.gv[here] = both[:, 2 * model :]
            sums[0] += total(both[:, :model].astype(f32))
            sums[1] += total(both[:, 2 * model :].astype(f32))
            grad = dot_last(both, k.attend_in[...])
            normal, inverse = normalize(k.after[row][...])
            grad, gain_grad, shift_grad = norm_back(grad, normal, inverse, gain[1:2])
            sums[2] += gain_grad
            sums[3] += shift_grad
            grad = k.gas[row][...] + grad
            k.gfs[row][...] = grad
            k.send(k.gfs[row])
            low = (0.5 * grad).astype(bf16)
            k.gl[here] = low
            sums[4] += total(low.astype(f32))
        k.send(k.gv)
        k.send(k.gl)
        for at in range(5):
            vec[at : at + 1] = sums[at]
        pairs = (0, n // 2)
        block = dot_first(k.na[...], joined[:, : 2 * model])
        for part in range(2):
            cut = slice(part * model, (part + 1) * model)
            keep_half(block[:, cut], core, k.mine, k.other, pairs, width + part * slim)
        high = k.g_table[...].astype(bf16)
        low = (k.g_table[...] - high.astype(f32)).astype(bf16)
        place = dot_first(k.sinusoid[...], high) + dot_first(k.sinusoid[...], low)
        keep_half(place, core, k.mine, k.other, pairs, width + 2 * slim)
        step = n // 2 // parts
        for part in range(parts):
            block = dot_first(k.act[part][...], k.gl[...])
            some = (part * step, (part + 1) * step)
            keep_half(block, core, k.mine, k.other, some)
            k.send(k.other, pl.ds(part * step, step))
            k.send(k.mine, pl.ds(part * step, step))

    half = sds((n // 2, width + 3 * slim, model), bf16)
    low = sds((tokens, model), bf16)
    return staged(
        "back",
        body,
        dict(
            gain=gain, gq=grads.gq, g_lo=grads.g_lo, left=each_of(halo[0]), g_hi=grads.g_hi,
            right=each_of(halo[1]), attend_in=attend_in, after=by_row(start.after, rows),
            gas=by_row(gas, rows), na=start.na, g_table=grads.g_table, sinusoid=sinusoid,
            act=[slab(start.act, (0, tokens), (at, PART)) for at in range(0, hidden, PART)],
        ),
        dict(
            other=half, mine=half, gv=low, gl=low, gfs=[sds((frames, model), f32)] * rows,
            vec=sds((8, model), f32),
        ),
        smem=[info],
        scratch=[pltpu.VMEM((tokens, 3 * model), bf16)],
        flops=2 * tokens * model * (hidden + 6 * model),
        moved=18 << 20,
        sends=2 * parts - 2,
    )


def keep_half(block, core, mine_ref, other_ref, rows, at=0):
    model = mine_ref.shape[2]
    pairs = rows[1] - rows[0]
    size = block.shape[0] // (2 * pairs)
    shaped = block.reshape(pairs, 2, size, model)
    even, odd = shaped[:, 0], shaped[:, 1]
    here = slice(*rows)
    mine_ref[here, at : at + size] = jnp.where(core == 0, even, odd).astype(bf16)
    other_ref[here, at : at + size] = jnp.where(core == 0, odd, even).astype(bf16)


def first_back(info, core_at, n, gl, feed_in, feed_out, start, gv):
    tokens, hidden = start.slope.shape
    model = gl.shape[1]
    parts = hidden // PART

    def body(k, info):
        core = info[core_at]
        step = n // 2 // parts
        back = 0.0
        block = dot_first(k.na[...], k.gv[...])
        keep_half(block, core, k.mine, k.other, (0, n // 2), hidden // n)
        for part in range(parts):
            cut = slice(part * PART, (part + 1) * PART)
            grad = dot_last(k.gl[...], k.w_out[part][...])
            grad = (grad * k.slope[part][...].astype(f32)).astype(bf16)
            k.fb[:, cut] = total(grad.astype(f32))
            block = dot_first(grad, k.n0[...])
            some = (part * step, (part + 1) * step)
            keep_half(block, core, k.mine, k.other, some)
            k.send(k.other, pl.ds(part * step, step))
            k.send(k.mine, pl.ds(part * step, step))
            back = back + dot_last(grad, k.w_in[part][...])
        k.gn[...] = back

    half = sds((n // 2, hidden // n + model // n, model), bf16)
    w_in, w_out = feed_slabs(feed_in, feed_out, 0)
    return staged(
        "first_back",
        body,
        dict(
            na=start.na, gv=gv, gl=gl, w_out=w_out,
            slope=[slab(start.slope, (0, tokens), (at, PART)) for at in range(0, hidden, PART)],
            n0=start.n0, w_in=w_in,
        ),
        dict(other=half, mine=half, fb=sds((1, hidden), f32), gn=sds((tokens, model), f32)),
        smem=[info],
        flops=2 * tokens * model * hidden * 3,
        moved=12 << 20,
        sends=2 * parts - 2,
    )


def last(features, gn, gfs, gain):
    rows, frames, model = features.shape

    def body(k):
        gain_grads, shift_grads = 0.0, 0.0
        for row in range(rows):
            here = slice(row * frames, (row + 1) * frames)
            normal, inverse = normalize(k.x[row][...].astype(f32))
            grad = k.gn[row][...]
            grad, gain_grad, shift_grad = norm_back(grad, normal, inverse, k.gain[0:1])
            k.out[row] = k.gfs[row][...] + grad
            k.send(k.out, row)
            gain_grads += gain_grad
            shift_grads += shift_grad
        k.vec[0:1] = gain_grads
        k.vec[1:2] = shift_grads

    ins = dict(
        gain=gain, x=[slab(features, row, (0, frames), (0, model)) for row in range(rows)],
        gn=[slab(gn, (row * frames, frames), (0, model)) for row in range(rows)], gfs=list(gfs),
    )
    return staged(
        "last",
        body,
        ins,
        dict(out=sds(features.shape, f32), vec=sds((8, model), f32)),
        flops=rows * frames * model * 20,
        moved=4 << 20,
        sends=rows - 1,
        limit=FOLD_LIMIT,
    )


def feed_weights(n, gi, nf, act, gl):
    tokens, model = nf.shape
    hidden = gi.shape[1]
    parts = hidden // PART
    size, slim = hidden // n, model // n
    step = n // parts
    room = 2 * slim if slim % 8 == 0 else 0

    def body(k):
        for part in range(parts):
            here = slice(part * step, (part + 1) * step)
            block = dot_first(k.gi[part][...], k.nf[...]).astype(bf16)
            k.out[here, :, :model] = block.reshape(step, size, model)
            block = dot_first(k.act[part][...], k.gl[...]).astype(bf16)
            k.out[here, :, model:] = block.reshape(step, size, model)
            k.send(k.out, pl.ds(part * step, step))

    ins = dict(
        nf=nf, gi=[slab(gi, (0, tokens), (at, PART)) for at in range(0, hidden, PART)], gl=gl,
        act=[slab(act, (0, tokens), (at, PART)) for at in range(0, hidden, PART)],
    )
    own = (n, size, 2 * model)
    shape = sds((n, size + room, 2 * model), bf16)
    return staged(
        "feed_weights",
        body,
        ins,
        dict(out=(shape, lambda ref: ref.at[:, pl.ds(0, size)] if room else ref, own)),
        flops=4 * tokens * model * hidden,
        moved=10 << 20,
        sends=parts - 1,
    ).out


def neighbours(last_block, first_block):
    devices = lax.axis_size("frames")
    up = [(i, i + 1) for i in range(devices - 1)]
    down = [(i + 1, i) for i in range(devices - 1)]
    return lax.ppermute(last_block, "frames", up), lax.ppermute(first_block, "frames", down)


def gather(copies):
    return lax.all_to_all(copies, DEVICES, 0, 0, tiled=True)


def scatter_sum(grads):
    return lax.psum_scatter(grads, "frames", scatter_dimension=0, tiled=True)


ROW_PAIR = [(0, 1), (1, 0)]
COLUMNS, IN_FLOAT = 1, 2


def swap(x, k):
    n = lax.axis_size("frames")
    return lax.ppermute(x, "frames", [(i, i ^ k) for i in range(n)])


def swaps(sends, group):
    k, size = group
    return [swap(send, k * one) for one, send in zip(range(1, size), sends)]


def fold(name, info, row_at, states, small=None):
    mines, gots, keeps, sends, plans = [], [], [], [], []
    for mine, got, how in states:
        size, height, model = mine.shape
        if isinstance(how, tuple):
            _, place, digits = how
            view = (size // (digits * place), digits, place, height, model)
            half = (view[0], place, height, model)
        else:
            view = mine.shape
            half = (size, height, model // 2) if how == COLUMNS else mine.shape
        n_sends = how[2] - 1 if isinstance(how, tuple) else int(how == COLUMNS)
        plans.append((len(gots), len(got), len(sends), n_sends, how))
        mines.append(mine.reshape(view))
        gots += [one.reshape(view) for one in got]
        keeps.append(sds(half, f32 if how == IN_FLOAT else bf16))
        sends += [sds(half, bf16)] * n_sends

    def body(k, info):
        for at, (got_at, n_got, send_at, _, how) in enumerate(plans):
            parts = [k.mine[at]] + [k.got[got_at + one] for one in range(n_got)]

            def added(*index):
                return sum(part[index].astype(f32) for part in parts)

            keep = k.keep[at]
            if how is None or how == IN_FLOAT:
                keep[...] = added(...).astype(keep.dtype)
            elif how == COLUMNS:
                half = keep.shape[2]
                both = [
                    added(slice(None), slice(None), slice(one * half, (one + 1) * half))
                    for one in range(2)
                ]
                first = info[row_at] == 0
                k.away[send_at][...] = jnp.where(first, both[1], both[0]).astype(bf16)
                k.send(k.away[send_at])
                keep[...] = jnp.where(first, both[0], both[1]).astype(bf16)
            else:
                digit = info[how[0]]
                for one in range(1, how[2]):
                    other = digit
                    for bit in (1, 2):
                        if one & bit:
                            other = other + bit * (1 - 2 * ((digit // bit) % 2))
                    k.away[send_at + one - 1][...] = added(slice(None), other).astype(bf16)
                    k.send(k.away[send_at + one - 1])
                keep[...] = added(slice(None), digit).astype(bf16)
        if small is not None:
            k.total[...] = sum(k.small[one][...] for one in range(len(small)))

    ins, outs = dict(mine=mines, got=gots), dict(keep=keeps, away=sends)
    if small is not None:
        ins |= dict(small=list(small))
        outs |= dict(total=sds(small[0].shape, f32))
    got = staged(name, body, ins, outs, smem=[info], flops=1 << 20, moved=2 << 20, limit=FOLD_LIMIT)
    results = []
    for at, (mine, _, how) in enumerate(states):
        size, height, model = mine.shape
        shape = (size // how[2], height, model) if isinstance(how, tuple) else got.keep[at].shape
        _, _, send_at, n_sends, _ = plans[at]
        away = [one.reshape(shape) for one in got.away[send_at : send_at + n_sends]]
        results.append((got.keep[at].reshape(shape), away))
    if small is not None:
        results.append(got.total)
    return results


def finish(info, row_at, a, b, b_got, early, width, slim):
    model = a.shape[1]

    def body(info, a, b, b_got, early, feed_in, feed_out, joined, attend, place, con_in, con_out):
        feed_in[0] = a[:width].T
        feed_in[1] = early[:width, :model].T
        first = info[row_at] == 0
        one, two = b[...].astype(f32), b_got[...].astype(f32)
        whole = jnp.concatenate([jnp.where(first, one, two), jnp.where(first, two, one)], axis=1)
        feed_out[0] = whole[:width]
        feed_out[1] = early[:width, model:]
        joined[:, :model] = whole[width : width + slim]
        joined[:, model : 2 * model] = whole[width + slim : width + 2 * slim]
        joined[:, 2 * model :] = a[width:]
        place[...] = whole[width + 2 * slim :]
        con_in[...] = early[width : width + slim]
        con_out[...] = early[width + slim :, :model]
        attend[...] = early[width + slim :, model:]

    def full(shape):
        return pl.BlockSpec(shape, lambda i: (0,) * len(shape))

    shapes = [
        (2, model, width), (2, width, model), (slim, 3 * model), (slim, model), (slim, model),
        (slim, 2 * model), (slim, model),
    ]
    return pl.pallas_call(
        body,
        grid=(1,),
        in_specs=[pl.BlockSpec(memory_space=pltpu.SMEM)]
        + [full(one.shape) for one in (a, b, b_got, early)],
        out_specs=[full(shape) for shape in shapes],
        out_shape=[sds(shape, f32) for shape in shapes],
        compiler_params=pltpu.CompilerParams(vmem_limit_bytes=FOLD_LIMIT),
        name="finish",
    )(info, a, b, b_got, early)


def per_device(
    features,
    lengths,
    windows,
    feed_in,
    feed_in_bias,
    feed_out,
    attend_in,
    attend_out,
    position_proj,
    convolve_in,
    convolve_out,
    depthwise,
    norm_gain,
    norm_shift,
    biases,
    cotangent,
):
    rows, frames, model = features.shape
    tokens = rows * frames
    n = lax.axis_size("frames")
    devices = lax.axis_size("rows") * n
    row_len = float(frames * n)
    me = lax.axis_index("frames")
    first_frame = me * frames
    hidden = feed_in.shape[2]
    ends_every = jnp.cumsum(lengths, axis=1, dtype=jnp.int32)
    ends_here = lax.dynamic_slice_in_dim(ends_every, lax.axis_index("rows") * rows, rows, 0)
    slots = ends_here.shape[1]
    ends = jnp.pad(
        ends_here.astype(f32), ((0, 8 - rows), (0, -slots % 128)), constant_values=row_len
    )
    groups, k = [(2, 2)], 4
    while k < n:
        groups.append((k, min(4, n // k)))
        k *= groups[-1][1]
    places = [lax.axis_index("rows"), me % 2] + [(me // k) % size for k, size in groups]
    info = jnp.concatenate(
        [first_frame[None].astype(jnp.int32), windows, ends_here[:, -1], jnp.stack(places)]
    )
    row_at = 1 + 2 * rows
    core_at = row_at + 1
    starts = jnp.arange(n, dtype=jnp.int32) * frames
    counts = jnp.clip(ends_every[:, -1][:, None] - starts[None, :], 0, frames)
    counts = jnp.sum(counts.reshape(-1, rows, n), axis=1).astype(f32).reshape(devices, 1)
    counts = jnp.broadcast_to(counts, (devices, 128))
    sinusoid = jnp.asarray(position_table(WIN, model))

    start = front(
        features, feed_in, feed_in_bias, feed_out, attend_in, norm_gain, norm_shift, biases
    )
    before, after = neighbours(start.hi, start.lo)
    query = queries(start.na, attend_in, biases, sinusoid, position_proj)
    mix = attend(
        row_len, info, ends, start, query, before, after, attend_out, convolve_in, norm_gain,
        norm_shift, biases,
    )
    rim_before, rim_after = neighbours(mix.last, mix.first)
    got = depth_conv(row_len, devices, info, ends, mix.gated, rim_before, rim_after, depthwise)
    mid = middle(
        devices, rows, info, gather(got.stats), counts, got.depth, mix.out, feed_in,
        feed_in_bias, feed_out, convolve_out, norm_gain, norm_shift, biases,
        cotangent.reshape(tokens, model),
    )
    edge_before, edge_after = neighbours(mid.last, mid.first)
    totals = gather(mid.totals)
    early = feed_weights(n, mid.gi, mid.nf, mid.act, mid.gl)
    totals, early = lax.optimization_barrier((totals, early))
    conv = conv_back(
        row_len, n, info, ends, depthwise, convolve_in, attend_out, norm_gain, totals, mid,
        edge_before, edge_after, rim_before, rim_after, mix, early,
    )
    early, gm = lax.optimization_barrier((conv.early, conv.gm))
    early = scatter_sum(early)
    grads = attend_back(start, query, before, after, mix.prob, gm)
    halo = neighbours(grads.g_after, grads.g_before)
    end = back(
        info, core_at, n, grads, halo, attend_in, start, conv.gas, norm_gain, sinusoid
    )
    b, b_got = end.mine, [swap(end.other, 1)]
    got = first_back(info, core_at, n, end.gl, feed_in, feed_out, start, end.gv)
    a, a_got = got.mine, [swap(got.other, 1)]
    ((b, b_send),) = fold("fold_b", info, row_at, [(b, b_got, COLUMNS)])
    b_got = [lax.ppermute(b_send[0], "rows", ROW_PAIR)]
    ((a, a_send),) = fold("fold_a", info, row_at, [(a, a_got, (core_at + 1, 1, 2))])
    a_got = swaps(a_send, groups[0])
    gn, a = lax.optimization_barrier((got.gn, a))
    ending = last(features, gn, end.gfs, norm_gain)

    vec_conv, vec_mid, vec_back, vec_last = conv.vec, mid.vec, end.vec, ending.vec
    small = jnp.concatenate(
        [
            vec_conv[:KERNEL],
            vec_last[0:1], vec_back[2:3], vec_conv[9:10], vec_mid[0:1], vec_mid[2:3],
            vec_last[1:2], vec_back[3:4], vec_conv[10:11], vec_mid[1:2], vec_mid[3:4],
            vec_back[0:2], vec_conv[13:14], vec_conv[11:13], vec_mid[4:5], vec_back[4:5],
            vec_mid[5:6], grads.vec[0:2],
            got.fb.reshape(-1, model), mid.fb.reshape(-1, model),
            jnp.zeros((3, model), f32),
        ],
        axis=0,
    )
    small = [small] + swaps([small] * 3, (1, 4))
    last_group = groups[-1]
    for at, group in enumerate(groups):
        deeper = at + 1 < len(groups)
        a_how = (core_at + 2 + at, 1, groups[at + 1][1]) if deeper else None
        states = [(a, a_got, a_how), (b, b_got, (core_at + 1 + at, 1, group[1]))]
        (a, a_send), (b, b_send), one = fold(f"fold_{at}", info, row_at, states, small)
        if deeper:
            a_got = swaps(a_send, groups[at + 1])
        else:
            early, a = lax.optimization_barrier((early, a))
            a_got = [lax.ppermute(a, "rows", ROW_PAIR)]
            early_got = [lax.ppermute(early, "rows", ROW_PAIR)]
        b_got = swaps(b_send, group)
        if at == 0:
            small = [one, lax.ppermute(one, "rows", ROW_PAIR)]
        elif deeper:
            small = [one] + swaps([one] * (group[1] - 1), group)
    states = [(b, b_got, None), (a, a_got, IN_FLOAT), (early, early_got, IN_FLOAT)]
    (b, _), (a, _), (early, _) = fold("fold_last", info, row_at, states)
    b_got = lax.ppermute(b, "rows", ROW_PAIR)
    small = [one] + swaps([one] * (last_group[1] - 1), last_group)
    slim = model // n
    width = hidden // n
    feed_in_grad, feed_out_grad, joined, *rest = finish(
        info, row_at, a[0], b[0], b_got[0], early[0], width, slim
    )
    small = sum(small)
    n_vectors = small.shape[0] - 3 - 2 * (hidden // model)
    vectors = jnp.concatenate([small[:n_vectors], vec_conv[14:16]], axis=0)
    thin = lax.dynamic_slice_in_dim(vectors, me * slim, slim, 1)
    feed_bias = small[n_vectors:-3].reshape(2, hidden)
    feed_bias = lax.dynamic_slice_in_dim(feed_bias, me * width, width, 1)
    return (
        mid.out.reshape(rows, frames, model),
        ending.out,
        feed_in_grad,
        feed_bias,
        feed_out_grad,
        joined,
        *rest,
        thin[:KERNEL],
        jnp.concatenate([thin[KERNEL : KERNEL + 5], thin[n_vectors + 1 :]], axis=0),
        jnp.concatenate([thin[KERNEL + 5 : KERNEL + 10], thin[n_vectors : n_vectors + 1]], axis=0),
        thin[KERNEL + 10 : n_vectors],
    )


def solution(mesh):
    placed = (
        P("rows", "frames", None),
        P(),
        P("rows"),
        P(),
        P(),
        P(),
        P(),
        P(),
        P(),
        P(),
        P(),
        P(),
        P(),
        P(),
        P(),
        P("rows", "frames", None),
    )
    return jax.shard_map(
        per_device,
        mesh=mesh,
        in_specs=placed,
        out_specs=(
            P("rows", "frames", None),
            P("rows", "frames", None),
            P(None, None, "frames"),
            P(None, "frames"),
            P(None, "frames", None),
            P("frames", None),
            P("frames", None),
            P("frames", None),
            P("frames", None),
            P("frames", None),
            P(None, "frames"),
            P(None, "frames"),
            P(None, "frames"),
            P(None, "frames"),
        ),
        check_vma=False,
    )
```

```python
import functools
import math
import types

import jax
import jax.numpy as jnp
import ml_dtypes
import numpy as np
from jax import lax
from jax.experimental import pallas as pl
from jax.experimental.pallas import tpu as pltpu
from jax.sharding import PartitionSpec as P

H = 8
DH = 64
KERNEL = 9
WIN = 128

HALF = KERNEL // 2
SPAN = 3 * WIN
MANY = 4
GROUPS = H // MANY
WIDE = MANY * DH
RIM = 16
RIM_GRAD = 8
eps_norm = 1e-05
negative = -1e30
f32 = jnp.float32
bf16 = jnp.bfloat16
DEVICES = ("rows", "frames")
VMEM_LIMIT = 60 * 1024 * 1024
FOLD_LIMIT = 14 * 1024 * 1024


def dot(left, right):
    return jnp.dot(left, right, preferred_element_type=f32)


def dot_last(left, right):
    return lax.dot_general(left, right, (((1,), (1,)), ((), ())), preferred_element_type=f32)


def dot_first(left, right):
    return lax.dot_general(left, right, (((0,), (0,)), ((), ())), preferred_element_type=f32)


def sigmoid(x):
    return 0.5 * jnp.tanh(0.5 * x) + 0.5


def total(x):
    return jnp.sum(x, axis=0, keepdims=True)


def normalize(values):
    centered = values - jnp.mean(values, axis=-1, keepdims=True)
    inverse = lax.rsqrt(jnp.mean(centered * centered, axis=-1, keepdims=True) + eps_norm)
    return centered * inverse, inverse


def norm_back(grad_out, normal, inverse, gain):
    scaled = grad_out * gain
    centred = scaled - jnp.mean(scaled, axis=-1, keepdims=True)
    grad_in = inverse * (centred - normal * jnp.mean(scaled * normal, axis=-1, keepdims=True))
    return grad_in, total(grad_out * normal), total(grad_out)


def position_table(width, model):
    offsets = (np.arange(2 * width + 1) - width).astype(np.float32)
    rates = np.exp(
        np.arange(model // 2).astype(np.float32) * np.float32(-2.0 * math.log(10000.0) / model)
    )
    angles = (offsets[:, None] * rates[None, :]).astype(np.float32)
    both = np.stack([np.sin(angles), np.cos(angles)], axis=2).reshape(2 * width + 1, model)
    padded = np.zeros((3 * width, model), np.float32)
    padded[: 2 * width + 1] = both
    return padded.astype(ml_dtypes.bfloat16)


def bounds(ends, at, row_len):
    low = jnp.max(jnp.where(ends <= at, ends, 0.0), axis=1, keepdims=True)
    high = jnp.min(jnp.where(ends > at, ends, row_len), axis=1, keepdims=True)
    return low, high


def column(count, offset):
    return lax.broadcasted_iota(jnp.int32, (count, 1), 0).astype(f32) + offset


def head_lanes(rows):
    return lax.broadcasted_iota(jnp.int32, (rows, WIDE), 1) // DH


def heads_apart(group):
    at = head_lanes(group.shape[0])
    zero = jnp.zeros_like(group)
    return jnp.concatenate([jnp.where(at == k, group, zero) for k in range(MANY)], axis=0)


def heads_joined(stacked):
    rows = stacked.shape[0] // MANY
    at = head_lanes(rows)
    joined = stacked[:rows]
    for k in range(1, MANY):
        joined = jnp.where(at == k, stacked[k * rows : (k + 1) * rows], joined)
    return joined


def beside(stacked):
    rows = stacked.shape[0] // MANY
    return jnp.concatenate([stacked[k * rows : (k + 1) * rows] for k in range(MANY)], axis=1)


def below(joined):
    width = joined.shape[1] // MANY
    return jnp.concatenate([joined[:, k * width : (k + 1) * width] for k in range(MANY)], axis=0)


def flip(rows):
    i = lax.broadcasted_iota(jnp.int32, (rows, rows), 0)
    j = lax.broadcasted_iota(jnp.int32, (rows, rows), 1)
    return (i + j == rows - 1).astype(f32).astype(bf16)


class Load:
    def __init__(self, source, buffer, sem):
        self.buffer, self.waited = buffer, False
        self.copy = pltpu.make_async_copy(source, buffer, sem)
        self.copy.start()

    def ready(self):
        if not self.waited:
            self.copy.wait()
            self.waited = True
        return self.buffer


class Loads:
    def __init__(self, items):
        self.items = items

    def __getitem__(self, at):
        return self.items[at].ready()


class Stage:
    def __init__(self, loads, stores, sems):
        self.sems, self.used, self.pending, self.targets = sems, 0, [], []
        self.named, self.all_loads = {}, []
        for name, pairs, single in loads:
            items = [Load(source, buffer, self.sem()) for source, buffer in pairs]
            self.all_loads += items
            self.named[name] = items[0] if single else Loads(items)
        for name, pairs, single in stores:
            self.targets += [[target, buffer, False] for target, buffer in pairs]
            buffers = [buffer for _, buffer in pairs]
            self.named[name] = buffers[0] if single else buffers

    def sem(self):
        self.used += 1
        return self.sems.at[self.used - 1]

    def __getattr__(self, name):
        found = self.named[name]
        return found.ready() if isinstance(found, Load) else found

    def send(self, buffer, at=None):
        entry = next(entry for entry in self.targets if entry[1] is buffer)
        target = entry[0]
        entry[2] = True
        if at is not None:
            target, buffer = target.at[at], buffer.at[at]
        copy = pltpu.make_async_copy(buffer, target, self.sem())
        copy.start()
        self.pending.append(copy)

    def finish(self):
        for _, buffer, sent in self.targets:
            if not sent:
                self.send(buffer)
        for load in self.all_loads:
            load.ready()
        for copy in self.pending:
            copy.wait()


def staged(
    name, body, ins, outs, smem=(), scratch=(), flops=0, moved=0, sends=0, filled=None,
    limit=VMEM_LIMIT, kept=None,
):
    operands, loads, stores, kept = [], [], [], kept or {}
    for key, items in ins.items():
        single = not isinstance(items, list)
        entries = []
        for item in [items] if single else items:
            array, view, shape = item if isinstance(item, tuple) else (item, None, item.shape)
            at = next((i for i, other in enumerate(operands) if other is array), None)
            if at is None:
                at = len(operands)
                operands.append(array)
            entries.append((at, view, shape, array.dtype))
        loads.append((key, entries, single))
    for key, items in outs.items():
        single = not isinstance(items, list)
        entries = [
            item if isinstance(item, tuple) else (item, None, item.shape)
            for item in ([items] if single else items)
        ]
        stores.append((key, entries, single))
    aliases = {}
    if filled is not None:
        aliases = {len(smem) + len(kept) + len(operands): 0}
        operands.append(filled)
    every_load = [entry for _, entries, _ in loads for entry in entries]
    every_store = [entry for _, entries, _ in stores for entry in entries]
    n_smem, n_ops, n_outs, n_loads = len(smem), len(operands), len(every_store), len(every_load)

    def run(*refs):
        cuts = [n_smem, len(kept), n_ops, n_outs, n_loads, n_outs, 1]
        taken, at = [], 0
        for cut in cuts:
            taken.append(refs[at : at + cut])
            at += cut
        scalars, here, given, targets, buffers, results, sems = taken
        buffers, places = iter(buffers), iter(zip(targets, results))
        placed_loads = [
            (
                key,
                [(given[i] if view is None else view(given[i]), next(buffers)) for i, view, _, _ in entries],
                single,
            )
            for key, entries, single in loads
        ]
        placed_stores = []
        for key, entries, single in stores:
            pairs = []
            for _, view, _ in entries:
                target, result = next(places)
                pairs.append((target if view is None else view(target), result))
            placed_stores.append((key, pairs, single))
        stage = Stage(placed_loads, placed_stores, sems[0])
        stage.named.update(zip(kept, here))
        body(stage, *scalars, *refs[at:])
        stage.finish()

    hbm = pl.BlockSpec(memory_space=pl.ANY)
    got = iter(
        pl.pallas_call(
            run,
            in_specs=[pl.BlockSpec(memory_space=pltpu.SMEM)] * n_smem
            + [pl.BlockSpec(memory_space=pltpu.VMEM)] * len(kept)
            + [hbm] * n_ops,
            out_specs=[hbm] * n_outs,
            out_shape=[shape for shape, _, _ in every_store],
            scratch_shapes=[pltpu.VMEM(shape, dtype) for _, _, shape, dtype in every_load]
            + [pltpu.VMEM(shape, whole.dtype) for whole, _, shape in every_store]
            + [pltpu.SemaphoreType.DMA((n_loads + n_outs + sends,))]
            + list(scratch),
            input_output_aliases=aliases,
            compiler_params=pltpu.CompilerParams(vmem_limit_bytes=limit),
            cost_estimate=pl.CostEstimate(flops=flops, bytes_accessed=moved, transcendentals=0),
            name=name,
        )(*smem, *kept.values(), *operands)
    )
    result = types.SimpleNamespace()
    for key, entries, single in stores:
        values = [next(got) for _ in entries]
        setattr(result, key, values[0] if single else values)
    return result


def sds(shape, dtype):
    return jax.ShapeDtypeStruct(shape, dtype)


def slab(array, *at):
    shape = tuple(a[1] for a in at if isinstance(a, tuple))
    index = tuple(pl.ds(*a) if isinstance(a, tuple) else a for a in at)
    return (array, lambda ref: ref.at[index], shape)


def by_row(array, rows):
    tokens, width = array.shape
    return [slab(array, (row * (tokens // rows), tokens // rows), (0, width)) for row in range(rows)]


def each_of(array):
    rows, size, width = array.shape
    return [slab(array, row, (0, size), (0, width)) for row in range(rows)]


PART = 1024


def activate(inner):
    half = 0.5 * inner
    turn = jnp.tanh(half)
    up = 1.0 + turn
    active = half * up
    return active, 0.5 * (up + active * (1.0 - turn))


def feed_slabs(feed_in, feed_out, module):
    _, model, hidden = feed_in.shape
    spans = [(part, PART) for part in range(0, hidden, PART)]
    w_in = [slab(feed_in, module, (0, model), span) for span in spans]
    w_out = [slab(feed_out, module, span, (0, model)) for span in spans]
    return w_in, w_out


def front(features, feed_in, feed_in_bias, feed_out, attend_in, gain, shift, bias):
    rows, frames, model = features.shape
    tokens = rows * frames
    hidden = feed_in.shape[2]
    parts = hidden // PART
    low = sds((tokens, model), bf16)

    def body(k):
        gain, shift = k.gain, k.shift
        x = k.x[...].reshape(tokens, model).astype(f32)
        normal, _ = normalize(x)
        k.n0[...] = (normal * gain[0:1] + shift[0:1]).astype(bf16)
        k.send(k.n0)
        for part in range(parts):
            cut = slice(part * PART, (part + 1) * PART)
            inner = dot(k.n0[...], k.w_in[part][...]) + k.b_in[0:1, cut]
            active, slope = activate(inner)
            k.act[:, cut] = active.astype(bf16)
            k.slope[:, cut] = slope.astype(bf16)
        k.send(k.slope)
        k.send(k.act)
        branch = k.bias[6:7]
        for part in range(parts):
            cut = slice(part * PART, (part + 1) * PART)
            branch = branch + dot(k.act[:, cut], k.w_out[part][...])
        after = x + 0.5 * branch
        k.after[...] = after
        k.send(k.after)
        normal, _ = normalize(after)
        normed = (normal * gain[1:2] + shift[1:2]).astype(bf16)
        k.na[...] = normed
        k.send(k.na)
        both = dot(normed, k.attend_in[...])
        keys = both[:, :model].astype(bf16)
        values = (both[:, model:] + k.bias[1:2]).astype(bf16)
        for row in range(rows):
            at = row * frames
            k.lo[row, :, :model] = keys[at : at + WIN]
            k.lo[row, :, model:] = values[at : at + WIN]
            k.hi[row, :, :model] = keys[at + WIN : at + frames]
            k.hi[row, :, model:] = values[at + WIN : at + frames]

    w_in, w_out = feed_slabs(feed_in, feed_out, 0)
    kv = sds((rows, WIN, 2 * model), bf16)
    return staged(
        "front",
        body,
        dict(
            x=features, gain=gain, shift=shift, b_in=feed_in_bias, w_in=w_in, bias=bias,
            w_out=w_out, attend_in=slab(attend_in, (0, model), (model, 2 * model)),
        ),
        dict(
            after=sds((tokens, model), f32), n0=low, na=low, lo=kv, hi=kv,
            act=sds((tokens, hidden), bf16), slope=sds((tokens, hidden), bf16),
        ),
        flops=2 * tokens * model * (2 * hidden + 2 * model),
        moved=16 << 20,
    )


def queries(na, attend_in, bias, sinusoid, proj):
    tokens, model = na.shape

    def body(k):
        query = dot(k.na[...], k.attend_in[...]) + k.bias[0:1]
        factor = 1.0 / math.sqrt(DH)
        k.qu[...] = ((query + k.bias[8:9]) * factor).astype(bf16)
        k.qv[...] = ((query + k.bias[9:10]) * factor).astype(bf16)
        k.table[...] = dot(k.sinusoid[...], k.proj[...]).astype(bf16)

    low = sds((tokens, model), bf16)
    return staged(
        "queries",
        body,
        dict(
            na=na, attend_in=slab(attend_in, (0, model), (0, model)), bias=bias,
            sinusoid=sinusoid, proj=proj,
        ),
        dict(qu=low, qv=low, table=sds((SPAN, model), bf16)),
        flops=2 * tokens * model * 2 * model,
        moved=4 << 20,
    )


def attend(
    row_len, info, ends, start, query, before, after, attend_out, convolve_in, gain, shift, bias
):
    rows = before.shape[0]
    tokens, model = start.after.shape
    frames = tokens // rows
    low = sds((tokens, model), bf16)

    def body(k, info):
        first_frame = info[0].astype(f32)
        turn = flip(WIN)
        key_at = lax.broadcasted_iota(jnp.int32, (WIN, SPAN), 1).astype(f32)
        table = k.table
        for row in range(rows):
            reach = info[1 + row].astype(f32)
            row_ends = k.ends[row : row + 1, :]
            for block in range(2):
                at = column(WIN, first_frame + WIN * block)
                lower, upper = bounds(row_ends, at, row_len)
                base = first_frame + (WIN * (block - 1))
                lower = jnp.maximum(lower, at - reach) - base
                upper = jnp.minimum(upper - 1.0, at + reach) - base
                allowed = ((key_at >= lower) & (key_at <= upper))[None]
                here = slice(row * frames + WIN * block, row * frames + WIN * (block + 1))
                some = [k.lo[row], k.hi[row]]
                some = some + [k.next[row]] if block else [k.before[row]] + some
                for group in range(GROUPS):
                    cut = slice(WIDE * group, WIDE * (group + 1))
                    cut_v = slice(model + WIDE * group, model + WIDE * (group + 1))
                    keys = jnp.concatenate([b[:, cut] for b in some], axis=0)
                    values = jnp.concatenate([b[:, cut_v] for b in some], axis=0)
                    spread = dot_last(heads_apart(k.qv[here, cut]), table[:, cut])
                    content = dot_last(heads_apart(k.qu[here, cut]), keys)
                    spread = pltpu.roll(
                        spread.reshape(MANY, WIN, SPAN), 0, 2, stride=1, stride_axis=1
                    )
                    scores = content.reshape(MANY, WIN, SPAN) + spread
                    scores = jnp.where(allowed, scores, negative)
                    powers = jnp.exp(scores - jnp.max(scores, axis=2, keepdims=True))
                    weights = powers * (1.0 / jnp.sum(powers, axis=2, keepdims=True))
                    weights = weights.astype(bf16).reshape(MANY * WIN, SPAN)
                    k.mixed[here, cut] = heads_joined(dot(weights, values)).astype(bf16)
                    k.prob[row][block, group] = dot(turn, beside(weights)).astype(bf16)
            k.send(k.prob[row])
        k.send(k.mixed)
        after_attend = k.after[...] + dot(k.mixed[...], k.attend_out[...]) + k.bias[2:3]
        k.out[...] = after_attend
        k.send(k.out)
        normal, _ = normalize(after_attend)
        normed = (normal * k.gain[2:3] + k.shift[2:3]).astype(bf16)
        k.nc[...] = normed
        k.send(k.nc)
        paired = dot(normed, k.convolve_in[...])
        value = paired[:, :model] + k.bias[3:4]
        gate = paired[:, model:] + k.bias[4:5]
        k.paired[:, :model] = value
        k.paired[:, model:] = gate
        k.send(k.paired)
        gated = (value * sigmoid(gate)).astype(bf16)
        k.gated[...] = gated
        for row in range(rows):
            k.first[row] = gated[row * frames : row * frames + RIM]
            k.last[row] = gated[(row + 1) * frames - RIM : (row + 1) * frames]

    rim = sds((rows, RIM, model), bf16)
    return staged(
        "attend",
        body,
        dict(
            ends=ends, table=query.table, qv=query.qv, qu=query.qu, lo=each_of(start.lo),
            hi=each_of(start.hi), before=each_of(before), next=each_of(after), after=start.after,
            attend_out=attend_out, bias=bias, gain=gain, shift=shift, convolve_in=convolve_in,
        ),
        dict(
            prob=[sds((2, GROUPS, WIN, MANY * SPAN), bf16)] * rows, mixed=low,
            out=sds((tokens, model), f32), nc=low, paired=sds((tokens, 2 * model), f32),
            gated=low, first=rim, last=rim,
        ),
        smem=[info],
        flops=16 * 8 * 256 * 384 * 128,
        moved=16 << 20,
    )


def valid_column(info, row, rows, frames):
    at = column(frames, info[0].astype(f32))
    return (at < info[1 + rows + row].astype(f32)).astype(f32)


def put_rows(ref, part, vector):
    model = ref.shape[1]
    per = vector.shape[1] // model
    for one in range(per):
        at = part * per + one
        ref[at : at + 1] = vector[:, one * model : (one + 1) * model]


def pack(ref, vectors):
    at = 0
    for vector in vectors:
        for k in range(0, vector.shape[1], 128):
            ref[at : at + 1, :] = vector[:, k : k + 128]
            at += 1


def by_rows(count, size, step, init=None):
    def one(i, carry):
        return step(pl.ds(pl.multiple_of(i * size, size), size), carry)

    return lax.fori_loop(0, count // size, one, init)


def by_lanes(width, step):
    def one(i, carry):
        step(pl.ds(pl.multiple_of(i * 128, 128), 128))
        return carry

    lax.fori_loop(0, width // 128, one, 0)


def spread(column):
    return jnp.broadcast_to(column, (column.shape[0], 128))


def tap_masks(keep_s, at, low, high):
    for tap in range(KERNEL):
        off = tap - HALF
        keep_s[tap] = spread(((at + off >= low) & (at + off < high)).astype(f32))


def depth_conv(row_len, devices, info, ends, gated, before, after, taps):
    rows = before.shape[0]
    tokens, model = gated.shape
    frames = tokens // rows

    def body(k, info, rim, keep_s, valid_s, sums, tile):
        start = info[0].astype(f32)
        counts = 0.0
        taps = k.taps
        for row in range(rows):
            here = slice(row * frames, (row + 1) * frames)
            at = column(frames, start)
            low, high = bounds(k.ends[row : row + 1, :], at, row_len)
            tap_masks(keep_s, at, low, high)
            valid = valid_column(info, row, rows, frames)
            valid_s[here] = spread(valid)
            counts += total(valid)
            rim[0:RIM] = k.before[row].astype(f32)
            rim[RIM : RIM + frames] = k.gated[row][...].astype(f32)
            rim[RIM + frames :] = k.after[row].astype(f32)

            def one(lanes):
                depth = jnp.zeros((frames, 128), f32)
                for tap in range(KERNEL):
                    off = tap - HALF
                    part = rim[RIM + off : RIM + off + frames, lanes] * keep_s[tap]
                    depth += taps[tap : tap + 1, lanes] * part
                k.depth[here, lanes] = depth
                sums[row : row + 1, lanes] = total(depth * valid_s[here])

            by_lanes(model, one)
            k.send(k.depth, pl.ds(row * frames, frames))
        first = total(sums[0:rows, :])
        mean = first / jnp.maximum(counts, 1.0)
        sums[rows : rows + 1, :] = mean

        def two(lanes):
            centered = k.depth[:, lanes] - sums[rows : rows + 1, lanes]
            sums[rows + 1 : rows + 2, lanes] = total(centered * centered * valid_s[...])

        by_lanes(model, two)
        pack(tile, [first, sums[rows + 1 : rows + 2, :]])
        k.stats[...] = jnp.broadcast_to(tile[...][None], k.stats.shape)

    return staged(
        "depth_conv",
        body,
        dict(ends=ends, taps=taps, gated=by_row(gated, rows)),
        dict(depth=sds((rows * frames, model), f32), stats=sds((devices, 8, 128), f32)),
        smem=[info],
        scratch=[
            pltpu.VMEM((frames + 2 * RIM, model), f32),
            pltpu.VMEM((KERNEL, frames, 128), f32),
            pltpu.VMEM((rows * frames, 128), f32),
            pltpu.VMEM((8, model), f32),
            pltpu.VMEM((8, 128), f32),
        ],
        kept=dict(before=before, after=after),
        flops=rows * frames * model * 30,
        moved=2 << 20,
        sends=rows - 1,
    )


def middle(
    devices, rows, info, stats, counts, depth, stream, feed_in, feed_in_bias, feed_out,
    convolve_out, gain, shift, bias, cotangent,
):
    tokens, model = depth.shape
    frames = tokens // rows
    hidden = feed_in.shape[2]
    parts = hidden // PART

    def body(k, info, conv_s, slope_s, tile):
        stats, each = k.stats, k.counts[:, 0:1]
        gain, shift, bias = k.gain, k.shift, k.bias
        count = total(each)
        means, inverses = [], []
        for at in range(model // 128):
            sums = stats[:, at, :]
            mean = total(sums) / count
            off = sums / jnp.maximum(each, 1.0) - mean
            spread = total(stats[:, model // 128 + at, :]) + total(each * off * off)
            means.append(mean)
            inverses.append(lax.rsqrt(spread / count + eps_norm))
        mean = jnp.concatenate(means, axis=1)
        inverse = jnp.concatenate(inverses, axis=1)
        k.inv[0:1] = inverse
        k.inv[1:2] = jnp.broadcast_to(1.0 / count, (1, model))
        normal = (k.depth[...] - mean) * inverse
        k.bn[...] = normal
        k.send(k.bn)
        batch = normal * gain[5:6] + shift[5:6]
        swished = (batch * sigmoid(batch)).astype(bf16)
        k.sw[...] = swished
        k.send(k.sw)
        after_conv = k.stream[...] + dot(swished, k.convolve_out[...]) + bias[5:6]
        conv_s[...] = after_conv
        normal, _ = normalize(after_conv)
        k.nf[...] = (normal * gain[3:4] + shift[3:4]).astype(bf16)
        k.send(k.nf)
        for part in range(parts):
            cut = slice(part * PART, (part + 1) * PART)
            inner = dot(k.nf[...], k.w_in[part][...]) + k.b_in[1:2, cut]
            active, slope = activate(inner)
            k.act[:, cut] = active.astype(bf16)
            slope_s[:, cut] = slope
        k.send(k.act)
        branch = bias[7:8]
        for part in range(parts):
            cut = slice(part * PART, (part + 1) * PART)
            branch = branch + dot(k.act[:, cut], k.w_out[part][...])
        normal, inverse = normalize(conv_s[...] + 0.5 * branch)
        valid = jnp.concatenate(
            [valid_column(info, row, rows, frames) for row in range(rows)], axis=0
        )
        k.out[...] = (valid * (normal * gain[4:5] + shift[4:5])).astype(bf16)
        k.send(k.out)
        grad = valid * k.cotangent[...].astype(f32)
        grad, gain_grad, shift_grad = norm_back(grad, normal, inverse, gain[4:5])
        k.gcs[...] = grad
        low = (0.5 * grad).astype(bf16)
        k.gl[...] = low
        k.send(k.gl)
        vec = k.vec
        vec[2:3] = gain_grad
        vec[3:4] = shift_grad
        vec[5:6] = total(low.astype(f32))
        back = 0.0
        for part in range(parts):
            cut = slice(part * PART, (part + 1) * PART)
            grad = (dot_last(k.gl[...], k.w_out[part][...]) * slope_s[:, cut]).astype(bf16)
            k.gi[:, cut] = grad
            put_rows(k.fb, part, total(grad.astype(f32)))
            back = back + dot_last(grad, k.w_in[part][...])
        k.send(k.gi)
        normal, inverse = normalize(conv_s[...])
        grad, gain_grad, shift_grad = norm_back(back, normal, inverse, gain[3:4])
        vec[0:1] = gain_grad
        vec[1:2] = shift_grad
        grad = k.gcs[...] + grad
        k.gcs[...] = grad
        k.send(k.gcs)
        low = grad.astype(bf16)
        k.gcl[...] = low
        k.send(k.gcl)
        vec[4:5] = total(low.astype(f32))
        bn = k.bn[...]
        batch = bn * gain[5:6] + shift[5:6]
        _, slope = activate(batch)
        grad = dot_last(low, k.convolve_out[...]) * slope
        k.gb[...] = grad
        k.send(k.gb)
        pack(tile, [total(grad), total(grad * bn)])
        k.totals[...] = jnp.broadcast_to(tile[...][None], k.totals.shape)
        k.send(k.totals)
        for row in range(rows):
            at, end = row * frames, (row + 1) * frames
            k.first[row, :, :model] = k.gb[at : at + RIM_GRAD]
            k.first[row, :, model:] = k.bn[at : at + RIM_GRAD]
            k.last[row, :, :model] = k.gb[end - RIM_GRAD : end]
            k.last[row, :, model:] = k.bn[end - RIM_GRAD : end]

    w_in, w_out = feed_slabs(feed_in, feed_out, 1)
    ins = dict(
        gain=gain, shift=shift, depth=depth, bias=bias,
        convolve_out=convolve_out, stream=stream, b_in=feed_in_bias, w_in=w_in, w_out=w_out,
        cotangent=cotangent,
    )
    low = sds((tokens, model), bf16)
    wide = sds((tokens, model), f32)
    rim = sds((rows, RIM_GRAD, 2 * model), f32)
    return staged(
        "middle",
        body,
        ins,
        dict(
            out=low, act=sds((tokens, hidden), bf16), gi=sds((tokens, hidden), bf16), nf=low,
            gl=low, sw=low, gcl=low, gcs=wide, gb=wide, bn=wide, inv=sds((8, model), f32),
            totals=sds((devices, 8, 128), f32), first=rim, last=rim, vec=sds((8, model), f32),
            fb=sds((hidden // model, model), f32),
        ),
        smem=[info],
        scratch=[
            pltpu.VMEM((tokens, model), f32),
            pltpu.VMEM((tokens, hidden), f32),
            pltpu.VMEM((8, 128), f32),
        ],
        kept=dict(stats=stats, counts=counts),
        flops=2 * tokens * model * (4 * hidden + 2 * model),
        moved=24 << 20,
    )


def conv_back(
    row_len, n, info, ends, taps, convolve_in, attend_out, gain, totals, mid, edge_before,
    edge_after, rim_before, rim_after, mix, early,
):
    tokens, model = mid.gb.shape
    rows = rim_before.shape[0]
    frames = tokens // rows
    slim = model // n
    room = slim % 8 == 0

    def body(k, info, grads, rim, keep_s, gp, gal):
        start = info[0].astype(f32)
        parts = model // 128
        sums = [total(k.totals[:, at, :]) for at in range(2 * parts)]
        total_a = jnp.concatenate(sums[:parts], axis=1)
        total_b = jnp.concatenate(sums[parts:], axis=1)
        inverse, per_count = k.inv[0:1], k.inv[1:2]
        gain, taps, vec = k.gain, k.taps, k.vec
        own_scale = inverse * gain[5:6]
        share_a = own_scale * total_a * per_count
        share_b = own_scale * total_b * per_count
        vec[14:15] = total_a
        vec[15:16] = total_b
        vec[0:9] = jnp.zeros((9, model), f32)
        vec[9:14] = jnp.zeros((5, model), f32)

        def grad_of(grad, normal, valid):
            grad = grad * own_scale - valid * (share_a + normal * share_b)
            return grad.astype(bf16).astype(f32)

        for row in range(rows):
            first = row * frames
            last = info[1 + rows + row].astype(f32)
            at = column(frames, start)
            low, high = bounds(k.ends[row : row + 1, :], at, row_len)
            tap_masks(keep_s, at, low, high)
            before, after = k.edge_before, k.edge_after
            edge_at = column(RIM_GRAD, start - RIM_GRAD)
            grads[0:RIM_GRAD] = grad_of(
                before[row, :, :model], before[row, :, model:], (edge_at < last).astype(f32)
            )
            for step in range(0, frames, 32):
                here = slice(step, step + 32)
                at = column(32, start + step)
                grads[RIM_GRAD + step : RIM_GRAD + step + 32] = grad_of(
                    k.gb[row][here], k.bn[row][here], (at < last).astype(f32)
                )
            edge_at = column(RIM_GRAD, start + frames)
            grads[RIM_GRAD + frames :] = grad_of(
                after[row, :, :model], after[row, :, model:], (edge_at < last).astype(f32)
            )
            rim[0:RIM] = k.rim_before[row].astype(f32)
            rim[RIM : RIM + frames] = k.gated[row][...].astype(f32)
            rim[RIM + frames :] = k.rim_after[row].astype(f32)
            paired = k.paired[row]
            half = frames // 2

            def one(i, carry):
                lane = pl.multiple_of(i * 128, 128)
                lanes, gates = pl.ds(lane, 128), pl.ds(model + lane, 128)
                for base in range(0, frames, half):
                    own = grads[RIM_GRAD + base : RIM_GRAD + base + half, lanes]
                    grad = jnp.zeros((half, 128), f32)
                    for tap in range(KERNEL):
                        off = base + tap - HALF
                        keep = keep_s[tap, base : base + half]
                        part = own * (rim[RIM + off : RIM + off + half, lanes] * keep)
                        vec[tap : tap + 1, lanes] += total(part)
                        mirror = KERNEL - 1 - tap
                        part = grads[RIM_GRAD + off : RIM_GRAD + off + half, lanes] * keep
                        grad += taps[mirror : mirror + 1, lanes] * part
                    sigma = sigmoid(paired[base : base + half, gates])
                    one = (grad * sigma).astype(bf16)
                    value = paired[base : base + half, lanes]
                    two = (grad * sigma * value * (1.0 - sigma)).astype(bf16)
                    here = slice(first + base, first + base + half)
                    gp[here, lanes] = one
                    gp[here, gates] = two
                    vec[11:12, lanes] += total(one.astype(f32))
                    vec[12:13, lanes] += total(two.astype(f32))
                return carry

            lax.fori_loop(0, model // 128, one, 0)
        grad = dot_last(gp[...], k.convolve_in[...])
        normal, inverse = normalize(k.after[...])
        grad, gain_grad, shift_grad = norm_back(grad, normal, inverse, gain[2:3])
        vec[9:10] = gain_grad
        vec[10:11] = shift_grad
        grad = k.gcs[...] + grad
        k.gas[...] = grad
        k.send(k.gas)
        low = grad.astype(bf16)
        gal[...] = low
        vec[13:14] = total(low.astype(f32))
        k.gm[...] = dot_last(gal[...], k.attend_out[...]).astype(bf16)
        k.send(k.gm)
        out = k.early
        out[:, :slim] = dot_first(k.nc[...], gp[...]).astype(bf16).reshape(n, slim, 2 * model)
        block = dot_first(k.sw[...], k.gcl[...]).astype(bf16)
        out[:, slim:, :model] = block.reshape(n, slim, model)
        block = dot_first(k.mixed[...], gal[...]).astype(bf16)
        out[:, slim:, model:] = block.reshape(n, slim, model)

    own = (n, 2 * slim, 2 * model)
    size = early.shape[1] - 2 * slim
    if room:
        out = (sds(early.shape, bf16), lambda ref: ref.at[:, pl.ds(size, 2 * slim)], own)
    else:
        out = sds(own, bf16)
    got = staged(
        "conv_back",
        body,
        dict(
            inv=mid.inv, gain=gain, ends=ends, taps=taps, rim_before=rim_before,
            rim_after=rim_after, gb=by_row(mid.gb, rows), bn=by_row(mid.bn, rows), gated=by_row(mix.gated, rows),
            paired=by_row(mix.paired, rows), convolve_in=convolve_in, after=mix.out, gcs=mid.gcs,
            attend_out=attend_out, nc=mix.nc, sw=mid.sw, gcl=mid.gcl, mixed=mix.mixed,
        ),
        dict(
            early=out, gas=sds((tokens, model), f32), gm=sds((tokens, model), bf16),
            vec=sds((16, model), f32),
        ),
        smem=[info],
        scratch=[
            pltpu.VMEM((frames + 2 * RIM_GRAD, model), f32),
            pltpu.VMEM((frames + 2 * RIM, model), f32),
            pltpu.VMEM((KERNEL, frames, 128), f32),
            pltpu.VMEM((tokens, 2 * model), bf16),
            pltpu.VMEM((tokens, model), bf16),
        ],
        kept=dict(totals=totals, edge_before=edge_before, edge_after=edge_after),
        flops=2 * tokens * model * 7 * model,
        moved=16 << 20,
        filled=early if room else None,
    )
    if not room:
        got.early = jnp.concatenate([early, got.early], axis=1)
    return got


def attend_back(start, query, before, after, probs, gm):
    rows = before.shape[0]
    tokens, model = query.qu.shape
    frames = tokens // rows
    factor = 1.0 / math.sqrt(DH)

    def body(k, acc, turned):
        g_table, vec, table = k.g_table, k.vec, k.table
        g_table[...] = jnp.zeros_like(g_table)
        vec[...] = jnp.zeros_like(vec)
        turn = flip(WIN)
        for row in range(rows):
            acc[...] = jnp.zeros_like(acc)
            for block in range(2):
                here = slice(WIN * block, WIN * (block + 1))
                span = slice(WIN * block, WIN * block + SPAN)
                turned[0] = dot(turn, k.gm[row][here]).astype(bf16)
                turned[1] = dot(turn, k.qu[row][here]).astype(bf16)
                turned[2] = dot(turn, k.qv[row][here]).astype(bf16)
                blocks = [k.lo[row], k.hi[row]]
                blocks = blocks + [k.next[row]] if block else [k.before[row]] + blocks
                prob = k.prob[2 * row + block]
                for group in range(GROUPS):
                    cut = slice(WIDE * group, WIDE * (group + 1))
                    cut_v = slice(model + WIDE * group, model + WIDE * (group + 1))
                    keys = jnp.concatenate([b[:, cut] for b in blocks], axis=0)
                    values = jnp.concatenate([b[:, cut_v] for b in blocks], axis=0)
                    weights = below(prob[group])
                    grad_mixed = heads_apart(turned[0, :, cut])
                    grad = dot_last(grad_mixed, values)
                    wide = weights.astype(f32)
                    delta = jnp.sum(wide * grad, axis=1, keepdims=True)
                    raw = (wide * (grad - delta)).astype(bf16)
                    acc[span, cut_v] += dot_first(weights, grad_mixed)
                    acc[span, cut] += dot_first(raw, heads_apart(turned[1, :, cut]))
                    grad_u = heads_joined(dot(raw, keys)) * factor
                    band = pltpu.roll(
                        raw.astype(f32).reshape(MANY, WIN, SPAN),
                        SPAN - (WIN - 1),
                        2,
                        stride=1,
                        stride_axis=1,
                    )
                    band = band.astype(bf16).reshape(MANY * WIN, SPAN)
                    grad_v = heads_joined(dot(band, table[:, cut])) * factor
                    g_table[:, cut] += dot_first(band, heads_apart(turned[2, :, cut]))
                    vec[0:1, cut] += total(grad_u)
                    vec[1:2, cut] += total(grad_v)
                    both = (grad_u + grad_v).astype(bf16)
                    k.gq[row][here, cut] = dot(turn, both).astype(bf16)
                if block == 0:
                    k.g_before[row] = acc[0:WIN].astype(bf16)
                    k.send(k.g_before, row)
            k.g_after[row] = acc[3 * WIN :].astype(bf16)
            k.send(k.g_after, row)
            k.g_lo[row][...] = acc[WIN : 2 * WIN]
            k.send(k.g_lo[row])
            k.g_hi[row][...] = acc[2 * WIN : 3 * WIN]
            k.send(k.g_hi[row])
            k.send(k.gq[row])

    ins = dict(
        gm=by_row(gm, rows), qu=by_row(query.qu, rows), qv=by_row(query.qv, rows),
        before=each_of(before), lo=each_of(start.lo), hi=each_of(start.hi),
        prob=[
            slab(prob, block, (0, GROUPS), (0, WIN), (0, MANY * SPAN))
            for prob in probs
            for block in range(2)
        ],
        table=query.table, next=each_of(after),
    )
    kv = (WIN, 2 * model)
    return staged(
        "attend_back",
        body,
        ins,
        dict(
            gq=[sds((frames, model), bf16)] * rows, g_before=sds((rows,) + kv, bf16),
            g_lo=[sds(kv, f32)] * rows, g_hi=[sds(kv, f32)] * rows,
            g_after=sds((rows,) + kv, bf16), g_table=sds((SPAN, model), f32),
            vec=sds((8, model), f32),
        ),
        scratch=[
            pltpu.VMEM((4 * WIN, 2 * model), f32),
            pltpu.VMEM((3, WIN, model), bf16),
        ],
        flops=16 * 14 * 256 * 384 * 128,
        moved=16 << 20,
        sends=2 * rows - 2,
    )


def back(info, core_at, n, grads, halo, attend_in, start, gas, gain, sinusoid):
    rows = len(grads.gq)
    tokens, model = start.after.shape
    frames = tokens // rows
    hidden = start.act.shape[1]
    parts = hidden // PART
    width, slim = hidden // n, model // n

    def body(k, info, joined):
        core = info[core_at]
        vec, gain = k.vec, k.gain
        sums = [0.0] * 5
        for row in range(rows):
            here = slice(row * frames, (row + 1) * frames)
            low_half = slice(row * frames, row * frames + WIN)
            high_half = slice(row * frames + WIN, (row + 1) * frames)
            joined[here, :model] = k.gq[row][...]
            pair = (k.g_lo[row][...] + k.left[row].astype(f32)).astype(bf16)
            joined[low_half, model:] = pair
            pair = (k.g_hi[row][...] + k.right[row].astype(f32)).astype(bf16)
            joined[high_half, model:] = pair
            both = joined[here]
            k.gv[here] = both[:, 2 * model :]
            sums[0] += total(both[:, :model].astype(f32))
            sums[1] += total(both[:, 2 * model :].astype(f32))
            grad = dot_last(both, k.attend_in[...])
            normal, inverse = normalize(k.after[row][...])
            grad, gain_grad, shift_grad = norm_back(grad, normal, inverse, gain[1:2])
            sums[2] += gain_grad
            sums[3] += shift_grad
            grad = k.gas[row][...] + grad
            k.gfs[row][...] = grad
            k.send(k.gfs[row])
            low = (0.5 * grad).astype(bf16)
            k.gl[here] = low
            sums[4] += total(low.astype(f32))
        k.send(k.gv)
        k.send(k.gl)
        for at in range(5):
            vec[at : at + 1] = sums[at]
        pairs = (0, n // 2)
        block = dot_first(k.na[...], joined[:, : 2 * model])
        for part in range(2):
            cut = slice(part * model, (part + 1) * model)
            keep_half(block[:, cut], core, k.mine, k.other, pairs, width + part * slim)
        high = k.g_table[...].astype(bf16)
        low = (k.g_table[...] - high.astype(f32)).astype(bf16)
        place = dot_first(k.sinusoid[...], high) + dot_first(k.sinusoid[...], low)
        keep_half(place, core, k.mine, k.other, pairs, width + 2 * slim)
        step = n // 2 // parts
        for part in range(parts):
            block = dot_first(k.act[part][...], k.gl[...])
            some = (part * step, (part + 1) * step)
            keep_half(block, core, k.mine, k.other, some)
            k.send(k.other, pl.ds(part * step, step))
            k.send(k.mine, pl.ds(part * step, step))

    half = sds((n // 2, width + 3 * slim, model), bf16)
    low = sds((tokens, model), bf16)
    return staged(
        "back",
        body,
        dict(
            gain=gain, gq=grads.gq, g_lo=grads.g_lo, g_hi=grads.g_hi, attend_in=attend_in, after=by_row(start.after, rows),
            gas=by_row(gas, rows), na=start.na, g_table=grads.g_table, sinusoid=sinusoid,
            act=[slab(start.act, (0, tokens), (at, PART)) for at in range(0, hidden, PART)],
        ),
        dict(
            other=half, mine=half, gv=low, gl=low, gfs=[sds((frames, model), f32)] * rows,
            vec=sds((8, model), f32),
        ),
        smem=[info],
        scratch=[pltpu.VMEM((tokens, 3 * model), bf16)],
        kept=dict(left=halo[0], right=halo[1]),
        flops=2 * tokens * model * (hidden + 6 * model),
        moved=18 << 20,
        sends=2 * parts - 2,
    )


def keep_half(block, core, mine_ref, other_ref, rows, at=0):
    model = mine_ref.shape[2]
    pairs = rows[1] - rows[0]
    size = block.shape[0] // (2 * pairs)
    shaped = block.reshape(pairs, 2, size, model)
    even, odd = shaped[:, 0], shaped[:, 1]
    here = slice(*rows)
    mine_ref[here, at : at + size] = jnp.where(core == 0, even, odd).astype(bf16)
    other_ref[here, at : at + size] = jnp.where(core == 0, odd, even).astype(bf16)


def first_back(info, core_at, n, gl, feed_in, feed_out, start, gv):
    tokens, hidden = start.slope.shape
    model = gl.shape[1]
    parts = hidden // PART

    def body(k, info):
        core = info[core_at]
        step = n // 2 // parts
        back = 0.0
        block = dot_first(k.na[...], k.gv[...])
        keep_half(block, core, k.mine, k.other, (0, n // 2), hidden // n)
        for part in range(parts):
            cut = slice(part * PART, (part + 1) * PART)
            grad = dot_last(k.gl[...], k.w_out[part][...])
            grad = (grad * k.slope[part][...].astype(f32)).astype(bf16)
            put_rows(k.fb, part, total(grad.astype(f32)))
            block = dot_first(grad, k.n0[...])
            some = (part * step, (part + 1) * step)
            keep_half(block, core, k.mine, k.other, some)
            k.send(k.other, pl.ds(part * step, step))
            k.send(k.mine, pl.ds(part * step, step))
            back = back + dot_last(grad, k.w_in[part][...])
        k.gn[...] = back

    half = sds((n // 2, hidden // n + model // n, model), bf16)
    w_in, w_out = feed_slabs(feed_in, feed_out, 0)
    return staged(
        "first_back",
        body,
        dict(
            na=start.na, gv=gv, gl=gl, w_out=w_out,
            slope=[slab(start.slope, (0, tokens), (at, PART)) for at in range(0, hidden, PART)],
            n0=start.n0, w_in=w_in,
        ),
        dict(other=half, mine=half, fb=sds((hidden // model, model), f32), gn=sds((tokens, model), f32)),
        smem=[info],
        flops=2 * tokens * model * hidden * 3,
        moved=12 << 20,
        sends=2 * parts - 2,
    )


def last(features, gn, gfs, gain):
    rows, frames, model = features.shape

    def body(k):
        gain_grads, shift_grads = 0.0, 0.0
        for row in range(rows):
            here = slice(row * frames, (row + 1) * frames)
            normal, inverse = normalize(k.x[row][...].astype(f32))
            grad = k.gn[row][...]
            grad, gain_grad, shift_grad = norm_back(grad, normal, inverse, k.gain[0:1])
            k.out[row] = k.gfs[row][...] + grad
            k.send(k.out, row)
            gain_grads += gain_grad
            shift_grads += shift_grad
        k.vec[0:1] = gain_grads
        k.vec[1:2] = shift_grads

    ins = dict(
        gain=gain, x=[slab(features, row, (0, frames), (0, model)) for row in range(rows)],
        gn=[slab(gn, (row * frames, frames), (0, model)) for row in range(rows)], gfs=list(gfs),
    )
    return staged(
        "last",
        body,
        ins,
        dict(out=sds(features.shape, f32), vec=sds((8, model), f32)),
        flops=rows * frames * model * 20,
        moved=4 << 20,
        sends=rows - 1,
        limit=FOLD_LIMIT,
    )


def feed_weights(n, gi, nf, act, gl):
    tokens, model = nf.shape
    hidden = gi.shape[1]
    parts = hidden // PART
    size, slim = hidden // n, model // n
    step = n // parts
    room = 2 * slim if slim % 8 == 0 else 0

    def body(k):
        for part in range(parts):
            here = slice(part * step, (part + 1) * step)
            block = dot_first(k.gi[part][...], k.nf[...]).astype(bf16)
            k.out[here, :, :model] = block.reshape(step, size, model)
            block = dot_first(k.act[part][...], k.gl[...]).astype(bf16)
            k.out[here, :, model:] = block.reshape(step, size, model)
            k.send(k.out, pl.ds(part * step, step))

    ins = dict(
        nf=nf, gi=[slab(gi, (0, tokens), (at, PART)) for at in range(0, hidden, PART)], gl=gl,
        act=[slab(act, (0, tokens), (at, PART)) for at in range(0, hidden, PART)],
    )
    own = (n, size, 2 * model)
    shape = sds((n, size + room, 2 * model), bf16)
    return staged(
        "feed_weights",
        body,
        ins,
        dict(out=(shape, lambda ref: ref.at[:, pl.ds(0, size)] if room else ref, own)),
        flops=4 * tokens * model * hidden,
        moved=10 << 20,
        sends=parts - 1,
    ).out


def neighbours(last_block, first_block):
    devices = lax.axis_size("frames")
    up = [(i, i + 1) for i in range(devices - 1)]
    down = [(i + 1, i) for i in range(devices - 1)]
    return lax.ppermute(last_block, "frames", up), lax.ppermute(first_block, "frames", down)


def gather(copies):
    return lax.all_to_all(copies, DEVICES, 0, 0, tiled=True)


def scatter_sum(grads):
    return lax.psum_scatter(grads, "frames", scatter_dimension=0, tiled=True)


ROW_PAIR = [(0, 1), (1, 0)]
COLUMNS, IN_FLOAT = 1, 2
N_VECTORS = KERNEL + 5 + 5 + 10


def swap(x, k):
    n = lax.axis_size("frames")
    return lax.ppermute(x, "frames", [(i, i ^ k) for i in range(n)])


def swaps(sends, group):
    k, size = group
    return [swap(send, k * one) for one, send in zip(range(1, size), sends)]


def fold(name, info, row_at, states, small=None):
    mines, gots, keeps, sends, plans = [], [], [], [], []
    for mine, got, how in states:
        size, height, model = mine.shape
        if isinstance(how, tuple):
            _, place, digits = how
            view = (size // (digits * place), digits, place, height, model)
            half = (view[0], place, height, model)
        else:
            view = mine.shape
            half = (size, height, model // 2) if how == COLUMNS else mine.shape
        n_sends = how[2] - 1 if isinstance(how, tuple) else int(how == COLUMNS)
        plans.append((len(gots), len(got), len(sends), n_sends, how))
        mines.append(mine.reshape(view))
        gots += [one.reshape(view) for one in got]
        keeps.append(sds(half, f32 if how == IN_FLOAT else bf16))
        sends += [sds(half, bf16)] * n_sends

    n_small = 0 if small is None else len(small)

    def body(info, *refs):
        cuts = [len(mines), len(gots), n_small, len(keeps), len(sends)]
        taken, at = [], 0
        for cut in cuts:
            taken.append(refs[at : at + cut])
            at += cut
        mine_refs, got_refs, small_refs, keep_refs, send_refs = taken
        for at, (got_at, n_got, send_at, _, how) in enumerate(plans):
            parts = [mine_refs[at], *got_refs[got_at : got_at + n_got]]

            def added(*index):
                return sum(part[index].astype(f32) for part in parts)

            keep = keep_refs[at]
            if how is None or how == IN_FLOAT:
                keep[...] = added(...).astype(keep.dtype)
            elif how == COLUMNS:
                half = keep.shape[2]
                both = [
                    added(slice(None), slice(None), slice(one * half, (one + 1) * half))
                    for one in range(2)
                ]
                first = info[row_at] == 0
                send_refs[send_at][...] = jnp.where(first, both[1], both[0]).astype(bf16)
                keep[...] = jnp.where(first, both[0], both[1]).astype(bf16)
            else:
                digit = info[how[0]]
                for one in range(1, how[2]):
                    other = digit
                    for bit in (1, 2):
                        if one & bit:
                            other = other + bit * (1 - 2 * ((digit // bit) % 2))
                    send_refs[send_at + one - 1][...] = added(slice(None), other).astype(bf16)
                keep[...] = added(slice(None), digit).astype(bf16)
        if n_small:
            refs[-1][...] = sum(one[...] for one in small_refs)

    shapes = keeps + sends + ([sds(small[0].shape, f32)] if n_small else [])
    here = pl.BlockSpec(memory_space=pltpu.VMEM)
    given = mines + gots + (list(small) if n_small else [])
    got = pl.pallas_call(
        body,
        in_specs=[pl.BlockSpec(memory_space=pltpu.SMEM)] + [here] * len(given),
        out_specs=[here] * len(shapes),
        out_shape=shapes,
        compiler_params=pltpu.CompilerParams(vmem_limit_bytes=FOLD_LIMIT),
        cost_estimate=pl.CostEstimate(flops=1 << 20, bytes_accessed=2 << 20, transcendentals=0),
        name=name,
    )(info, *given)
    kept, away = got[: len(keeps)], got[len(keeps) : len(keeps) + len(sends)]
    results = []
    for at, (mine, _, how) in enumerate(states):
        size, height, model = mine.shape
        shape = (size // how[2], height, model) if isinstance(how, tuple) else kept[at].shape
        _, _, send_at, n_sends, _ = plans[at]
        some = [one.reshape(shape) for one in away[send_at : send_at + n_sends]]
        results.append((kept[at].reshape(shape), some))
    if n_small:
        results.append(got[-1])
    return results


def finish(info, row_at, frames, a, b, b_got, early, small, totals, width, slim):
    model = a.shape[1]
    feed_rows = small[0].shape[0] - N_VECTORS
    per = feed_rows // 2

    def body(info, a, b, b_got, early, totals, *refs):
        sums, refs = refs[: len(small)], refs[len(small) :]
        feed_in, feed_out, joined, attend, place, con_in, con_out, *refs = refs
        depth, gain, shift, bias, feed_bias, vectors = refs
        feed_in[0] = a[:width].T
        feed_in[1] = early[:width, :model].T
        first = info[row_at] == 0
        one, two = b[...].astype(f32), b_got[...].astype(f32)
        whole = jnp.concatenate([jnp.where(first, one, two), jnp.where(first, two, one)], axis=1)
        feed_out[0] = whole[:width]
        feed_out[1] = early[:width, model:]
        joined[:, :model] = whole[width : width + slim]
        joined[:, model : 2 * model] = whole[width + slim : width + 2 * slim]
        joined[:, 2 * model :] = a[width:]
        place[...] = whole[width + 2 * slim :]
        con_in[...] = early[width : width + slim]
        con_out[...] = early[width + slim :, :model]
        attend[...] = early[width + slim :, model:]
        me = info[0] // frames
        end = N_VECTORS + feed_rows
        vectors[end:] = jnp.zeros((vectors.shape[0] - end, model), f32)
        vectors[:end] = sum(one[...] for one in sums)
        vectors[end : end + 2] = totals[...]
        own = pltpu.roll(vectors[...], lax.rem(model - me * slim, model), 1)[:, :slim]
        depth[...] = own[:KERNEL]
        gain[0:5] = own[KERNEL : KERNEL + 5]
        gain[5:6] = own[end + 1 : end + 2]
        shift[0:5] = own[KERNEL + 5 : KERNEL + 10]
        shift[5:6] = own[end : end + 1]
        bias[...] = own[KERNEL + 10 : N_VECTORS]
        at = me * width
        for module in range(2):
            row = vectors[pl.ds(N_VECTORS + module * per + at // model, 1), :]
            row = pltpu.roll(row, lax.rem(model - lax.rem(at, model), model), 1)
            feed_bias[module : module + 1] = row[:, :width]

    def full(shape):
        return pl.BlockSpec(shape, lambda i: (0,) * len(shape))

    shapes = [
        (2, model, width), (2, width, model), (slim, 3 * model), (slim, model), (slim, model),
        (slim, 2 * model), (slim, model), (KERNEL, slim), (6, slim), (6, slim), (10, slim),
        (2, width),
    ]
    given = (a, b, b_got, early, totals, *small)
    return pl.pallas_call(
        body,
        grid=(1,),
        in_specs=[pl.BlockSpec(memory_space=pltpu.SMEM)] + [full(one.shape) for one in given],
        out_specs=[full(shape) for shape in shapes],
        out_shape=[sds(shape, f32) for shape in shapes],
        scratch_shapes=[pltpu.VMEM((-(-(N_VECTORS + feed_rows + 2) // 8) * 8, model), f32)],
        compiler_params=pltpu.CompilerParams(vmem_limit_bytes=FOLD_LIMIT),
        name="finish",
    )(info, *given)


def per_device(
    features,
    lengths,
    windows,
    feed_in,
    feed_in_bias,
    feed_out,
    attend_in,
    attend_out,
    position_proj,
    convolve_in,
    convolve_out,
    depthwise,
    norm_gain,
    norm_shift,
    biases,
    cotangent,
):
    rows, frames, model = features.shape
    tokens = rows * frames
    n = lax.axis_size("frames")
    devices = lax.axis_size("rows") * n
    row_len = float(frames * n)
    me = lax.axis_index("frames")
    first_frame = me * frames
    hidden = feed_in.shape[2]
    ends_every = jnp.cumsum(lengths, axis=1, dtype=jnp.int32)
    ends_here = lax.dynamic_slice_in_dim(ends_every, lax.axis_index("rows") * rows, rows, 0)
    slots = ends_here.shape[1]
    ends = jnp.pad(
        ends_here.astype(f32), ((0, 8 - rows), (0, -slots % 128)), constant_values=row_len
    )
    groups, k = [(2, 2)], 4
    while k < n:
        groups.append((k, min(4, n // k)))
        k *= groups[-1][1]
    places = [lax.axis_index("rows"), me % 2] + [(me // k) % size for k, size in groups]
    info = jnp.concatenate(
        [first_frame[None].astype(jnp.int32), windows, ends_here[:, -1], jnp.stack(places)]
    )
    row_at = 1 + 2 * rows
    core_at = row_at + 1
    starts = jnp.arange(n, dtype=jnp.int32) * frames
    counts = jnp.clip(ends_every[:, -1][:, None] - starts[None, :], 0, frames)
    counts = jnp.sum(counts.reshape(-1, rows, n), axis=1).astype(f32).reshape(devices, 1)
    counts = jnp.broadcast_to(counts, (devices, 128))
    sinusoid = jnp.asarray(position_table(WIN, model))

    start = front(
        features, feed_in, feed_in_bias, feed_out, attend_in, norm_gain, norm_shift, biases
    )
    before, after = neighbours(start.hi, start.lo)
    query = queries(start.na, attend_in, biases, sinusoid, position_proj)
    mix = attend(
        row_len, info, ends, start, query, before, after, attend_out, convolve_in, norm_gain,
        norm_shift, biases,
    )
    rim_before, rim_after = neighbours(mix.last, mix.first)
    got = depth_conv(row_len, devices, info, ends, mix.gated, rim_before, rim_after, depthwise)
    mid = middle(
        devices, rows, info, gather(got.stats), counts, got.depth, mix.out, feed_in,
        feed_in_bias, feed_out, convolve_out, norm_gain, norm_shift, biases,
        cotangent.reshape(tokens, model),
    )
    edge_before, edge_after = neighbours(mid.last, mid.first)
    totals = gather(mid.totals)
    early = feed_weights(n, mid.gi, mid.nf, mid.act, mid.gl)
    totals, early = lax.optimization_barrier((totals, early))
    conv = conv_back(
        row_len, n, info, ends, depthwise, convolve_in, attend_out, norm_gain, totals, mid,
        edge_before, edge_after, rim_before, rim_after, mix, early,
    )
    early, gm = lax.optimization_barrier((conv.early, conv.gm))
    early = scatter_sum(early)
    grads = attend_back(start, query, before, after, mix.prob, gm)
    halo = neighbours(grads.g_after, grads.g_before)
    end = back(
        info, core_at, n, grads, halo, attend_in, start, conv.gas, norm_gain, sinusoid
    )
    b, b_got = end.mine, [swap(end.other, 1)]
    got = first_back(info, core_at, n, end.gl, feed_in, feed_out, start, end.gv)
    a, a_got = got.mine, [swap(got.other, 1)]
    ((b, b_send),) = fold("fold_b", info, row_at, [(b, b_got, COLUMNS)])
    b_got = [lax.ppermute(b_send[0], "rows", ROW_PAIR)]
    ((a, a_send),) = fold("fold_a", info, row_at, [(a, a_got, (core_at + 1, 1, 2))])
    a_got = swaps(a_send, groups[0])
    gn, a = lax.optimization_barrier((got.gn, a))
    ending = last(features, gn, end.gfs, norm_gain)

    vec_conv, vec_mid, vec_back, vec_last = conv.vec, mid.vec, end.vec, ending.vec
    small = jnp.concatenate(
        [
            vec_conv[:KERNEL],
            vec_last[0:1], vec_back[2:3], vec_conv[9:10], vec_mid[0:1], vec_mid[2:3],
            vec_last[1:2], vec_back[3:4], vec_conv[10:11], vec_mid[1:2], vec_mid[3:4],
            vec_back[0:2], vec_conv[13:14], vec_conv[11:13], vec_mid[4:5], vec_back[4:5],
            vec_mid[5:6], grads.vec[0:2],
            got.fb, mid.fb,
        ],
        axis=0,
    )
    small = [small] + swaps([small] * 3, (1, 4))
    last_group = groups[-1]
    for at, group in enumerate(groups):
        deeper = at + 1 < len(groups)
        a_how = (core_at + 2 + at, 1, groups[at + 1][1]) if deeper else None
        states = [(a, a_got, a_how), (b, b_got, (core_at + 1 + at, 1, group[1]))]
        (a, a_send), (b, b_send), one = fold(f"fold_{at}", info, row_at, states, small)
        if deeper:
            a_got = swaps(a_send, groups[at + 1])
        else:
            early, a = lax.optimization_barrier((early, a))
            a_got = [lax.ppermute(a, "rows", ROW_PAIR)]
            early_got = [lax.ppermute(early, "rows", ROW_PAIR)]
        b_got = swaps(b_send, group)
        if at == 0:
            small = [one, lax.ppermute(one, "rows", ROW_PAIR)]
        elif deeper:
            small = [one] + swaps([one] * (group[1] - 1), group)
    states = [(b, b_got, None), (a, a_got, IN_FLOAT), (early, early_got, IN_FLOAT)]
    (b, _), (a, _), (early, _) = fold("fold_last", info, row_at, states)
    b_got = lax.ppermute(b, "rows", ROW_PAIR)
    small = [one] + swaps([one] * (last_group[1] - 1), last_group)
    slim = model // n
    width = hidden // n
    feed_in_grad, feed_out_grad, joined, *rest, depth, gain, shift, bias, feed_bias = finish(
        info, row_at, frames, a[0], b[0], b_got[0], early[0], small, vec_conv[14:16], width, slim
    )
    return (
        mid.out.reshape(rows, frames, model),
        ending.out,
        feed_in_grad,
        feed_bias,
        feed_out_grad,
        joined,
        *rest,
        depth,
        gain,
        shift,
        bias,
    )


def solution(mesh):
    placed = (
        P("rows", "frames", None),
        P(),
        P("rows"),
        P(),
        P(),
        P(),
        P(),
        P(),
        P(),
        P(),
        P(),
        P(),
        P(),
        P(),
        P(),
        P("rows", "frames", None),
    )
    return jax.shard_map(
        per_device,
        mesh=mesh,
        in_specs=placed,
        out_specs=(
            P("rows", "frames", None),
            P("rows", "frames", None),
            P(None, None, "frames"),
            P(None, "frames"),
            P(None, "frames", None),
            P("frames", None),
            P("frames", None),
            P("frames", None),
            P("frames", None),
            P("frames", None),
            P(None, "frames"),
            P(None, "frames"),
            P(None, "frames"),
            P(None, "frames"),
        ),
        check_vma=False,
    )
```

```python
import functools
import math
import types

import jax
import jax.numpy as jnp
import ml_dtypes
import numpy as np
from jax import lax
from jax.experimental import pallas as pl
from jax.experimental.pallas import tpu as pltpu
from jax.sharding import PartitionSpec as P

H = 8
DH = 64
KERNEL = 9
WIN = 128

HALF = KERNEL // 2
SPAN = 3 * WIN
MANY = 4
GROUPS = H // MANY
WIDE = MANY * DH
RIM = 16
RIM_GRAD = 8
eps_norm = 1e-05
negative = -1e30
f32 = jnp.float32
bf16 = jnp.bfloat16
DEVICES = ("rows", "frames")
VMEM_LIMIT = 60 * 1024 * 1024
FOLD_LIMIT = 14 * 1024 * 1024


def dot(left, right):
    return jnp.dot(left, right, preferred_element_type=f32)


def dot_last(left, right):
    return lax.dot_general(left, right, (((1,), (1,)), ((), ())), preferred_element_type=f32)


def dot_first(left, right):
    return lax.dot_general(left, right, (((0,), (0,)), ((), ())), preferred_element_type=f32)


def sigmoid(x):
    return 0.5 * jnp.tanh(0.5 * x) + 0.5


def total(x):
    return jnp.sum(x, axis=0, keepdims=True)


def normalize(values):
    centered = values - jnp.mean(values, axis=-1, keepdims=True)
    inverse = lax.rsqrt(jnp.mean(centered * centered, axis=-1, keepdims=True) + eps_norm)
    return centered * inverse, inverse


def norm_back(grad_out, normal, inverse, gain):
    scaled = grad_out * gain
    centred = scaled - jnp.mean(scaled, axis=-1, keepdims=True)
    grad_in = inverse * (centred - normal * jnp.mean(scaled * normal, axis=-1, keepdims=True))
    return grad_in, total(grad_out * normal), total(grad_out)


def position_table(width, model):
    offsets = (np.arange(2 * width + 1) - width).astype(np.float32)
    rates = np.exp(
        np.arange(model // 2).astype(np.float32) * np.float32(-2.0 * math.log(10000.0) / model)
    )
    angles = (offsets[:, None] * rates[None, :]).astype(np.float32)
    both = np.stack([np.sin(angles), np.cos(angles)], axis=2).reshape(2 * width + 1, model)
    padded = np.zeros((3 * width, model), np.float32)
    padded[: 2 * width + 1] = both
    return padded.astype(ml_dtypes.bfloat16)


def bounds(ends, at, row_len):
    low = jnp.max(jnp.where(ends <= at, ends, 0.0), axis=1, keepdims=True)
    high = jnp.min(jnp.where(ends > at, ends, row_len), axis=1, keepdims=True)
    return low, high


def column(count, offset):
    return lax.broadcasted_iota(jnp.int32, (count, 1), 0).astype(f32) + offset


def head_lanes(rows):
    return lax.broadcasted_iota(jnp.int32, (rows, WIDE), 1) // DH


def heads_apart(group):
    at = head_lanes(group.shape[0])
    zero = jnp.zeros_like(group)
    return jnp.concatenate([jnp.where(at == k, group, zero) for k in range(MANY)], axis=0)


def heads_joined(stacked):
    rows = stacked.shape[0] // MANY
    at = head_lanes(rows)
    joined = stacked[:rows]
    for k in range(1, MANY):
        joined = jnp.where(at == k, stacked[k * rows : (k + 1) * rows], joined)
    return joined


def beside(stacked):
    rows = stacked.shape[0] // MANY
    return jnp.concatenate([stacked[k * rows : (k + 1) * rows] for k in range(MANY)], axis=1)


def below(joined):
    width = joined.shape[1] // MANY
    return jnp.concatenate([joined[:, k * width : (k + 1) * width] for k in range(MANY)], axis=0)


def windows(width):
    return [slice(at, at + WIN) for at in range(0, width, WIN)]


def flip(rows):
    i = lax.broadcasted_iota(jnp.int32, (rows, rows), 0)
    j = lax.broadcasted_iota(jnp.int32, (rows, rows), 1)
    return (i + j == rows - 1).astype(f32).astype(bf16)


class Load:
    def __init__(self, source, buffer, sem):
        self.buffer, self.waited = buffer, False
        self.copy = pltpu.make_async_copy(source, buffer, sem)
        self.copy.start()

    def ready(self):
        if not self.waited:
            self.copy.wait()
            self.waited = True
        return self.buffer


class Loads:
    def __init__(self, items):
        self.items = items

    def __getitem__(self, at):
        return self.items[at].ready()


class Stage:
    def __init__(self, loads, stores, sems):
        self.sems, self.used, self.pending, self.targets = sems, 0, [], []
        self.named, self.all_loads = {}, []
        for name, pairs, single in loads:
            items = [Load(source, buffer, self.sem()) for source, buffer in pairs]
            self.all_loads += items
            self.named[name] = items[0] if single else Loads(items)
        for name, pairs, single in stores:
            self.targets += [[target, buffer, False] for target, buffer in pairs]
            buffers = [buffer for _, buffer in pairs]
            self.named[name] = buffers[0] if single else buffers

    def sem(self):
        self.used += 1
        return self.sems.at[self.used - 1]

    def __getattr__(self, name):
        found = self.named[name]
        return found.ready() if isinstance(found, Load) else found

    def send(self, buffer, at=None):
        entry = next(entry for entry in self.targets if entry[1] is buffer)
        target = entry[0]
        entry[2] = True
        if at is not None:
            target, buffer = target.at[at], buffer.at[at]
        copy = pltpu.make_async_copy(buffer, target, self.sem())
        copy.start()
        self.pending.append(copy)

    def finish(self):
        for _, buffer, sent in self.targets:
            if not sent:
                self.send(buffer)
        for load in self.all_loads:
            load.ready()
        for copy in self.pending:
            copy.wait()


def staged(
    name, body, ins, outs, smem=(), scratch=(), flops=0, moved=0, sends=0, filled=None,
    limit=VMEM_LIMIT, kept=None,
):
    operands, loads, stores, kept = [], [], [], kept or {}
    for key, items in ins.items():
        single = not isinstance(items, list)
        entries = []
        for item in [items] if single else items:
            array, view, shape = item if isinstance(item, tuple) else (item, None, item.shape)
            at = next((i for i, other in enumerate(operands) if other is array), None)
            if at is None:
                at = len(operands)
                operands.append(array)
            entries.append((at, view, shape, array.dtype))
        loads.append((key, entries, single))
    for key, items in outs.items():
        single = not isinstance(items, list)
        entries = [
            item if isinstance(item, tuple) else (item, None, item.shape)
            for item in ([items] if single else items)
        ]
        stores.append((key, entries, single))
    aliases = {}
    if filled is not None:
        aliases = {len(smem) + len(kept) + len(operands): 0}
        operands.append(filled)
    every_load = [entry for _, entries, _ in loads for entry in entries]
    every_store = [entry for _, entries, _ in stores for entry in entries]
    n_smem, n_ops, n_outs, n_loads = len(smem), len(operands), len(every_store), len(every_load)

    def run(*refs):
        cuts = [n_smem, len(kept), n_ops, n_outs, n_loads, n_outs, 1]
        taken, at = [], 0
        for cut in cuts:
            taken.append(refs[at : at + cut])
            at += cut
        scalars, here, given, targets, buffers, results, sems = taken
        buffers, places = iter(buffers), iter(zip(targets, results))
        placed_loads = [
            (
                key,
                [(given[i] if view is None else view(given[i]), next(buffers)) for i, view, _, _ in entries],
                single,
            )
            for key, entries, single in loads
        ]
        placed_stores = []
        for key, entries, single in stores:
            pairs = []
            for _, view, _ in entries:
                target, result = next(places)
                pairs.append((target if view is None else view(target), result))
            placed_stores.append((key, pairs, single))
        stage = Stage(placed_loads, placed_stores, sems[0])
        stage.named.update(zip(kept, here))
        body(stage, *scalars, *refs[at:])
        stage.finish()

    hbm = pl.BlockSpec(memory_space=pl.ANY)
    got = iter(
        pl.pallas_call(
            run,
            in_specs=[pl.BlockSpec(memory_space=pltpu.SMEM)] * n_smem
            + [pl.BlockSpec(memory_space=pltpu.VMEM)] * len(kept)
            + [hbm] * n_ops,
            out_specs=[hbm] * n_outs,
            out_shape=[shape for shape, _, _ in every_store],
            scratch_shapes=[pltpu.VMEM(shape, dtype) for _, _, shape, dtype in every_load]
            + [pltpu.VMEM(shape, whole.dtype) for whole, _, shape in every_store]
            + [pltpu.SemaphoreType.DMA((n_loads + n_outs + sends,))]
            + list(scratch),
            input_output_aliases=aliases,
            compiler_params=pltpu.CompilerParams(vmem_limit_bytes=limit),
            cost_estimate=pl.CostEstimate(flops=flops, bytes_accessed=moved, transcendentals=0),
            name=name,
        )(*smem, *kept.values(), *operands)
    )
    result = types.SimpleNamespace()
    for key, entries, single in stores:
        values = [next(got) for _ in entries]
        setattr(result, key, values[0] if single else values)
    return result


def sds(shape, dtype):
    return jax.ShapeDtypeStruct(shape, dtype)


def slab(array, *at):
    shape = tuple(a[1] for a in at if isinstance(a, tuple))
    index = tuple(pl.ds(*a) if isinstance(a, tuple) else a for a in at)
    return (array, lambda ref: ref.at[index], shape)


def by_row(array, rows):
    tokens, width = array.shape
    return [slab(array, (row * (tokens // rows), tokens // rows), (0, width)) for row in range(rows)]


def each_of(array):
    rows, size, width = array.shape
    return [slab(array, row, (0, size), (0, width)) for row in range(rows)]


PART = 1024


def activate(inner):
    half = 0.5 * inner
    turn = jnp.tanh(half)
    up = 1.0 + turn
    active = half * up
    return active, 0.5 * (up + active * (1.0 - turn))


def feed_slabs(feed_in, feed_out, module):
    _, model, hidden = feed_in.shape
    spans = [(part, PART) for part in range(0, hidden, PART)]
    w_in = [slab(feed_in, module, (0, model), span) for span in spans]
    w_out = [slab(feed_out, module, span, (0, model)) for span in spans]
    return w_in, w_out


def front(features, feed_in, feed_in_bias, feed_out, attend_in, gain, shift, bias):
    rows, frames, model = features.shape
    tokens = rows * frames
    hidden = feed_in.shape[2]
    parts = hidden // PART
    low = sds((tokens, model), bf16)

    def body(k):
        gain, shift = k.gain, k.shift
        x = k.x[...].reshape(tokens, model).astype(f32)
        normal, _ = normalize(x)
        k.n0[...] = (normal * gain[0:1] + shift[0:1]).astype(bf16)
        k.send(k.n0)
        for part in range(parts):
            cut = slice(part * PART, (part + 1) * PART)
            inner = dot(k.n0[...], k.w_in[part][...]) + k.b_in[0:1, cut]
            active, slope = activate(inner)
            k.act[:, cut] = active.astype(bf16)
            k.slope[:, cut] = slope.astype(bf16)
        k.send(k.slope)
        k.send(k.act)
        branch = k.bias[6:7]
        for part in range(parts):
            cut = slice(part * PART, (part + 1) * PART)
            branch = branch + dot(k.act[:, cut], k.w_out[part][...])
        after = x + 0.5 * branch
        k.after[...] = after
        k.send(k.after)
        normal, _ = normalize(after)
        normed = (normal * gain[1:2] + shift[1:2]).astype(bf16)
        k.na[...] = normed
        k.send(k.na)
        both = dot(normed, k.attend_in[...])
        keys = both[:, :model].astype(bf16)
        values = (both[:, model:] + k.bias[1:2]).astype(bf16)
        for row in range(rows):
            at = row * frames
            k.lo[row, :, :model] = keys[at : at + WIN]
            k.lo[row, :, model:] = values[at : at + WIN]
            k.hi[row, :, :model] = keys[at + WIN : at + frames]
            k.hi[row, :, model:] = values[at + WIN : at + frames]

    w_in, w_out = feed_slabs(feed_in, feed_out, 0)
    kv = sds((rows, WIN, 2 * model), bf16)
    return staged(
        "front",
        body,
        dict(
            x=features, gain=gain, shift=shift, b_in=feed_in_bias, w_in=w_in, bias=bias,
            w_out=w_out, attend_in=slab(attend_in, (0, model), (model, 2 * model)),
        ),
        dict(
            after=sds((tokens, model), f32), n0=low, na=low, lo=kv, hi=kv,
            act=sds((tokens, hidden), bf16), slope=sds((tokens, hidden), bf16),
        ),
        flops=2 * tokens * model * (2 * hidden + 2 * model),
        moved=16 << 20,
    )


def queries(na, attend_in, bias, sinusoid, proj):
    tokens, model = na.shape

    def body(k):
        query = dot(k.na[...], k.attend_in[...]) + k.bias[0:1]
        factor = 1.0 / math.sqrt(DH)
        k.qu[...] = ((query + k.bias[8:9]) * factor).astype(bf16)
        k.qv[...] = ((query + k.bias[9:10]) * factor).astype(bf16)
        k.table[...] = dot(k.sinusoid[...], k.proj[...]).astype(bf16)

    low = sds((tokens, model), bf16)
    return staged(
        "queries",
        body,
        dict(
            na=na, attend_in=slab(attend_in, (0, model), (0, model)), bias=bias,
            sinusoid=sinusoid, proj=proj,
        ),
        dict(qu=low, qv=low, table=sds((SPAN, model), bf16)),
        flops=2 * tokens * model * 2 * model,
        moved=4 << 20,
    )


def attend(
    row_len, info, ends, start, query, before, after, attend_out, convolve_in, gain, shift, bias
):
    rows = before.shape[0]
    tokens, model = start.after.shape
    frames = tokens // rows
    low = sds((tokens, model), bf16)

    def body(k, info):
        first_frame = info[0].astype(f32)
        turn = flip(WIN)
        key_at = lax.broadcasted_iota(jnp.int32, (WIN, SPAN), 1).astype(f32)
        table = k.table
        ones = jnp.ones((SPAN, WIN), bf16)
        for row in range(rows):
            reach = info[1 + row].astype(f32)
            row_ends = k.ends[row : row + 1, :]
            for block in range(2):
                at = column(WIN, first_frame + WIN * block)
                lower, upper = bounds(row_ends, at, row_len)
                base = first_frame + (WIN * (block - 1))
                lower = jnp.maximum(lower, at - reach) - base
                upper = jnp.minimum(upper - 1.0, at + reach) - base
                allowed = ((key_at >= lower) & (key_at <= upper))[None]
                here = slice(row * frames + WIN * block, row * frames + WIN * (block + 1))
                some = [k.lo[row], k.hi[row]]
                some = some + [k.next[row]] if block else [k.before[row]] + some
                for group in range(GROUPS):
                    cut = slice(WIDE * group, WIDE * (group + 1))
                    cut_v = slice(model + WIDE * group, model + WIDE * (group + 1))
                    keys = jnp.concatenate([b[:, cut] for b in some], axis=0)
                    values = jnp.concatenate([b[:, cut_v] for b in some], axis=0)
                    spread = dot_last(heads_apart(k.qv[here, cut]), table[:, cut])
                    content = dot_last(heads_apart(k.qu[here, cut]), keys)
                    spread = pltpu.roll(
                        spread.reshape(MANY, WIN, SPAN), 0, 2, stride=1, stride_axis=1
                    )
                    scores = content.reshape(MANY, WIN, SPAN) + spread
                    scores = jnp.where(allowed, scores, negative)
                    powers = jnp.exp(scores - jnp.max(scores, axis=2, keepdims=True))
                    powers = powers.reshape(MANY * WIN, SPAN)
                    inverse = 1.0 / dot(powers.astype(bf16), ones)
                    weights = jnp.concatenate(
                        [powers[:, cut] * inverse for cut in windows(SPAN)], axis=1
                    ).astype(bf16)
                    k.mixed[here, cut] = heads_joined(dot(weights, values)).astype(bf16)
                    k.prob[row][block, group] = dot(turn, beside(weights)).astype(bf16)
            k.send(k.prob[row])
        k.send(k.mixed)
        after_attend = k.after[...] + dot(k.mixed[...], k.attend_out[...]) + k.bias[2:3]
        k.out[...] = after_attend
        k.send(k.out)
        normal, _ = normalize(after_attend)
        normed = (normal * k.gain[2:3] + k.shift[2:3]).astype(bf16)
        k.nc[...] = normed
        k.send(k.nc)
        paired = dot(normed, k.convolve_in[...])
        value = paired[:, :model] + k.bias[3:4]
        gate = paired[:, model:] + k.bias[4:5]
        sigma = sigmoid(gate)
        gated = value * sigma
        k.factors[:, :model] = sigma.astype(bf16)
        k.factors[:, model:] = (gated * (1.0 - sigma)).astype(bf16)
        k.send(k.factors)
        gated = gated.astype(bf16)
        k.gated[...] = gated
        for row in range(rows):
            k.first[row] = gated[row * frames : row * frames + RIM]
            k.last[row] = gated[(row + 1) * frames - RIM : (row + 1) * frames]

    rim = sds((rows, RIM, model), bf16)
    return staged(
        "attend",
        body,
        dict(
            ends=ends, table=query.table, qv=query.qv, qu=query.qu, lo=each_of(start.lo),
            hi=each_of(start.hi), before=each_of(before), next=each_of(after), after=start.after,
            attend_out=attend_out, bias=bias, gain=gain, shift=shift, convolve_in=convolve_in,
        ),
        dict(
            prob=[sds((2, GROUPS, WIN, MANY * SPAN), bf16)] * rows, mixed=low,
            out=sds((tokens, model), f32), nc=low, factors=sds((tokens, 2 * model), bf16),
            gated=low, first=rim, last=rim,
        ),
        smem=[info],
        flops=16 * 8 * 256 * 384 * 128,
        moved=16 << 20,
    )


def valid_column(info, row, rows, frames):
    at = column(frames, info[0].astype(f32))
    return (at < info[1 + rows + row].astype(f32)).astype(f32)


def put_rows(ref, part, vector):
    model = ref.shape[1]
    per = vector.shape[1] // model
    for one in range(per):
        at = part * per + one
        ref[at : at + 1] = vector[:, one * model : (one + 1) * model]


def pack(ref, vectors):
    at = 0
    for vector in vectors:
        for k in range(0, vector.shape[1], 128):
            ref[at : at + 1, :] = vector[:, k : k + 128]
            at += 1


def by_rows(count, size, step, init=None):
    def one(i, carry):
        return step(pl.ds(pl.multiple_of(i * size, size), size), carry)

    return lax.fori_loop(0, count // size, one, init)


def by_lanes(width, step):
    def one(i, carry):
        step(pl.ds(pl.multiple_of(i * 128, 128), 128))
        return carry

    lax.fori_loop(0, width // 128, one, 0)


def spread(column):
    return jnp.broadcast_to(column, (column.shape[0], 128))


def tap_masks(keep_s, at, low, high):
    for tap in range(KERNEL):
        off = tap - HALF
        keep_s[tap] = spread(((at + off >= low) & (at + off < high)).astype(f32))


def depth_conv(row_len, devices, info, ends, gated, before, after, taps):
    rows = before.shape[0]
    tokens, model = gated.shape
    frames = tokens // rows

    def body(k, info, rim, keep_s, valid_s, sums, tile):
        start = info[0].astype(f32)
        counts = 0.0
        taps = k.taps
        for row in range(rows):
            here = slice(row * frames, (row + 1) * frames)
            at = column(frames, start)
            low, high = bounds(k.ends[row : row + 1, :], at, row_len)
            tap_masks(keep_s, at, low, high)
            valid = valid_column(info, row, rows, frames)
            valid_s[here] = spread(valid)
            counts += total(valid)
            rim[0:RIM] = k.before[row].astype(f32)
            rim[RIM : RIM + frames] = k.gated[row][...].astype(f32)
            rim[RIM + frames :] = k.after[row].astype(f32)

            def one(lanes):
                depth = jnp.zeros((frames, 128), f32)
                for tap in range(KERNEL):
                    off = tap - HALF
                    part = rim[RIM + off : RIM + off + frames, lanes] * keep_s[tap]
                    depth += taps[tap : tap + 1, lanes] * part
                k.depth[here, lanes] = depth
                sums[row : row + 1, lanes] = total(depth * valid_s[here])

            by_lanes(model, one)
            k.send(k.depth, pl.ds(row * frames, frames))
        first = total(sums[0:rows, :])
        mean = first / jnp.maximum(counts, 1.0)
        sums[rows : rows + 1, :] = mean

        def two(lanes):
            centered = k.depth[:, lanes] - sums[rows : rows + 1, lanes]
            sums[rows + 1 : rows + 2, lanes] = total(centered * centered * valid_s[...])

        by_lanes(model, two)
        pack(tile, [first, sums[rows + 1 : rows + 2, :]])
        k.stats[...] = jnp.broadcast_to(tile[...][None], k.stats.shape)

    return staged(
        "depth_conv",
        body,
        dict(ends=ends, taps=taps, gated=by_row(gated, rows)),
        dict(depth=sds((rows * frames, model), f32), stats=sds((devices, 8, 128), f32)),
        smem=[info],
        scratch=[
            pltpu.VMEM((frames + 2 * RIM, model), f32),
            pltpu.VMEM((KERNEL, frames, 128), f32),
            pltpu.VMEM((rows * frames, 128), f32),
            pltpu.VMEM((8, model), f32),
            pltpu.VMEM((8, 128), f32),
        ],
        kept=dict(before=before, after=after),
        flops=rows * frames * model * 30,
        moved=2 << 20,
        sends=rows - 1,
    )


def middle(
    devices, rows, info, stats, counts, depth, stream, feed_in, feed_in_bias, feed_out,
    convolve_out, gain, shift, bias, cotangent,
):
    tokens, model = depth.shape
    frames = tokens // rows
    hidden = feed_in.shape[2]
    parts = hidden // PART

    def body(k, info, conv_s, bn_s, slope_s, tile):
        stats, each = k.stats, k.counts[:, 0:1]
        gain, shift, bias = k.gain, k.shift, k.bias
        count = total(each)
        means, inverses = [], []
        for at in range(model // 128):
            sums = stats[:, at, :]
            mean = total(sums) / count
            off = sums / jnp.maximum(each, 1.0) - mean
            spread = total(stats[:, model // 128 + at, :]) + total(each * off * off)
            means.append(mean)
            inverses.append(lax.rsqrt(spread / count + eps_norm))
        mean = jnp.concatenate(means, axis=1)
        inverse = jnp.concatenate(inverses, axis=1)
        k.inv[0:1] = inverse
        k.inv[1:2] = jnp.broadcast_to(1.0 / count, (1, model))
        normal = (k.depth[...] - mean) * inverse
        bn_s[...] = normal
        k.bn[...] = normal.astype(bf16)
        k.send(k.bn)
        batch = normal * gain[5:6] + shift[5:6]
        swished = (batch * sigmoid(batch)).astype(bf16)
        k.sw[...] = swished
        k.send(k.sw)
        after_conv = k.stream[...] + dot(swished, k.convolve_out[...]) + bias[5:6]
        conv_s[...] = after_conv
        normal, _ = normalize(after_conv)
        k.nf[...] = (normal * gain[3:4] + shift[3:4]).astype(bf16)
        k.send(k.nf)
        for part in range(parts):
            cut = slice(part * PART, (part + 1) * PART)
            inner = dot(k.nf[...], k.w_in[part][...]) + k.b_in[1:2, cut]
            active, slope = activate(inner)
            k.act[:, cut] = active.astype(bf16)
            slope_s[:, cut] = slope
        k.send(k.act)
        branch = bias[7:8]
        for part in range(parts):
            cut = slice(part * PART, (part + 1) * PART)
            branch = branch + dot(k.act[:, cut], k.w_out[part][...])
        normal, inverse = normalize(conv_s[...] + 0.5 * branch)
        valid = jnp.concatenate(
            [valid_column(info, row, rows, frames) for row in range(rows)], axis=0
        )
        k.out[...] = (valid * (normal * gain[4:5] + shift[4:5])).astype(bf16)
        k.send(k.out)
        grad = valid * k.cotangent[...].astype(f32)
        grad, gain_grad, shift_grad = norm_back(grad, normal, inverse, gain[4:5])
        k.gcs[...] = grad
        low = (0.5 * grad).astype(bf16)
        k.gl[...] = low
        k.send(k.gl)
        vec = k.vec
        vec[2:3] = gain_grad
        vec[3:4] = shift_grad
        vec[5:6] = total(low.astype(f32))
        back = 0.0
        for part in range(parts):
            cut = slice(part * PART, (part + 1) * PART)
            grad = (dot_last(k.gl[...], k.w_out[part][...]) * slope_s[:, cut]).astype(bf16)
            k.gi[:, cut] = grad
            put_rows(k.fb, part, total(grad.astype(f32)))
            back = back + dot_last(grad, k.w_in[part][...])
        k.send(k.gi)
        normal, inverse = normalize(conv_s[...])
        grad, gain_grad, shift_grad = norm_back(back, normal, inverse, gain[3:4])
        vec[0:1] = gain_grad
        vec[1:2] = shift_grad
        grad = k.gcs[...] + grad
        k.gcs[...] = grad
        k.send(k.gcs)
        low = grad.astype(bf16)
        k.gcl[...] = low
        k.send(k.gcl)
        vec[4:5] = total(low.astype(f32))
        bn = bn_s[...]
        batch = bn * gain[5:6] + shift[5:6]
        _, slope = activate(batch)
        grad = dot_last(low, k.convolve_out[...]) * slope
        k.gb[...] = grad.astype(bf16)
        k.send(k.gb)
        pack(tile, [total(grad), total(grad * bn)])
        k.totals[...] = jnp.broadcast_to(tile[...][None], k.totals.shape)
        k.send(k.totals)
        for row in range(rows):
            at, end = row * frames, (row + 1) * frames
            k.first[row, :, :model] = grad[at : at + RIM_GRAD]
            k.first[row, :, model:] = bn[at : at + RIM_GRAD]
            k.last[row, :, :model] = grad[end - RIM_GRAD : end]
            k.last[row, :, model:] = bn[end - RIM_GRAD : end]

    w_in, w_out = feed_slabs(feed_in, feed_out, 1)
    ins = dict(
        gain=gain, shift=shift, depth=depth, bias=bias,
        convolve_out=convolve_out, stream=stream, b_in=feed_in_bias, w_in=w_in, w_out=w_out,
        cotangent=cotangent,
    )
    low = sds((tokens, model), bf16)
    wide = sds((tokens, model), f32)
    rim = sds((rows, RIM_GRAD, 2 * model), f32)
    return staged(
        "middle",
        body,
        ins,
        dict(
            out=low, act=sds((tokens, hidden), bf16), gi=sds((tokens, hidden), bf16), nf=low,
            gl=low, sw=low, gcl=low, gcs=wide, gb=low, bn=low, inv=sds((8, model), f32),
            totals=sds((devices, 8, 128), f32), first=rim, last=rim, vec=sds((8, model), f32),
            fb=sds((hidden // model, model), f32),
        ),
        smem=[info],
        scratch=[
            pltpu.VMEM((tokens, model), f32),
            pltpu.VMEM((tokens, model), f32),
            pltpu.VMEM((tokens, hidden), f32),
            pltpu.VMEM((8, 128), f32),
        ],
        kept=dict(stats=stats, counts=counts),
        flops=2 * tokens * model * (4 * hidden + 2 * model),
        moved=24 << 20,
    )


def conv_back(
    row_len, n, info, ends, taps, convolve_in, attend_out, gain, totals, mid, edge_before,
    edge_after, rim_before, rim_after, mix, early,
):
    tokens, model = mid.gb.shape
    rows = rim_before.shape[0]
    frames = tokens // rows
    slim = model // n
    room = slim % 8 == 0

    def body(k, info, grads, rim, keep_s, gp, gal):
        start = info[0].astype(f32)
        parts = model // 128
        sums = [total(k.totals[:, at, :]) for at in range(2 * parts)]
        total_a = jnp.concatenate(sums[:parts], axis=1)
        total_b = jnp.concatenate(sums[parts:], axis=1)
        inverse, per_count = k.inv[0:1], k.inv[1:2]
        gain, taps, vec = k.gain, k.taps, k.vec
        own_scale = inverse * gain[5:6]
        share_a = own_scale * total_a * per_count
        share_b = own_scale * total_b * per_count
        vec[14:15] = total_a
        vec[15:16] = total_b
        vec[0:9] = jnp.zeros((9, model), f32)
        vec[9:14] = jnp.zeros((5, model), f32)

        def grad_of(grad, normal, valid):
            grad = grad * own_scale - valid * (share_a + normal * share_b)
            return grad.astype(bf16).astype(f32)

        for row in range(rows):
            first = row * frames
            last = info[1 + rows + row].astype(f32)
            at = column(frames, start)
            low, high = bounds(k.ends[row : row + 1, :], at, row_len)
            tap_masks(keep_s, at, low, high)
            before, after = k.edge_before, k.edge_after
            edge_at = column(RIM_GRAD, start - RIM_GRAD)
            grads[0:RIM_GRAD] = grad_of(
                before[row, :, :model], before[row, :, model:], (edge_at < last).astype(f32)
            )
            for step in range(0, frames, 32):
                here = slice(step, step + 32)
                at = column(32, start + step)
                grads[RIM_GRAD + step : RIM_GRAD + step + 32] = grad_of(
                    k.gb[row][here].astype(f32),
                    k.bn[row][here].astype(f32),
                    (at < last).astype(f32),
                )
            edge_at = column(RIM_GRAD, start + frames)
            grads[RIM_GRAD + frames :] = grad_of(
                after[row, :, :model], after[row, :, model:], (edge_at < last).astype(f32)
            )
            rim[0:RIM] = k.rim_before[row].astype(f32)
            rim[RIM : RIM + frames] = k.gated[row][...].astype(f32)
            rim[RIM + frames :] = k.rim_after[row].astype(f32)
            factors = k.factors[row]
            half = frames // 2

            def one(i, carry):
                lane = pl.multiple_of(i * 128, 128)
                lanes, gates = pl.ds(lane, 128), pl.ds(model + lane, 128)
                for base in range(0, frames, half):
                    own = grads[RIM_GRAD + base : RIM_GRAD + base + half, lanes]
                    grad = jnp.zeros((half, 128), f32)
                    for tap in range(KERNEL):
                        off = base + tap - HALF
                        keep = keep_s[tap, base : base + half]
                        part = own * (rim[RIM + off : RIM + off + half, lanes] * keep)
                        vec[tap : tap + 1, lanes] += total(part)
                        mirror = KERNEL - 1 - tap
                        part = grads[RIM_GRAD + off : RIM_GRAD + off + half, lanes] * keep
                        grad += taps[mirror : mirror + 1, lanes] * part
                    one = (grad * factors[base : base + half, lanes].astype(f32)).astype(bf16)
                    two = (grad * factors[base : base + half, gates].astype(f32)).astype(bf16)
                    here = slice(first + base, first + base + half)
                    gp[here, lanes] = one
                    gp[here, gates] = two
                    vec[11:12, lanes] += total(one.astype(f32))
                    vec[12:13, lanes] += total(two.astype(f32))
                return carry

            lax.fori_loop(0, model // 128, one, 0)
        grad = dot_last(gp[...], k.convolve_in[...])
        normal, inverse = normalize(k.after[...])
        grad, gain_grad, shift_grad = norm_back(grad, normal, inverse, gain[2:3])
        vec[9:10] = gain_grad
        vec[10:11] = shift_grad
        grad = k.gcs[...] + grad
        k.gas[...] = grad
        k.send(k.gas)
        low = grad.astype(bf16)
        gal[...] = low
        vec[13:14] = total(low.astype(f32))
        k.gm[...] = dot_last(gal[...], k.attend_out[...]).astype(bf16)
        k.send(k.gm)
        out = k.early
        out[:, :slim] = dot_first(k.nc[...], gp[...]).astype(bf16).reshape(n, slim, 2 * model)
        block = dot_first(k.sw[...], k.gcl[...]).astype(bf16)
        out[:, slim:, :model] = block.reshape(n, slim, model)
        block = dot_first(k.mixed[...], gal[...]).astype(bf16)
        out[:, slim:, model:] = block.reshape(n, slim, model)

    own = (n, 2 * slim, 2 * model)
    size = early.shape[1] - 2 * slim
    if room:
        out = (sds(early.shape, bf16), lambda ref: ref.at[:, pl.ds(size, 2 * slim)], own)
    else:
        out = sds(own, bf16)
    got = staged(
        "conv_back",
        body,
        dict(
            inv=mid.inv, gain=gain, ends=ends, taps=taps, rim_before=rim_before,
            rim_after=rim_after, gb=by_row(mid.gb, rows), bn=by_row(mid.bn, rows), gated=by_row(mix.gated, rows),
            factors=by_row(mix.factors, rows), convolve_in=convolve_in, after=mix.out, gcs=mid.gcs,
            attend_out=attend_out, nc=mix.nc, sw=mid.sw, gcl=mid.gcl, mixed=mix.mixed,
        ),
        dict(
            early=out, gas=sds((tokens, model), f32), gm=sds((tokens, model), bf16),
            vec=sds((16, model), f32),
        ),
        smem=[info],
        scratch=[
            pltpu.VMEM((frames + 2 * RIM_GRAD, model), f32),
            pltpu.VMEM((frames + 2 * RIM, model), f32),
            pltpu.VMEM((KERNEL, frames, 128), f32),
            pltpu.VMEM((tokens, 2 * model), bf16),
            pltpu.VMEM((tokens, model), bf16),
        ],
        kept=dict(totals=totals, edge_before=edge_before, edge_after=edge_after),
        flops=2 * tokens * model * 7 * model,
        moved=16 << 20,
        filled=early if room else None,
    )
    if not room:
        got.early = jnp.concatenate([early, got.early], axis=1)
    return got


def attend_back(start, query, before, after, probs, gm):
    rows = before.shape[0]
    tokens, model = query.qu.shape
    frames = tokens // rows
    factor = 1.0 / math.sqrt(DH)

    def body(k, acc, turned):
        g_table, vec, table = k.g_table, k.vec, k.table
        g_table[...] = jnp.zeros_like(g_table)
        vec[...] = jnp.zeros_like(vec)
        turn = flip(WIN)
        for row in range(rows):
            acc[...] = jnp.zeros_like(acc)
            for block in range(2):
                here = slice(WIN * block, WIN * (block + 1))
                span = slice(WIN * block, WIN * block + SPAN)
                turned[0] = dot(turn, k.gm[row][here]).astype(bf16)
                turned[1] = dot(turn, k.qu[row][here]).astype(bf16)
                turned[2] = dot(turn, k.qv[row][here]).astype(bf16)
                blocks = [k.lo[row], k.hi[row]]
                blocks = blocks + [k.next[row]] if block else [k.before[row]] + blocks
                prob = k.prob[2 * row + block]
                for group in range(GROUPS):
                    cut = slice(WIDE * group, WIDE * (group + 1))
                    cut_v = slice(model + WIDE * group, model + WIDE * (group + 1))
                    keys = jnp.concatenate([b[:, cut] for b in blocks], axis=0)
                    values = jnp.concatenate([b[:, cut_v] for b in blocks], axis=0)
                    weights = below(prob[group])
                    grad_mixed = heads_apart(turned[0, :, cut])
                    grad = dot_last(grad_mixed, values)
                    wide = weights.astype(f32)
                    delta = jnp.sum(wide * grad, axis=1, keepdims=True)
                    raw = (wide * (grad - delta)).astype(bf16)
                    acc[span, cut_v] += dot_first(weights, grad_mixed)
                    acc[span, cut] += dot_first(raw, heads_apart(turned[1, :, cut]))
                    grad_u = heads_joined(dot(raw, keys)) * factor
                    band = pltpu.roll(
                        raw.astype(f32).reshape(MANY, WIN, SPAN),
                        SPAN - (WIN - 1),
                        2,
                        stride=1,
                        stride_axis=1,
                    )
                    band = band.astype(bf16).reshape(MANY * WIN, SPAN)
                    grad_v = heads_joined(dot(band, table[:, cut])) * factor
                    g_table[:, cut] += dot_first(band, heads_apart(turned[2, :, cut]))
                    vec[0:1, cut] += total(grad_u)
                    vec[1:2, cut] += total(grad_v)
                    both = (grad_u + grad_v).astype(bf16)
                    k.gq[row][here, cut] = dot(turn, both).astype(bf16)
                if block == 0:
                    k.g_before[row] = acc[0:WIN].astype(bf16)
                    k.send(k.g_before, row)
            k.g_after[row] = acc[3 * WIN :].astype(bf16)
            k.send(k.g_after, row)
            k.g_lo[row][...] = acc[WIN : 2 * WIN]
            k.send(k.g_lo[row])
            k.g_hi[row][...] = acc[2 * WIN : 3 * WIN]
            k.send(k.g_hi[row])
            k.send(k.gq[row])

    ins = dict(
        gm=by_row(gm, rows), qu=by_row(query.qu, rows), qv=by_row(query.qv, rows),
        before=each_of(before), lo=each_of(start.lo), hi=each_of(start.hi),
        prob=[
            slab(prob, block, (0, GROUPS), (0, WIN), (0, MANY * SPAN))
            for prob in probs
            for block in range(2)
        ],
        table=query.table, next=each_of(after),
    )
    kv = (WIN, 2 * model)
    return staged(
        "attend_back",
        body,
        ins,
        dict(
            gq=[sds((frames, model), bf16)] * rows, g_before=sds((rows,) + kv, bf16),
            g_lo=[sds(kv, f32)] * rows, g_hi=[sds(kv, f32)] * rows,
            g_after=sds((rows,) + kv, bf16), g_table=sds((SPAN, model), f32),
            vec=sds((8, model), f32),
        ),
        scratch=[
            pltpu.VMEM((4 * WIN, 2 * model), f32),
            pltpu.VMEM((3, WIN, model), bf16),
        ],
        flops=16 * 14 * 256 * 384 * 128,
        moved=16 << 20,
        sends=2 * rows - 2,
    )


def place_weights(info, core_at, n, grads, start, sinusoid):
    tokens, model = start.na.shape
    slim = model // n

    def body(k, info):
        core = info[core_at]
        pairs = (0, n // 2)
        rows = [ref[...] for ref in (k.gq[at] for at in range(len(grads.gq)))]
        block = dot_first(k.na[...], jnp.concatenate(rows, axis=0))
        keep_half(block, core, k.mine, k.other, pairs)
        high = k.g_table[...].astype(bf16)
        low = (k.g_table[...] - high.astype(f32)).astype(bf16)
        place = dot_first(k.sinusoid[...], high) + dot_first(k.sinusoid[...], low)
        keep_half(place, core, k.mine, k.other, pairs, slim)

    half = sds((n // 2, 2 * slim, model), bf16)
    return staged(
        "place_weights",
        body,
        dict(na=start.na, gq=list(grads.gq), g_table=grads.g_table, sinusoid=sinusoid),
        dict(mine=half, other=half),
        smem=[info],
        flops=2 * tokens * model * 2 * model,
        moved=4 << 20,
    )


def back(info, core_at, n, grads, halo, attend_in, start, gas, gain, placed):
    rows = len(grads.gq)
    tokens, model = start.after.shape
    frames = tokens // rows
    hidden = start.act.shape[1]
    parts = hidden // PART
    width, slim = hidden // n, model // n

    def body(k, info, joined):
        core = info[core_at]
        vec, gain = k.vec, k.gain
        sums = [0.0] * 5
        for row in range(rows):
            here = slice(row * frames, (row + 1) * frames)
            low_half = slice(row * frames, row * frames + WIN)
            high_half = slice(row * frames + WIN, (row + 1) * frames)
            joined[here, :model] = k.gq[row][...]
            pair = (k.g_lo[row][...] + k.left[row].astype(f32)).astype(bf16)
            joined[low_half, model:] = pair
            pair = (k.g_hi[row][...] + k.right[row].astype(f32)).astype(bf16)
            joined[high_half, model:] = pair
            both = joined[here]
            k.gv[here] = both[:, 2 * model :]
            sums[0] += total(both[:, :model].astype(f32))
            sums[1] += total(both[:, 2 * model :].astype(f32))
            grad = dot_last(both, k.attend_in[...])
            normal, inverse = normalize(k.after[row][...])
            grad, gain_grad, shift_grad = norm_back(grad, normal, inverse, gain[1:2])
            sums[2] += gain_grad
            sums[3] += shift_grad
            grad = k.gas[row][...] + grad
            k.gfs[row][...] = grad
            k.send(k.gfs[row])
            low = (0.5 * grad).astype(bf16)
            k.gl[here] = low
            sums[4] += total(low.astype(f32))
        k.send(k.gv)
        k.send(k.gl)
        for at in range(5):
            vec[at : at + 1] = sums[at]
        pairs = (0, n // 2)
        block = dot_first(k.na[...], joined[:, model : 2 * model])
        keep_half(block, core, k.mine, k.other, pairs, width + slim)
        for mine, placed in ((k.mine, k.mine_placed), (k.other, k.other_placed)):
            mine[:, width : width + slim] = placed[:, :slim]
            mine[:, width + 2 * slim :] = placed[:, slim:]
        step = n // 2 // parts
        for part in range(parts):
            block = dot_first(k.act[part][...], k.gl[...])
            some = (part * step, (part + 1) * step)
            keep_half(block, core, k.mine, k.other, some)
            k.send(k.other, pl.ds(part * step, step))
            k.send(k.mine, pl.ds(part * step, step))

    half = sds((n // 2, width + 3 * slim, model), bf16)
    low = sds((tokens, model), bf16)
    return staged(
        "back",
        body,
        dict(
            gain=gain, gq=grads.gq, g_lo=grads.g_lo, g_hi=grads.g_hi, attend_in=attend_in, after=by_row(start.after, rows),
            gas=by_row(gas, rows), na=start.na, mine_placed=placed.mine, other_placed=placed.other,
            act=[slab(start.act, (0, tokens), (at, PART)) for at in range(0, hidden, PART)],
        ),
        dict(
            other=half, mine=half, gv=low, gl=low, gfs=[sds((frames, model), f32)] * rows,
            vec=sds((8, model), f32),
        ),
        smem=[info],
        scratch=[pltpu.VMEM((tokens, 3 * model), bf16)],
        kept=dict(left=halo[0], right=halo[1]),
        flops=2 * tokens * model * (hidden + 6 * model),
        moved=18 << 20,
        sends=2 * parts - 2,
    )


def keep_half(block, core, mine_ref, other_ref, rows, at=0):
    model = mine_ref.shape[2]
    pairs = rows[1] - rows[0]
    size = block.shape[0] // (2 * pairs)
    shaped = block.reshape(pairs, 2, size, model)
    even, odd = shaped[:, 0], shaped[:, 1]
    here = slice(*rows)
    mine_ref[here, at : at + size] = jnp.where(core == 0, even, odd).astype(bf16)
    other_ref[here, at : at + size] = jnp.where(core == 0, odd, even).astype(bf16)


def first_back(info, core_at, n, gl, feed_in, feed_out, start, gv):
    tokens, hidden = start.slope.shape
    model = gl.shape[1]
    parts = hidden // PART

    def body(k, info):
        core = info[core_at]
        step = n // 2 // parts
        back = 0.0
        block = dot_first(k.na[...], k.gv[...])
        keep_half(block, core, k.mine, k.other, (0, n // 2), hidden // n)
        for part in range(parts):
            cut = slice(part * PART, (part + 1) * PART)
            grad = dot_last(k.gl[...], k.w_out[part][...])
            grad = (grad * k.slope[part][...].astype(f32)).astype(bf16)
            put_rows(k.fb, part, total(grad.astype(f32)))
            block = dot_first(grad, k.n0[...])
            some = (part * step, (part + 1) * step)
            keep_half(block, core, k.mine, k.other, some)
            k.send(k.other, pl.ds(part * step, step))
            k.send(k.mine, pl.ds(part * step, step))
            back = back + dot_last(grad, k.w_in[part][...])
        k.gn[...] = back

    half = sds((n // 2, hidden // n + model // n, model), bf16)
    w_in, w_out = feed_slabs(feed_in, feed_out, 0)
    return staged(
        "first_back",
        body,
        dict(
            na=start.na, gv=gv, gl=gl, w_out=w_out,
            slope=[slab(start.slope, (0, tokens), (at, PART)) for at in range(0, hidden, PART)],
            n0=start.n0, w_in=w_in,
        ),
        dict(other=half, mine=half, fb=sds((hidden // model, model), f32), gn=sds((tokens, model), f32)),
        smem=[info],
        flops=2 * tokens * model * hidden * 3,
        moved=12 << 20,
        sends=2 * parts - 2,
    )


def last(features, gn, gfs, gain):
    rows, frames, model = features.shape

    def body(k):
        gain_grads, shift_grads = 0.0, 0.0
        for row in range(rows):
            here = slice(row * frames, (row + 1) * frames)
            normal, inverse = normalize(k.x[row][...].astype(f32))
            grad = k.gn[row][...]
            grad, gain_grad, shift_grad = norm_back(grad, normal, inverse, k.gain[0:1])
            k.out[row] = k.gfs[row][...] + grad
            k.send(k.out, row)
            gain_grads += gain_grad
            shift_grads += shift_grad
        k.vec[0:1] = gain_grads
        k.vec[1:2] = shift_grads

    ins = dict(
        gain=gain, x=[slab(features, row, (0, frames), (0, model)) for row in range(rows)],
        gn=[slab(gn, (row * frames, frames), (0, model)) for row in range(rows)], gfs=list(gfs),
    )
    return staged(
        "last",
        body,
        ins,
        dict(out=sds(features.shape, f32), vec=sds((8, model), f32)),
        flops=rows * frames * model * 20,
        moved=4 << 20,
        sends=rows - 1,
        limit=FOLD_LIMIT,
    )


def feed_weights(n, gi, nf, act, gl):
    tokens, model = nf.shape
    hidden = gi.shape[1]
    parts = hidden // PART
    size, slim = hidden // n, model // n
    step = n // parts
    room = 2 * slim if slim % 8 == 0 else 0

    def body(k):
        for part in range(parts):
            here = slice(part * step, (part + 1) * step)
            block = dot_first(k.gi[part][...], k.nf[...]).astype(bf16)
            k.out[here, :, :model] = block.reshape(step, size, model)
            block = dot_first(k.act[part][...], k.gl[...]).astype(bf16)
            k.out[here, :, model:] = block.reshape(step, size, model)
            k.send(k.out, pl.ds(part * step, step))

    ins = dict(
        nf=nf, gi=[slab(gi, (0, tokens), (at, PART)) for at in range(0, hidden, PART)], gl=gl,
        act=[slab(act, (0, tokens), (at, PART)) for at in range(0, hidden, PART)],
    )
    own = (n, size, 2 * model)
    shape = sds((n, size + room, 2 * model), bf16)
    return staged(
        "feed_weights",
        body,
        ins,
        dict(out=(shape, lambda ref: ref.at[:, pl.ds(0, size)] if room else ref, own)),
        flops=4 * tokens * model * hidden,
        moved=10 << 20,
        sends=parts - 1,
    ).out


def neighbours(last_block, first_block):
    devices = lax.axis_size("frames")
    up = [(i, i + 1) for i in range(devices - 1)]
    down = [(i + 1, i) for i in range(devices - 1)]
    return lax.ppermute(last_block, "frames", up), lax.ppermute(first_block, "frames", down)


def gather(copies):
    return lax.all_to_all(copies, DEVICES, 0, 0, tiled=True)


def scatter_sum(grads):
    return lax.psum_scatter(grads, "frames", scatter_dimension=0, tiled=True)


ROW_PAIR = [(0, 1), (1, 0)]
COLUMNS, IN_FLOAT = 1, 2
N_VECTORS = KERNEL + 5 + 5 + 10


def swap(x, k):
    n = lax.axis_size("frames")
    return lax.ppermute(x, "frames", [(i, i ^ k) for i in range(n)])


def swaps(sends, group):
    k, size = group
    return [swap(send, k * one) for one, send in zip(range(1, size), sends)]


def fold(name, info, row_at, states, small=None):
    mines, gots, keeps, sends, plans = [], [], [], [], []
    for mine, got, how in states:
        size, height, model = mine.shape
        if isinstance(how, tuple):
            _, place, digits = how
            view = (size // (digits * place), digits, place, height, model)
            half = (view[0], place, height, model)
        else:
            view = mine.shape
            half = (size, height, model // 2) if how == COLUMNS else mine.shape
        n_sends = how[2] - 1 if isinstance(how, tuple) else int(how == COLUMNS)
        plans.append((len(gots), len(got), len(sends), n_sends, how))
        mines.append(mine.reshape(view))
        gots += [one.reshape(view) for one in got]
        keeps.append(sds(half, f32 if how == IN_FLOAT else bf16))
        sends += [sds(half, bf16)] * n_sends

    n_small = 0 if small is None else len(small)

    def body(info, *refs):
        cuts = [len(mines), len(gots), n_small, len(keeps), len(sends)]
        taken, at = [], 0
        for cut in cuts:
            taken.append(refs[at : at + cut])
            at += cut
        mine_refs, got_refs, small_refs, keep_refs, send_refs = taken
        for at, (got_at, n_got, send_at, _, how) in enumerate(plans):
            parts = [mine_refs[at], *got_refs[got_at : got_at + n_got]]

            def added(*index):
                return sum(part[index].astype(f32) for part in parts)

            keep = keep_refs[at]
            if how is None or how == IN_FLOAT:
                keep[...] = added(...).astype(keep.dtype)
            elif how == COLUMNS:
                half = keep.shape[2]
                both = [
                    added(slice(None), slice(None), slice(one * half, (one + 1) * half))
                    for one in range(2)
                ]
                first = info[row_at] == 0
                send_refs[send_at][...] = jnp.where(first, both[1], both[0]).astype(bf16)
                keep[...] = jnp.where(first, both[0], both[1]).astype(bf16)
            else:
                digit = info[how[0]]
                for one in range(1, how[2]):
                    other = digit
                    for bit in (1, 2):
                        if one & bit:
                            other = other + bit * (1 - 2 * ((digit // bit) % 2))
                    send_refs[send_at + one - 1][...] = added(slice(None), other).astype(bf16)
                keep[...] = added(slice(None), digit).astype(bf16)
        if n_small:
            refs[-1][...] = sum(one[...] for one in small_refs)

    shapes = keeps + sends + ([sds(small[0].shape, f32)] if n_small else [])
    here = pl.BlockSpec(memory_space=pltpu.VMEM)
    given = mines + gots + (list(small) if n_small else [])
    got = pl.pallas_call(
        body,
        in_specs=[pl.BlockSpec(memory_space=pltpu.SMEM)] + [here] * len(given),
        out_specs=[here] * len(shapes),
        out_shape=shapes,
        compiler_params=pltpu.CompilerParams(vmem_limit_bytes=FOLD_LIMIT),
        cost_estimate=pl.CostEstimate(flops=1 << 20, bytes_accessed=2 << 20, transcendentals=0),
        name=name,
    )(info, *given)
    kept, away = got[: len(keeps)], got[len(keeps) : len(keeps) + len(sends)]
    results = []
    for at, (mine, _, how) in enumerate(states):
        size, height, model = mine.shape
        shape = (size // how[2], height, model) if isinstance(how, tuple) else kept[at].shape
        _, _, send_at, n_sends, _ = plans[at]
        some = [one.reshape(shape) for one in away[send_at : send_at + n_sends]]
        results.append((kept[at].reshape(shape), some))
    if n_small:
        results.append(got[-1])
    return results


def finish(info, row_at, frames, a, b, b_got, early, small, totals, width, slim):
    model = a.shape[1]
    feed_rows = small[0].shape[0] - N_VECTORS
    per = feed_rows // 2

    def body(info, a, b, b_got, early, totals, *refs):
        sums, refs = refs[: len(small)], refs[len(small) :]
        feed_in, feed_out, joined, attend, place, con_in, con_out, *refs = refs
        depth, gain, shift, bias, feed_bias, vectors = refs
        feed_in[0] = a[:width].T
        feed_in[1] = early[:width, :model].T
        first = info[row_at] == 0
        one, two = b[...].astype(f32), b_got[...].astype(f32)
        whole = jnp.concatenate([jnp.where(first, one, two), jnp.where(first, two, one)], axis=1)
        feed_out[0] = whole[:width]
        feed_out[1] = early[:width, model:]
        joined[:, :model] = whole[width : width + slim]
        joined[:, model : 2 * model] = whole[width + slim : width + 2 * slim]
        joined[:, 2 * model :] = a[width:]
        place[...] = whole[width + 2 * slim :]
        con_in[...] = early[width : width + slim]
        con_out[...] = early[width + slim :, :model]
        attend[...] = early[width + slim :, model:]
        me = info[0] // frames
        end = N_VECTORS + feed_rows
        vectors[end:] = jnp.zeros((vectors.shape[0] - end, model), f32)
        vectors[:end] = sum(one[...] for one in sums)
        vectors[end : end + 2] = totals[...]
        own = pltpu.roll(vectors[...], lax.rem(model - me * slim, model), 1)[:, :slim]
        depth[...] = own[:KERNEL]
        gain[0:5] = own[KERNEL : KERNEL + 5]
        gain[5:6] = own[end + 1 : end + 2]
        shift[0:5] = own[KERNEL + 5 : KERNEL + 10]
        shift[5:6] = own[end : end + 1]
        bias[...] = own[KERNEL + 10 : N_VECTORS]
        at = me * width
        for module in range(2):
            row = vectors[pl.ds(N_VECTORS + module * per + at // model, 1), :]
            row = pltpu.roll(row, lax.rem(model - lax.rem(at, model), model), 1)
            feed_bias[module : module + 1] = row[:, :width]

    def full(shape):
        return pl.BlockSpec(shape, lambda i: (0,) * len(shape))

    shapes = [
        (2, model, width), (2, width, model), (slim, 3 * model), (slim, model), (slim, model),
        (slim, 2 * model), (slim, model), (KERNEL, slim), (6, slim), (6, slim), (10, slim),
        (2, width),
    ]
    given = (a, b, b_got, early, totals, *small)
    return pl.pallas_call(
        body,
        grid=(1,),
        in_specs=[pl.BlockSpec(memory_space=pltpu.SMEM)] + [full(one.shape) for one in given],
        out_specs=[full(shape) for shape in shapes],
        out_shape=[sds(shape, f32) for shape in shapes],
        scratch_shapes=[pltpu.VMEM((-(-(N_VECTORS + feed_rows + 2) // 8) * 8, model), f32)],
        compiler_params=pltpu.CompilerParams(vmem_limit_bytes=FOLD_LIMIT),
        name="finish",
    )(info, *given)


def per_device(
    features,
    lengths,
    windows,
    feed_in,
    feed_in_bias,
    feed_out,
    attend_in,
    attend_out,
    position_proj,
    convolve_in,
    convolve_out,
    depthwise,
    norm_gain,
    norm_shift,
    biases,
    cotangent,
):
    rows, frames, model = features.shape
    tokens = rows * frames
    n = lax.axis_size("frames")
    devices = lax.axis_size("rows") * n
    row_len = float(frames * n)
    me = lax.axis_index("frames")
    first_frame = me * frames
    hidden = feed_in.shape[2]
    ends_every = jnp.cumsum(lengths, axis=1, dtype=jnp.int32)
    ends_here = lax.dynamic_slice_in_dim(ends_every, lax.axis_index("rows") * rows, rows, 0)
    slots = ends_here.shape[1]
    ends = jnp.pad(
        ends_here.astype(f32), ((0, 8 - rows), (0, -slots % 128)), constant_values=row_len
    )
    groups, k = [(2, 2)], 4
    while k < n:
        groups.append((k, min(4, n // k)))
        k *= groups[-1][1]
    places = [lax.axis_index("rows"), me % 2] + [(me // k) % size for k, size in groups]
    info = jnp.concatenate(
        [first_frame[None].astype(jnp.int32), windows, ends_here[:, -1], jnp.stack(places)]
    )
    row_at = 1 + 2 * rows
    core_at = row_at + 1
    starts = jnp.arange(n, dtype=jnp.int32) * frames
    counts = jnp.clip(ends_every[:, -1][:, None] - starts[None, :], 0, frames)
    counts = jnp.sum(counts.reshape(-1, rows, n), axis=1).astype(f32).reshape(devices, 1)
    counts = jnp.broadcast_to(counts, (devices, 128))
    sinusoid = jnp.asarray(position_table(WIN, model))

    start = front(
        features, feed_in, feed_in_bias, feed_out, attend_in, norm_gain, norm_shift, biases
    )
    before, after = neighbours(start.hi, start.lo)
    query = queries(start.na, attend_in, biases, sinusoid, position_proj)
    mix = attend(
        row_len, info, ends, start, query, before, after, attend_out, convolve_in, norm_gain,
        norm_shift, biases,
    )
    rim_before, rim_after = neighbours(mix.last, mix.first)
    got = depth_conv(row_len, devices, info, ends, mix.gated, rim_before, rim_after, depthwise)
    mid = middle(
        devices, rows, info, gather(got.stats), counts, got.depth, mix.out, feed_in,
        feed_in_bias, feed_out, convolve_out, norm_gain, norm_shift, biases,
        cotangent.reshape(tokens, model),
    )
    edge_before, edge_after = neighbours(mid.last, mid.first)
    totals = gather(mid.totals)
    early = feed_weights(n, mid.gi, mid.nf, mid.act, mid.gl)
    totals, early = lax.optimization_barrier((totals, early))
    conv = conv_back(
        row_len, n, info, ends, depthwise, convolve_in, attend_out, norm_gain, totals, mid,
        edge_before, edge_after, rim_before, rim_after, mix, early,
    )
    early, gm = lax.optimization_barrier((conv.early, conv.gm))
    early = scatter_sum(early)
    grads = attend_back(start, query, before, after, mix.prob, gm)
    halo = neighbours(grads.g_after, grads.g_before)
    placed = place_weights(info, core_at, n, grads, start, sinusoid)
    end = back(info, core_at, n, grads, halo, attend_in, start, conv.gas, norm_gain, placed)
    b, b_got = end.mine, [swap(end.other, 1)]
    got = first_back(info, core_at, n, end.gl, feed_in, feed_out, start, end.gv)
    a, a_got = got.mine, [swap(got.other, 1)]
    ((b, b_send),) = fold("fold_b", info, row_at, [(b, b_got, COLUMNS)])
    b_got = [lax.ppermute(b_send[0], "rows", ROW_PAIR)]
    ((a, a_send),) = fold("fold_a", info, row_at, [(a, a_got, (core_at + 1, 1, 2))])
    a_got = swaps(a_send, groups[0])
    gn, a = lax.optimization_barrier((got.gn, a))
    ending = last(features, gn, end.gfs, norm_gain)

    vec_conv, vec_mid, vec_back, vec_last = conv.vec, mid.vec, end.vec, ending.vec
    small = jnp.concatenate(
        [
            vec_conv[:KERNEL],
            vec_last[0:1], vec_back[2:3], vec_conv[9:10], vec_mid[0:1], vec_mid[2:3],
            vec_last[1:2], vec_back[3:4], vec_conv[10:11], vec_mid[1:2], vec_mid[3:4],
            vec_back[0:2], vec_conv[13:14], vec_conv[11:13], vec_mid[4:5], vec_back[4:5],
            vec_mid[5:6], grads.vec[0:2],
            got.fb, mid.fb,
        ],
        axis=0,
    )
    small = [small] + swaps([small] * 3, (1, 4))
    last_group = groups[-1]
    for at, group in enumerate(groups):
        deeper = at + 1 < len(groups)
        a_how = (core_at + 2 + at, 1, groups[at + 1][1]) if deeper else None
        states = [(a, a_got, a_how), (b, b_got, (core_at + 1 + at, 1, group[1]))]
        (a, a_send), (b, b_send), one = fold(f"fold_{at}", info, row_at, states, small)
        if deeper:
            a_got = swaps(a_send, groups[at + 1])
        else:
            early, a = lax.optimization_barrier((early, a))
            a_got = [lax.ppermute(a, "rows", ROW_PAIR)]
            early_got = [lax.ppermute(early, "rows", ROW_PAIR)]
        b_got = swaps(b_send, group)
        if at == 0:
            small = [one, lax.ppermute(one, "rows", ROW_PAIR)]
        elif deeper:
            small = [one] + swaps([one] * (group[1] - 1), group)
    states = [(b, b_got, None), (a, a_got, IN_FLOAT), (early, early_got, IN_FLOAT)]
    (b, _), (a, _), (early, _) = fold("fold_last", info, row_at, states)
    b_got = lax.ppermute(b, "rows", ROW_PAIR)
    small = [one] + swaps([one] * (last_group[1] - 1), last_group)
    slim = model // n
    width = hidden // n
    feed_in_grad, feed_out_grad, joined, *rest, depth, gain, shift, bias, feed_bias = finish(
        info, row_at, frames, a[0], b[0], b_got[0], early[0], small, vec_conv[14:16], width, slim
    )
    return (
        mid.out.reshape(rows, frames, model),
        ending.out,
        feed_in_grad,
        feed_bias,
        feed_out_grad,
        joined,
        *rest,
        depth,
        gain,
        shift,
        bias,
    )


def solution(mesh):
    placed = (
        P("rows", "frames", None),
        P(),
        P("rows"),
        P(),
        P(),
        P(),
        P(),
        P(),
        P(),
        P(),
        P(),
        P(),
        P(),
        P(),
        P(),
        P("rows", "frames", None),
    )
    return jax.shard_map(
        per_device,
        mesh=mesh,
        in_specs=placed,
        out_specs=(
            P("rows", "frames", None),
            P("rows", "frames", None),
            P(None, None, "frames"),
            P(None, "frames"),
            P(None, "frames", None),
            P("frames", None),
            P("frames", None),
            P("frames", None),
            P("frames", None),
            P("frames", None),
            P(None, "frames"),
            P(None, "frames"),
            P(None, "frames"),
            P(None, "frames"),
        ),
        check_vma=False,
    )
```

```python
import functools
import math
import types

import jax
import jax.numpy as jnp
import ml_dtypes
import numpy as np
from jax import lax
from jax.experimental import pallas as pl
from jax.experimental.pallas import tpu as pltpu
from jax.sharding import PartitionSpec as P

H = 8
DH = 64
KERNEL = 9
WIN = 128

HALF = KERNEL // 2
SPAN = 3 * WIN
MANY = 4
GROUPS = H // MANY
WIDE = MANY * DH
RIM = 16
RIM_GRAD = 8
eps_norm = 1e-05
negative = -1e30
f32 = jnp.float32
bf16 = jnp.bfloat16
DEVICES = ("rows", "frames")
VMEM_LIMIT = 60 * 1024 * 1024
FOLD_LIMIT = 14 * 1024 * 1024


def dot(left, right):
    return jnp.dot(left, right, preferred_element_type=f32)


def dot_last(left, right):
    return lax.dot_general(left, right, (((1,), (1,)), ((), ())), preferred_element_type=f32)


def dot_first(left, right):
    return lax.dot_general(left, right, (((0,), (0,)), ((), ())), preferred_element_type=f32)


def sigmoid(x):
    return 0.5 * jnp.tanh(0.5 * x) + 0.5


def total(x):
    return jnp.sum(x, axis=0, keepdims=True)


def normalize(values):
    centered = values - jnp.mean(values, axis=-1, keepdims=True)
    inverse = lax.rsqrt(jnp.mean(centered * centered, axis=-1, keepdims=True) + eps_norm)
    return centered * inverse, inverse


def norm_back(grad_out, normal, inverse, gain):
    scaled = grad_out * gain
    centred = scaled - jnp.mean(scaled, axis=-1, keepdims=True)
    grad_in = inverse * (centred - normal * jnp.mean(scaled * normal, axis=-1, keepdims=True))
    return grad_in, total(grad_out * normal), total(grad_out)


def position_table(width, model):
    offsets = (np.arange(2 * width + 1) - width).astype(np.float32)
    rates = np.exp(
        np.arange(model // 2).astype(np.float32) * np.float32(-2.0 * math.log(10000.0) / model)
    )
    angles = (offsets[:, None] * rates[None, :]).astype(np.float32)
    both = np.stack([np.sin(angles), np.cos(angles)], axis=2).reshape(2 * width + 1, model)
    padded = np.zeros((3 * width, model), np.float32)
    padded[: 2 * width + 1] = both
    return padded.astype(ml_dtypes.bfloat16)


def bounds(ends, at, row_len):
    low = jnp.max(jnp.where(ends <= at, ends, 0.0), axis=1, keepdims=True)
    high = jnp.min(jnp.where(ends > at, ends, row_len), axis=1, keepdims=True)
    return low, high


def column(count, offset):
    return lax.broadcasted_iota(jnp.int32, (count, 1), 0).astype(f32) + offset


def head_lanes(rows):
    return lax.broadcasted_iota(jnp.int32, (rows, WIDE), 1) // DH


def heads_apart(group):
    at = head_lanes(group.shape[0])
    zero = jnp.zeros_like(group)
    return jnp.concatenate([jnp.where(at == k, group, zero) for k in range(MANY)], axis=0)


def heads_joined(stacked):
    rows = stacked.shape[0] // MANY
    at = head_lanes(rows)
    joined = stacked[:rows]
    for k in range(1, MANY):
        joined = jnp.where(at == k, stacked[k * rows : (k + 1) * rows], joined)
    return joined


def beside(stacked):
    rows = stacked.shape[0] // MANY
    return jnp.concatenate([stacked[k * rows : (k + 1) * rows] for k in range(MANY)], axis=1)


def below(joined):
    width = joined.shape[1] // MANY
    return jnp.concatenate([joined[:, k * width : (k + 1) * width] for k in range(MANY)], axis=0)


def windows(width):
    return [slice(at, at + WIN) for at in range(0, width, WIN)]


def flip(rows):
    i = lax.broadcasted_iota(jnp.int32, (rows, rows), 0)
    j = lax.broadcasted_iota(jnp.int32, (rows, rows), 1)
    return (i + j == rows - 1).astype(f32).astype(bf16)


class Load:
    def __init__(self, source, buffer, sem):
        self.buffer, self.waited = buffer, False
        self.copy = pltpu.make_async_copy(source, buffer, sem)
        self.copy.start()

    def ready(self):
        if not self.waited:
            self.copy.wait()
            self.waited = True
        return self.buffer


class Loads:
    def __init__(self, items):
        self.items = items

    def __getitem__(self, at):
        return self.items[at].ready()


class Stage:
    def __init__(self, loads, stores, sems):
        self.sems, self.used, self.pending, self.targets = sems, 0, [], []
        self.named, self.all_loads = {}, []
        while loads:
            run = [loads.pop(0)]
            while not run[0][2] and loads and len(loads[0][1]) == len(run[0][1]) > 1:
                run.append(loads.pop(0))
            items = [[] for _ in run]
            for at in range(len(run[0][1])):
                for (_, pairs, _), own in zip(run, items):
                    source, buffer = pairs[at]
                    own.append(Load(source, buffer, self.sem()))
            for (name, _, single), own in zip(run, items):
                self.all_loads += own
                self.named[name] = own[0] if single else Loads(own)
        for name, pairs, single in stores:
            self.targets += [[target, buffer, False] for target, buffer in pairs]
            buffers = [buffer for _, buffer in pairs]
            self.named[name] = buffers[0] if single else buffers

    def sem(self):
        self.used += 1
        return self.sems.at[self.used - 1]

    def __getattr__(self, name):
        found = self.named[name]
        return found.ready() if isinstance(found, Load) else found

    def send(self, buffer, at=None):
        entry = next(entry for entry in self.targets if entry[1] is buffer)
        target = entry[0]
        entry[2] = True
        if at is not None:
            target, buffer = target.at[at], buffer.at[at]
        copy = pltpu.make_async_copy(buffer, target, self.sem())
        copy.start()
        self.pending.append(copy)

    def finish(self):
        for _, buffer, sent in self.targets:
            if not sent:
                self.send(buffer)
        for load in self.all_loads:
            load.ready()
        for copy in self.pending:
            copy.wait()


def staged(
    name, body, ins, outs, smem=(), scratch=(), flops=0, moved=0, sends=0, filled=None,
    limit=VMEM_LIMIT, kept=None,
):
    operands, loads, stores, kept = [], [], [], kept or {}
    for key, items in ins.items():
        single = not isinstance(items, list)
        entries = []
        for item in [items] if single else items:
            array, view, shape = item if isinstance(item, tuple) else (item, None, item.shape)
            at = next((i for i, other in enumerate(operands) if other is array), None)
            if at is None:
                at = len(operands)
                operands.append(array)
            entries.append((at, view, shape, array.dtype))
        loads.append((key, entries, single))
    for key, items in outs.items():
        single = not isinstance(items, list)
        entries = [
            item if isinstance(item, tuple) else (item, None, item.shape)
            for item in ([items] if single else items)
        ]
        stores.append((key, entries, single))
    aliases = {}
    if filled is not None:
        aliases = {len(smem) + len(kept) + len(operands): 0}
        operands.append(filled)
    every_load = [entry for _, entries, _ in loads for entry in entries]
    every_store = [entry for _, entries, _ in stores for entry in entries]
    n_smem, n_ops, n_outs, n_loads = len(smem), len(operands), len(every_store), len(every_load)

    def run(*refs):
        cuts = [n_smem, len(kept), n_ops, n_outs, n_loads, n_outs, 1]
        taken, at = [], 0
        for cut in cuts:
            taken.append(refs[at : at + cut])
            at += cut
        scalars, here, given, targets, buffers, results, sems = taken
        buffers, places = iter(buffers), iter(zip(targets, results))
        placed_loads = [
            (
                key,
                [(given[i] if view is None else view(given[i]), next(buffers)) for i, view, _, _ in entries],
                single,
            )
            for key, entries, single in loads
        ]
        placed_stores = []
        for key, entries, single in stores:
            pairs = []
            for _, view, _ in entries:
                target, result = next(places)
                pairs.append((target if view is None else view(target), result))
            placed_stores.append((key, pairs, single))
        stage = Stage(placed_loads, placed_stores, sems[0])
        stage.named.update(zip(kept, here))
        body(stage, *scalars, *refs[at:])
        stage.finish()

    hbm = pl.BlockSpec(memory_space=pl.ANY)
    got = iter(
        pl.pallas_call(
            run,
            in_specs=[pl.BlockSpec(memory_space=pltpu.SMEM)] * n_smem
            + [pl.BlockSpec(memory_space=pltpu.VMEM)] * len(kept)
            + [hbm] * n_ops,
            out_specs=[hbm] * n_outs,
            out_shape=[shape for shape, _, _ in every_store],
            scratch_shapes=[pltpu.VMEM(shape, dtype) for _, _, shape, dtype in every_load]
            + [pltpu.VMEM(shape, whole.dtype) for whole, _, shape in every_store]
            + [pltpu.SemaphoreType.DMA((n_loads + n_outs + sends,))]
            + list(scratch),
            input_output_aliases=aliases,
            compiler_params=pltpu.CompilerParams(vmem_limit_bytes=limit),
            cost_estimate=pl.CostEstimate(flops=flops, bytes_accessed=moved, transcendentals=0),
            name=name,
        )(*smem, *kept.values(), *operands)
    )
    result = types.SimpleNamespace()
    for key, entries, single in stores:
        values = [next(got) for _ in entries]
        setattr(result, key, values[0] if single else values)
    return result


def sds(shape, dtype):
    return jax.ShapeDtypeStruct(shape, dtype)


def slab(array, *at):
    shape = tuple(a[1] for a in at if isinstance(a, tuple))
    index = tuple(pl.ds(*a) if isinstance(a, tuple) else a for a in at)
    return (array, lambda ref: ref.at[index], shape)


def by_row(array, rows):
    tokens, width = array.shape
    return [slab(array, (row * (tokens // rows), tokens // rows), (0, width)) for row in range(rows)]


def each_of(array):
    rows, size, width = array.shape
    return [slab(array, row, (0, size), (0, width)) for row in range(rows)]


PART = 1024


def activate(inner):
    half = 0.5 * inner
    turn = jnp.tanh(half)
    up = 1.0 + turn
    active = half * up
    return active, 0.5 * (up + active * (1.0 - turn))


def feed_slabs(feed_in, feed_out, module):
    _, model, hidden = feed_in.shape
    spans = [(part, PART) for part in range(0, hidden, PART)]
    w_in = [slab(feed_in, module, (0, model), span) for span in spans]
    w_out = [slab(feed_out, module, span, (0, model)) for span in spans]
    return w_in, w_out


def front(features, feed_in, feed_in_bias, feed_out, attend_in, gain, shift, bias):
    rows, frames, model = features.shape
    tokens = rows * frames
    hidden = feed_in.shape[2]
    parts = hidden // PART
    low = sds((tokens, model), bf16)

    def body(k):
        gain, shift = k.gain, k.shift
        x = k.x[...].reshape(tokens, model).astype(f32)
        normal, _ = normalize(x)
        k.n0[...] = (normal * gain[0:1] + shift[0:1]).astype(bf16)
        k.send(k.n0)
        for part in range(parts):
            cut = slice(part * PART, (part + 1) * PART)
            inner = dot(k.n0[...], k.w_in[part][...]) + k.b_in[0:1, cut]
            active, _ = activate(inner)
            k.act[:, cut] = active.astype(bf16)
        k.send(k.act)
        branch = k.bias[6:7]
        for part in range(parts):
            cut = slice(part * PART, (part + 1) * PART)
            branch = branch + dot(k.act[:, cut], k.w_out[part][...])
        after = x + 0.5 * branch
        k.after[...] = after
        k.send(k.after)
        normal, _ = normalize(after)
        normed = (normal * gain[1:2] + shift[1:2]).astype(bf16)
        k.na[...] = normed
        k.send(k.na)
        both = dot(normed, k.attend_in[...])
        keys = both[:, :model].astype(bf16)
        values = (both[:, model:] + k.bias[1:2]).astype(bf16)
        for row in range(rows):
            at = row * frames
            k.lo[row, :, :model] = keys[at : at + WIN]
            k.lo[row, :, model:] = values[at : at + WIN]
            k.hi[row, :, :model] = keys[at + WIN : at + frames]
            k.hi[row, :, model:] = values[at + WIN : at + frames]

    w_in, w_out = feed_slabs(feed_in, feed_out, 0)
    kv = sds((rows, WIN, 2 * model), bf16)
    return staged(
        "front",
        body,
        dict(
            x=features, gain=gain, shift=shift, b_in=feed_in_bias, w_in=w_in, bias=bias,
            w_out=w_out, attend_in=slab(attend_in, (0, model), (model, 2 * model)),
        ),
        dict(
            after=sds((tokens, model), f32), n0=low, na=low, lo=kv, hi=kv,
            act=sds((tokens, hidden), bf16),
        ),
        flops=2 * tokens * model * (2 * hidden + 2 * model),
        moved=16 << 20,
    )


def queries(start, feed_in, feed_in_bias, attend_in, bias, sinusoid, proj):
    tokens, model = start.na.shape
    hidden = feed_in.shape[2]
    parts = hidden // PART

    def body(k):
        query = dot(k.na[...], k.attend_in[...]) + k.bias[0:1]
        factor = 1.0 / math.sqrt(DH)
        k.qu[...] = ((query + k.bias[8:9]) * factor).astype(bf16)
        k.qv[...] = ((query + k.bias[9:10]) * factor).astype(bf16)
        k.send(k.qu)
        k.send(k.qv)
        k.table[...] = dot(k.sinusoid[...], k.proj[...]).astype(bf16)
        k.send(k.table)
        for part in range(parts):
            cut = slice(part * PART, (part + 1) * PART)
            inner = dot(k.n0[...], k.w_in[part][...]) + k.b_in[0:1, cut]
            _, slope = activate(inner)
            k.slope[:, cut] = slope.astype(bf16)

    low = sds((tokens, model), bf16)
    spans = [(at, PART) for at in range(0, hidden, PART)]
    w_in = [slab(feed_in, 0, (0, model), span) for span in spans]
    return staged(
        "queries",
        body,
        dict(
            na=start.na, attend_in=slab(attend_in, (0, model), (0, model)), bias=bias,
            sinusoid=sinusoid, proj=proj, n0=start.n0, b_in=feed_in_bias, w_in=w_in,
        ),
        dict(
            qu=low, qv=low, table=sds((SPAN, model), bf16), slope=sds((tokens, hidden), bf16)
        ),
        flops=2 * tokens * model * (hidden + 2 * model),
        moved=10 << 20,
    )


def attend(
    row_len, info, ends, start, query, before, after, attend_out, convolve_in, gain, shift, bias
):
    rows = before.shape[0]
    tokens, model = start.after.shape
    frames = tokens // rows
    low = sds((tokens, model), bf16)

    def body(k, info):
        first_frame = info[0].astype(f32)
        turn = flip(WIN)
        key_at = lax.broadcasted_iota(jnp.int32, (WIN, SPAN), 1).astype(f32)
        table = k.table
        ones = jnp.ones((SPAN, WIN), bf16)
        for row in range(rows):
            reach = info[1 + row].astype(f32)
            row_ends = k.ends[row : row + 1, :]
            for block in range(2):
                at = column(WIN, first_frame + WIN * block)
                lower, upper = bounds(row_ends, at, row_len)
                base = first_frame + (WIN * (block - 1))
                lower = jnp.maximum(lower, at - reach) - base
                upper = jnp.minimum(upper - 1.0, at + reach) - base
                allowed = ((key_at >= lower) & (key_at <= upper))[None]
                here = slice(row * frames + WIN * block, row * frames + WIN * (block + 1))
                some = [k.lo[row], k.hi[row]]
                some = some + [k.next[row]] if block else [k.before[row]] + some
                for group in range(GROUPS):
                    cut = slice(WIDE * group, WIDE * (group + 1))
                    cut_v = slice(model + WIDE * group, model + WIDE * (group + 1))
                    keys = jnp.concatenate([b[:, cut] for b in some], axis=0)
                    values = jnp.concatenate([b[:, cut_v] for b in some], axis=0)
                    spread = dot_last(heads_apart(k.qv[here, cut]), table[:, cut])
                    content = dot_last(heads_apart(k.qu[here, cut]), keys)
                    spread = pltpu.roll(
                        spread.reshape(MANY, WIN, SPAN), 0, 2, stride=1, stride_axis=1
                    )
                    scores = content.reshape(MANY, WIN, SPAN) + spread
                    scores = jnp.where(allowed, scores, negative)
                    powers = jnp.exp(scores - jnp.max(scores, axis=2, keepdims=True))
                    powers = powers.reshape(MANY * WIN, SPAN)
                    inverse = 1.0 / dot(powers.astype(bf16), ones)
                    weights = jnp.concatenate(
                        [powers[:, cut] * inverse for cut in windows(SPAN)], axis=1
                    ).astype(bf16)
                    k.mixed[here, cut] = heads_joined(dot(weights, values)).astype(bf16)
                    k.prob[row][block, group] = dot(turn, beside(weights)).astype(bf16)
            k.send(k.prob[row])
        k.send(k.mixed)
        after_attend = k.after[...] + dot(k.mixed[...], k.attend_out[...]) + k.bias[2:3]
        k.out[...] = after_attend
        k.send(k.out)
        normal, _ = normalize(after_attend)
        normed = (normal * k.gain[2:3] + k.shift[2:3]).astype(bf16)
        k.nc[...] = normed
        k.send(k.nc)
        paired = dot(normed, k.convolve_in[...])
        value = paired[:, :model] + k.bias[3:4]
        gate = paired[:, model:] + k.bias[4:5]
        sigma = sigmoid(gate)
        gated = value * sigma
        k.factors[:, :model] = sigma.astype(bf16)
        k.factors[:, model:] = (gated * (1.0 - sigma)).astype(bf16)
        k.send(k.factors)
        gated = gated.astype(bf16)
        k.gated[...] = gated
        for row in range(rows):
            k.first[row] = gated[row * frames : row * frames + RIM]
            k.last[row] = gated[(row + 1) * frames - RIM : (row + 1) * frames]

    rim = sds((rows, RIM, model), bf16)
    return staged(
        "attend",
        body,
        dict(
            ends=ends, table=query.table, qv=query.qv, qu=query.qu, lo=each_of(start.lo),
            hi=each_of(start.hi), before=each_of(before), next=each_of(after), after=start.after,
            attend_out=attend_out, bias=bias, gain=gain, shift=shift, convolve_in=convolve_in,
        ),
        dict(
            prob=[sds((2, GROUPS, WIN, MANY * SPAN), bf16)] * rows, mixed=low,
            out=sds((tokens, model), f32), nc=low, factors=sds((tokens, 2 * model), bf16),
            gated=low, first=rim, last=rim,
        ),
        smem=[info],
        flops=16 * 8 * 256 * 384 * 128,
        moved=16 << 20,
    )


def valid_column(info, row, rows, frames):
    at = column(frames, info[0].astype(f32))
    return (at < info[1 + rows + row].astype(f32)).astype(f32)


def put_rows(ref, part, vector):
    model = ref.shape[1]
    per = vector.shape[1] // model
    for one in range(per):
        at = part * per + one
        ref[at : at + 1] = vector[:, one * model : (one + 1) * model]


def pack(ref, vectors):
    at = 0
    for vector in vectors:
        for k in range(0, vector.shape[1], 128):
            ref[at : at + 1, :] = vector[:, k : k + 128]
            at += 1


def by_rows(count, size, step, init=None):
    def one(i, carry):
        return step(pl.ds(pl.multiple_of(i * size, size), size), carry)

    return lax.fori_loop(0, count // size, one, init)


def by_lanes(width, step):
    def one(i, carry):
        step(pl.ds(pl.multiple_of(i * 128, 128), 128))
        return carry

    lax.fori_loop(0, width // 128, one, 0)


def spread(column):
    return jnp.broadcast_to(column, (column.shape[0], 128))


def tap_masks(keep_s, at, low, high):
    for tap in range(KERNEL):
        off = tap - HALF
        keep_s[tap] = spread(((at + off >= low) & (at + off < high)).astype(f32))


def depth_conv(row_len, devices, info, ends, gated, before, after, taps):
    rows = before.shape[0]
    tokens, model = gated.shape
    frames = tokens // rows

    def body(k, info, rim, keep_s, valid_s, sums, tile):
        start = info[0].astype(f32)
        counts = 0.0
        taps = k.taps
        for row in range(rows):
            here = slice(row * frames, (row + 1) * frames)
            at = column(frames, start)
            low, high = bounds(k.ends[row : row + 1, :], at, row_len)
            tap_masks(keep_s, at, low, high)
            valid = valid_column(info, row, rows, frames)
            valid_s[here] = spread(valid)
            counts += total(valid)
            rim[0:RIM] = k.before[row].astype(f32)
            rim[RIM : RIM + frames] = k.gated[row][...].astype(f32)
            rim[RIM + frames :] = k.after[row].astype(f32)

            def one(lanes):
                depth = jnp.zeros((frames, 128), f32)
                for tap in range(KERNEL):
                    off = tap - HALF
                    part = rim[RIM + off : RIM + off + frames, lanes] * keep_s[tap]
                    depth += taps[tap : tap + 1, lanes] * part
                k.depth[here, lanes] = depth
                sums[row : row + 1, lanes] = total(depth * valid_s[here])

            by_lanes(model, one)
            k.send(k.depth, pl.ds(row * frames, frames))
        first = total(sums[0:rows, :])
        mean = first / jnp.maximum(counts, 1.0)
        sums[rows : rows + 1, :] = mean

        def two(lanes):
            centered = k.depth[:, lanes] - sums[rows : rows + 1, lanes]
            sums[rows + 1 : rows + 2, lanes] = total(centered * centered * valid_s[...])

        by_lanes(model, two)
        pack(tile, [first, sums[rows + 1 : rows + 2, :]])
        k.stats[...] = jnp.broadcast_to(tile[...][None], k.stats.shape)

    return staged(
        "depth_conv",
        body,
        dict(ends=ends, taps=taps, gated=by_row(gated, rows)),
        dict(depth=sds((rows * frames, model), f32), stats=sds((devices, 8, 128), f32)),
        smem=[info],
        scratch=[
            pltpu.VMEM((frames + 2 * RIM, model), f32),
            pltpu.VMEM((KERNEL, frames, 128), f32),
            pltpu.VMEM((rows * frames, 128), f32),
            pltpu.VMEM((8, model), f32),
            pltpu.VMEM((8, 128), f32),
        ],
        kept=dict(before=before, after=after),
        flops=rows * frames * model * 30,
        moved=2 << 20,
        sends=rows - 1,
    )


def middle(
    devices, rows, info, stats, counts, depth, stream, feed_in, feed_in_bias, feed_out,
    convolve_out, gain, shift, bias, cotangent,
):
    tokens, model = depth.shape
    frames = tokens // rows
    hidden = feed_in.shape[2]
    parts = hidden // PART

    def body(k, info, conv_s, bn_s, slope_s, tile):
        stats, each = k.stats, k.counts[:, 0:1]
        gain, shift, bias = k.gain, k.shift, k.bias
        count = total(each)
        means, inverses = [], []
        for at in range(model // 128):
            sums = stats[:, at, :]
            mean = total(sums) / count
            off = sums / jnp.maximum(each, 1.0) - mean
            spread = total(stats[:, model // 128 + at, :]) + total(each * off * off)
            means.append(mean)
            inverses.append(lax.rsqrt(spread / count + eps_norm))
        mean = jnp.concatenate(means, axis=1)
        inverse = jnp.concatenate(inverses, axis=1)
        k.inv[0:1] = inverse
        k.inv[1:2] = jnp.broadcast_to(1.0 / count, (1, model))
        normal = (k.depth[...] - mean) * inverse
        bn_s[...] = normal
        k.bn[...] = normal.astype(bf16)
        k.send(k.bn)
        batch = normal * gain[5:6] + shift[5:6]
        swished = (batch * sigmoid(batch)).astype(bf16)
        k.sw[...] = swished
        k.send(k.sw)
        after_conv = k.stream[...] + dot(swished, k.convolve_out[...]) + bias[5:6]
        conv_s[...] = after_conv
        normal, _ = normalize(after_conv)
        k.nf[...] = (normal * gain[3:4] + shift[3:4]).astype(bf16)
        k.send(k.nf)
        for part in range(parts):
            cut = slice(part * PART, (part + 1) * PART)
            inner = dot(k.nf[...], k.w_in[part][...]) + k.b_in[1:2, cut]
            active, slope = activate(inner)
            k.act[:, cut] = active.astype(bf16)
            slope_s[:, cut] = slope
        k.send(k.act)
        branch = bias[7:8]
        for part in range(parts):
            cut = slice(part * PART, (part + 1) * PART)
            branch = branch + dot(k.act[:, cut], k.w_out[part][...])
        normal, inverse = normalize(conv_s[...] + 0.5 * branch)
        valid = jnp.concatenate(
            [valid_column(info, row, rows, frames) for row in range(rows)], axis=0
        )
        k.out[...] = (valid * (normal * gain[4:5] + shift[4:5])).astype(bf16)
        k.send(k.out)
        grad = valid * k.cotangent[...].astype(f32)
        grad, gain_grad, shift_grad = norm_back(grad, normal, inverse, gain[4:5])
        k.gcs[...] = grad
        low = (0.5 * grad).astype(bf16)
        k.gl[...] = low
        k.send(k.gl)
        vec = k.vec
        vec[2:3] = gain_grad
        vec[3:4] = shift_grad
        vec[5:6] = total(low.astype(f32))
        back = 0.0
        for part in range(parts):
            cut = slice(part * PART, (part + 1) * PART)
            grad = (dot_last(k.gl[...], k.w_out[part][...]) * slope_s[:, cut]).astype(bf16)
            k.gi[:, cut] = grad
            put_rows(k.fb, part, total(grad.astype(f32)))
            back = back + dot_last(grad, k.w_in[part][...])
        k.send(k.gi)
        normal, inverse = normalize(conv_s[...])
        grad, gain_grad, shift_grad = norm_back(back, normal, inverse, gain[3:4])
        vec[0:1] = gain_grad
        vec[1:2] = shift_grad
        grad = k.gcs[...] + grad
        k.gcs[...] = grad
        k.send(k.gcs)
        low = grad.astype(bf16)
        k.gcl[...] = low
        k.send(k.gcl)
        vec[4:5] = total(low.astype(f32))
        bn = bn_s[...]
        batch = bn * gain[5:6] + shift[5:6]
        _, slope = activate(batch)
        grad = dot_last(low, k.convolve_out[...]) * slope
        k.gb[...] = grad.astype(bf16)
        k.send(k.gb)
        pack(tile, [total(grad), total(grad * bn)])
        k.totals[...] = jnp.broadcast_to(tile[...][None], k.totals.shape)
        k.send(k.totals)
        for row in range(rows):
            at, end = row * frames, (row + 1) * frames
            k.first[row, :, :model] = grad[at : at + RIM_GRAD]
            k.first[row, :, model:] = bn[at : at + RIM_GRAD]
            k.last[row, :, :model] = grad[end - RIM_GRAD : end]
            k.last[row, :, model:] = bn[end - RIM_GRAD : end]

    w_in, w_out = feed_slabs(feed_in, feed_out, 1)
    ins = dict(
        gain=gain, shift=shift, depth=depth, bias=bias,
        convolve_out=convolve_out, stream=stream, b_in=feed_in_bias, w_in=w_in,
        cotangent=cotangent, w_out=w_out,
    )
    low = sds((tokens, model), bf16)
    wide = sds((tokens, model), f32)
    rim = sds((rows, RIM_GRAD, 2 * model), f32)
    return staged(
        "middle",
        body,
        ins,
        dict(
            out=low, act=sds((tokens, hidden), bf16), gi=sds((tokens, hidden), bf16), nf=low,
            gl=low, sw=low, gcl=low, gcs=wide, gb=low, bn=low, inv=sds((8, model), f32),
            totals=sds((devices, 8, 128), f32), first=rim, last=rim, vec=sds((8, model), f32),
            fb=sds((hidden // model, model), f32),
        ),
        smem=[info],
        scratch=[
            pltpu.VMEM((tokens, model), f32),
            pltpu.VMEM((tokens, model), f32),
            pltpu.VMEM((tokens, hidden), f32),
            pltpu.VMEM((8, 128), f32),
        ],
        kept=dict(stats=stats, counts=counts),
        flops=2 * tokens * model * (4 * hidden + 2 * model),
        moved=24 << 20,
    )


def conv_back(
    row_len, n, info, ends, taps, convolve_in, attend_out, gain, totals, mid, edge_before,
    edge_after, rim_before, rim_after, mix, early,
):
    tokens, model = mid.gb.shape
    rows = rim_before.shape[0]
    frames = tokens // rows
    slim = model // n
    room = slim % 8 == 0

    def body(k, info, grads, rim, keep_s, gp, gal):
        start = info[0].astype(f32)
        parts = model // 128
        sums = [total(k.totals[:, at, :]) for at in range(2 * parts)]
        total_a = jnp.concatenate(sums[:parts], axis=1)
        total_b = jnp.concatenate(sums[parts:], axis=1)
        inverse, per_count = k.inv[0:1], k.inv[1:2]
        gain, taps, vec = k.gain, k.taps, k.vec
        own_scale = inverse * gain[5:6]
        share_a = own_scale * total_a * per_count
        share_b = own_scale * total_b * per_count
        vec[14:15] = total_a
        vec[15:16] = total_b
        vec[0:9] = jnp.zeros((9, model), f32)
        vec[9:14] = jnp.zeros((5, model), f32)

        def grad_of(grad, normal, valid):
            grad = grad * own_scale - valid * (share_a + normal * share_b)
            return grad.astype(bf16).astype(f32)

        for row in range(rows):
            first = row * frames
            last = info[1 + rows + row].astype(f32)
            at = column(frames, start)
            low, high = bounds(k.ends[row : row + 1, :], at, row_len)
            tap_masks(keep_s, at, low, high)
            before, after = k.edge_before, k.edge_after
            edge_at = column(RIM_GRAD, start - RIM_GRAD)
            grads[0:RIM_GRAD] = grad_of(
                before[row, :, :model], before[row, :, model:], (edge_at < last).astype(f32)
            )
            for step in range(0, frames, 32):
                here = slice(step, step + 32)
                at = column(32, start + step)
                grads[RIM_GRAD + step : RIM_GRAD + step + 32] = grad_of(
                    k.gb[row][here].astype(f32),
                    k.bn[row][here].astype(f32),
                    (at < last).astype(f32),
                )
            edge_at = column(RIM_GRAD, start + frames)
            grads[RIM_GRAD + frames :] = grad_of(
                after[row, :, :model], after[row, :, model:], (edge_at < last).astype(f32)
            )
            rim[0:RIM] = k.rim_before[row].astype(f32)
            rim[RIM : RIM + frames] = k.gated[row][...].astype(f32)
            rim[RIM + frames :] = k.rim_after[row].astype(f32)
            factors = k.factors[row]
            half = frames // 2

            def one(i, carry):
                lane = pl.multiple_of(i * 128, 128)
                lanes, gates = pl.ds(lane, 128), pl.ds(model + lane, 128)
                for base in range(0, frames, half):
                    own = grads[RIM_GRAD + base : RIM_GRAD + base + half, lanes]
                    grad = jnp.zeros((half, 128), f32)
                    for tap in range(KERNEL):
                        off = base + tap - HALF
                        keep = keep_s[tap, base : base + half]
                        part = own * (rim[RIM + off : RIM + off + half, lanes] * keep)
                        vec[tap : tap + 1, lanes] += total(part)
                        mirror = KERNEL - 1 - tap
                        part = grads[RIM_GRAD + off : RIM_GRAD + off + half, lanes] * keep
                        grad += taps[mirror : mirror + 1, lanes] * part
                    one = (grad * factors[base : base + half, lanes].astype(f32)).astype(bf16)
                    two = (grad * factors[base : base + half, gates].astype(f32)).astype(bf16)
                    here = slice(first + base, first + base + half)
                    gp[here, lanes] = one
                    gp[here, gates] = two
                    vec[11:12, lanes] += total(one.astype(f32))
                    vec[12:13, lanes] += total(two.astype(f32))
                return carry

            lax.fori_loop(0, model // 128, one, 0)
        grad = dot_last(gp[...], k.convolve_in[...])
        normal, inverse = normalize(k.after[...])
        grad, gain_grad, shift_grad = norm_back(grad, normal, inverse, gain[2:3])
        vec[9:10] = gain_grad
        vec[10:11] = shift_grad
        grad = k.gcs[...] + grad
        k.gas[...] = grad
        k.send(k.gas)
        low = grad.astype(bf16)
        gal[...] = low
        vec[13:14] = total(low.astype(f32))
        k.gm[...] = dot_last(gal[...], k.attend_out[...]).astype(bf16)
        k.send(k.gm)
        out = k.early
        out[:, :slim] = dot_first(k.nc[...], gp[...]).astype(bf16).reshape(n, slim, 2 * model)
        block = dot_first(k.sw[...], k.gcl[...]).astype(bf16)
        out[:, slim:, :model] = block.reshape(n, slim, model)
        block = dot_first(k.mixed[...], gal[...]).astype(bf16)
        out[:, slim:, model:] = block.reshape(n, slim, model)

    own = (n, 2 * slim, 2 * model)
    size = early.shape[1] - 2 * slim
    if room:
        out = (sds(early.shape, bf16), lambda ref: ref.at[:, pl.ds(size, 2 * slim)], own)
    else:
        out = sds(own, bf16)
    got = staged(
        "conv_back",
        body,
        dict(
            inv=mid.inv, gain=gain, ends=ends, taps=taps, rim_before=rim_before,
            rim_after=rim_after, gb=by_row(mid.gb, rows), bn=by_row(mid.bn, rows), gated=by_row(mix.gated, rows),
            factors=by_row(mix.factors, rows), convolve_in=convolve_in, after=mix.out, gcs=mid.gcs,
            attend_out=attend_out, nc=mix.nc, sw=mid.sw, gcl=mid.gcl, mixed=mix.mixed,
        ),
        dict(
            early=out, gas=sds((tokens, model), f32), gm=sds((tokens, model), bf16),
            vec=sds((16, model), f32),
        ),
        smem=[info],
        scratch=[
            pltpu.VMEM((frames + 2 * RIM_GRAD, model), f32),
            pltpu.VMEM((frames + 2 * RIM, model), f32),
            pltpu.VMEM((KERNEL, frames, 128), f32),
            pltpu.VMEM((tokens, 2 * model), bf16),
            pltpu.VMEM((tokens, model), bf16),
        ],
        kept=dict(totals=totals, edge_before=edge_before, edge_after=edge_after),
        flops=2 * tokens * model * 7 * model,
        moved=16 << 20,
        filled=early if room else None,
    )
    if not room:
        got.early = jnp.concatenate([early, got.early], axis=1)
    return got


def attend_back(start, query, before, after, probs, gm):
    rows = before.shape[0]
    tokens, model = query.qu.shape
    frames = tokens // rows
    factor = 1.0 / math.sqrt(DH)

    def body(k, acc, turned):
        g_table, vec, table = k.g_table, k.vec, k.table
        g_table[...] = jnp.zeros_like(g_table)
        vec[...] = jnp.zeros_like(vec)
        turn = flip(WIN)
        for row in range(rows):
            acc[...] = jnp.zeros_like(acc)
            for block in range(2):
                here = slice(WIN * block, WIN * (block + 1))
                span = slice(WIN * block, WIN * block + SPAN)
                turned[0] = dot(turn, k.gm[row][here]).astype(bf16)
                turned[1] = dot(turn, k.qu[row][here]).astype(bf16)
                turned[2] = dot(turn, k.qv[row][here]).astype(bf16)
                blocks = [k.lo[row], k.hi[row]]
                blocks = blocks + [k.next[row]] if block else [k.before[row]] + blocks
                prob = k.prob[row]
                for group in range(GROUPS):
                    cut = slice(WIDE * group, WIDE * (group + 1))
                    cut_v = slice(model + WIDE * group, model + WIDE * (group + 1))
                    keys = jnp.concatenate([b[:, cut] for b in blocks], axis=0)
                    values = jnp.concatenate([b[:, cut_v] for b in blocks], axis=0)
                    weights = below(prob[block, group])
                    grad_mixed = heads_apart(turned[0, :, cut])
                    grad = dot_last(grad_mixed, values)
                    wide = weights.astype(f32)
                    delta = jnp.sum(wide * grad, axis=1, keepdims=True)
                    raw = (wide * (grad - delta)).astype(bf16)
                    acc[span, cut_v] += dot_first(weights, grad_mixed)
                    acc[span, cut] += dot_first(raw, heads_apart(turned[1, :, cut]))
                    grad_u = heads_joined(dot(raw, keys)) * factor
                    band = pltpu.roll(
                        raw.astype(f32).reshape(MANY, WIN, SPAN),
                        SPAN - (WIN - 1),
                        2,
                        stride=1,
                        stride_axis=1,
                    )
                    band = band.astype(bf16).reshape(MANY * WIN, SPAN)
                    grad_v = heads_joined(dot(band, table[:, cut])) * factor
                    g_table[:, cut] += dot_first(band, heads_apart(turned[2, :, cut]))
                    vec[0:1, cut] += total(grad_u)
                    vec[1:2, cut] += total(grad_v)
                    both = (grad_u + grad_v).astype(bf16)
                    k.gq[row][here, cut] = dot(turn, both).astype(bf16)
                if block == 0:
                    k.g_before[row] = acc[0:WIN].astype(bf16)
                    k.send(k.g_before, row)
            k.g_after[row] = acc[3 * WIN :].astype(bf16)
            k.send(k.g_after, row)
            k.g_lo[row][...] = acc[WIN : 2 * WIN]
            k.send(k.g_lo[row])
            k.g_hi[row][...] = acc[2 * WIN : 3 * WIN]
            k.send(k.g_hi[row])
            k.send(k.gq[row])

    ins = dict(
        table=query.table, gm=by_row(gm, rows), qu=by_row(query.qu, rows),
        qv=by_row(query.qv, rows), before=each_of(before), lo=each_of(start.lo),
        hi=each_of(start.hi), prob=list(probs), next=each_of(after),
    )
    kv = (WIN, 2 * model)
    return staged(
        "attend_back",
        body,
        ins,
        dict(
            gq=[sds((frames, model), bf16)] * rows, g_before=sds((rows,) + kv, bf16),
            g_lo=[sds(kv, f32)] * rows, g_hi=[sds(kv, f32)] * rows,
            g_after=sds((rows,) + kv, bf16), g_table=sds((SPAN, model), f32),
            vec=sds((8, model), f32),
        ),
        scratch=[
            pltpu.VMEM((4 * WIN, 2 * model), f32),
            pltpu.VMEM((3, WIN, model), bf16),
        ],
        flops=16 * 14 * 256 * 384 * 128,
        moved=16 << 20,
        sends=2 * rows - 2,
    )


def place_weights(info, core_at, n, grads, start, sinusoid):
    tokens, model = start.na.shape
    slim = model // n

    def body(k, info):
        core = info[core_at]
        pairs = (0, n // 2)
        rows = [ref[...] for ref in (k.gq[at] for at in range(len(grads.gq)))]
        block = dot_first(k.na[...], jnp.concatenate(rows, axis=0))
        keep_half(block, core, k.mine, k.other, pairs)
        high = k.g_table[...].astype(bf16)
        low = (k.g_table[...] - high.astype(f32)).astype(bf16)
        place = dot_first(k.sinusoid[...], high) + dot_first(k.sinusoid[...], low)
        keep_half(place, core, k.mine, k.other, pairs, slim)

    half = sds((n // 2, 2 * slim, model), bf16)
    return staged(
        "place_weights",
        body,
        dict(na=start.na, gq=list(grads.gq), g_table=grads.g_table, sinusoid=sinusoid),
        dict(mine=half, other=half),
        smem=[info],
        flops=2 * tokens * model * 2 * model,
        moved=4 << 20,
    )


def back(info, core_at, n, grads, halo, attend_in, start, gas, gain, placed):
    rows = len(grads.gq)
    tokens, model = start.after.shape
    frames = tokens // rows
    hidden = start.act.shape[1]
    parts = hidden // PART
    width, slim = hidden // n, model // n

    def body(k, info, joined):
        core = info[core_at]
        vec, gain = k.vec, k.gain
        sums = [0.0] * 5
        for row in range(rows):
            here = slice(row * frames, (row + 1) * frames)
            low_half = slice(row * frames, row * frames + WIN)
            high_half = slice(row * frames + WIN, (row + 1) * frames)
            joined[here, :model] = k.gq[row][...]
            pair = (k.g_lo[row][...] + k.left[row].astype(f32)).astype(bf16)
            joined[low_half, model:] = pair
            pair = (k.g_hi[row][...] + k.right[row].astype(f32)).astype(bf16)
            joined[high_half, model:] = pair
            both = joined[here]
            k.gv[here] = both[:, 2 * model :]
            sums[0] += total(both[:, :model].astype(f32))
            sums[1] += total(both[:, 2 * model :].astype(f32))
            grad = dot_last(both, k.attend_in[...])
            normal, inverse = normalize(k.after[row][...])
            grad, gain_grad, shift_grad = norm_back(grad, normal, inverse, gain[1:2])
            sums[2] += gain_grad
            sums[3] += shift_grad
            grad = k.gas[row][...] + grad
            k.gfs[row][...] = grad
            k.send(k.gfs[row])
            low = (0.5 * grad).astype(bf16)
            k.gl[here] = low
            sums[4] += total(low.astype(f32))
        k.send(k.gv)
        k.send(k.gl)
        for at in range(5):
            vec[at : at + 1] = sums[at]
        pairs = (0, n // 2)
        block = dot_first(k.na[...], joined[:, model : 2 * model])
        keep_half(block, core, k.mine, k.other, pairs, width + slim)
        for mine, placed in ((k.mine, k.mine_placed), (k.other, k.other_placed)):
            mine[:, width : width + slim] = placed[:, :slim]
            mine[:, width + 2 * slim :] = placed[:, slim:]
        step = n // 2 // parts
        for part in range(parts):
            block = dot_first(k.act[part][...], k.gl[...])
            some = (part * step, (part + 1) * step)
            keep_half(block, core, k.mine, k.other, some)
            k.send(k.other, pl.ds(part * step, step))
            k.send(k.mine, pl.ds(part * step, step))

    half = sds((n // 2, width + 3 * slim, model), bf16)
    low = sds((tokens, model), bf16)
    return staged(
        "back",
        body,
        dict(
            gain=gain, gq=grads.gq, g_lo=grads.g_lo, g_hi=grads.g_hi, attend_in=attend_in, after=by_row(start.after, rows),
            gas=by_row(gas, rows), na=start.na, mine_placed=placed.mine, other_placed=placed.other,
            act=[slab(start.act, (0, tokens), (at, PART)) for at in range(0, hidden, PART)],
        ),
        dict(
            other=half, mine=half, gv=low, gl=low, gfs=[sds((frames, model), f32)] * rows,
            vec=sds((8, model), f32),
        ),
        smem=[info],
        scratch=[pltpu.VMEM((tokens, 3 * model), bf16)],
        kept=dict(left=halo[0], right=halo[1]),
        flops=2 * tokens * model * (hidden + 6 * model),
        moved=18 << 20,
        sends=2 * parts - 2,
    )


def keep_half(block, core, mine_ref, other_ref, rows, at=0):
    model = mine_ref.shape[2]
    pairs = rows[1] - rows[0]
    size = block.shape[0] // (2 * pairs)
    shaped = block.reshape(pairs, 2, size, model)
    even, odd = shaped[:, 0], shaped[:, 1]
    here = slice(*rows)
    mine_ref[here, at : at + size] = jnp.where(core == 0, even, odd).astype(bf16)
    other_ref[here, at : at + size] = jnp.where(core == 0, odd, even).astype(bf16)


def first_back(info, core_at, n, gl, feed_in, feed_out, start, gv):
    tokens, hidden = start.slope.shape
    model = gl.shape[1]
    parts = hidden // PART

    def body(k, info):
        core = info[core_at]
        step = n // 2 // parts
        back = 0.0
        block = dot_first(k.na[...], k.gv[...])
        keep_half(block, core, k.mine, k.other, (0, n // 2), hidden // n)
        for part in range(parts):
            cut = slice(part * PART, (part + 1) * PART)
            grad = dot_last(k.gl[...], k.w_out[part][...])
            grad = (grad * k.slope[part][...].astype(f32)).astype(bf16)
            put_rows(k.fb, part, total(grad.astype(f32)))
            block = dot_first(grad, k.n0[...])
            some = (part * step, (part + 1) * step)
            keep_half(block, core, k.mine, k.other, some)
            k.send(k.other, pl.ds(part * step, step))
            k.send(k.mine, pl.ds(part * step, step))
            back = back + dot_last(grad, k.w_in[part][...])
        k.gn[...] = back

    half = sds((n // 2, hidden // n + model // n, model), bf16)
    w_in, w_out = feed_slabs(feed_in, feed_out, 0)
    return staged(
        "first_back",
        body,
        dict(
            na=start.na, gv=gv, gl=gl, w_out=w_out,
            slope=[slab(start.slope, (0, tokens), (at, PART)) for at in range(0, hidden, PART)],
            n0=start.n0, w_in=w_in,
        ),
        dict(other=half, mine=half, fb=sds((hidden // model, model), f32), gn=sds((tokens, model), f32)),
        smem=[info],
        flops=2 * tokens * model * hidden * 3,
        moved=12 << 20,
        sends=2 * parts - 2,
    )


def last(features, gn, gfs, gain):
    rows, frames, model = features.shape

    def body(k):
        gain_grads, shift_grads = 0.0, 0.0
        for row in range(rows):
            here = slice(row * frames, (row + 1) * frames)
            normal, inverse = normalize(k.x[row][...].astype(f32))
            grad = k.gn[row][...]
            grad, gain_grad, shift_grad = norm_back(grad, normal, inverse, k.gain[0:1])
            k.out[row] = k.gfs[row][...] + grad
            k.send(k.out, row)
            gain_grads += gain_grad
            shift_grads += shift_grad
        k.vec[0:1] = gain_grads
        k.vec[1:2] = shift_grads

    ins = dict(
        gain=gain, x=[slab(features, row, (0, frames), (0, model)) for row in range(rows)],
        gn=[slab(gn, (row * frames, frames), (0, model)) for row in range(rows)], gfs=list(gfs),
    )
    return staged(
        "last",
        body,
        ins,
        dict(out=sds(features.shape, f32), vec=sds((8, model), f32)),
        flops=rows * frames * model * 20,
        moved=4 << 20,
        sends=rows - 1,
        limit=FOLD_LIMIT,
    )


def feed_weights(n, gi, nf, act, gl):
    tokens, model = nf.shape
    hidden = gi.shape[1]
    parts = hidden // PART
    size, slim = hidden // n, model // n
    step = n // parts
    room = 2 * slim if slim % 8 == 0 else 0

    def body(k):
        for part in range(parts):
            here = slice(part * step, (part + 1) * step)
            block = dot_first(k.gi[part][...], k.nf[...]).astype(bf16)
            k.out[here, :, :model] = block.reshape(step, size, model)
            block = dot_first(k.act[part][...], k.gl[...]).astype(bf16)
            k.out[here, :, model:] = block.reshape(step, size, model)
            k.send(k.out, pl.ds(part * step, step))

    ins = dict(
        nf=nf, gi=[slab(gi, (0, tokens), (at, PART)) for at in range(0, hidden, PART)], gl=gl,
        act=[slab(act, (0, tokens), (at, PART)) for at in range(0, hidden, PART)],
    )
    own = (n, size, 2 * model)
    shape = sds((n, size + room, 2 * model), bf16)
    return staged(
        "feed_weights",
        body,
        ins,
        dict(out=(shape, lambda ref: ref.at[:, pl.ds(0, size)] if room else ref, own)),
        flops=4 * tokens * model * hidden,
        moved=10 << 20,
        sends=parts - 1,
    ).out


def neighbours(last_block, first_block):
    devices = lax.axis_size("frames")
    up = [(i, i + 1) for i in range(devices - 1)]
    down = [(i + 1, i) for i in range(devices - 1)]
    return lax.ppermute(last_block, "frames", up), lax.ppermute(first_block, "frames", down)


def gather(copies):
    return lax.all_to_all(copies, DEVICES, 0, 0, tiled=True)


def scatter_sum(grads):
    return lax.psum_scatter(grads, "frames", scatter_dimension=0, tiled=True)


ROW_PAIR = [(0, 1), (1, 0)]
COLUMNS, IN_FLOAT = 1, 2
N_VECTORS = KERNEL + 5 + 5 + 10


def swap(x, k):
    n = lax.axis_size("frames")
    return lax.ppermute(x, "frames", [(i, i ^ k) for i in range(n)])


def swaps(sends, group):
    k, size = group
    return [swap(send, k * one) for one, send in zip(range(1, size), sends)]


def fold(name, info, row_at, states, small=None):
    mines, gots, keeps, sends, plans = [], [], [], [], []
    for mine, got, how in states:
        size, height, model = mine.shape
        if isinstance(how, tuple):
            _, place, digits = how
            view = (size // (digits * place), digits, place, height, model)
            half = (view[0], place, height, model)
        else:
            view = mine.shape
            half = (size, height, model // 2) if how == COLUMNS else mine.shape
        n_sends = how[2] - 1 if isinstance(how, tuple) else int(how == COLUMNS)
        plans.append((len(gots), len(got), len(sends), n_sends, how))
        mines.append(mine.reshape(view))
        gots += [one.reshape(view) for one in got]
        keeps.append(sds(half, f32 if how == IN_FLOAT else bf16))
        sends += [sds(half, bf16)] * n_sends

    n_small = 0 if small is None else len(small)

    def body(info, *refs):
        cuts = [len(mines), len(gots), n_small, len(keeps), len(sends)]
        taken, at = [], 0
        for cut in cuts:
            taken.append(refs[at : at + cut])
            at += cut
        mine_refs, got_refs, small_refs, keep_refs, send_refs = taken
        for at, (got_at, n_got, send_at, _, how) in enumerate(plans):
            parts = [mine_refs[at], *got_refs[got_at : got_at + n_got]]

            def added(*index):
                return sum(part[index].astype(f32) for part in parts)

            keep = keep_refs[at]
            if how is None or how == IN_FLOAT:
                keep[...] = added(...).astype(keep.dtype)
            elif how == COLUMNS:
                half = keep.shape[2]
                both = [
                    added(slice(None), slice(None), slice(one * half, (one + 1) * half))
                    for one in range(2)
                ]
                first = info[row_at] == 0
                send_refs[send_at][...] = jnp.where(first, both[1], both[0]).astype(bf16)
                keep[...] = jnp.where(first, both[0], both[1]).astype(bf16)
            else:
                digit = info[how[0]]
                for one in range(1, how[2]):
                    other = digit
                    for bit in (1, 2):
                        if one & bit:
                            other = other + bit * (1 - 2 * ((digit // bit) % 2))
                    send_refs[send_at + one - 1][...] = added(slice(None), other).astype(bf16)
                keep[...] = added(slice(None), digit).astype(bf16)
        if n_small:
            refs[-1][...] = sum(one[...] for one in small_refs)

    shapes = keeps + sends + ([sds(small[0].shape, f32)] if n_small else [])
    here = pl.BlockSpec(memory_space=pltpu.VMEM)
    given = mines + gots + (list(small) if n_small else [])
    got = pl.pallas_call(
        body,
        in_specs=[pl.BlockSpec(memory_space=pltpu.SMEM)] + [here] * len(given),
        out_specs=[here] * len(shapes),
        out_shape=shapes,
        compiler_params=pltpu.CompilerParams(vmem_limit_bytes=FOLD_LIMIT),
        cost_estimate=pl.CostEstimate(flops=1 << 20, bytes_accessed=2 << 20, transcendentals=0),
        name=name,
    )(info, *given)
    kept, away = got[: len(keeps)], got[len(keeps) : len(keeps) + len(sends)]
    results = []
    for at, (mine, _, how) in enumerate(states):
        size, height, model = mine.shape
        shape = (size // how[2], height, model) if isinstance(how, tuple) else kept[at].shape
        _, _, send_at, n_sends, _ = plans[at]
        some = [one.reshape(shape) for one in away[send_at : send_at + n_sends]]
        results.append((kept[at].reshape(shape), some))
    if n_small:
        results.append(got[-1])
    return results


def finish(info, row_at, frames, a, b, b_got, early, small, totals, width, slim):
    model = a.shape[1]
    feed_rows = small[0].shape[0] - N_VECTORS
    per = feed_rows // 2

    def body(info, a, b, b_got, early, totals, *refs):
        sums, refs = refs[: len(small)], refs[len(small) :]
        feed_in, feed_out, joined, attend, place, con_in, con_out, *refs = refs
        depth, gain, shift, bias, feed_bias, vectors = refs
        feed_in[0] = a[:width].T
        feed_in[1] = early[:width, :model].T
        first = info[row_at] == 0
        one, two = b[...].astype(f32), b_got[...].astype(f32)
        whole = jnp.concatenate([jnp.where(first, one, two), jnp.where(first, two, one)], axis=1)
        feed_out[0] = whole[:width]
        feed_out[1] = early[:width, model:]
        joined[:, :model] = whole[width : width + slim]
        joined[:, model : 2 * model] = whole[width + slim : width + 2 * slim]
        joined[:, 2 * model :] = a[width:]
        place[...] = whole[width + 2 * slim :]
        con_in[...] = early[width : width + slim]
        con_out[...] = early[width + slim :, :model]
        attend[...] = early[width + slim :, model:]
        me = info[0] // frames
        end = N_VECTORS + feed_rows
        vectors[end:] = jnp.zeros((vectors.shape[0] - end, model), f32)
        vectors[:end] = sum(one[...] for one in sums)
        vectors[end : end + 2] = totals[...]
        own = pltpu.roll(vectors[...], lax.rem(model - me * slim, model), 1)[:, :slim]
        depth[...] = own[:KERNEL]
        gain[0:5] = own[KERNEL : KERNEL + 5]
        gain[5:6] = own[end + 1 : end + 2]
        shift[0:5] = own[KERNEL + 5 : KERNEL + 10]
        shift[5:6] = own[end : end + 1]
        bias[...] = own[KERNEL + 10 : N_VECTORS]
        at = me * width
        for module in range(2):
            row = vectors[pl.ds(N_VECTORS + module * per + at // model, 1), :]
            row = pltpu.roll(row, lax.rem(model - lax.rem(at, model), model), 1)
            feed_bias[module : module + 1] = row[:, :width]

    def full(shape):
        return pl.BlockSpec(shape, lambda i: (0,) * len(shape))

    shapes = [
        (2, model, width), (2, width, model), (slim, 3 * model), (slim, model), (slim, model),
        (slim, 2 * model), (slim, model), (KERNEL, slim), (6, slim), (6, slim), (10, slim),
        (2, width),
    ]
    given = (a, b, b_got, early, totals, *small)
    return pl.pallas_call(
        body,
        grid=(1,),
        in_specs=[pl.BlockSpec(memory_space=pltpu.SMEM)] + [full(one.shape) for one in given],
        out_specs=[full(shape) for shape in shapes],
        out_shape=[sds(shape, f32) for shape in shapes],
        scratch_shapes=[pltpu.VMEM((-(-(N_VECTORS + feed_rows + 2) // 8) * 8, model), f32)],
        compiler_params=pltpu.CompilerParams(vmem_limit_bytes=FOLD_LIMIT),
        name="finish",
    )(info, *given)


def per_device(
    features,
    lengths,
    windows,
    feed_in,
    feed_in_bias,
    feed_out,
    attend_in,
    attend_out,
    position_proj,
    convolve_in,
    convolve_out,
    depthwise,
    norm_gain,
    norm_shift,
    biases,
    cotangent,
):
    rows, frames, model = features.shape
    tokens = rows * frames
    n = lax.axis_size("frames")
    devices = lax.axis_size("rows") * n
    row_len = float(frames * n)
    me = lax.axis_index("frames")
    first_frame = me * frames
    hidden = feed_in.shape[2]
    ends_every = jnp.cumsum(lengths, axis=1, dtype=jnp.int32)
    ends_here = lax.dynamic_slice_in_dim(ends_every, lax.axis_index("rows") * rows, rows, 0)
    slots = ends_here.shape[1]
    ends = jnp.pad(
        ends_here.astype(f32), ((0, 8 - rows), (0, -slots % 128)), constant_values=row_len
    )
    groups, k = [(2, 2)], 4
    while k < n:
        groups.append((k, min(4, n // k)))
        k *= groups[-1][1]
    places = [lax.axis_index("rows"), me % 2] + [(me // k) % size for k, size in groups]
    info = jnp.concatenate(
        [first_frame[None].astype(jnp.int32), windows, ends_here[:, -1], jnp.stack(places)]
    )
    row_at = 1 + 2 * rows
    core_at = row_at + 1
    starts = jnp.arange(n, dtype=jnp.int32) * frames
    counts = jnp.clip(ends_every[:, -1][:, None] - starts[None, :], 0, frames)
    counts = jnp.sum(counts.reshape(-1, rows, n), axis=1).astype(f32).reshape(devices, 1)
    counts = jnp.broadcast_to(counts, (devices, 128))
    sinusoid = jnp.asarray(position_table(WIN, model))

    start = front(
        features, feed_in, feed_in_bias, feed_out, attend_in, norm_gain, norm_shift, biases
    )
    before, after = neighbours(start.hi, start.lo)
    query = queries(
        start, feed_in, feed_in_bias, attend_in, biases, sinusoid, position_proj
    )
    start.slope = query.slope
    mix = attend(
        row_len, info, ends, start, query, before, after, attend_out, convolve_in, norm_gain,
        norm_shift, biases,
    )
    rim_before, rim_after = neighbours(mix.last, mix.first)
    got = depth_conv(row_len, devices, info, ends, mix.gated, rim_before, rim_after, depthwise)
    mid = middle(
        devices, rows, info, gather(got.stats), counts, got.depth, mix.out, feed_in,
        feed_in_bias, feed_out, convolve_out, norm_gain, norm_shift, biases,
        cotangent.reshape(tokens, model),
    )
    edge_before, edge_after = neighbours(mid.last, mid.first)
    totals = gather(mid.totals)
    early = feed_weights(n, mid.gi, mid.nf, mid.act, mid.gl)
    totals, early = lax.optimization_barrier((totals, early))
    conv = conv_back(
        row_len, n, info, ends, depthwise, convolve_in, attend_out, norm_gain, totals, mid,
        edge_before, edge_after, rim_before, rim_after, mix, early,
    )
    early, gm = lax.optimization_barrier((conv.early, conv.gm))
    early = scatter_sum(early)
    grads = attend_back(start, query, before, after, mix.prob, gm)
    halo = neighbours(grads.g_after, grads.g_before)
    placed = place_weights(info, core_at, n, grads, start, sinusoid)
    end = back(info, core_at, n, grads, halo, attend_in, start, conv.gas, norm_gain, placed)
    b, b_got = end.mine, [swap(end.other, 1)]
    got = first_back(info, core_at, n, end.gl, feed_in, feed_out, start, end.gv)
    a, a_got = got.mine, [swap(got.other, 1)]
    ((b, b_send),) = fold("fold_b", info, row_at, [(b, b_got, COLUMNS)])
    b_got = [lax.ppermute(b_send[0], "rows", ROW_PAIR)]
    ((a, a_send),) = fold("fold_a", info, row_at, [(a, a_got, (core_at + 1, 1, 2))])
    a_got = swaps(a_send, groups[0])
    gn, a = lax.optimization_barrier((got.gn, a))
    ending = last(features, gn, end.gfs, norm_gain)

    vec_conv, vec_mid, vec_back, vec_last = conv.vec, mid.vec, end.vec, ending.vec
    small = jnp.concatenate(
        [
            vec_conv[:KERNEL],
            vec_last[0:1], vec_back[2:3], vec_conv[9:10], vec_mid[0:1], vec_mid[2:3],
            vec_last[1:2], vec_back[3:4], vec_conv[10:11], vec_mid[1:2], vec_mid[3:4],
            vec_back[0:2], vec_conv[13:14], vec_conv[11:13], vec_mid[4:5], vec_back[4:5],
            vec_mid[5:6], grads.vec[0:2],
            got.fb, mid.fb,
        ],
        axis=0,
    )
    small = [small] + swaps([small] * 3, (1, 4))
    last_group = groups[-1]
    for at, group in enumerate(groups):
        deeper = at + 1 < len(groups)
        a_how = (core_at + 2 + at, 1, groups[at + 1][1]) if deeper else None
        states = [(a, a_got, a_how), (b, b_got, (core_at + 1 + at, 1, group[1]))]
        (a, a_send), (b, b_send), one = fold(f"fold_{at}", info, row_at, states, small)
        if deeper:
            a_got = swaps(a_send, groups[at + 1])
        else:
            early, a = lax.optimization_barrier((early, a))
            a_got = [lax.ppermute(a, "rows", ROW_PAIR)]
            early_got = [lax.ppermute(early, "rows", ROW_PAIR)]
        b_got = swaps(b_send, group)
        if at == 0:
            small = [one, lax.ppermute(one, "rows", ROW_PAIR)]
        elif deeper:
            small = [one] + swaps([one] * (group[1] - 1), group)
    states = [(b, b_got, None), (a, a_got, IN_FLOAT), (early, early_got, IN_FLOAT)]
    (b, _), (a, _), (early, _) = fold("fold_last", info, row_at, states)
    b_got = lax.ppermute(b, "rows", ROW_PAIR)
    small = [one] + swaps([one] * (last_group[1] - 1), last_group)
    slim = model // n
    width = hidden // n
    feed_in_grad, feed_out_grad, joined, *rest, depth, gain, shift, bias, feed_bias = finish(
        info, row_at, frames, a[0], b[0], b_got[0], early[0], small, vec_conv[14:16], width, slim
    )
    return (
        mid.out.reshape(rows, frames, model),
        ending.out,
        feed_in_grad,
        feed_bias,
        feed_out_grad,
        joined,
        *rest,
        depth,
        gain,
        shift,
        bias,
    )


def solution(mesh):
    placed = (
        P("rows", "frames", None),
        P(),
        P("rows"),
        P(),
        P(),
        P(),
        P(),
        P(),
        P(),
        P(),
        P(),
        P(),
        P(),
        P(),
        P(),
        P("rows", "frames", None),
    )
    return jax.shard_map(
        per_device,
        mesh=mesh,
        in_specs=placed,
        out_specs=(
            P("rows", "frames", None),
            P("rows", "frames", None),
            P(None, None, "frames"),
            P(None, "frames"),
            P(None, "frames", None),
            P("frames", None),
            P("frames", None),
            P("frames", None),
            P("frames", None),
            P("frames", None),
            P(None, "frames"),
            P(None, "frames"),
            P(None, "frames"),
            P(None, "frames"),
        ),
        check_vma=False,
    )
```

```python
import functools
import math
import types

import jax
import jax.numpy as jnp
import ml_dtypes
import numpy as np
from jax import lax
from jax.experimental import pallas as pl
from jax.experimental.pallas import tpu as pltpu
from jax.sharding import PartitionSpec as P

H = 8
DH = 64
KERNEL = 9
WIN = 128

HALF = KERNEL // 2
SPAN = 3 * WIN
MANY = 4
GROUPS = H // MANY
WIDE = MANY * DH
RIM = 16
RIM_GRAD = 8
eps_norm = 1e-05
negative = -1e30
f32 = jnp.float32
bf16 = jnp.bfloat16
DEVICES = ("rows", "frames")
VMEM_LIMIT = 60 * 1024 * 1024
FOLD_LIMIT = 14 * 1024 * 1024


def dot(left, right):
    return jnp.dot(left, right, preferred_element_type=f32)


def dot_last(left, right):
    return lax.dot_general(left, right, (((1,), (1,)), ((), ())), preferred_element_type=f32)


def dot_first(left, right):
    return lax.dot_general(left, right, (((0,), (0,)), ((), ())), preferred_element_type=f32)


def sigmoid(x):
    return 0.5 * jnp.tanh(0.5 * x) + 0.5


def total(x):
    return jnp.sum(x, axis=0, keepdims=True)


def normalize(values):
    centered = values - jnp.mean(values, axis=-1, keepdims=True)
    inverse = lax.rsqrt(jnp.mean(centered * centered, axis=-1, keepdims=True) + eps_norm)
    return centered * inverse, inverse


def norm_back(grad_out, normal, inverse, gain):
    scaled = grad_out * gain
    centred = scaled - jnp.mean(scaled, axis=-1, keepdims=True)
    grad_in = inverse * (centred - normal * jnp.mean(scaled * normal, axis=-1, keepdims=True))
    return grad_in, total(grad_out * normal), total(grad_out)


def position_table(width, model):
    offsets = (np.arange(2 * width + 1) - width).astype(np.float32)
    rates = np.exp(
        np.arange(model // 2).astype(np.float32) * np.float32(-2.0 * math.log(10000.0) / model)
    )
    angles = (offsets[:, None] * rates[None, :]).astype(np.float32)
    both = np.stack([np.sin(angles), np.cos(angles)], axis=2).reshape(2 * width + 1, model)
    padded = np.zeros((3 * width, model), np.float32)
    padded[: 2 * width + 1] = both
    return padded.astype(ml_dtypes.bfloat16)


def bounds(ends, at, row_len):
    low = jnp.max(jnp.where(ends <= at, ends, 0.0), axis=1, keepdims=True)
    high = jnp.min(jnp.where(ends > at, ends, row_len), axis=1, keepdims=True)
    return low, high


def column(count, offset):
    return lax.broadcasted_iota(jnp.int32, (count, 1), 0).astype(f32) + offset


def head_lanes(rows):
    return lax.broadcasted_iota(jnp.int32, (rows, WIDE), 1) // DH


def heads_apart(group):
    at = head_lanes(group.shape[0])
    zero = jnp.zeros_like(group)
    return jnp.concatenate([jnp.where(at == k, group, zero) for k in range(MANY)], axis=0)


def heads_joined(stacked):
    rows = stacked.shape[0] // MANY
    at = head_lanes(rows)
    joined = stacked[:rows]
    for k in range(1, MANY):
        joined = jnp.where(at == k, stacked[k * rows : (k + 1) * rows], joined)
    return joined


def beside(stacked):
    rows = stacked.shape[0] // MANY
    return jnp.concatenate([stacked[k * rows : (k + 1) * rows] for k in range(MANY)], axis=1)


def below(joined):
    width = joined.shape[1] // MANY
    return jnp.concatenate([joined[:, k * width : (k + 1) * width] for k in range(MANY)], axis=0)


def windows(width):
    return [slice(at, at + WIN) for at in range(0, width, WIN)]


def flip(rows):
    i = lax.broadcasted_iota(jnp.int32, (rows, rows), 0)
    j = lax.broadcasted_iota(jnp.int32, (rows, rows), 1)
    return (i + j == rows - 1).astype(f32).astype(bf16)


class Load:
    def __init__(self, source, buffer, sem):
        self.buffer, self.waited = buffer, False
        self.copy = pltpu.make_async_copy(source, buffer, sem)
        self.copy.start()

    def ready(self):
        if not self.waited:
            self.copy.wait()
            self.waited = True
        return self.buffer


class Loads:
    def __init__(self, items):
        self.items = items

    def __getitem__(self, at):
        return self.items[at].ready()


class Stage:
    def __init__(self, loads, stores, sems):
        self.sems, self.used, self.pending, self.targets = sems, 0, [], []
        self.named, self.all_loads = {}, []
        while loads:
            run = [loads.pop(0)]
            while not run[0][2] and loads and len(loads[0][1]) == len(run[0][1]) > 1:
                run.append(loads.pop(0))
            items = [[] for _ in run]
            for at in range(len(run[0][1])):
                for (_, pairs, _), own in zip(run, items):
                    source, buffer = pairs[at]
                    own.append(Load(source, buffer, self.sem()))
            for (name, _, single), own in zip(run, items):
                self.all_loads += own
                self.named[name] = own[0] if single else Loads(own)
        for name, pairs, single in stores:
            self.targets += [[target, buffer, False] for target, buffer in pairs]
            buffers = [buffer for _, buffer in pairs]
            self.named[name] = buffers[0] if single else buffers

    def sem(self):
        self.used += 1
        return self.sems.at[self.used - 1]

    def __getattr__(self, name):
        found = self.named[name]
        return found.ready() if isinstance(found, Load) else found

    def send(self, buffer, at=None):
        entry = next(entry for entry in self.targets if entry[1] is buffer)
        target = entry[0]
        entry[2] = True
        if at is not None:
            target, buffer = target.at[at], buffer.at[at]
        copy = pltpu.make_async_copy(buffer, target, self.sem())
        copy.start()
        self.pending.append(copy)

    def finish(self):
        for _, buffer, sent in self.targets:
            if not sent:
                self.send(buffer)
        for load in self.all_loads:
            load.ready()
        for copy in self.pending:
            copy.wait()


def staged(
    name, body, ins, outs, smem=(), scratch=(), flops=0, moved=0, sends=0, filled=None,
    limit=VMEM_LIMIT, kept=None,
):
    operands, loads, stores, kept = [], [], [], kept or {}
    for key, items in ins.items():
        single = not isinstance(items, list)
        entries = []
        for item in [items] if single else items:
            array, view, shape = item if isinstance(item, tuple) else (item, None, item.shape)
            at = next((i for i, other in enumerate(operands) if other is array), None)
            if at is None:
                at = len(operands)
                operands.append(array)
            entries.append((at, view, shape, array.dtype))
        loads.append((key, entries, single))
    for key, items in outs.items():
        single = not isinstance(items, list)
        entries = [
            item if isinstance(item, tuple) else (item, None, item.shape)
            for item in ([items] if single else items)
        ]
        stores.append((key, entries, single))
    aliases = {}
    if filled is not None:
        aliases = {len(smem) + len(kept) + len(operands): 0}
        operands.append(filled)
    every_load = [entry for _, entries, _ in loads for entry in entries]
    every_store = [entry for _, entries, _ in stores for entry in entries]
    n_smem, n_ops, n_outs, n_loads = len(smem), len(operands), len(every_store), len(every_load)

    def run(*refs):
        cuts = [n_smem, len(kept), n_ops, n_outs, n_loads, n_outs, 1]
        taken, at = [], 0
        for cut in cuts:
            taken.append(refs[at : at + cut])
            at += cut
        scalars, here, given, targets, buffers, results, sems = taken
        buffers, places = iter(buffers), iter(zip(targets, results))
        placed_loads = [
            (
                key,
                [(given[i] if view is None else view(given[i]), next(buffers)) for i, view, _, _ in entries],
                single,
            )
            for key, entries, single in loads
        ]
        placed_stores = []
        for key, entries, single in stores:
            pairs = []
            for _, view, _ in entries:
                target, result = next(places)
                pairs.append((target if view is None else view(target), result))
            placed_stores.append((key, pairs, single))
        stage = Stage(placed_loads, placed_stores, sems[0])
        stage.named.update(zip(kept, here))
        body(stage, *scalars, *refs[at:])
        stage.finish()

    hbm = pl.BlockSpec(memory_space=pl.ANY)
    got = iter(
        pl.pallas_call(
            run,
            in_specs=[pl.BlockSpec(memory_space=pltpu.SMEM)] * n_smem
            + [pl.BlockSpec(memory_space=pltpu.VMEM)] * len(kept)
            + [hbm] * n_ops,
            out_specs=[hbm] * n_outs,
            out_shape=[shape for shape, _, _ in every_store],
            scratch_shapes=[pltpu.VMEM(shape, dtype) for _, _, shape, dtype in every_load]
            + [pltpu.VMEM(shape, whole.dtype) for whole, _, shape in every_store]
            + [pltpu.SemaphoreType.DMA((n_loads + n_outs + sends,))]
            + list(scratch),
            input_output_aliases=aliases,
            compiler_params=pltpu.CompilerParams(vmem_limit_bytes=limit),
            cost_estimate=pl.CostEstimate(flops=flops, bytes_accessed=moved, transcendentals=0),
            name=name,
        )(*smem, *kept.values(), *operands)
    )
    result = types.SimpleNamespace()
    for key, entries, single in stores:
        values = [next(got) for _ in entries]
        setattr(result, key, values[0] if single else values)
    return result


def sds(shape, dtype):
    return jax.ShapeDtypeStruct(shape, dtype)


def slab(array, *at):
    shape = tuple(a[1] for a in at if isinstance(a, tuple))
    index = tuple(pl.ds(*a) if isinstance(a, tuple) else a for a in at)
    return (array, lambda ref: ref.at[index], shape)


def by_row(array, rows):
    tokens, width = array.shape
    return [slab(array, (row * (tokens // rows), tokens // rows), (0, width)) for row in range(rows)]


def each_of(array):
    rows, size, width = array.shape
    return [slab(array, row, (0, size), (0, width)) for row in range(rows)]


PART = 1024


def activate(inner):
    half = 0.5 * inner
    turn = jnp.tanh(half)
    up = 1.0 + turn
    active = half * up
    return active, 0.5 * (up + active * (1.0 - turn))


def feed_slabs(feed_in, feed_out, module):
    _, model, hidden = feed_in.shape
    spans = [(part, PART) for part in range(0, hidden, PART)]
    w_in = [slab(feed_in, module, (0, model), span) for span in spans]
    w_out = [slab(feed_out, module, span, (0, model)) for span in spans]
    return w_in, w_out


def front(features, feed_in, feed_in_bias, feed_out, attend_in, gain, shift, bias):
    rows, frames, model = features.shape
    tokens = rows * frames
    hidden = feed_in.shape[2]
    parts = hidden // PART
    low = sds((tokens, model), bf16)

    def body(k):
        gain, shift = k.gain, k.shift
        x = k.x[...].reshape(tokens, model).astype(f32)
        normal, _ = normalize(x)
        k.n0[...] = (normal * gain[0:1] + shift[0:1]).astype(bf16)
        k.send(k.n0)
        for part in range(parts):
            cut = slice(part * PART, (part + 1) * PART)
            inner = dot(k.n0[...], k.w_in[part][...]) + k.b_in[0:1, cut]
            active, _ = activate(inner)
            k.act[:, cut] = active.astype(bf16)
        k.send(k.act)
        branch = k.bias[6:7]
        for part in range(parts):
            cut = slice(part * PART, (part + 1) * PART)
            branch = branch + dot(k.act[:, cut], k.w_out[part][...])
        after = x + 0.5 * branch
        k.after[...] = after
        k.send(k.after)
        normal, _ = normalize(after)
        normed = (normal * gain[1:2] + shift[1:2]).astype(bf16)
        k.na[...] = normed
        k.send(k.na)
        both = dot(normed, k.attend_in[...])
        keys = both[:, :model].astype(bf16)
        values = (both[:, model:] + k.bias[1:2]).astype(bf16)
        for row in range(rows):
            at = row * frames
            k.lo[row, :, :model] = keys[at : at + WIN]
            k.lo[row, :, model:] = values[at : at + WIN]
            k.hi[row, :, :model] = keys[at + WIN : at + frames]
            k.hi[row, :, model:] = values[at + WIN : at + frames]

    w_in, w_out = feed_slabs(feed_in, feed_out, 0)
    kv = sds((rows, WIN, 2 * model), bf16)
    return staged(
        "front",
        body,
        dict(
            x=features, gain=gain, shift=shift, b_in=feed_in_bias, w_in=w_in, bias=bias,
            w_out=w_out, attend_in=slab(attend_in, (0, model), (model, 2 * model)),
        ),
        dict(
            after=sds((tokens, model), f32), n0=low, na=low, lo=kv, hi=kv,
            act=sds((tokens, hidden), bf16),
        ),
        flops=2 * tokens * model * (2 * hidden + 2 * model),
        moved=16 << 20,
    )


def queries(start, feed_in, feed_in_bias, attend_in, bias, sinusoid, proj):
    tokens, model = start.na.shape
    hidden = feed_in.shape[2]
    parts = hidden // PART

    def body(k):
        query = dot(k.na[...], k.attend_in[...]) + k.bias[0:1]
        factor = 1.0 / math.sqrt(DH)
        k.qu[...] = ((query + k.bias[8:9]) * factor).astype(bf16)
        k.qv[...] = ((query + k.bias[9:10]) * factor).astype(bf16)
        k.send(k.qu)
        k.send(k.qv)
        k.table[...] = dot(k.sinusoid[...], k.proj[...]).astype(bf16)
        k.send(k.table)
        for part in range(parts):
            cut = slice(part * PART, (part + 1) * PART)
            inner = dot(k.n0[...], k.w_in[part][...]) + k.b_in[0:1, cut]
            _, slope = activate(inner)
            k.slope[:, cut] = slope.astype(bf16)

    low = sds((tokens, model), bf16)
    spans = [(at, PART) for at in range(0, hidden, PART)]
    w_in = [slab(feed_in, 0, (0, model), span) for span in spans]
    return staged(
        "queries",
        body,
        dict(
            na=start.na, attend_in=slab(attend_in, (0, model), (0, model)), bias=bias,
            sinusoid=sinusoid, proj=proj, n0=start.n0, b_in=feed_in_bias, w_in=w_in,
        ),
        dict(
            qu=low, qv=low, table=sds((SPAN, model), bf16), slope=sds((tokens, hidden), bf16)
        ),
        flops=2 * tokens * model * (hidden + 2 * model),
        moved=10 << 20,
    )


def attend(
    row_len, info, ends, start, query, before, after, attend_out, convolve_in, gain, shift, bias
):
    rows = before.shape[0]
    tokens, model = start.after.shape
    frames = tokens // rows
    low = sds((tokens, model), bf16)

    def body(k, info):
        first_frame = info[0].astype(f32)
        turn = flip(WIN)
        key_at = lax.broadcasted_iota(jnp.int32, (WIN, SPAN), 1).astype(f32)
        table = k.table
        ones = jnp.ones((SPAN, WIN), bf16)
        for row in range(rows):
            reach = info[1 + row].astype(f32)
            row_ends = k.ends[row : row + 1, :]
            for block in range(2):
                at = column(WIN, first_frame + WIN * block)
                lower, upper = bounds(row_ends, at, row_len)
                base = first_frame + (WIN * (block - 1))
                lower = jnp.maximum(lower, at - reach) - base
                upper = jnp.minimum(upper - 1.0, at + reach) - base
                allowed = ((key_at >= lower) & (key_at <= upper))[None]
                here = slice(row * frames + WIN * block, row * frames + WIN * (block + 1))
                some = [k.lo[row], k.hi[row]]
                some = some + [k.next.at[row]] if block else [k.before.at[row]] + some
                for group in range(GROUPS):
                    cut = slice(WIDE * group, WIDE * (group + 1))
                    cut_v = slice(model + WIDE * group, model + WIDE * (group + 1))
                    keys = jnp.concatenate([b[:, cut] for b in some], axis=0)
                    values = jnp.concatenate([b[:, cut_v] for b in some], axis=0)
                    spread = dot_last(heads_apart(k.qv[here, cut]), table[:, cut])
                    content = dot_last(heads_apart(k.qu[here, cut]), keys)
                    spread = pltpu.roll(
                        spread.reshape(MANY, WIN, SPAN), 0, 2, stride=1, stride_axis=1
                    )
                    scores = content.reshape(MANY, WIN, SPAN) + spread
                    scores = jnp.where(allowed, scores, negative)
                    powers = jnp.exp(scores - jnp.max(scores, axis=2, keepdims=True))
                    powers = powers.reshape(MANY * WIN, SPAN)
                    inverse = 1.0 / dot(powers.astype(bf16), ones)
                    weights = jnp.concatenate(
                        [powers[:, cut] * inverse for cut in windows(SPAN)], axis=1
                    ).astype(bf16)
                    k.mixed[here, cut] = heads_joined(dot(weights, values)).astype(bf16)
                    k.prob[row][block, group] = dot(turn, beside(weights)).astype(bf16)
            k.send(k.prob[row])
        k.send(k.mixed)
        after_attend = k.after[...] + dot(k.mixed[...], k.attend_out[...]) + k.bias[2:3]
        k.out[...] = after_attend
        k.send(k.out)
        normal, _ = normalize(after_attend)
        normed = (normal * k.gain[2:3] + k.shift[2:3]).astype(bf16)
        k.nc[...] = normed
        k.send(k.nc)
        paired = dot(normed, k.convolve_in[...])
        value = paired[:, :model] + k.bias[3:4]
        gate = paired[:, model:] + k.bias[4:5]
        sigma = sigmoid(gate)
        gated = value * sigma
        k.factors[:, :model] = sigma.astype(bf16)
        k.factors[:, model:] = (gated * (1.0 - sigma)).astype(bf16)
        k.send(k.factors)
        gated = gated.astype(bf16)
        k.gated[...] = gated
        for row in range(rows):
            k.first[row] = gated[row * frames : row * frames + RIM]
            k.last[row] = gated[(row + 1) * frames - RIM : (row + 1) * frames]

    rim = sds((rows, RIM, model), bf16)
    return staged(
        "attend",
        body,
        dict(
            ends=ends, table=query.table, qv=query.qv, qu=query.qu, lo=each_of(start.lo),
            hi=each_of(start.hi), after=start.after, attend_out=attend_out, bias=bias, gain=gain, shift=shift, convolve_in=convolve_in,
        ),
        dict(
            prob=[sds((2, GROUPS, WIN, MANY * SPAN), bf16)] * rows, mixed=low,
            out=sds((tokens, model), f32), nc=low, factors=sds((tokens, 2 * model), bf16),
            gated=low, first=rim, last=rim,
        ),
        smem=[info],
        kept=dict(before=before, next=after),
        flops=16 * 8 * 256 * 384 * 128,
        moved=16 << 20,
    )


def valid_column(info, row, rows, frames):
    at = column(frames, info[0].astype(f32))
    return (at < info[1 + rows + row].astype(f32)).astype(f32)


def put_rows(ref, part, vector):
    model = ref.shape[1]
    per = vector.shape[1] // model
    for one in range(per):
        at = part * per + one
        ref[at : at + 1] = vector[:, one * model : (one + 1) * model]


def pack(ref, vectors):
    at = 0
    for vector in vectors:
        for k in range(0, vector.shape[1], 128):
            ref[at : at + 1, :] = vector[:, k : k + 128]
            at += 1


def by_rows(count, size, step, init=None):
    def one(i, carry):
        return step(pl.ds(pl.multiple_of(i * size, size), size), carry)

    return lax.fori_loop(0, count // size, one, init)


def by_lanes(width, step):
    def one(i, carry):
        step(pl.ds(pl.multiple_of(i * 128, 128), 128))
        return carry

    lax.fori_loop(0, width // 128, one, 0)


def spread(column):
    return jnp.broadcast_to(column, (column.shape[0], 128))


def tap_masks(keep_s, at, low, high):
    for tap in range(KERNEL):
        off = tap - HALF
        keep_s[tap] = spread(((at + off >= low) & (at + off < high)).astype(f32))


def depth_conv(row_len, devices, info, ends, gated, before, after, taps):
    rows = before.shape[0]
    tokens, model = gated.shape
    frames = tokens // rows

    def body(k, info, rim, keep_s, valid_s, sums, tile):
        start = info[0].astype(f32)
        counts = 0.0
        taps = k.taps
        for row in range(rows):
            here = slice(row * frames, (row + 1) * frames)
            at = column(frames, start)
            low, high = bounds(k.ends[row : row + 1, :], at, row_len)
            tap_masks(keep_s, at, low, high)
            valid = valid_column(info, row, rows, frames)
            valid_s[here] = spread(valid)
            counts += total(valid)
            rim[0:RIM] = k.before[row].astype(f32)
            rim[RIM : RIM + frames] = k.gated[row][...].astype(f32)
            rim[RIM + frames :] = k.after[row].astype(f32)

            def one(lanes):
                depth = jnp.zeros((frames, 128), f32)
                for tap in range(KERNEL):
                    off = tap - HALF
                    part = rim[RIM + off : RIM + off + frames, lanes] * keep_s[tap]
                    depth += taps[tap : tap + 1, lanes] * part
                k.depth[here, lanes] = depth
                sums[row : row + 1, lanes] = total(depth * valid_s[here])

            by_lanes(model, one)
            k.send(k.depth, pl.ds(row * frames, frames))
        first = total(sums[0:rows, :])
        mean = first / jnp.maximum(counts, 1.0)
        sums[rows : rows + 1, :] = mean

        def two(lanes):
            centered = k.depth[:, lanes] - sums[rows : rows + 1, lanes]
            sums[rows + 1 : rows + 2, lanes] = total(centered * centered * valid_s[...])

        by_lanes(model, two)
        pack(tile, [first, sums[rows + 1 : rows + 2, :]])
        k.stats[...] = jnp.broadcast_to(tile[...][None], k.stats.shape)

    return staged(
        "depth_conv",
        body,
        dict(ends=ends, taps=taps, gated=by_row(gated, rows)),
        dict(depth=sds((rows * frames, model), f32), stats=sds((devices, 8, 128), f32)),
        smem=[info],
        scratch=[
            pltpu.VMEM((frames + 2 * RIM, model), f32),
            pltpu.VMEM((KERNEL, frames, 128), f32),
            pltpu.VMEM((rows * frames, 128), f32),
            pltpu.VMEM((8, model), f32),
            pltpu.VMEM((8, 128), f32),
        ],
        kept=dict(before=before, after=after),
        flops=rows * frames * model * 30,
        moved=2 << 20,
        sends=rows - 1,
    )


def middle(
    devices, rows, info, stats, counts, depth, stream, feed_in, feed_in_bias, feed_out,
    convolve_out, gain, shift, bias, cotangent,
):
    tokens, model = depth.shape
    frames = tokens // rows
    hidden = feed_in.shape[2]
    parts = hidden // PART

    def body(k, info, conv_s, bn_s, slope_s, tile):
        stats, each = k.stats, k.counts[:, 0:1]
        gain, shift, bias = k.gain, k.shift, k.bias
        count = total(each)
        means, inverses = [], []
        for at in range(model // 128):
            sums = stats[:, at, :]
            mean = total(sums) / count
            off = sums / jnp.maximum(each, 1.0) - mean
            spread = total(stats[:, model // 128 + at, :]) + total(each * off * off)
            means.append(mean)
            inverses.append(lax.rsqrt(spread / count + eps_norm))
        mean = jnp.concatenate(means, axis=1)
        inverse = jnp.concatenate(inverses, axis=1)
        k.inv[0:1] = inverse
        k.inv[1:2] = jnp.broadcast_to(1.0 / count, (1, model))
        normal = (k.depth[...] - mean) * inverse
        bn_s[...] = normal
        k.bn[...] = normal.astype(bf16)
        k.send(k.bn)
        batch = normal * gain[5:6] + shift[5:6]
        swished = (batch * sigmoid(batch)).astype(bf16)
        k.sw[...] = swished
        k.send(k.sw)
        after_conv = k.stream[...] + dot(swished, k.convolve_out[...]) + bias[5:6]
        conv_s[...] = after_conv
        normal, _ = normalize(after_conv)
        k.nf[...] = (normal * gain[3:4] + shift[3:4]).astype(bf16)
        k.send(k.nf)
        for part in range(parts):
            cut = slice(part * PART, (part + 1) * PART)
            inner = dot(k.nf[...], k.w_in[part][...]) + k.b_in[1:2, cut]
            active, slope = activate(inner)
            k.act[:, cut] = active.astype(bf16)
            slope_s[:, cut] = slope
        k.send(k.act)
        branch = bias[7:8]
        for part in range(parts):
            cut = slice(part * PART, (part + 1) * PART)
            branch = branch + dot(k.act[:, cut], k.w_out[part][...])
        normal, inverse = normalize(conv_s[...] + 0.5 * branch)
        valid = jnp.concatenate(
            [valid_column(info, row, rows, frames) for row in range(rows)], axis=0
        )
        k.out[...] = (valid * (normal * gain[4:5] + shift[4:5])).astype(bf16)
        k.send(k.out)
        grad = valid * k.cotangent[...].astype(f32)
        grad, gain_grad, shift_grad = norm_back(grad, normal, inverse, gain[4:5])
        k.gcs[...] = grad
        low = (0.5 * grad).astype(bf16)
        k.gl[...] = low
        k.send(k.gl)
        vec = k.vec
        vec[2:3] = gain_grad
        vec[3:4] = shift_grad
        vec[5:6] = total(low.astype(f32))
        back = 0.0
        for part in range(parts):
            cut = slice(part * PART, (part + 1) * PART)
            grad = (dot_last(k.gl[...], k.w_out[part][...]) * slope_s[:, cut]).astype(bf16)
            k.gi[:, cut] = grad
            put_rows(k.fb, part, total(grad.astype(f32)))
            back = back + dot_last(grad, k.w_in[part][...])
        k.send(k.gi)
        normal, inverse = normalize(conv_s[...])
        grad, gain_grad, shift_grad = norm_back(back, normal, inverse, gain[3:4])
        vec[0:1] = gain_grad
        vec[1:2] = shift_grad
        grad = k.gcs[...] + grad
        k.gcs[...] = grad
        k.send(k.gcs)
        low = grad.astype(bf16)
        k.gcl[...] = low
        k.send(k.gcl)
        vec[4:5] = total(low.astype(f32))
        bn = bn_s[...]
        batch = bn * gain[5:6] + shift[5:6]
        _, slope = activate(batch)
        grad = dot_last(low, k.convolve_out[...]) * slope
        k.gb[...] = grad.astype(bf16)
        k.send(k.gb)
        pack(tile, [total(grad), total(grad * bn)])
        k.totals[...] = jnp.broadcast_to(tile[...][None], k.totals.shape)
        k.send(k.totals)
        for row in range(rows):
            at, end = row * frames, (row + 1) * frames
            k.first[row, :, :model] = grad[at : at + RIM_GRAD]
            k.first[row, :, model:] = bn[at : at + RIM_GRAD]
            k.last[row, :, :model] = grad[end - RIM_GRAD : end]
            k.last[row, :, model:] = bn[end - RIM_GRAD : end]

    w_in, w_out = feed_slabs(feed_in, feed_out, 1)
    ins = dict(
        gain=gain, shift=shift, depth=depth, bias=bias,
        convolve_out=convolve_out, stream=stream, b_in=feed_in_bias, w_in=w_in,
        cotangent=cotangent, w_out=w_out,
    )
    low = sds((tokens, model), bf16)
    wide = sds((tokens, model), f32)
    rim = sds((rows, RIM_GRAD, 2 * model), f32)
    return staged(
        "middle",
        body,
        ins,
        dict(
            out=low, act=sds((tokens, hidden), bf16), gi=sds((tokens, hidden), bf16), nf=low,
            gl=low, sw=low, gcl=low, gcs=wide, gb=low, bn=low, inv=sds((8, model), f32),
            totals=sds((devices, 8, 128), f32), first=rim, last=rim, vec=sds((8, model), f32),
            fb=sds((hidden // model, model), f32),
        ),
        smem=[info],
        scratch=[
            pltpu.VMEM((tokens, model), f32),
            pltpu.VMEM((tokens, model), f32),
            pltpu.VMEM((tokens, hidden), f32),
            pltpu.VMEM((8, 128), f32),
        ],
        kept=dict(stats=stats, counts=counts),
        flops=2 * tokens * model * (4 * hidden + 2 * model),
        moved=24 << 20,
    )


def conv_back(
    row_len, n, info, ends, taps, convolve_in, attend_out, gain, totals, mid, edge_before,
    edge_after, rim_before, rim_after, mix, early,
):
    tokens, model = mid.gb.shape
    rows = rim_before.shape[0]
    frames = tokens // rows
    slim = model // n
    room = slim % 8 == 0

    def body(k, info, grads, rim, keep_s, gp, gal):
        start = info[0].astype(f32)
        parts = model // 128
        sums = [total(k.totals[:, at, :]) for at in range(2 * parts)]
        total_a = jnp.concatenate(sums[:parts], axis=1)
        total_b = jnp.concatenate(sums[parts:], axis=1)
        inverse, per_count = k.inv[0:1], k.inv[1:2]
        gain, taps, vec = k.gain, k.taps, k.vec
        own_scale = inverse * gain[5:6]
        share_a = own_scale * total_a * per_count
        share_b = own_scale * total_b * per_count
        vec[14:15] = total_a
        vec[15:16] = total_b
        vec[0:9] = jnp.zeros((9, model), f32)
        vec[9:14] = jnp.zeros((5, model), f32)

        def grad_of(grad, normal, valid):
            grad = grad * own_scale - valid * (share_a + normal * share_b)
            return grad.astype(bf16).astype(f32)

        for row in range(rows):
            first = row * frames
            last = info[1 + rows + row].astype(f32)
            at = column(frames, start)
            low, high = bounds(k.ends[row : row + 1, :], at, row_len)
            tap_masks(keep_s, at, low, high)
            before, after = k.edge_before, k.edge_after
            edge_at = column(RIM_GRAD, start - RIM_GRAD)
            grads[0:RIM_GRAD] = grad_of(
                before[row, :, :model], before[row, :, model:], (edge_at < last).astype(f32)
            )
            for step in range(0, frames, 32):
                here = slice(step, step + 32)
                at = column(32, start + step)
                grads[RIM_GRAD + step : RIM_GRAD + step + 32] = grad_of(
                    k.gb[row][here].astype(f32),
                    k.bn[row][here].astype(f32),
                    (at < last).astype(f32),
                )
            edge_at = column(RIM_GRAD, start + frames)
            grads[RIM_GRAD + frames :] = grad_of(
                after[row, :, :model], after[row, :, model:], (edge_at < last).astype(f32)
            )
            rim[0:RIM] = k.rim_before[row].astype(f32)
            rim[RIM : RIM + frames] = k.gated[row][...].astype(f32)
            rim[RIM + frames :] = k.rim_after[row].astype(f32)
            factors = k.factors[row]
            half = frames // 2

            def one(i, carry):
                lane = pl.multiple_of(i * 128, 128)
                lanes, gates = pl.ds(lane, 128), pl.ds(model + lane, 128)
                for base in range(0, frames, half):
                    own = grads[RIM_GRAD + base : RIM_GRAD + base + half, lanes]
                    grad = jnp.zeros((half, 128), f32)
                    for tap in range(KERNEL):
                        off = base + tap - HALF
                        keep = keep_s[tap, base : base + half]
                        part = own * (rim[RIM + off : RIM + off + half, lanes] * keep)
                        vec[tap : tap + 1, lanes] += total(part)
                        mirror = KERNEL - 1 - tap
                        part = grads[RIM_GRAD + off : RIM_GRAD + off + half, lanes] * keep
                        grad += taps[mirror : mirror + 1, lanes] * part
                    one = (grad * factors[base : base + half, lanes].astype(f32)).astype(bf16)
                    two = (grad * factors[base : base + half, gates].astype(f32)).astype(bf16)
                    here = slice(first + base, first + base + half)
                    gp[here, lanes] = one
                    gp[here, gates] = two
                    vec[11:12, lanes] += total(one.astype(f32))
                    vec[12:13, lanes] += total(two.astype(f32))
                return carry

            lax.fori_loop(0, model // 128, one, 0)
        grad = dot_last(gp[...], k.convolve_in[...])
        normal, inverse = normalize(k.after[...])
        grad, gain_grad, shift_grad = norm_back(grad, normal, inverse, gain[2:3])
        vec[9:10] = gain_grad
        vec[10:11] = shift_grad
        grad = k.gcs[...] + grad
        k.gas[...] = grad
        k.send(k.gas)
        low = grad.astype(bf16)
        gal[...] = low
        vec[13:14] = total(low.astype(f32))
        k.gm[...] = dot_last(gal[...], k.attend_out[...]).astype(bf16)
        k.send(k.gm)
        out = k.early
        out[:, :slim] = dot_first(k.nc[...], gp[...]).astype(bf16).reshape(n, slim, 2 * model)
        block = dot_first(k.sw[...], k.gcl[...]).astype(bf16)
        out[:, slim:, :model] = block.reshape(n, slim, model)
        block = dot_first(k.mixed[...], gal[...]).astype(bf16)
        out[:, slim:, model:] = block.reshape(n, slim, model)

    own = (n, 2 * slim, 2 * model)
    size = early.shape[1] - 2 * slim
    if room:
        out = (sds(early.shape, bf16), lambda ref: ref.at[:, pl.ds(size, 2 * slim)], own)
    else:
        out = sds(own, bf16)
    got = staged(
        "conv_back",
        body,
        dict(
            inv=mid.inv, gain=gain, ends=ends, taps=taps, rim_before=rim_before,
            rim_after=rim_after, gb=by_row(mid.gb, rows), bn=by_row(mid.bn, rows), gated=by_row(mix.gated, rows),
            factors=by_row(mix.factors, rows), convolve_in=convolve_in, after=mix.out, gcs=mid.gcs,
            attend_out=attend_out, nc=mix.nc, sw=mid.sw, gcl=mid.gcl, mixed=mix.mixed,
        ),
        dict(
            early=out, gas=sds((tokens, model), f32), gm=sds((tokens, model), bf16),
            vec=sds((16, model), f32),
        ),
        smem=[info],
        scratch=[
            pltpu.VMEM((frames + 2 * RIM_GRAD, model), f32),
            pltpu.VMEM((frames + 2 * RIM, model), f32),
            pltpu.VMEM((KERNEL, frames, 128), f32),
            pltpu.VMEM((tokens, 2 * model), bf16),
            pltpu.VMEM((tokens, model), bf16),
        ],
        kept=dict(totals=totals, edge_before=edge_before, edge_after=edge_after),
        flops=2 * tokens * model * 7 * model,
        moved=16 << 20,
        filled=early if room else None,
    )
    if not room:
        got.early = jnp.concatenate([early, got.early], axis=1)
    return got


def attend_back(start, query, before, after, probs, gm):
    rows = before.shape[0]
    tokens, model = query.qu.shape
    frames = tokens // rows
    factor = 1.0 / math.sqrt(DH)

    def body(k, acc, turned):
        g_table, vec, table = k.g_table, k.vec, k.table
        g_table[...] = jnp.zeros_like(g_table)
        vec[...] = jnp.zeros_like(vec)
        turn = flip(WIN)
        for row in range(rows):
            acc[...] = jnp.zeros_like(acc)
            for block in range(2):
                here = slice(WIN * block, WIN * (block + 1))
                span = slice(WIN * block, WIN * block + SPAN)
                turned[0] = dot(turn, k.gm[row][here]).astype(bf16)
                turned[1] = dot(turn, k.qu[row][here]).astype(bf16)
                turned[2] = dot(turn, k.qv[row][here]).astype(bf16)
                blocks = [k.lo[row], k.hi[row]]
                blocks = blocks + [k.next[row]] if block else [k.before[row]] + blocks
                prob = k.prob[row]
                for group in range(GROUPS):
                    cut = slice(WIDE * group, WIDE * (group + 1))
                    cut_v = slice(model + WIDE * group, model + WIDE * (group + 1))
                    keys = jnp.concatenate([b[:, cut] for b in blocks], axis=0)
                    values = jnp.concatenate([b[:, cut_v] for b in blocks], axis=0)
                    weights = below(prob[block, group])
                    grad_mixed = heads_apart(turned[0, :, cut])
                    grad = dot_last(grad_mixed, values)
                    wide = weights.astype(f32)
                    delta = jnp.sum(wide * grad, axis=1, keepdims=True)
                    raw = (wide * (grad - delta)).astype(bf16)
                    acc[span, cut_v] += dot_first(weights, grad_mixed)
                    acc[span, cut] += dot_first(raw, heads_apart(turned[1, :, cut]))
                    grad_u = heads_joined(dot(raw, keys)) * factor
                    band = pltpu.roll(
                        raw.astype(f32).reshape(MANY, WIN, SPAN),
                        SPAN - (WIN - 1),
                        2,
                        stride=1,
                        stride_axis=1,
                    )
                    band = band.astype(bf16).reshape(MANY * WIN, SPAN)
                    grad_v = heads_joined(dot(band, table[:, cut])) * factor
                    g_table[:, cut] += dot_first(band, heads_apart(turned[2, :, cut]))
                    vec[0:1, cut] += total(grad_u)
                    vec[1:2, cut] += total(grad_v)
                    both = (grad_u + grad_v).astype(bf16)
                    k.gq[row][here, cut] = dot(turn, both).astype(bf16)
                if block == 0:
                    k.g_before[row] = acc[0:WIN].astype(bf16)
                    k.send(k.g_before, row)
            k.g_after[row] = acc[3 * WIN :].astype(bf16)
            k.send(k.g_after, row)
            k.g_lo[row][...] = acc[WIN : 2 * WIN]
            k.send(k.g_lo[row])
            k.g_hi[row][...] = acc[2 * WIN : 3 * WIN]
            k.send(k.g_hi[row])
            k.send(k.gq[row])

    ins = dict(
        table=query.table, gm=by_row(gm, rows), qu=by_row(query.qu, rows),
        qv=by_row(query.qv, rows), before=each_of(before), lo=each_of(start.lo),
        hi=each_of(start.hi), prob=list(probs), next=each_of(after),
    )
    kv = (WIN, 2 * model)
    return staged(
        "attend_back",
        body,
        ins,
        dict(
            gq=[sds((frames, model), bf16)] * rows, g_before=sds((rows,) + kv, bf16),
            g_lo=[sds(kv, f32)] * rows, g_hi=[sds(kv, f32)] * rows,
            g_after=sds((rows,) + kv, bf16), g_table=sds((SPAN, model), f32),
            vec=sds((8, model), f32),
        ),
        scratch=[
            pltpu.VMEM((4 * WIN, 2 * model), f32),
            pltpu.VMEM((3, WIN, model), bf16),
        ],
        flops=16 * 14 * 256 * 384 * 128,
        moved=16 << 20,
        sends=2 * rows - 2,
    )


def place_weights(info, core_at, n, grads, start, sinusoid):
    tokens, model = start.na.shape
    slim = model // n

    def body(k, info):
        core = info[core_at]
        pairs = (0, n // 2)
        rows = [ref[...] for ref in (k.gq[at] for at in range(len(grads.gq)))]
        block = dot_first(k.na[...], jnp.concatenate(rows, axis=0))
        keep_half(block, core, k.mine, k.other, pairs)
        high = k.g_table[...].astype(bf16)
        low = (k.g_table[...] - high.astype(f32)).astype(bf16)
        place = dot_first(k.sinusoid[...], high) + dot_first(k.sinusoid[...], low)
        keep_half(place, core, k.mine, k.other, pairs, slim)

    half = sds((n // 2, 2 * slim, model), bf16)
    return staged(
        "place_weights",
        body,
        dict(na=start.na, gq=list(grads.gq), g_table=grads.g_table, sinusoid=sinusoid),
        dict(mine=half, other=half),
        smem=[info],
        flops=2 * tokens * model * 2 * model,
        moved=4 << 20,
    )


def back(info, core_at, n, grads, halo, attend_in, start, gas, gain, placed):
    rows = len(grads.gq)
    tokens, model = start.after.shape
    frames = tokens // rows
    hidden = start.act.shape[1]
    parts = hidden // PART
    width, slim = hidden // n, model // n

    def body(k, info, joined):
        core = info[core_at]
        vec, gain = k.vec, k.gain
        sums = [0.0] * 5
        for row in range(rows):
            here = slice(row * frames, (row + 1) * frames)
            low_half = slice(row * frames, row * frames + WIN)
            high_half = slice(row * frames + WIN, (row + 1) * frames)
            joined[here, :model] = k.gq[row][...]
            pair = (k.g_lo[row][...] + k.left[row].astype(f32)).astype(bf16)
            joined[low_half, model:] = pair
            pair = (k.g_hi[row][...] + k.right[row].astype(f32)).astype(bf16)
            joined[high_half, model:] = pair
            both = joined[here]
            k.gv[here] = both[:, 2 * model :]
            sums[0] += total(both[:, :model].astype(f32))
            sums[1] += total(both[:, 2 * model :].astype(f32))
            grad = dot_last(both, k.attend_in[...])
            normal, inverse = normalize(k.after[row][...])
            grad, gain_grad, shift_grad = norm_back(grad, normal, inverse, gain[1:2])
            sums[2] += gain_grad
            sums[3] += shift_grad
            grad = k.gas[row][...] + grad
            k.gfs[row][...] = grad
            k.send(k.gfs[row])
            low = (0.5 * grad).astype(bf16)
            k.gl[here] = low
            sums[4] += total(low.astype(f32))
        k.send(k.gv)
        k.send(k.gl)
        for at in range(5):
            vec[at : at + 1] = sums[at]
        pairs = (0, n // 2)
        block = dot_first(k.na[...], joined[:, model : 2 * model])
        keep_half(block, core, k.mine, k.other, pairs, width + slim)
        for mine, placed in ((k.mine, k.mine_placed), (k.other, k.other_placed)):
            mine[:, width : width + slim] = placed[:, :slim]
            mine[:, width + 2 * slim :] = placed[:, slim:]
        step = n // 2 // parts
        for part in range(parts):
            block = dot_first(k.act[part][...], k.gl[...])
            some = (part * step, (part + 1) * step)
            keep_half(block, core, k.mine, k.other, some)
            k.send(k.other, pl.ds(part * step, step))
            k.send(k.mine, pl.ds(part * step, step))

    half = sds((n // 2, width + 3 * slim, model), bf16)
    low = sds((tokens, model), bf16)
    return staged(
        "back",
        body,
        dict(
            gain=gain, gq=grads.gq, g_lo=grads.g_lo, g_hi=grads.g_hi, attend_in=attend_in, after=by_row(start.after, rows),
            gas=by_row(gas, rows), na=start.na, mine_placed=placed.mine, other_placed=placed.other,
            act=[slab(start.act, (0, tokens), (at, PART)) for at in range(0, hidden, PART)],
        ),
        dict(
            other=half, mine=half, gv=low, gl=low, gfs=[sds((frames, model), f32)] * rows,
            vec=sds((8, model), f32),
        ),
        smem=[info],
        scratch=[pltpu.VMEM((tokens, 3 * model), bf16)],
        kept=dict(left=halo[0], right=halo[1]),
        flops=2 * tokens * model * (hidden + 6 * model),
        moved=18 << 20,
        sends=2 * parts - 2,
    )


def keep_half(block, core, mine_ref, other_ref, rows, at=0):
    model = mine_ref.shape[2]
    pairs = rows[1] - rows[0]
    size = block.shape[0] // (2 * pairs)
    shaped = block.reshape(pairs, 2, size, model)
    even, odd = shaped[:, 0], shaped[:, 1]
    here = slice(*rows)
    mine_ref[here, at : at + size] = jnp.where(core == 0, even, odd).astype(bf16)
    other_ref[here, at : at + size] = jnp.where(core == 0, odd, even).astype(bf16)


def first_back(info, core_at, n, gl, feed_in, feed_out, start, gv):
    tokens, hidden = start.slope.shape
    model = gl.shape[1]
    parts = hidden // PART

    def body(k, info):
        core = info[core_at]
        step = n // 2 // parts
        back = 0.0
        block = dot_first(k.na[...], k.gv[...])
        keep_half(block, core, k.mine, k.other, (0, n // 2), hidden // n)
        for part in range(parts):
            cut = slice(part * PART, (part + 1) * PART)
            grad = dot_last(k.gl[...], k.w_out[part][...])
            grad = (grad * k.slope[part][...].astype(f32)).astype(bf16)
            put_rows(k.fb, part, total(grad.astype(f32)))
            block = dot_first(grad, k.n0[...])
            some = (part * step, (part + 1) * step)
            keep_half(block, core, k.mine, k.other, some)
            k.send(k.other, pl.ds(part * step, step))
            k.send(k.mine, pl.ds(part * step, step))
            back = back + dot_last(grad, k.w_in[part][...])
        k.gn[...] = back

    half = sds((n // 2, hidden // n + model // n, model), bf16)
    w_in, w_out = feed_slabs(feed_in, feed_out, 0)
    return staged(
        "first_back",
        body,
        dict(
            na=start.na, gv=gv, gl=gl, w_out=w_out,
            slope=[slab(start.slope, (0, tokens), (at, PART)) for at in range(0, hidden, PART)],
            n0=start.n0, w_in=w_in,
        ),
        dict(other=half, mine=half, fb=sds((hidden // model, model), f32), gn=sds((tokens, model), f32)),
        smem=[info],
        flops=2 * tokens * model * hidden * 3,
        moved=12 << 20,
        sends=2 * parts - 2,
    )


def last(features, gn, gfs, gain):
    rows, frames, model = features.shape

    def body(k):
        gain_grads, shift_grads = 0.0, 0.0
        for row in range(rows):
            here = slice(row * frames, (row + 1) * frames)
            normal, inverse = normalize(k.x[row][...].astype(f32))
            grad = k.gn[row][...]
            grad, gain_grad, shift_grad = norm_back(grad, normal, inverse, k.gain[0:1])
            k.out[row] = k.gfs[row][...] + grad
            k.send(k.out, row)
            gain_grads += gain_grad
            shift_grads += shift_grad
        k.vec[0:1] = gain_grads
        k.vec[1:2] = shift_grads

    ins = dict(
        gain=gain, x=[slab(features, row, (0, frames), (0, model)) for row in range(rows)],
        gn=[slab(gn, (row * frames, frames), (0, model)) for row in range(rows)], gfs=list(gfs),
    )
    return staged(
        "last",
        body,
        ins,
        dict(out=sds(features.shape, f32), vec=sds((8, model), f32)),
        flops=rows * frames * model * 20,
        moved=4 << 20,
        sends=rows - 1,
        limit=FOLD_LIMIT,
    )


def feed_weights(n, gi, nf, act, gl):
    tokens, model = nf.shape
    hidden = gi.shape[1]
    parts = hidden // PART
    size, slim = hidden // n, model // n
    step = n // parts
    room = 2 * slim if slim % 8 == 0 else 0

    def body(k):
        for part in range(parts):
            here = slice(part * step, (part + 1) * step)
            block = dot_first(k.gi[part][...], k.nf[...]).astype(bf16)
            k.out[here, :, :model] = block.reshape(step, size, model)
            block = dot_first(k.act[part][...], k.gl[...]).astype(bf16)
            k.out[here, :, model:] = block.reshape(step, size, model)
            k.send(k.out, pl.ds(part * step, step))

    ins = dict(
        nf=nf, gi=[slab(gi, (0, tokens), (at, PART)) for at in range(0, hidden, PART)], gl=gl,
        act=[slab(act, (0, tokens), (at, PART)) for at in range(0, hidden, PART)],
    )
    own = (n, size, 2 * model)
    shape = sds((n, size + room, 2 * model), bf16)
    return staged(
        "feed_weights",
        body,
        ins,
        dict(out=(shape, lambda ref: ref.at[:, pl.ds(0, size)] if room else ref, own)),
        flops=4 * tokens * model * hidden,
        moved=10 << 20,
        sends=parts - 1,
    ).out


def neighbours(last_block, first_block):
    devices = lax.axis_size("frames")
    up = [(i, i + 1) for i in range(devices - 1)]
    down = [(i + 1, i) for i in range(devices - 1)]
    return lax.ppermute(last_block, "frames", up), lax.ppermute(first_block, "frames", down)


def gather(copies):
    return lax.all_to_all(copies, DEVICES, 0, 0, tiled=True)


def scatter_sum(grads):
    return lax.psum_scatter(grads, "frames", scatter_dimension=0, tiled=True)


ROW_PAIR = [(0, 1), (1, 0)]
COLUMNS, IN_FLOAT = 1, 2
N_VECTORS = KERNEL + 5 + 5 + 10


def swap(x, k):
    n = lax.axis_size("frames")
    return lax.ppermute(x, "frames", [(i, i ^ k) for i in range(n)])


def swaps(sends, group):
    k, size = group
    return [swap(send, k * one) for one, send in zip(range(1, size), sends)]


def fold(name, info, row_at, states, small=None):
    mines, gots, keeps, sends, plans = [], [], [], [], []
    for mine, got, how in states:
        size, height, model = mine.shape
        if isinstance(how, tuple):
            _, place, digits = how
            view = (size // (digits * place), digits, place, height, model)
            half = (view[0], place, height, model)
        else:
            view = mine.shape
            half = (size, height, model // 2) if how == COLUMNS else mine.shape
        n_sends = how[2] - 1 if isinstance(how, tuple) else int(how == COLUMNS)
        plans.append((len(gots), len(got), len(sends), n_sends, how))
        mines.append(mine.reshape(view))
        gots += [one.reshape(view) for one in got]
        keeps.append(sds(half, f32 if how == IN_FLOAT else bf16))
        sends += [sds(half, bf16)] * n_sends

    n_small = 0 if small is None else len(small)

    def body(info, *refs):
        cuts = [len(mines), len(gots), n_small, len(keeps), len(sends)]
        taken, at = [], 0
        for cut in cuts:
            taken.append(refs[at : at + cut])
            at += cut
        mine_refs, got_refs, small_refs, keep_refs, send_refs = taken
        for at, (got_at, n_got, send_at, _, how) in enumerate(plans):
            parts = [mine_refs[at], *got_refs[got_at : got_at + n_got]]

            def added(*index):
                return sum(part[index].astype(f32) for part in parts)

            keep = keep_refs[at]
            if how is None or how == IN_FLOAT:
                keep[...] = added(...).astype(keep.dtype)
            elif how == COLUMNS:
                half = keep.shape[2]
                both = [
                    added(slice(None), slice(None), slice(one * half, (one + 1) * half))
                    for one in range(2)
                ]
                first = info[row_at] == 0
                send_refs[send_at][...] = jnp.where(first, both[1], both[0]).astype(bf16)
                keep[...] = jnp.where(first, both[0], both[1]).astype(bf16)
            else:
                digit = info[how[0]]
                for one in range(1, how[2]):
                    other = digit
                    for bit in (1, 2):
                        if one & bit:
                            other = other + bit * (1 - 2 * ((digit // bit) % 2))
                    send_refs[send_at + one - 1][...] = added(slice(None), other).astype(bf16)
                keep[...] = added(slice(None), digit).astype(bf16)
        if n_small:
            refs[-1][...] = sum(one[...] for one in small_refs)

    shapes = keeps + sends + ([sds(small[0].shape, f32)] if n_small else [])
    here = pl.BlockSpec(memory_space=pltpu.VMEM)
    given = mines + gots + (list(small) if n_small else [])
    got = pl.pallas_call(
        body,
        in_specs=[pl.BlockSpec(memory_space=pltpu.SMEM)] + [here] * len(given),
        out_specs=[here] * len(shapes),
        out_shape=shapes,
        compiler_params=pltpu.CompilerParams(vmem_limit_bytes=FOLD_LIMIT),
        cost_estimate=pl.CostEstimate(flops=1 << 20, bytes_accessed=2 << 20, transcendentals=0),
        name=name,
    )(info, *given)
    kept, away = got[: len(keeps)], got[len(keeps) : len(keeps) + len(sends)]
    results = []
    for at, (mine, _, how) in enumerate(states):
        size, height, model = mine.shape
        shape = (size // how[2], height, model) if isinstance(how, tuple) else kept[at].shape
        _, _, send_at, n_sends, _ = plans[at]
        some = [one.reshape(shape) for one in away[send_at : send_at + n_sends]]
        results.append((kept[at].reshape(shape), some))
    if n_small:
        results.append(got[-1])
    return results


def finish(info, row_at, frames, a, b, b_got, early, small, totals, width, slim):
    model = a.shape[1]
    feed_rows = small[0].shape[0] - N_VECTORS
    per = feed_rows // 2

    def body(info, a, b, b_got, early, totals, *refs):
        sums, refs = refs[: len(small)], refs[len(small) :]
        feed_in, feed_out, joined, attend, place, con_in, con_out, *refs = refs
        depth, gain, shift, bias, feed_bias, vectors = refs
        feed_in[0] = a[:width].T
        feed_in[1] = early[:width, :model].T
        first = info[row_at] == 0
        one, two = b[...].astype(f32), b_got[...].astype(f32)
        whole = jnp.concatenate([jnp.where(first, one, two), jnp.where(first, two, one)], axis=1)
        feed_out[0] = whole[:width]
        feed_out[1] = early[:width, model:]
        joined[:, :model] = whole[width : width + slim]
        joined[:, model : 2 * model] = whole[width + slim : width + 2 * slim]
        joined[:, 2 * model :] = a[width:]
        place[...] = whole[width + 2 * slim :]
        con_in[...] = early[width : width + slim]
        con_out[...] = early[width + slim :, :model]
        attend[...] = early[width + slim :, model:]
        me = info[0] // frames
        end = N_VECTORS + feed_rows
        vectors[end:] = jnp.zeros((vectors.shape[0] - end, model), f32)
        vectors[:end] = sum(one[...] for one in sums)
        vectors[end : end + 2] = totals[...]
        own = pltpu.roll(vectors[...], lax.rem(model - me * slim, model), 1)[:, :slim]
        depth[...] = own[:KERNEL]
        gain[0:5] = own[KERNEL : KERNEL + 5]
        gain[5:6] = own[end + 1 : end + 2]
        shift[0:5] = own[KERNEL + 5 : KERNEL + 10]
        shift[5:6] = own[end : end + 1]
        bias[...] = own[KERNEL + 10 : N_VECTORS]
        at = me * width
        for module in range(2):
            row = vectors[pl.ds(N_VECTORS + module * per + at // model, 1), :]
            row = pltpu.roll(row, lax.rem(model - lax.rem(at, model), model), 1)
            feed_bias[module : module + 1] = row[:, :width]

    def full(shape):
        return pl.BlockSpec(shape, lambda i: (0,) * len(shape))

    shapes = [
        (2, model, width), (2, width, model), (slim, 3 * model), (slim, model), (slim, model),
        (slim, 2 * model), (slim, model), (KERNEL, slim), (6, slim), (6, slim), (10, slim),
        (2, width),
    ]
    given = (a, b, b_got, early, totals, *small)
    return pl.pallas_call(
        body,
        grid=(1,),
        in_specs=[pl.BlockSpec(memory_space=pltpu.SMEM)] + [full(one.shape) for one in given],
        out_specs=[full(shape) for shape in shapes],
        out_shape=[sds(shape, f32) for shape in shapes],
        scratch_shapes=[pltpu.VMEM((-(-(N_VECTORS + feed_rows + 2) // 8) * 8, model), f32)],
        compiler_params=pltpu.CompilerParams(vmem_limit_bytes=FOLD_LIMIT),
        name="finish",
    )(info, *given)


def per_device(
    features,
    lengths,
    windows,
    feed_in,
    feed_in_bias,
    feed_out,
    attend_in,
    attend_out,
    position_proj,
    convolve_in,
    convolve_out,
    depthwise,
    norm_gain,
    norm_shift,
    biases,
    cotangent,
):
    rows, frames, model = features.shape
    tokens = rows * frames
    n = lax.axis_size("frames")
    devices = lax.axis_size("rows") * n
    row_len = float(frames * n)
    me = lax.axis_index("frames")
    first_frame = me * frames
    hidden = feed_in.shape[2]
    ends_every = jnp.cumsum(lengths, axis=1, dtype=jnp.int32)
    ends_here = lax.dynamic_slice_in_dim(ends_every, lax.axis_index("rows") * rows, rows, 0)
    slots = ends_here.shape[1]
    ends = jnp.pad(
        ends_here.astype(f32), ((0, 8 - rows), (0, -slots % 128)), constant_values=row_len
    )
    groups, k = [(2, 2)], 4
    while k < n:
        groups.append((k, min(4, n // k)))
        k *= groups[-1][1]
    places = [lax.axis_index("rows"), me % 2] + [(me // k) % size for k, size in groups]
    info = jnp.concatenate(
        [first_frame[None].astype(jnp.int32), windows, ends_here[:, -1], jnp.stack(places)]
    )
    row_at = 1 + 2 * rows
    core_at = row_at + 1
    starts = jnp.arange(n, dtype=jnp.int32) * frames
    counts = jnp.clip(ends_every[:, -1][:, None] - starts[None, :], 0, frames)
    counts = jnp.sum(counts.reshape(-1, rows, n), axis=1).astype(f32).reshape(devices, 1)
    counts = jnp.broadcast_to(counts, (devices, 128))
    sinusoid = jnp.asarray(position_table(WIN, model))

    start = front(
        features, feed_in, feed_in_bias, feed_out, attend_in, norm_gain, norm_shift, biases
    )
    before, after = neighbours(start.hi, start.lo)
    query = queries(
        start, feed_in, feed_in_bias, attend_in, biases, sinusoid, position_proj
    )
    start.slope = query.slope
    mix = attend(
        row_len, info, ends, start, query, before, after, attend_out, convolve_in, norm_gain,
        norm_shift, biases,
    )
    rim_before, rim_after = neighbours(mix.last, mix.first)
    got = depth_conv(row_len, devices, info, ends, mix.gated, rim_before, rim_after, depthwise)
    mid = middle(
        devices, rows, info, gather(got.stats), counts, got.depth, mix.out, feed_in,
        feed_in_bias, feed_out, convolve_out, norm_gain, norm_shift, biases,
        cotangent.reshape(tokens, model),
    )
    edge_before, edge_after = neighbours(mid.last, mid.first)
    totals = gather(mid.totals)
    early = feed_weights(n, mid.gi, mid.nf, mid.act, mid.gl)
    totals, early = lax.optimization_barrier((totals, early))
    conv = conv_back(
        row_len, n, info, ends, depthwise, convolve_in, attend_out, norm_gain, totals, mid,
        edge_before, edge_after, rim_before, rim_after, mix, early,
    )
    early, gm = lax.optimization_barrier((conv.early, conv.gm))
    early = scatter_sum(early)
    grads = attend_back(start, query, before, after, mix.prob, gm)
    halo = neighbours(grads.g_after, grads.g_before)
    placed = place_weights(info, core_at, n, grads, start, sinusoid)
    end = back(info, core_at, n, grads, halo, attend_in, start, conv.gas, norm_gain, placed)
    b, b_got = end.mine, [swap(end.other, 1)]
    got = first_back(info, core_at, n, end.gl, feed_in, feed_out, start, end.gv)
    a, a_got = got.mine, [swap(got.other, 1)]
    ((b, b_send),) = fold("fold_b", info, row_at, [(b, b_got, COLUMNS)])
    b_got = [lax.ppermute(b_send[0], "rows", ROW_PAIR)]
    ((a, a_send),) = fold("fold_a", info, row_at, [(a, a_got, (core_at + 1, 1, 2))])
    a_got = swaps(a_send, groups[0])
    gn, a = lax.optimization_barrier((got.gn, a))
    ending = last(features, gn, end.gfs, norm_gain)

    vec_conv, vec_mid, vec_back, vec_last = conv.vec, mid.vec, end.vec, ending.vec
    small = jnp.concatenate(
        [
            vec_conv[:KERNEL],
            vec_last[0:1], vec_back[2:3], vec_conv[9:10], vec_mid[0:1], vec_mid[2:3],
            vec_last[1:2], vec_back[3:4], vec_conv[10:11], vec_mid[1:2], vec_mid[3:4],
            vec_back[0:2], vec_conv[13:14], vec_conv[11:13], vec_mid[4:5], vec_back[4:5],
            vec_mid[5:6], grads.vec[0:2],
            got.fb, mid.fb,
        ],
        axis=0,
    )
    small = [small] + swaps([small] * 3, (1, 4))
    last_group = groups[-1]
    for at, group in enumerate(groups):
        deeper = at + 1 < len(groups)
        a_how = (core_at + 2 + at, 1, groups[at + 1][1]) if deeper else None
        states = [(a, a_got, a_how), (b, b_got, (core_at + 1 + at, 1, group[1]))]
        (a, a_send), (b, b_send), one = fold(f"fold_{at}", info, row_at, states, small)
        if deeper:
            a_got = swaps(a_send, groups[at + 1])
        else:
            early, a = lax.optimization_barrier((early, a))
            a_got = [lax.ppermute(a, "rows", ROW_PAIR)]
            early_got = [lax.ppermute(early, "rows", ROW_PAIR)]
        b_got = swaps(b_send, group)
        if at == 0:
            small = [one, lax.ppermute(one, "rows", ROW_PAIR)]
        elif deeper:
            small = [one] + swaps([one] * (group[1] - 1), group)
    states = [(b, b_got, None), (a, a_got, IN_FLOAT), (early, early_got, IN_FLOAT)]
    (b, _), (a, _), (early, _) = fold("fold_last", info, row_at, states)
    b_got = lax.ppermute(b, "rows", ROW_PAIR)
    small = [one] + swaps([one] * (last_group[1] - 1), last_group)
    slim = model // n
    width = hidden // n
    feed_in_grad, feed_out_grad, joined, *rest, depth, gain, shift, bias, feed_bias = finish(
        info, row_at, frames, a[0], b[0], b_got[0], early[0], small, vec_conv[14:16], width, slim
    )
    return (
        mid.out.reshape(rows, frames, model),
        ending.out,
        feed_in_grad,
        feed_bias,
        feed_out_grad,
        joined,
        *rest,
        depth,
        gain,
        shift,
        bias,
    )


def solution(mesh):
    placed = (
        P("rows", "frames", None),
        P(),
        P("rows"),
        P(),
        P(),
        P(),
        P(),
        P(),
        P(),
        P(),
        P(),
        P(),
        P(),
        P(),
        P(),
        P("rows", "frames", None),
    )
    return jax.shard_map(
        per_device,
        mesh=mesh,
        in_specs=placed,
        out_specs=(
            P("rows", "frames", None),
            P("rows", "frames", None),
            P(None, None, "frames"),
            P(None, "frames"),
            P(None, "frames", None),
            P("frames", None),
            P("frames", None),
            P("frames", None),
            P("frames", None),
            P("frames", None),
            P(None, "frames"),
            P(None, "frames"),
            P(None, "frames"),
            P(None, "frames"),
        ),
        check_vma=False,
    )
```
